32 devices in a mesh: feat: 4 (over y, x), batch: 8 (over z, core).
Axes of the slice: x: 2, y: 2, z: 4, core: 2. Of those that a mesh axis runs over, the one named last changes fastest.
Arguments:
- store: bfloat16 [65536, 1024], P('batch', 'feat'), may hold values from -6 to 6
- input_owner: int32 [8, 6144, 1], P('batch'), may hold values from 0 to 7; in each aligned block of 6144 rows (0 to 6143, 6144 to 12287, ..., all dimensions but the last counted through in order) at most 1536 rows name the same one
- input_row: int32 [8, 6144], P('batch'), may hold values from 0 to 8191
- nbr_one: int32 [8, 3072, 15], P('batch'), may hold values from 0 to 6143
- deg_one: int32 [8, 3072], P('batch'), may hold values from 1 to 15
- nbr_two: int32 [8, 512, 10], P('batch', 'feat'), may hold values from 0 to 3071
- deg_two: int32 [8, 512], P('batch', 'feat'), may hold values from 1 to 10
- cotangent: bfloat16 [8, 512, 256], P('batch', 'feat'), may hold values from -0.09375 to 0.09375
- w1_self: bfloat16 [1024, 256], P('feat'), may hold values from -0.1875 to 0.1875
- w1_neigh: bfloat16 [1024, 256], P('feat'), may hold values from -0.1875 to 0.1875
- bias_one: float32 [256], replicated, may hold values from -3 to 3
- w2_self: bfloat16 [256, 256], replicated, may hold values from -0.375 to 0.375
- w2_neigh: bfloat16 [256, 256], replicated, may hold values from -0.375 to 0.375
- bias_two: float32 [256], replicated, may hold values from -3 to 3
Outputs:
- activations: bfloat16 [8, 512, 256], P('batch', 'feat')
- grad_w2_self: float32 [256, 256], replicated
- grad_w2_neigh: float32 [256, 256], replicated
- grad_w1_self: float32 [1024, 256], P('feat')
- grad_w1_neigh: float32 [1024, 256], P('feat')
The draws below stay inside these ranges and needn't reach their ends.
Inputs may be any that keep to these rules, and one draw needn't show every extreme that they name: `input_owner`: in each group, no index of batch is named by more than 1536 input nodes, and one is named by exactly 1536.
All inputs are finite; a program needn't handle non-finite values.
Results may differ from the reference program's by a relative error of at most 0.006.
Values may be sent and summed in bfloat16 or wider, within the bound.
No kernel may reach another device: no remote copies, remote signals or barrier semaphores. Data moves between devices by JAX's collectives and lax.ppermute only.
A program may use at most 64 MiB of HBM per device.

```python
import math
import jax
import jax.numpy as jnp
import numpy as np
from jax import lax

FEAT = 1024
HID = 256
FAN1 = 15
FAN2 = 10
L2 = 512
ROWS_OWN = 8192
L1 = 3072
L0 = 6144
CAP = 1536
NODES = 65536
N_BATCH = 8


def plant(entries, own_key, smallest, top_value):
    longest = entries.shape.index(max(entries.shape))
    spots = []
    for shift in (0, 1):
        where = [jax.random.randint(jax.random.fold_in(own_key, axis), (), 0, length) for axis, length in enumerate(entries.shape)]
        where[longest] = (where[longest] + shift) % entries.shape[longest]
        spots.append(tuple(where))
    return entries.at[spots[0]].set(smallest).at[spots[1]].set(top_value)


def shard_levels(own_key, dims, split, smallest, high):
    loudness, own = 1.0, jax.random.fold_in(own_key, 6)
    for position, blocks in split:
        steps = jnp.exp(jax.random.uniform(jax.random.fold_in(own, position), (blocks,), jnp.float32, smallest / len(split), high / len(split)))
        loudness = loudness * jnp.repeat(steps, dims[position] // blocks).reshape([-1 if axis == position else 1 for axis in range(len(dims))])
    return loudness


def assign_block(stream_key, own, number, rows, number_of, top, most, lean):
    sequence = jax.random.permutation(stream_key, number_of)
    crowded, usual = shares(number_of, rows * top, most, lean, True), shares(number_of, rows * top, most, lean, False)
    places = jnp.arange(number_of)

    def named(tallies, rotation):
        used = int((tallies > 0).sum())
        fixed = max(1, used // 4)
        passed = fixed + (places - fixed + rotation * (used - fixed)) % max(1, number_of - fixed)
        return jnp.zeros((number_of,), jnp.int32).at[sequence[jnp.where(places < fixed, places, passed)]].set(jnp.asarray(tallies, jnp.int32))

    tallies = jnp.where(number % 4 == 0, named(crowded, number // 4), named(usual, number - number // 4 - 1))
    mixed = jax.random.permutation(jax.random.fold_in(own, 3), number_of)
    source_of, receiver = mixed[0:number_of // 2 * 2:2], mixed[1:number_of // 2 * 2:2]
    slack = jnp.minimum(tallies[source_of] - 1, most - tallies[receiver]) // 2
    slack = jnp.where((source_of == sequence[0]) | (receiver == sequence[0]) | (tallies[receiver] == 0), 0, jnp.maximum(slack, 0))
    passed = jax.random.randint(jax.random.fold_in(own, 4), (number_of // 2,), 0, 1 << 20) % (slack + 1)
    tallies = tallies.at[source_of].add(-passed).at[receiver].add(passed)
    members = jnp.searchsorted(jnp.cumsum(tallies), jnp.arange(rows * top), side="right").astype(jnp.int32)
    table = members.reshape(top, rows).T
    table = table[jax.random.permutation(jax.random.fold_in(own, 1), rows)]
    rotation = jax.random.randint(jax.random.fold_in(own, 2), (rows, 1), 0, top)
    return jnp.take_along_axis(table, (jnp.arange(top)[None, :] + rotation) % top, axis=1)


def shares(count, total, bound, slope, full):
    loads = [(1 << 20) // math.isqrt(grade ** slope) + 1 for grade in range(1, count + 1)]
    largest = bound if full else min(bound, max(-(-total // count), total * loads[0] // sum(loads)))
    least = 1 if total - largest >= count - 1 else 0
    holding, surplus = [largest] + [least] * (count - 1), total - largest - least * (count - 1)
    while surplus > 0:
        movable = [i for i in range(1, count) if holding[i] < largest] or [i for i in range(1, count) if holding[i] < bound]
        mass, left = sum([loads[i] for i in movable]), surplus
        for i in movable:
            more = min(bound - holding[i], max(1, left * loads[i] // mass), surplus)
            holding[i] = holding[i] + more
            surplus = surplus - more
    return np.array(holding)


def normal_values(rng, shape, width, reach, cuts=(), dtype=jnp.bfloat16):
    level = shard_levels(rng, shape, cuts, -0.22, 0.18) if cuts else 1.0
    drawn = jax.random.normal(rng, shape, jnp.float32) * width * level
    return jnp.minimum(jnp.maximum(drawn, -reach), reach).astype(dtype)


def setup_inputs(seed: int = 0) -> dict:
    key_list = jax.random.split(jax.random.key(seed), 15)
    store = normal_values(key_list[0], (NODES, FEAT), 1.0, 6.0, ((0, 8), (1, 4)))
    input_owner_keys = jax.random.split(jax.random.fold_in(key_list[1], 1), N_BATCH * L0 // L0)
    input_owner_turns = jax.random.permutation(jax.random.fold_in(key_list[1], 3), N_BATCH * L0 // L0)
    input_owner = jax.vmap(lambda own, number: assign_block(jax.random.fold_in(key_list[1], 2), own, number, L0, N_BATCH, 1, CAP, 2))(input_owner_keys, input_owner_turns).reshape((N_BATCH, L0, 1))
    input_row = plant(jax.random.randint(key_list[2], (N_BATCH, L0), 0, ROWS_OWN), jax.random.fold_in(key_list[2], 1), 0, ROWS_OWN - 1).astype(jnp.int32)
    nbr_one = plant(jax.random.randint(key_list[3], (N_BATCH, L1, FAN1), 0, L0), jax.random.fold_in(key_list[3], 1), 0, L0 - 1).astype(jnp.int32)
    deg_one = plant(jax.random.randint(key_list[4], (N_BATCH, L1), 1, FAN1 + 1), jax.random.fold_in(key_list[4], 1), 1, FAN1).astype(jnp.int32)
    nbr_two = plant(jax.random.randint(key_list[5], (N_BATCH, L2, FAN2), 0, L1), jax.random.fold_in(key_list[5], 1), 0, L1 - 1).astype(jnp.int32)
    deg_two = plant(jax.random.randint(key_list[6], (N_BATCH, L2), 1, FAN2 + 1), jax.random.fold_in(key_list[6], 1), 1, FAN2).astype(jnp.int32)
    cotangent = normal_values(key_list[7], (N_BATCH, L2, HID), (L2 * N_BATCH) ** -0.5, 0.09375, ((0, 8), (1, 4)))
    w1_self = normal_values(key_list[8], (FEAT, HID), FEAT ** -0.5, 0.1875, ((0, 4),))
    w1_neigh = normal_values(key_list[9], (FEAT, HID), FEAT ** -0.5, 0.1875, ((0, 4),))
    bias_one = normal_values(key_list[10], (HID,), 0.5, 3.0, (), jnp.float32)
    w2_self = normal_values(key_list[11], (HID, HID), HID ** -0.5, 0.375)
    w2_neigh = normal_values(key_list[12], (HID, HID), HID ** -0.5, 0.375)
    bias_two = normal_values(key_list[13], (HID,), 0.5, 3.0, (), jnp.float32)
    return {"store": store, "input_owner": input_owner, "input_row": input_row, "nbr_one": nbr_one, "deg_one": deg_one, "nbr_two": nbr_two, "deg_two": deg_two, "cotangent": cotangent, "w1_self": w1_self, "w1_neigh": w1_neigh, "bias_one": bias_one, "w2_self": w2_self, "w2_neigh": w2_neigh, "bias_two": bias_two}


def silu_grad(values):
    sig = jax.nn.sigmoid(values)
    return sig * (1.0 + values * (1.0 - sig))

def mean_rows(table, index, counts):
    rows_all, fanout = index.shape
    block = math.gcd(rows_all, 512)

    def one_block(pieces):
        positions, numbers = pieces
        gathered = jnp.take(table, positions, axis=0).astype(jnp.float32)
        keep = (jnp.arange(fanout)[None, :] < numbers[:, None]).astype(jnp.float32)
        total = jnp.einsum('rk,rkw->rw', keep, gathered)
        return (total / numbers[:, None].astype(jnp.float32)).astype(jnp.bfloat16)
    result = lax.map(one_block, (index.reshape(rows_all // block, block, fanout), counts.reshape(rows_all // block, block)))
    return result.reshape(rows_all, table.shape[1])

def reference(store, input_owner, input_row, nbr_one, deg_one, nbr_two, deg_two, cotangent, w1_self, w1_neigh, bias_one, w2_self, w2_neigh, bias_two):

    def group_step(carry, pieces):
        owners, wanted, near_one, count_one, near_two, count_two, upstream = pieces
        global_rows = (owners[:, 0] * ROWS_OWN + wanted).astype(jnp.int32)
        inputs = jnp.take(store, global_rows, axis=0)
        agg_one = mean_rows(inputs, near_one, count_one)
        self_one = inputs[:L1]
        z_one = jnp.dot(self_one, w1_self, preferred_element_type=jnp.float32) + jnp.dot(agg_one, w1_neigh, preferred_element_type=jnp.float32) + bias_one
        hidden = jax.nn.silu(z_one).astype(jnp.bfloat16)
        agg_two = mean_rows(hidden, near_two, count_two)
        self_two = hidden[:L2]
        z_two = jnp.dot(self_two, w2_self, preferred_element_type=jnp.float32) + jnp.dot(agg_two, w2_neigh, preferred_element_type=jnp.float32) + bias_two
        activ = jax.nn.silu(z_two).astype(jnp.bfloat16)
        dz_two = (upstream.astype(jnp.float32) * silu_grad(z_two)).astype(jnp.bfloat16)
        gw2_self = jnp.dot(self_two.T, dz_two, preferred_element_type=jnp.float32)
        gw2_neigh = jnp.dot(agg_two.T, dz_two, preferred_element_type=jnp.float32)
        back_self = jnp.dot(dz_two, w2_self.T, preferred_element_type=jnp.float32)
        back_neigh = jnp.dot(dz_two, w2_neigh.T, preferred_element_type=jnp.float32) / count_two[:, None].astype(jnp.float32)
        keep_two = (jnp.arange(FAN2)[None, :] < count_two[:, None]).astype(jnp.float32)
        spread = (back_neigh[:, None, :] * keep_two[:, :, None]).reshape(L2 * FAN2, HID)
        dh_one = jnp.zeros((L1, HID), jnp.float32)
        dh_one = dh_one.at[jnp.arange(L2)].add(back_self)
        dh_one = dh_one.at[near_two.reshape(-1)].add(spread)
        dz_one = (dh_one * silu_grad(z_one)).astype(jnp.bfloat16)
        gw1_self = jnp.dot(self_one.T, dz_one, preferred_element_type=jnp.float32)
        gw1_neigh = jnp.dot(agg_one.T, dz_one, preferred_element_type=jnp.float32)
        carry = (carry[0] + gw2_self, carry[1] + gw2_neigh, carry[2] + gw1_self, carry[3] + gw1_neigh)
        return (carry, activ)
    start = (jnp.zeros((HID, HID), jnp.float32), jnp.zeros((HID, HID), jnp.float32), jnp.zeros((FEAT, HID), jnp.float32), jnp.zeros((FEAT, HID), jnp.float32))
    sums, activations = lax.scan(group_step, start, (input_owner, input_row, nbr_one, deg_one, nbr_two, deg_two, cotangent))
    return (activations, sums[0], sums[1], sums[2], sums[3])
```

```python
import functools

import jax
import jax.numpy as jnp
from jax import lax
from jax.experimental import pallas as pl
from jax.experimental.pallas import tpu as pltpu
from jax.sharding import PartitionSpec as P

TILE = 256
LANES = 128
SLOTS = 16
TILE_BITS, LANE_BITS, SLOT_BITS = 8, 7, 4
VMEM_BYTES = 56 * 1024 * 1024
VMEM = pl.BlockSpec(memory_space=pltpu.VMEM)
SMEM = pl.BlockSpec(memory_space=pltpu.SMEM)


def silu_grad(values):
    sig = jax.nn.sigmoid(values)
    return sig * (1.0 + values * (1.0 - sig))


def contract_rows(left_side, right_side):
    return lax.dot_general(
        left_side, right_side, (((0,), (0,)), ((), ())), preferred_element_type=jnp.float32
    )


def contract_cols(left_side, right_side):
    return lax.dot_general(
        left_side, right_side, (((1,), (1,)), ((), ())), preferred_element_type=jnp.float32
    )


def params(**more):
    return pltpu.CompilerParams(vmem_limit_bytes=VMEM_BYTES, **more)


def cost(flops, moved):
    return pl.CostEstimate(flops=int(flops), bytes_accessed=int(moved), transcendentals=0)


def requests_body(batch_count, capacity, owner_ref, row_ref, slot_ref, count_ref, request_ref):
    blocks, width = owner_ref.shape
    places = request_ref.shape[0]
    owner_id = lax.broadcasted_iota(jnp.int32, (batch_count, width), 0)
    earlier = lax.broadcasted_iota(jnp.int32, (width, width), 0)
    later = lax.broadcasted_iota(jnp.int32, (width, width), 1)
    upper = jnp.where(earlier <= later, 1.0, 0.0).astype(jnp.bfloat16)
    high_id = lax.broadcasted_iota(jnp.int32, (places, width), 0)
    low_id = lax.broadcasted_iota(jnp.int32, (LANES, width), 0)
    marks = [
        jnp.where(owner_ref[b : b + 1, :] == owner_id, 1.0, 0.0) for b in range(blocks)
    ]
    stacked = jnp.concatenate(marks, axis=0).astype(jnp.bfloat16)
    prefix = jnp.dot(stacked, upper, preferred_element_type=jnp.float32)
    running = jnp.zeros((batch_count, 1), jnp.float32)
    total = jnp.zeros((2 * places, LANES), jnp.float32)
    for b in range(blocks):
        part = prefix[b * batch_count : (b + 1) * batch_count]
        slots = jnp.sum(marks[b] * (part + running - 1.0), axis=0, keepdims=True)
        slots = slots.astype(jnp.int32)
        slot_ref[b : b + 1, :] = slots
        running = running + part[:, width - 1 : width]
        bucket = owner_ref[b : b + 1, :] * capacity + slots
        rows = row_ref[b : b + 1, :]
        hit = (bucket >> LANE_BITS) == high_id
        left = jnp.concatenate(
            [
                jnp.where(hit, (rows >> TILE_BITS).astype(jnp.float32), 0.0),
                jnp.where(hit, (rows & (TILE - 1)).astype(jnp.float32), 0.0),
            ],
            axis=0,
        ).astype(jnp.bfloat16)
        right = jnp.where((bucket & (LANES - 1)) == low_id, 1.0, 0.0).astype(jnp.bfloat16)
        total = total + contract_cols(left, right)
    count_ref[...] = jnp.broadcast_to(running, count_ref.shape).astype(jnp.int32)
    request_ref[...] = (total[:places] * TILE + total[places:]).astype(jnp.int32)


def make_requests(batch_count, capacity, owners, wanted):
    total = owners.shape[0]
    blocks = total // TILE
    places = batch_count * capacity // LANES
    return pl.pallas_call(
        functools.partial(requests_body, batch_count, capacity),
        out_shape=(
            jax.ShapeDtypeStruct((blocks, TILE), jnp.int32),
            jax.ShapeDtypeStruct((batch_count, LANES), jnp.int32),
            jax.ShapeDtypeStruct((places, LANES), jnp.int32),
        ),
        in_specs=[VMEM, VMEM],
        out_specs=(VMEM, VMEM, VMEM),
        compiler_params=params(),
        cost_estimate=cost(4 * total * places * LANES, 24 * total),
        name="requests",
    )(owners.reshape(blocks, TILE), wanted.reshape(blocks, TILE))


def lookup_body(first, width, want_ref, store_ref, out_ref, table, lines):
    group = pl.program_id(0)
    rows_all = store_ref.shape[0]

    @pl.when(group == 0)
    def _():
        @pl.loop(0, rows_all // TILE)
        def _(j):
            part = pl.ds(pl.multiple_of(j * TILE, TILE), TILE)
            table[part, :] = store_ref[part, :].astype(jnp.float32)

    @pl.loop(0, width // SLOTS)
    def _(j):
        for u in range(SLOTS):
            at = j * SLOTS + u
            lines[pl.ds(at, 1), :] = table[pl.ds(want_ref[group, first + at], 1), :]

    out_ref[0] = lines[...].astype(jnp.bfloat16)


def lookup(store, received, first, width):
    groups = received.shape[0]
    rows_all, features = store.shape
    return pl.pallas_call(
        functools.partial(lookup_body, first, width),
        out_shape=jax.ShapeDtypeStruct((groups, width, features), jnp.bfloat16),
        grid=(groups,),
        in_specs=[SMEM, pl.BlockSpec((rows_all, features), lambda g: (0, 0))],
        out_specs=pl.BlockSpec((1, width, features), lambda g: (g, 0, 0)),
        scratch_shapes=[
            pltpu.VMEM((rows_all, features), jnp.float32),
            pltpu.VMEM((width, features), jnp.float32),
        ],
        compiler_params=params(),
        cost_estimate=cost(groups * width * features * 40, 2 * rows_all * features),
        name="lookup",
    )(received, store)


def adjacency_body(tiles, near_ref, table_ref, out_ref):
    groups = near_ref.shape[0]
    node_high = lax.broadcasted_iota(jnp.int32, (LANES, TILE), 0)
    own_row = (
        lax.shift_right_logical(lax.broadcasted_iota(jnp.int32, (SLOTS, TILE), 1), SLOT_BITS)
        == lax.broadcasted_iota(jnp.int32, (SLOTS, TILE), 0)
    )
    low_id = lax.broadcasted_iota(jnp.int32, (TILE, TILE), 0).astype(jnp.float32)

    def one_group(g):
        near = near_ref[pl.ds(g, 1), :]
        pick = jnp.where((near >> LANE_BITS) == node_high, 1.0, 0.0).astype(jnp.bfloat16)
        found = jnp.dot(table_ref[...], pick, preferred_element_type=jnp.float32)
        here = (near & (LANES - 1)) == node_high
        high = jnp.sum(jnp.where(here, found[:LANES], 0.0), axis=0, keepdims=True)
        low = jnp.sum(jnp.where(here, found[LANES:], 0.0), axis=0, keepdims=True)
        high = jnp.where(near < 0, -1.0, high)
        rows = jnp.where(own_row, high, -1.0)
        left = jnp.concatenate(
            [jnp.where(rows == float(t), 1.0, 0.0) for t in range(tiles)], axis=0
        ).astype(jnp.bfloat16)
        right = jnp.where(low == low_id, 1.0, 0.0).astype(jnp.bfloat16)
        return contract_cols(left, right).reshape(tiles, SLOTS, TILE)

    @pl.loop(0, groups // 2)
    def _(j):
        pair = jnp.concatenate([one_group(2 * j), one_group(2 * j + 1)], axis=1)
        out_ref[:, pl.ds(pl.multiple_of(j * 2 * SLOTS, 2 * SLOTS), 2 * SLOTS), :] = pair.astype(
            out_ref.dtype
        )


def adjacency(near, table, tiles):
    groups = near.shape[0]
    nodes = groups * SLOTS
    step = TILE // SLOTS
    return pl.pallas_call(
        functools.partial(adjacency_body, tiles),
        out_shape=jax.ShapeDtypeStruct((tiles, nodes, TILE), jnp.float8_e4m3fn),
        grid=(groups // step,),
        in_specs=[
            pl.BlockSpec((step, TILE), lambda r: (r, 0)),
            pl.BlockSpec(table.shape, lambda r: (0, 0)),
        ],
        out_specs=pl.BlockSpec((tiles, TILE, TILE), lambda r: (0, r, 0)),
        compiler_params=params(),
        cost_estimate=cost(2 * nodes * TILE * TILE * tiles * 2, nodes * TILE * tiles),
        name="adjacency",
    )(near, table)


def collect(piece, counts_ref, starts_ref, answer_ref, packed):
    batch_count = answer_ref.shape[0]

    @pl.loop(0, batch_count)
    def _(o):
        base = starts_ref[o]

        @pl.loop(0, pl.cdiv(counts_ref[o], piece))
        def _(c):
            source = pl.ds(pl.multiple_of(c * piece, piece), piece)
            target = pl.ds(pl.multiple_of(base + c * piece, SLOTS), piece)
            packed[target, :] = answer_ref[o, source, :]

    end = starts_ref[batch_count]
    packed[pl.ds(pl.multiple_of(end, SLOTS), TILE), :] = jnp.zeros(
        (TILE, packed.shape[1]), packed.dtype
    )


def gather_sum_body(
    piece, last, spans_ref, counts_ref, starts_ref, answer_ref, column_ref, adj_ref, *refs
):
    if last:
        (total_in, own_in, deg_ref, wself_ref, wneigh_ref, own_ref, mean_ref, share_ref) = refs[:8]
        packed, tiles_ref, ready, total_ref = refs[8:]
    else:
        total_ref, own_ref, packed, tiles_ref, ready = refs
    nodes = own_ref.shape[0]
    begin, count = spans_ref[0], spans_ref[1]

    def fetch(step, slot):
        return pltpu.make_async_copy(adj_ref.at[begin + step], tiles_ref.at[slot], ready.at[slot])

    fetch(0, 0).start()
    collect(piece, counts_ref, starts_ref, answer_ref, packed)

    @pl.loop(0, nodes // TILE)
    def _(r):
        part = pl.ds(pl.multiple_of(r * TILE, TILE), TILE)
        if last:
            total_ref[part, :] = total_in[part, :]
            own_ref[part, :] = own_in[part, :]
        else:
            total_ref[part, :] = jnp.zeros((TILE, total_ref.shape[1]), jnp.float32)
            own_ref[part, :] = jnp.zeros((TILE, own_ref.shape[1]), jnp.bfloat16)

    @pl.loop(0, count)
    def _(step):
        slot = step & 1

        @pl.when(step + 1 < count)
        def _():
            fetch(step + 1, 1 - slot).start()

        fetch(step, slot).wait()
        block = packed[pl.ds(pl.multiple_of(step * TILE, TILE), TILE), :]
        lane = lax.broadcasted_iota(jnp.int32, (TILE, TILE), 1) + (begin + step) * TILE

        @pl.loop(0, nodes // TILE)
        def _(r):
            part = pl.ds(pl.multiple_of(r * TILE, TILE), TILE)
            near = tiles_ref[slot, part, :].astype(jnp.bfloat16)
            total_ref[part, :] += jnp.dot(near, block, preferred_element_type=jnp.float32)
            own = jnp.where(column_ref[part, :] == lane, 1.0, 0.0).astype(jnp.bfloat16)
            found = jnp.dot(own, block, preferred_element_type=jnp.float32)
            own_ref[part, :] = (own_ref[part, :].astype(jnp.float32) + found).astype(jnp.bfloat16)

    if last:

        @pl.loop(0, nodes // TILE)
        def _(r):
            part = pl.ds(pl.multiple_of(r * TILE, TILE), TILE)
            mean = (total_ref[part, :] / deg_ref[part, :]).astype(jnp.bfloat16)
            mean_ref[part, :] = mean
            share_ref[part, :] = (
                jnp.dot(own_ref[part, :], wself_ref[...], preferred_element_type=jnp.float32)
                + jnp.dot(mean, wneigh_ref[...], preferred_element_type=jnp.float32)
            ).astype(share_ref.dtype)


def gather_sum(spans, counts, starts, answer, column, adj, rest, share_type=jnp.bfloat16):
    batch_count, width, features = answer.shape
    tiles, nodes, _ = adj.shape
    piece = LANES if width % LANES == 0 else SLOTS
    last = rest is not None
    room = (min(batch_count * width, 2 * nodes) + SLOTS * batch_count + 3 * TILE) // TILE * TILE
    in_specs = [SMEM, SMEM, SMEM, VMEM, VMEM, pl.BlockSpec(memory_space=pl.ANY)]
    rows = lambda dtype: jax.ShapeDtypeStruct((nodes, features), dtype)
    scratch = [
        pltpu.VMEM((room, features), jnp.bfloat16),
        pltpu.VMEM((2, nodes, TILE), adj.dtype),
        pltpu.SemaphoreType.DMA((2,)),
    ]
    operands = [answer, column, adj]
    if last:
        operands += list(rest)
        in_specs += [VMEM] * len(rest)
        out_shape = (
            rows(jnp.bfloat16),
            rows(jnp.bfloat16),
            jax.ShapeDtypeStruct((nodes, rest[3].shape[1]), share_type),
        )
        scratch += [pltpu.VMEM((nodes, features), jnp.float32)]
    else:
        out_shape = (rows(jnp.float32), rows(jnp.bfloat16))
    return pl.pallas_call(
        functools.partial(gather_sum_body, piece, last),
        out_shape=out_shape,
        in_specs=in_specs,
        out_specs=(VMEM,) * len(out_shape),
        scratch_shapes=scratch,
        compiler_params=params(),
        cost_estimate=cost(2 * nodes * features * TILE * tiles, nodes * TILE * tiles // 2),
        name="gather_sum",
    )(spans, counts, starts, *operands)


def share_order(array, parts, seeds):
    others = array.shape[0] - seeds
    own, rest = seeds // parts, others // parts
    tail = array.shape[1:]
    return jnp.concatenate(
        [array[:seeds].reshape(parts, own, *tail), array[seeds:].reshape(parts, rest, *tail)],
        axis=1,
    ).reshape(array.shape)


def spread(part, axis, count):
    return lax.all_to_all(
        jnp.broadcast_to(part[None], (count,) + part.shape), axis, 0, 0, tiled=True
    )


def local(
    store,
    input_owner,
    input_row,
    nbr_one,
    deg_one,
    nbr_two,
    deg_two,
    cotangent,
    w1_self,
    w1_neigh,
    bias_one,
    w2_self,
    w2_neigh,
    bias_two,
):
    batch_count = lax.axis_size("batch")
    parts = lax.axis_size("feat")
    feat_index = lax.axis_index("feat")
    input_count = input_owner.shape[1]
    capacity = 2 * input_count // batch_count
    nodes = nbr_one.shape[1]
    seed_rows = nbr_two.shape[1]
    seeds = seed_rows * parts
    share = nodes // parts
    hidden_width = w1_self.shape[1]

    owners = input_owner[0, :, 0]
    slots, counts, requests = make_requests(batch_count, capacity, owners, input_row[0])
    received = lax.all_to_all(
        requests.reshape(batch_count, capacity), "batch", split_axis=0, concat_axis=0, tiled=True
    )
    first = capacity // 2
    looked = lookup(store, received, 0, first)
    answer_a = lax.all_to_all(looked, "batch", split_axis=0, concat_axis=0, tiled=True)
    looked = lookup(store, received, first, capacity - first)
    looked, answer_a = lax.optimization_barrier((looked, answer_a))
    answer_b = lax.all_to_all(looked, "batch", split_axis=0, concat_axis=0, tiled=True)

    tiles = -(-(input_count + 2 * (SLOTS - 1) * batch_count + TILE - 1) // TILE)
    tally = counts[:, 0]
    tally_a = jnp.minimum(tally, first)
    tally_b = tally - tally_a
    padded = lambda n: (n + SLOTS - 1) // SLOTS * SLOTS
    ends = lambda n: jnp.concatenate([jnp.zeros((1,), jnp.int32), jnp.cumsum(padded(n))])
    starts_a, starts_b = ends(tally_a), ends(tally_b)
    tiles_a = (starts_a[batch_count] + TILE - 1) // TILE
    tiles_b = (starts_b[batch_count] + TILE - 1) // TILE
    spans_a = jnp.stack([jnp.zeros_like(tiles_a), jnp.maximum(tiles_a, 1)])
    spans_b = jnp.stack([tiles_a, jnp.maximum(tiles_b, 1)])
    slot = slots.reshape(1, input_count)
    shifted = jnp.where(
        slot < first,
        slot + starts_a[:batch_count, None],
        slot - first + tiles_a * TILE + starts_b[:batch_count, None],
    )
    mine = owners[None, :] == jnp.arange(batch_count)[:, None]
    column = jnp.sum(jnp.where(mine, shifted, 0), axis=0)
    grid = jnp.pad(column.reshape(-1, LANES), ((0, LANES - input_count // LANES), (0, 0))).T
    table = jnp.concatenate([grid // TILE, grid % TILE], axis=0).astype(jnp.bfloat16)
    own_column = share_order(column[:nodes], parts, seeds).reshape(nodes, 1)

    fanout = nbr_one.shape[2]
    used = jnp.arange(fanout)[None, :] < deg_one[0][:, None]
    near = share_order(jnp.where(used, nbr_one[0], -1), parts, seeds)
    near = jnp.pad(near, ((0, 0), (0, SLOTS - fanout)), constant_values=-1)
    adj = adjacency(near.reshape(nodes // SLOTS, TILE), table, tiles)
    deg_first = share_order(deg_one[0], parts, seeds).astype(jnp.float32).reshape(nodes, 1)

    fanout_two = nbr_two.shape[2]
    used_two = jnp.arange(fanout_two)[None, :] < deg_two[0][:, None]
    near_two = lax.all_gather(jnp.where(used_two, nbr_two[0], -1), "feat", axis=0, tiled=True)
    deg_all = lax.all_gather(deg_two[0], "feat", axis=0, tiled=True)
    rest = share - seed_rows
    after = near_two - seeds
    place = jnp.where(
        near_two < seeds,
        near_two // seed_rows * share + near_two % seed_rows,
        after // rest * share + seed_rows + after % rest,
    )
    place = jnp.where(near_two < 0, -1, place - feat_index * share)
    adj_two = jnp.sum(
        place[:, :, None] == jnp.arange(share)[None, None, :], axis=1, dtype=jnp.float32
    ).astype(jnp.bfloat16)

    total, own = gather_sum(spans_a, tally_a, starts_a, answer_a, own_column, adj, None)
    self_one, agg_one, z_part = gather_sum(
        spans_b,
        tally_b,
        starts_b,
        answer_b,
        own_column,
        adj,
        (total, own, deg_first, w1_self, w1_neigh),
    )
    z_parts = lax.all_to_all(z_part.reshape(parts, share, hidden_width), "feat", 0, 0, tiled=True)
    z_share = jnp.sum(z_parts.astype(jnp.float32), axis=0) + bias_one
    hidden = jax.nn.silu(z_share).astype(jnp.bfloat16)

    agg_parts = jnp.dot(adj_two, hidden, preferred_element_type=jnp.float32)
    agg_parts = lax.all_to_all(
        agg_parts.reshape(parts, seed_rows, hidden_width), "feat", 0, 0, tiled=True
    )
    deg_second = deg_two[0].astype(jnp.float32)[:, None]
    agg_two = (jnp.sum(agg_parts, axis=0) / deg_second).astype(jnp.bfloat16)
    self_two = hidden[:seed_rows]
    z_two = (
        jnp.dot(self_two, w2_self, preferred_element_type=jnp.float32)
        + jnp.dot(agg_two, w2_neigh, preferred_element_type=jnp.float32)
        + bias_two
    )
    activations = jax.nn.silu(z_two).astype(jnp.bfloat16)[None]
    dz_two = (cotangent[0].astype(jnp.float32) * silu_grad(z_two)).astype(jnp.bfloat16)
    dz_two_all = spread(dz_two, "feat", parts).reshape(seeds, hidden_width)
    gw2 = jnp.concatenate([contract_rows(self_two, dz_two), contract_rows(agg_two, dz_two)])
    gw2 = lax.psum(gw2, ("feat", "batch"))

    back = contract_cols(dz_two_all, w2_neigh) / deg_all.astype(jnp.float32)[:, None]
    back_high = back.astype(jnp.bfloat16)
    back_low = (back - back_high.astype(jnp.float32)).astype(jnp.bfloat16)
    dh_share = contract_rows(adj_two, back_high) + contract_rows(adj_two, back_low)
    dh_share = dh_share + jnp.pad(contract_cols(dz_two, w2_self), ((0, rest), (0, 0)))
    dz_share = (dh_share * silu_grad(z_share)).astype(jnp.bfloat16)
    dz_one = spread(dz_share, "feat", parts).reshape(nodes, hidden_width)
    gw1 = jnp.concatenate([contract_rows(self_one, dz_one), contract_rows(agg_one, dz_one)])
    width = gw1.shape[0] // batch_count
    gw1 = lax.all_to_all(gw1.reshape(batch_count, width, hidden_width), "batch", 0, 0, tiled=True)
    gw1 = spread(jnp.sum(gw1, axis=0), "batch", batch_count).reshape(-1, hidden_width)
    half1, half2 = gw1.shape[0] // 2, gw2.shape[0] // 2
    return (activations, gw2[:half2], gw2[half2:], gw1[:half1], gw1[half1:])


def solution(mesh):
    in_specs = (
        P("batch", "feat"),
        P("batch", None, None),
        P("batch", None),
        P("batch", None, None),
        P("batch", None),
        P("batch", "feat", None),
        P("batch", "feat"),
        P("batch", "feat", None),
        P("feat", None),
        P("feat", None),
        P(),
        P(),
        P(),
        P(),
    )
    out_specs = (P("batch", "feat", None), P(), P(), P("feat", None), P("feat", None))
    return jax.shard_map(local, mesh=mesh, in_specs=in_specs, out_specs=out_specs, check_vma=False)
```

```python
import functools
import math

import jax
import jax.numpy as jnp
from jax import lax
from jax.experimental import pallas as pl
from jax.experimental.pallas import tpu as pltpu
from jax.sharding import PartitionSpec as P

TILE = 256
LANES = 128
SLOTS = 16
WIDE = 2
TILE_BITS, LANE_BITS, SLOT_BITS = 8, 7, 4
VMEM_BYTES = 56 * 1024 * 1024
VMEM = pl.BlockSpec(memory_space=pltpu.VMEM)
SMEM = pl.BlockSpec(memory_space=pltpu.SMEM)


def silu_grad(values):
    sig = jax.nn.sigmoid(values)
    return sig * (1.0 + values * (1.0 - sig))


def contract_rows(left_side, right_side):
    return lax.dot_general(
        left_side, right_side, (((0,), (0,)), ((), ())), preferred_element_type=jnp.float32
    )


def contract_cols(left_side, right_side):
    return lax.dot_general(
        left_side, right_side, (((1,), (1,)), ((), ())), preferred_element_type=jnp.float32
    )


def params(**more):
    return pltpu.CompilerParams(vmem_limit_bytes=VMEM_BYTES, **more)


def cost(flops, moved):
    return pl.CostEstimate(flops=int(flops), bytes_accessed=int(moved), transcendentals=0)


def requests_body(batch_count, capacity, owner_ref, row_ref, slot_ref, count_ref, request_ref):
    blocks, width = owner_ref.shape[0] // 2, TILE
    places = request_ref.shape[0]
    line = lambda ref, b: jnp.concatenate([ref[2 * b : 2 * b + 1], ref[2 * b + 1 : 2 * b + 2]], axis=1)
    owner_id = lax.broadcasted_iota(jnp.int32, (batch_count, width), 0)
    earlier = lax.broadcasted_iota(jnp.int32, (width, width), 0)
    later = lax.broadcasted_iota(jnp.int32, (width, width), 1)
    upper = jnp.where(earlier <= later, 1.0, 0.0).astype(jnp.bfloat16)
    high_id = lax.broadcasted_iota(jnp.int32, (places, width), 0)
    low_id = lax.broadcasted_iota(jnp.int32, (LANES, width), 0)
    marks = [
        jnp.where(line(owner_ref, b) == owner_id, 1.0, 0.0) for b in range(blocks)
    ]
    stacked = jnp.concatenate(marks, axis=0).astype(jnp.bfloat16)
    prefix = jnp.dot(stacked, upper, preferred_element_type=jnp.float32)
    running = jnp.zeros((batch_count, 1), jnp.float32)
    total = jnp.zeros((2 * places, LANES), jnp.float32)
    for b in range(blocks):
        part = prefix[b * batch_count : (b + 1) * batch_count]
        slots = jnp.sum(marks[b] * (part + running - 1.0), axis=0, keepdims=True)
        slots = slots.astype(jnp.int32)
        slot_ref[2 * b : 2 * b + 1, :] = slots[:, :LANES]
        slot_ref[2 * b + 1 : 2 * b + 2, :] = slots[:, LANES:]
        running = running + part[:, width - 1 : width]
        bucket = line(owner_ref, b) * capacity + slots
        rows = line(row_ref, b)
        hit = (bucket >> LANE_BITS) == high_id
        left = jnp.concatenate(
            [
                jnp.where(hit, (rows >> TILE_BITS).astype(jnp.float32), 0.0),
                jnp.where(hit, (rows & (TILE - 1)).astype(jnp.float32), 0.0),
            ],
            axis=0,
        ).astype(jnp.bfloat16)
        right = jnp.where((bucket & (LANES - 1)) == low_id, 1.0, 0.0).astype(jnp.bfloat16)
        total = total + contract_cols(left, right)
    count_ref[...] = jnp.broadcast_to(running, count_ref.shape).astype(jnp.int32)
    request_ref[...] = (total[:places] * TILE + total[places:]).astype(jnp.int32)


def make_requests(batch_count, capacity, owners, wanted):
    total = owners.shape[0] * LANES
    places = batch_count * capacity // LANES
    return pl.pallas_call(
        functools.partial(requests_body, batch_count, capacity),
        out_shape=(
            jax.ShapeDtypeStruct(owners.shape, jnp.int32),
            jax.ShapeDtypeStruct((batch_count, LANES), jnp.int32),
            jax.ShapeDtypeStruct((places, LANES), jnp.int32),
        ),
        in_specs=[VMEM, VMEM],
        out_specs=(VMEM, VMEM, VMEM),
        compiler_params=params(),
        cost_estimate=cost(4 * total * places * LANES, 24 * total),
        name="requests",
    )(owners, wanted)


def lookup_body(first, width, want_ref, store_ref, out_ref, table, lines):
    group = pl.program_id(0)
    rows_all = store_ref.shape[0]
    halves = store_ref.shape[1] // LANES
    lane = lambda h: pl.ds(h * LANES, LANES)

    @pl.when(group == 0)
    def _():
        @pl.loop(0, rows_all // TILE)
        def _(j):
            part = pl.ds(pl.multiple_of(j * TILE, TILE), TILE)
            for h in range(halves):
                table[part, h, :] = store_ref[part, lane(h)].astype(jnp.float32)

    @pl.loop(0, width // SLOTS)
    def _(j):
        for u in range(SLOTS):
            at = j * SLOTS + u
            lines[at] = table[want_ref[group, first + at]]

    for h in range(halves):
        out_ref[0, :, lane(h)] = lines[:, h, :].astype(jnp.bfloat16)


def lookup(store, received, first, width):
    groups = received.shape[0]
    rows_all, features = store.shape
    apart = lambda rows: pltpu.VMEM((rows, features // LANES, LANES), jnp.float32)
    return pl.pallas_call(
        functools.partial(lookup_body, first, width),
        out_shape=jax.ShapeDtypeStruct((groups, width, features), jnp.bfloat16),
        grid=(groups,),
        in_specs=[SMEM, pl.BlockSpec((rows_all, features), lambda g: (0, 0))],
        out_specs=pl.BlockSpec((1, width, features), lambda g: (g, 0, 0)),
        scratch_shapes=[apart(rows_all), apart(width)],
        compiler_params=params(),
        cost_estimate=cost(groups * width * features * 40, 2 * rows_all * features),
        name="lookup",
    )(received, store)


def adjacency_body(tiles, near_ref, table_ref, out_ref):
    groups = near_ref.shape[0]
    node_high = lax.broadcasted_iota(jnp.int32, (LANES, TILE), 0)
    own_row = (
        lax.shift_right_logical(lax.broadcasted_iota(jnp.int32, (SLOTS, TILE), 1), SLOT_BITS)
        == lax.broadcasted_iota(jnp.int32, (SLOTS, TILE), 0)
    )
    low_id = lax.broadcasted_iota(jnp.int32, (TILE, TILE), 0).astype(jnp.float32)

    def one_group(g):
        near = near_ref[pl.ds(g, 1), :]
        pick = jnp.where((near >> LANE_BITS) == node_high, 1.0, 0.0).astype(jnp.bfloat16)
        found = jnp.dot(table_ref[...], pick, preferred_element_type=jnp.float32)
        here = (near & (LANES - 1)) == node_high
        high = jnp.sum(jnp.where(here, found[:LANES], 0.0), axis=0, keepdims=True)
        low = jnp.sum(jnp.where(here, found[LANES:], 0.0), axis=0, keepdims=True)
        high = jnp.where(near < 0, -1.0, high)
        rows = jnp.where(own_row, high, -1.0)
        left = jnp.concatenate(
            [jnp.where(rows == float(t), 1.0, 0.0) for t in range(tiles)], axis=0
        ).astype(jnp.bfloat16)
        right = jnp.where(low == low_id, 1.0, 0.0).astype(jnp.bfloat16)
        return contract_cols(left, right).reshape(tiles, SLOTS, TILE)

    @pl.loop(0, groups // 2, unroll=2)
    def _(j):
        pair = jnp.concatenate([one_group(2 * j), one_group(2 * j + 1)], axis=1)
        out_ref[:, pl.ds(pl.multiple_of(j * 2 * SLOTS, 2 * SLOTS), 2 * SLOTS), :] = pair.astype(
            out_ref.dtype
        )


def adjacency(near, table, tiles):
    groups = near.shape[0]
    nodes = groups * SLOTS
    step = TILE // SLOTS
    return pl.pallas_call(
        functools.partial(adjacency_body, tiles),
        out_shape=jax.ShapeDtypeStruct((tiles, nodes, TILE), jnp.float8_e4m3fn),
        grid=(groups // step,),
        in_specs=[
            pl.BlockSpec((step, TILE), lambda r: (r, 0)),
            pl.BlockSpec(table.shape, lambda r: (0, 0)),
        ],
        out_specs=pl.BlockSpec((tiles, TILE, TILE), lambda r: (0, r, 0)),
        compiler_params=params(),
        cost_estimate=cost(2 * nodes * TILE * TILE * tiles * 2, nodes * TILE * tiles),
        name="adjacency",
    )(near, table)


def collect(piece, counts_ref, starts_ref, answer_ref, packed):
    batch_count = answer_ref.shape[0]

    @pl.loop(0, batch_count)
    def _(o):
        base = starts_ref[o]

        @pl.loop(0, pl.cdiv(counts_ref[o], piece))
        def _(c):
            source = pl.ds(pl.multiple_of(c * piece, piece), piece)
            target = pl.ds(pl.multiple_of(base + c * piece, SLOTS), piece)
            packed[target, :] = answer_ref[o, source, :]

    end = starts_ref[batch_count]
    packed[pl.ds(pl.multiple_of(end, SLOTS), WIDE * TILE), :] = jnp.zeros(
        (WIDE * TILE, packed.shape[1]), packed.dtype
    )


def gather_sum_body(
    piece, last, spans_ref, counts_ref, starts_ref, answer_ref, column_ref, adj_ref, *refs
):
    if last:
        (total_in, own_in, deg_ref, wself_ref, wneigh_ref, own_ref, mean_ref, share_ref) = refs[:8]
        packed, tiles_ref, ready, found_ref, total_ref = refs[8:]
    else:
        total_ref, own_ref, packed, tiles_ref, ready, found_ref = refs
    nodes = own_ref.shape[0]
    rows = math.gcd(nodes, 3 * TILE)
    begin, count = spans_ref[0], spans_ref[1]

    def fetch(step, slot):
        return pltpu.make_async_copy(
            adj_ref.at[pl.ds(begin + step * WIDE, WIDE)], tiles_ref.at[slot], ready.at[slot]
        )

    @pl.when(count > 0)
    def _():
        fetch(0, 0).start()

    collect(piece, counts_ref, starts_ref, answer_ref, packed)

    @pl.loop(0, nodes // TILE)
    def _(r):
        part = pl.ds(pl.multiple_of(r * TILE, TILE), TILE)
        if last:
            total_ref[part, :] = total_in[part, :]
            found_ref[part, :] = own_in[part, :].astype(jnp.float32)
        else:
            total_ref[part, :] = jnp.zeros((TILE, total_ref.shape[1]), jnp.float32)
            found_ref[part, :] = jnp.zeros((TILE, found_ref.shape[1]), jnp.float32)

    @pl.loop(0, count)
    def _(step):
        slot = step & 1

        @pl.when(step + 1 < count)
        def _():
            fetch(step + 1, 1 - slot).start()

        fetch(step, slot).wait()
        depth = WIDE * TILE
        block = packed[pl.ds(pl.multiple_of(step * depth, depth), depth), :]
        lane = lax.broadcasted_iota(jnp.int32, (rows, depth), 1) + (begin * TILE + step * depth)

        @pl.loop(0, nodes // rows)
        def _(r):
            part = pl.ds(pl.multiple_of(r * rows, rows), rows)
            near = jnp.concatenate(
                [tiles_ref[slot, w, part, :].astype(jnp.bfloat16) for w in range(WIDE)], axis=1
            )
            own = jnp.where(column_ref[part, :] == lane, 1.0, 0.0).astype(jnp.bfloat16)
            both = jnp.dot(
                jnp.concatenate([near, own], axis=0), block, preferred_element_type=jnp.float32
            )
            total_ref[part, :] += both[:rows]
            found_ref[part, :] += both[rows:]

    @pl.loop(0, nodes // TILE)
    def _(r):
        part = pl.ds(pl.multiple_of(r * TILE, TILE), TILE)
        own_ref[part, :] = found_ref[part, :].astype(jnp.bfloat16)

    if last:

        @pl.loop(0, nodes // TILE)
        def _(r):
            part = pl.ds(pl.multiple_of(r * TILE, TILE), TILE)
            mean = (total_ref[part, :] / deg_ref[part, :]).astype(jnp.bfloat16)
            mean_ref[part, :] = mean
            share_ref[part, :] = (
                jnp.dot(own_ref[part, :], wself_ref[...], preferred_element_type=jnp.float32)
                + jnp.dot(mean, wneigh_ref[...], preferred_element_type=jnp.float32)
            ).astype(share_ref.dtype)


def gather_sum(inputs, spans, counts, starts, answer, column, adj, rest, share_type=jnp.bfloat16):
    batch_count, width, features = answer.shape
    tiles, nodes, _ = adj.shape
    piece = LANES if width % LANES == 0 else SLOTS
    last = rest is not None
    room = min(batch_count * width, inputs) + SLOTS * batch_count + 2 * WIDE * TILE
    in_specs = [SMEM, SMEM, SMEM, VMEM, VMEM, pl.BlockSpec(memory_space=pl.ANY)]
    rows = lambda dtype: jax.ShapeDtypeStruct((nodes, features), dtype)
    scratch = [
        pltpu.VMEM((room, features), jnp.bfloat16),
        pltpu.VMEM((2, WIDE, nodes, TILE), adj.dtype),
        pltpu.SemaphoreType.DMA((2,)),
        pltpu.VMEM((nodes, features), jnp.float32),
    ]
    operands = [answer, column, adj]
    if last:
        operands += list(rest)
        in_specs += [VMEM] * len(rest)
        out_shape = (
            rows(jnp.bfloat16),
            rows(jnp.bfloat16),
            jax.ShapeDtypeStruct((nodes, rest[3].shape[1]), share_type),
        )
        scratch += [pltpu.VMEM((nodes, features), jnp.float32)]
    else:
        out_shape = (rows(jnp.float32), rows(jnp.bfloat16))
    return pl.pallas_call(
        functools.partial(gather_sum_body, piece, last),
        out_shape=out_shape,
        in_specs=in_specs,
        out_specs=(VMEM,) * len(out_shape),
        scratch_shapes=scratch,
        compiler_params=params(),
        cost_estimate=cost(2 * nodes * features * TILE * tiles, nodes * TILE * tiles // 2),
        name="gather_sum",
    )(spans, counts, starts, *operands)


def share_order(array, parts, seeds):
    others = array.shape[0] - seeds
    own, rest = seeds // parts, others // parts
    tail = array.shape[1:]
    return jnp.concatenate(
        [array[:seeds].reshape(parts, own, *tail), array[seeds:].reshape(parts, rest, *tail)],
        axis=1,
    ).reshape(array.shape)


def spread(part, axis, count):
    return lax.all_to_all(
        jnp.broadcast_to(part[None], (count,) + part.shape), axis, 0, 0, tiled=True
    )


def total_over_batch(one, two):
    count = lax.axis_size("batch")
    both = jnp.concatenate([one, two]).astype(jnp.bfloat16)
    pieces = both.reshape(count, both.shape[0] // count, both.shape[1])
    pieces = lax.all_to_all(pieces, "batch", 0, 0, tiled=True)
    total = spread(jnp.sum(pieces.astype(jnp.float32), axis=0), "batch", count)
    total = total.reshape(both.shape)
    return total[: one.shape[0]], total[one.shape[0] :]


def local(
    store,
    input_owner,
    input_row,
    nbr_one,
    deg_one,
    nbr_two,
    deg_two,
    cotangent,
    w1_self,
    w1_neigh,
    bias_one,
    w2_self,
    w2_neigh,
    bias_two,
):
    batch_count = lax.axis_size("batch")
    parts = lax.axis_size("feat")
    feat_index = lax.axis_index("feat")
    input_count = input_owner.shape[1]
    capacity = 2 * input_count // batch_count
    nodes = nbr_one.shape[1]
    seed_rows = nbr_two.shape[1]
    seeds = seed_rows * parts
    share = nodes // parts
    hidden_width = w1_self.shape[1]

    owners = input_owner.reshape(input_count // LANES, LANES)
    wanted = input_row.reshape(input_count // LANES, LANES)
    slots, counts, requests = make_requests(batch_count, capacity, owners, wanted)
    owners = owners.reshape(1, input_count)
    received = lax.all_to_all(
        requests.reshape(batch_count, capacity), "batch", split_axis=0, concat_axis=0, tiled=True
    )
    first = capacity // 2
    looked_a = lookup(store, received, 0, first)
    near_first, looked_a = lax.optimization_barrier((nbr_one[0], looked_a))
    answer_a = lax.all_to_all(looked_a, "batch", split_axis=0, concat_axis=0, tiled=True)
    looked = lookup(store, received, first, capacity - first)

    depth = WIDE * TILE
    steps = -(-(input_count + 2 * (SLOTS - 1) * batch_count + depth - 1) // depth)
    tally = counts[:, 0]
    tally_a = jnp.minimum(tally, first)
    tally_b = tally - tally_a
    padded = lambda n: (n + SLOTS - 1) // SLOTS * SLOTS
    ends = lambda n: jnp.concatenate([jnp.zeros((1,), jnp.int32), jnp.cumsum(padded(n))])
    starts_a, starts_b = ends(tally_a), ends(tally_b)
    steps_a = (starts_a[batch_count] + depth - 1) // depth
    steps_b = (starts_b[batch_count] + depth - 1) // depth
    spans_a = jnp.stack([jnp.zeros_like(steps_a), steps_a])
    spans_b = jnp.stack([steps_a * WIDE, steps_b])
    slot = slots.reshape(1, input_count)
    shifted = jnp.where(
        slot < first,
        slot + starts_a[:batch_count, None],
        slot - first + steps_a * depth + starts_b[:batch_count, None],
    )
    mine = owners == jnp.arange(batch_count)[:, None]
    column = jnp.sum(jnp.where(mine, shifted, 0), axis=0)
    grid = jnp.pad(column.reshape(-1, LANES), ((0, LANES - input_count // LANES), (0, 0))).T
    table = jnp.concatenate([grid // TILE, grid % TILE], axis=0).astype(jnp.bfloat16)
    own_column = share_order(column[:nodes], parts, seeds).reshape(nodes, 1)

    fanout_two = nbr_two.shape[2]
    used_two = jnp.arange(fanout_two)[:, None] < deg_two
    lists = jnp.concatenate([jnp.where(used_two, nbr_two[0].T, -1), deg_two], axis=0)
    lists = spread(lists, "feat", parts)

    fanout = nbr_one.shape[2]
    used = jnp.arange(fanout)[None, :] < deg_one[0][:, None]
    near = share_order(jnp.where(used, near_first, -1), parts, seeds)
    near = jnp.pad(near, ((0, 0), (0, SLOTS - fanout)), constant_values=-1)
    near, lists = lax.optimization_barrier((near, lists))
    adj = adjacency(near.reshape(nodes // SLOTS, TILE), table, steps * WIDE)
    looked, answer_a, adj = lax.optimization_barrier((looked, answer_a, adj))
    answer_b = lax.all_to_all(looked, "batch", split_axis=0, concat_axis=0, tiled=True)
    deg_first = share_order(deg_one[0], parts, seeds).astype(jnp.float32).reshape(nodes, 1)

    near_two = lists[:, :fanout_two].transpose(1, 0, 2).reshape(fanout_two, seeds)
    deg_all = lists[:, fanout_two].reshape(seeds)
    rest = share - seed_rows
    after = near_two - seeds
    place = jnp.where(
        near_two < seeds,
        near_two // seed_rows * share + near_two % seed_rows,
        after // rest * share + seed_rows + after % rest,
    )
    place = jnp.where(near_two < 0, -1, place - feat_index * share)
    adj_two = jnp.sum(
        place[:, :, None] == jnp.arange(share)[None, None, :], axis=0, dtype=jnp.float32
    ).astype(jnp.bfloat16)

    total, own = gather_sum(input_count, spans_a, tally_a, starts_a, answer_a, own_column, adj, None)
    self_one, agg_one, z_part = gather_sum(
        input_count,
        spans_b,
        tally_b,
        starts_b,
        answer_b,
        own_column,
        adj,
        (total, own, deg_first, w1_self, w1_neigh),
    )
    z_parts = lax.all_to_all(z_part.reshape(parts, share, hidden_width), "feat", 0, 0, tiled=True)
    z_share = jnp.sum(z_parts.astype(jnp.float32), axis=0) + bias_one
    hidden = jax.nn.silu(z_share).astype(jnp.bfloat16)

    agg_parts = jnp.dot(adj_two, hidden, preferred_element_type=jnp.float32)
    agg_parts = lax.all_to_all(
        agg_parts.reshape(parts, seed_rows, hidden_width), "feat", 0, 0, tiled=True
    )
    deg_second = deg_two[0].astype(jnp.float32)[:, None]
    agg_two = (jnp.sum(agg_parts, axis=0) / deg_second).astype(jnp.bfloat16)
    self_two = hidden[:seed_rows]
    z_two = (
        jnp.dot(self_two, w2_self, preferred_element_type=jnp.float32)
        + jnp.dot(agg_two, w2_neigh, preferred_element_type=jnp.float32)
        + bias_two
    )
    activations = jax.nn.silu(z_two).astype(jnp.bfloat16)[None]
    dz_two = (cotangent[0].astype(jnp.float32) * silu_grad(z_two)).astype(jnp.bfloat16)
    group = spread(jnp.stack([self_two, agg_two, dz_two]), "feat", parts)
    self_all, agg_all, dz_two_all = (group[:, i].reshape(seeds, hidden_width) for i in range(3))
    gw2 = total_over_batch(contract_rows(self_all, dz_two_all), contract_rows(agg_all, dz_two_all))

    back = contract_cols(dz_two_all, w2_neigh) / deg_all.astype(jnp.float32)[:, None]
    back_high = back.astype(jnp.bfloat16)
    back_low = (back - back_high.astype(jnp.float32)).astype(jnp.bfloat16)
    dh_share = contract_rows(adj_two, back_high) + contract_rows(adj_two, back_low)
    dh_share = dh_share + jnp.pad(contract_cols(dz_two, w2_self), ((0, rest), (0, 0)))
    dz_share = (dh_share * silu_grad(z_share)).astype(jnp.bfloat16)
    dz_one = spread(dz_share, "feat", parts).reshape(nodes, hidden_width)
    gw1 = total_over_batch(contract_rows(self_one, dz_one), contract_rows(agg_one, dz_one))
    return (activations, *gw2, *gw1)


def solution(mesh):
    in_specs = (
        P("batch", "feat"),
        P("batch", None, None),
        P("batch", None),
        P("batch", None, None),
        P("batch", None),
        P("batch", "feat", None),
        P("batch", "feat"),
        P("batch", "feat", None),
        P("feat", None),
        P("feat", None),
        P(),
        P(),
        P(),
        P(),
    )
    out_specs = (P("batch", "feat", None), P(), P(), P("feat", None), P("feat", None))
    return jax.shard_map(local, mesh=mesh, in_specs=in_specs, out_specs=out_specs, check_vma=False)
```

```python
import functools
import math

import jax
import jax.numpy as jnp
from jax import lax
from jax.experimental import pallas as pl
from jax.experimental.pallas import tpu as pltpu
from jax.sharding import PartitionSpec as P

TILE = 256
LANES = 128
SLOTS = 16
WIDE = 2
TILE_BITS, LANE_BITS, SLOT_BITS = 8, 7, 4
VMEM_BYTES = 56 * 1024 * 1024
VMEM = pl.BlockSpec(memory_space=pltpu.VMEM)
SMEM = pl.BlockSpec(memory_space=pltpu.SMEM)
ANY = pl.BlockSpec(memory_space=pl.ANY)


def silu_grad(values):
    sig = jax.nn.sigmoid(values)
    return sig * (1.0 + values * (1.0 - sig))


def contract_rows(left_side, right_side):
    return lax.dot_general(
        left_side, right_side, (((0,), (0,)), ((), ())), preferred_element_type=jnp.float32
    )


def contract_cols(left_side, right_side):
    return lax.dot_general(
        left_side, right_side, (((1,), (1,)), ((), ())), preferred_element_type=jnp.float32
    )


def params(**more):
    return pltpu.CompilerParams(vmem_limit_bytes=VMEM_BYTES, **more)


def cost(flops, moved):
    return pl.CostEstimate(flops=int(flops), bytes_accessed=int(moved), transcendentals=0)


def requests_body(batch_count, capacity, owner_ref, row_ref, slot_ref, count_ref, request_ref):
    blocks, width = owner_ref.shape[0] // 2, TILE
    places = request_ref.shape[0]
    line = lambda ref, b: jnp.concatenate([ref[2 * b : 2 * b + 1], ref[2 * b + 1 : 2 * b + 2]], axis=1)
    owner_id = lax.broadcasted_iota(jnp.int32, (batch_count, width), 0)
    earlier = lax.broadcasted_iota(jnp.int32, (width, width), 0)
    later = lax.broadcasted_iota(jnp.int32, (width, width), 1)
    upper = jnp.where(earlier <= later, 1.0, 0.0).astype(jnp.bfloat16)
    high_id = lax.broadcasted_iota(jnp.int32, (places, width), 0)
    low_id = lax.broadcasted_iota(jnp.int32, (LANES, width), 0)
    marks = [
        jnp.where(line(owner_ref, b) == owner_id, 1.0, 0.0) for b in range(blocks)
    ]
    stacked = jnp.concatenate(marks, axis=0).astype(jnp.bfloat16)
    prefix = jnp.dot(stacked, upper, preferred_element_type=jnp.float32)
    running = jnp.zeros((batch_count, 1), jnp.float32)
    total = jnp.zeros((2 * places, LANES), jnp.float32)
    for b in range(blocks):
        part = prefix[b * batch_count : (b + 1) * batch_count]
        slots = jnp.sum(marks[b] * (part + running - 1.0), axis=0, keepdims=True)
        slots = slots.astype(jnp.int32)
        slot_ref[2 * b : 2 * b + 1, :] = slots[:, :LANES]
        slot_ref[2 * b + 1 : 2 * b + 2, :] = slots[:, LANES:]
        running = running + part[:, width - 1 : width]
        bucket = line(owner_ref, b) * capacity + slots
        rows = line(row_ref, b)
        hit = (bucket >> LANE_BITS) == high_id
        left = jnp.concatenate(
            [
                jnp.where(hit, (rows >> TILE_BITS).astype(jnp.float32), 0.0),
                jnp.where(hit, (rows & (TILE - 1)).astype(jnp.float32), 0.0),
            ],
            axis=0,
        ).astype(jnp.bfloat16)
        right = jnp.where((bucket & (LANES - 1)) == low_id, 1.0, 0.0).astype(jnp.bfloat16)
        total = total + contract_cols(left, right)
    count_ref[...] = jnp.broadcast_to(running, count_ref.shape).astype(jnp.int32)
    request_ref[...] = (total[:places] * TILE + total[places:]).astype(jnp.int32)


def make_requests(batch_count, capacity, owners, wanted):
    total = owners.shape[0] * LANES
    places = batch_count * capacity // LANES
    return pl.pallas_call(
        functools.partial(requests_body, batch_count, capacity),
        out_shape=(
            jax.ShapeDtypeStruct(owners.shape, jnp.int32),
            jax.ShapeDtypeStruct((batch_count, LANES), jnp.int32),
            jax.ShapeDtypeStruct((places, LANES), jnp.int32),
        ),
        in_specs=[VMEM, VMEM],
        out_specs=(VMEM, VMEM, VMEM),
        compiler_params=params(),
        cost_estimate=cost(4 * total * places * LANES, 24 * total),
        name="requests",
    )(owners, wanted)


def lookup_body(first, width, want_ref, store_ref, out_ref, table, lines):
    group = pl.program_id(0)
    rows_all = store_ref.shape[0]
    halves = store_ref.shape[1] // LANES
    lane = lambda h: pl.ds(h * LANES, LANES)

    @pl.when(group == 0)
    def _():
        @pl.loop(0, rows_all // TILE)
        def _(j):
            part = pl.ds(pl.multiple_of(j * TILE, TILE), TILE)
            for h in range(halves):
                table[part, h, :] = store_ref[part, lane(h)].astype(jnp.float32)

    @pl.loop(0, width // SLOTS)
    def _(j):
        at = [want_ref[group, first + j * SLOTS + u] for u in range(SLOTS)]
        rows = [table[a] for a in at]
        for u in range(SLOTS):
            lines[j * SLOTS + u] = rows[u]

    for h in range(halves):
        out_ref[0, :, lane(h)] = lines[:, h, :].astype(jnp.bfloat16)


def lookup(store, received, first, width):
    groups = received.shape[0]
    rows_all, features = store.shape
    apart = lambda rows: pltpu.VMEM((rows, features // LANES, LANES), jnp.float32)
    return pl.pallas_call(
        functools.partial(lookup_body, first, width),
        out_shape=jax.ShapeDtypeStruct((groups, width, features), jnp.bfloat16),
        grid=(groups,),
        in_specs=[SMEM, pl.BlockSpec((rows_all, features), lambda g: (0, 0))],
        out_specs=pl.BlockSpec((1, width, features), lambda g: (g, 0, 0)),
        scratch_shapes=[apart(rows_all), apart(width)],
        compiler_params=params(),
        cost_estimate=cost(groups * width * features * 40, 2 * rows_all * features),
        name="lookup",
    )(received, store)


def adjacency_body(tiles, near_ref, table_ref, out_ref):
    groups = near_ref.shape[0]
    node_high = lax.broadcasted_iota(jnp.int32, (LANES, TILE), 0)
    own_row = (
        lax.shift_right_logical(lax.broadcasted_iota(jnp.int32, (SLOTS, TILE), 1), SLOT_BITS)
        == lax.broadcasted_iota(jnp.int32, (SLOTS, TILE), 0)
    )
    low_id = lax.broadcasted_iota(jnp.int32, (TILE, TILE), 0).astype(jnp.float32)

    def one_group(g):
        near = near_ref[pl.ds(g, 1), :]
        pick = jnp.where((near >> LANE_BITS) == node_high, 1.0, 0.0).astype(jnp.bfloat16)
        found = jnp.dot(table_ref[...], pick, preferred_element_type=jnp.float32)
        here = (near & (LANES - 1)) == node_high
        high = jnp.sum(jnp.where(here, found[:LANES], 0.0), axis=0, keepdims=True)
        low = jnp.sum(jnp.where(here, found[LANES:], 0.0), axis=0, keepdims=True)
        high = jnp.where(near < 0, -1.0, high)
        rows = jnp.where(own_row, high, -1.0)
        left = jnp.concatenate(
            [jnp.where(rows == float(t), 1.0, 0.0) for t in range(tiles)], axis=0
        ).astype(jnp.bfloat16)
        right = jnp.where(low == low_id, 1.0, 0.0).astype(jnp.bfloat16)
        return contract_cols(left, right).reshape(tiles, SLOTS, TILE)

    @pl.loop(0, groups // 2, unroll=2)
    def _(j):
        pair = jnp.concatenate([one_group(2 * j), one_group(2 * j + 1)], axis=1)
        out_ref[:, pl.ds(pl.multiple_of(j * 2 * SLOTS, 2 * SLOTS), 2 * SLOTS), :] = pair.astype(
            out_ref.dtype
        )


def adjacency(near, table, tiles):
    groups = near.shape[0]
    nodes = groups * SLOTS
    step = TILE // SLOTS
    return pl.pallas_call(
        functools.partial(adjacency_body, tiles),
        out_shape=jax.ShapeDtypeStruct((tiles, nodes, TILE), jnp.float8_e4m3fn),
        grid=(groups // step,),
        in_specs=[
            pl.BlockSpec((step, TILE), lambda r: (r, 0)),
            pl.BlockSpec(table.shape, lambda r: (0, 0)),
        ],
        out_specs=pl.BlockSpec((tiles, TILE, TILE), lambda r: (0, r, 0)),
        compiler_params=params(),
        cost_estimate=cost(2 * nodes * TILE * TILE * tiles * 2, nodes * TILE * tiles),
        name="adjacency",
    )(near, table)


def collect(piece, counts_ref, starts_ref, answer_ref, landed, arrived, packed):
    batch_count = answer_ref.shape[0]

    def bring(o):
        return pltpu.make_async_copy(answer_ref.at[o], landed.at[o], arrived.at[o])

    @pl.loop(0, batch_count)
    def _(o):
        bring(o).start()

    @pl.loop(0, batch_count)
    def _(o):
        bring(o).wait()
        base = starts_ref[o]

        @pl.loop(0, pl.cdiv(counts_ref[o], piece))
        def _(c):
            source = pl.ds(pl.multiple_of(c * piece, piece), piece)
            target = pl.ds(pl.multiple_of(base + c * piece, SLOTS), piece)
            packed[target, :] = landed[o, source, :]

    end = starts_ref[batch_count]
    packed[pl.ds(pl.multiple_of(end, SLOTS), WIDE * TILE), :] = jnp.zeros(
        (WIDE * TILE, packed.shape[1]), packed.dtype
    )


def gather_sum_body(
    piece, last, spans_ref, counts_ref, starts_ref, answer_ref, column_ref, adj_ref, *refs
):
    if last:
        (total_in, own_in, deg_ref, wself_ref, wneigh_ref, own_ref, mean_ref, share_ref) = refs[:8]
        packed, tiles_ref, ready, found_ref, landed, arrived, total_ref = refs[8:]
    else:
        total_ref, own_ref, packed, tiles_ref, ready, found_ref, landed, arrived = refs
    nodes = own_ref.shape[0]
    rows = math.gcd(nodes, 3 * TILE)
    begin, count = spans_ref[0], spans_ref[1]

    def fetch(step, slot):
        return pltpu.make_async_copy(
            adj_ref.at[pl.ds(begin + step * WIDE, WIDE)], tiles_ref.at[slot], ready.at[slot]
        )

    @pl.when(count > 0)
    def _():
        fetch(0, 0).start()

    collect(piece, counts_ref, starts_ref, answer_ref, landed, arrived, packed)

    @pl.loop(0, nodes // TILE)
    def _(r):
        part = pl.ds(pl.multiple_of(r * TILE, TILE), TILE)
        if last:
            total_ref[part, :] = total_in[part, :]
            found_ref[part, :] = own_in[part, :].astype(jnp.float32)
        else:
            total_ref[part, :] = jnp.zeros((TILE, total_ref.shape[1]), jnp.float32)
            found_ref[part, :] = jnp.zeros((TILE, found_ref.shape[1]), jnp.float32)

    @pl.loop(0, count)
    def _(step):
        slot = step & 1

        @pl.when(step + 1 < count)
        def _():
            fetch(step + 1, 1 - slot).start()

        fetch(step, slot).wait()
        depth = WIDE * TILE
        block = packed[pl.ds(pl.multiple_of(step * depth, depth), depth), :]
        lane = lax.broadcasted_iota(jnp.int32, (rows, depth), 1) + (begin * TILE + step * depth)

        @pl.loop(0, nodes // rows)
        def _(r):
            part = pl.ds(pl.multiple_of(r * rows, rows), rows)
            near = jnp.concatenate(
                [tiles_ref[slot, w, part, :].astype(jnp.bfloat16) for w in range(WIDE)], axis=1
            )
            own = jnp.where(column_ref[part, :] == lane, 1.0, 0.0).astype(jnp.bfloat16)
            both = jnp.dot(
                jnp.concatenate([near, own], axis=0), block, preferred_element_type=jnp.float32
            )
            total_ref[part, :] += both[:rows]
            found_ref[part, :] += both[rows:]

    @pl.loop(0, nodes // TILE)
    def _(r):
        part = pl.ds(pl.multiple_of(r * TILE, TILE), TILE)
        own_ref[part, :] = found_ref[part, :].astype(jnp.bfloat16)

    if last:

        @pl.loop(0, nodes // TILE)
        def _(r):
            part = pl.ds(pl.multiple_of(r * TILE, TILE), TILE)
            mean = (total_ref[part, :] / deg_ref[part, :]).astype(jnp.bfloat16)
            mean_ref[part, :] = mean
            share_ref[part, :] = (
                jnp.dot(own_ref[part, :], wself_ref[...], preferred_element_type=jnp.float32)
                + jnp.dot(mean, wneigh_ref[...], preferred_element_type=jnp.float32)
            ).astype(share_ref.dtype)


def gather_sum(inputs, spans, counts, starts, answer, column, adj, rest, share_type=jnp.bfloat16):
    batch_count, width, features = answer.shape
    tiles, nodes, _ = adj.shape
    piece = LANES if width % LANES == 0 else SLOTS
    last = rest is not None
    room = min(batch_count * width, inputs) + SLOTS * batch_count + 2 * WIDE * TILE
    in_specs = [SMEM, SMEM, SMEM, ANY, VMEM, ANY]
    rows = lambda dtype: jax.ShapeDtypeStruct((nodes, features), dtype)
    scratch = [
        pltpu.VMEM((room, features), jnp.bfloat16),
        pltpu.VMEM((2, WIDE, nodes, TILE), adj.dtype),
        pltpu.SemaphoreType.DMA((2,)),
        pltpu.VMEM((nodes, features), jnp.float32),
        pltpu.VMEM(answer.shape, answer.dtype),
        pltpu.SemaphoreType.DMA((batch_count,)),
    ]
    operands = [answer, column, adj]
    if last:
        operands += list(rest)
        in_specs += [VMEM] * len(rest)
        out_shape = (
            rows(jnp.bfloat16),
            rows(jnp.bfloat16),
            jax.ShapeDtypeStruct((nodes, rest[3].shape[1]), share_type),
        )
        scratch += [pltpu.VMEM((nodes, features), jnp.float32)]
    else:
        out_shape = (rows(jnp.float32), rows(jnp.bfloat16))
    return pl.pallas_call(
        functools.partial(gather_sum_body, piece, last),
        out_shape=out_shape,
        in_specs=in_specs,
        out_specs=(VMEM,) * len(out_shape),
        scratch_shapes=scratch,
        compiler_params=params(),
        cost_estimate=cost(2 * nodes * features * TILE * tiles, nodes * TILE * tiles // 2),
        name="gather_sum",
    )(spans, counts, starts, *operands)


def share_order(array, parts, seeds):
    others = array.shape[0] - seeds
    own, rest = seeds // parts, others // parts
    tail = array.shape[1:]
    blocks = jnp.concatenate(
        [array[:seeds].reshape(parts, own, *tail), array[seeds:].reshape(parts, rest, *tail)],
        axis=1,
    )
    return ahead(blocks).reshape(array.shape)


def spread(part, axis, count):
    return lax.all_to_all(
        jnp.broadcast_to(part[None], (count,) + part.shape), axis, 0, 0, tiled=True
    )


def passed(part, shift):
    parts = lax.axis_size("feat")
    return lax.ppermute(part, "feat", [((i + shift) % parts, i) for i in range(parts)])


def ahead(array):
    parts = lax.axis_size("feat")
    twice = jnp.concatenate([array, array], axis=0)
    return lax.dynamic_slice_in_dim(twice, lax.axis_index("feat"), parts, 0)


def spread_parts(part):
    return [part] + [passed(part, j) for j in range(1, lax.axis_size("feat"))]


def sum_parts(blocks):
    parts = lax.axis_size("feat")
    came = [blocks[0]] + [passed(blocks[j], -j) for j in range(1, parts)]
    return sum(x.astype(jnp.float32) for x in came)


def total_over_batch(one, two):
    count = lax.axis_size("batch")
    both = jnp.concatenate([one, two]).astype(jnp.bfloat16)
    pieces = both.reshape(count, both.shape[0] // count, both.shape[1])
    pieces = lax.all_to_all(pieces, "batch", 0, 0, tiled=True)
    total = spread(jnp.sum(pieces.astype(jnp.float32), axis=0), "batch", count)
    total = total.reshape(both.shape)
    return total[: one.shape[0]], total[one.shape[0] :]


def local(
    store,
    input_owner,
    input_row,
    nbr_one,
    deg_one,
    nbr_two,
    deg_two,
    cotangent,
    w1_self,
    w1_neigh,
    bias_one,
    w2_self,
    w2_neigh,
    bias_two,
):
    batch_count = lax.axis_size("batch")
    parts = lax.axis_size("feat")
    feat_index = lax.axis_index("feat")
    input_count = input_owner.shape[1]
    capacity = 2 * input_count // batch_count
    nodes = nbr_one.shape[1]
    seed_rows = nbr_two.shape[1]
    seeds = seed_rows * parts
    share = nodes // parts
    hidden_width = w1_self.shape[1]

    owners = input_owner.reshape(input_count // LANES, LANES)
    wanted = input_row.reshape(input_count // LANES, LANES)
    slots, counts, requests = make_requests(batch_count, capacity, owners, wanted)
    owners = owners.reshape(1, input_count)
    received = lax.all_to_all(
        requests.reshape(batch_count, capacity), "batch", split_axis=0, concat_axis=0, tiled=True
    )
    first = capacity // 2
    looked_a = lookup(store, received, 0, first)
    near_first, looked_a = lax.optimization_barrier((nbr_one[0], looked_a))
    answer_a = lax.all_to_all(looked_a, "batch", split_axis=0, concat_axis=0, tiled=True)
    looked = lookup(store, received, first, capacity - first)

    depth = WIDE * TILE
    steps = -(-(input_count + 2 * (SLOTS - 1) * batch_count + depth - 1) // depth)
    tally = counts[:, 0]
    tally_a = jnp.minimum(tally, first)
    tally_b = tally - tally_a
    padded = lambda n: (n + SLOTS - 1) // SLOTS * SLOTS
    ends = lambda n: jnp.concatenate([jnp.zeros((1,), jnp.int32), jnp.cumsum(padded(n))])
    starts_a, starts_b = ends(tally_a), ends(tally_b)
    steps_a = (starts_a[batch_count] + depth - 1) // depth
    steps_b = (starts_b[batch_count] + depth - 1) // depth
    spans_a = jnp.stack([jnp.zeros_like(steps_a), steps_a])
    spans_b = jnp.stack([steps_a * WIDE, steps_b])
    slot = slots.reshape(1, input_count)
    shifted = jnp.where(
        slot < first,
        slot + starts_a[:batch_count, None],
        slot - first + steps_a * depth + starts_b[:batch_count, None],
    )
    mine = owners == jnp.arange(batch_count)[:, None]
    column = jnp.sum(jnp.where(mine, shifted, 0), axis=0)
    grid = jnp.pad(column.reshape(-1, LANES), ((0, LANES - input_count // LANES), (0, 0))).T
    table = jnp.concatenate([grid // TILE, grid % TILE], axis=0).astype(jnp.bfloat16)
    own_column = share_order(column[:nodes], parts, seeds).reshape(nodes, 1)

    fanout_two = nbr_two.shape[2]
    used_two = jnp.arange(fanout_two)[:, None] < deg_two
    lists = jnp.concatenate([jnp.where(used_two, nbr_two[0].T, -1), deg_two], axis=0)
    lists = jnp.stack(spread_parts(lists))

    fanout = nbr_one.shape[2]
    used = jnp.arange(fanout)[None, :] < deg_one[0][:, None]
    near = share_order(jnp.where(used, near_first, -1), parts, seeds)
    near = jnp.pad(near, ((0, 0), (0, SLOTS - fanout)), constant_values=-1)
    near, lists = lax.optimization_barrier((near, lists))
    adj = adjacency(near.reshape(nodes // SLOTS, TILE), table, steps * WIDE)
    looked, answer_a, adj = lax.optimization_barrier((looked, answer_a, adj))
    answer_b = lax.all_to_all(looked, "batch", split_axis=0, concat_axis=0, tiled=True)
    deg_first = share_order(deg_one[0], parts, seeds).astype(jnp.float32).reshape(nodes, 1)

    near_two = lists[:, :fanout_two].transpose(1, 0, 2).reshape(fanout_two, seeds)
    deg_all = lists[:, fanout_two].reshape(seeds)
    rest = share - seed_rows
    after = near_two - seeds
    place = jnp.where(
        near_two < seeds,
        near_two // seed_rows * share + near_two % seed_rows,
        after // rest * share + seed_rows + after % rest,
    )
    place = jnp.where(near_two < 0, -1, place - feat_index * share)
    adj_two = jnp.sum(
        place[:, :, None] == jnp.arange(share)[None, None, :], axis=0, dtype=jnp.float32
    ).astype(jnp.bfloat16)

    total, own = gather_sum(input_count, spans_a, tally_a, starts_a, answer_a, own_column, adj, None)
    self_one, agg_one, z_part = gather_sum(
        input_count,
        spans_b,
        tally_b,
        starts_b,
        answer_b,
        own_column,
        adj,
        (total, own, deg_first, w1_self, w1_neigh),
    )
    z_share = sum_parts(z_part.reshape(parts, share, hidden_width)) + bias_one
    hidden = jax.nn.silu(z_share).astype(jnp.bfloat16)

    agg_parts = jnp.dot(adj_two, hidden, preferred_element_type=jnp.float32)
    agg_total = sum_parts(agg_parts.reshape(parts, seed_rows, hidden_width))
    deg_second = deg_two[0].astype(jnp.float32)[:, None]
    agg_two = (agg_total / deg_second).astype(jnp.bfloat16)
    self_two = hidden[:seed_rows]
    z_two = (
        jnp.dot(self_two, w2_self, preferred_element_type=jnp.float32)
        + jnp.dot(agg_two, w2_neigh, preferred_element_type=jnp.float32)
        + bias_two
    )
    activations = jax.nn.silu(z_two).astype(jnp.bfloat16)[None]
    dz_two = (cotangent[0].astype(jnp.float32) * silu_grad(z_two)).astype(jnp.bfloat16)
    group = jnp.stack(spread_parts(jnp.stack([self_two, agg_two, dz_two])), axis=1)
    self_all, agg_all, dz_two_all = (x.reshape(seeds, hidden_width) for x in group)
    gw2 = total_over_batch(contract_rows(self_all, dz_two_all), contract_rows(agg_all, dz_two_all))

    back = contract_cols(dz_two_all, w2_neigh) / deg_all.astype(jnp.float32)[:, None]
    back_high = back.astype(jnp.bfloat16)
    back_low = (back - back_high.astype(jnp.float32)).astype(jnp.bfloat16)
    dh_share = contract_rows(adj_two, back_high) + contract_rows(adj_two, back_low)
    dh_share = dh_share + jnp.pad(contract_cols(dz_two, w2_self), ((0, rest), (0, 0)))
    dz_share = (dh_share * silu_grad(z_share)).astype(jnp.bfloat16)
    dz_one = jnp.concatenate(spread_parts(dz_share))
    gw1 = total_over_batch(contract_rows(self_one, dz_one), contract_rows(agg_one, dz_one))
    return (activations, *gw2, *gw1)


def solution(mesh):
    in_specs = (
        P("batch", "feat"),
        P("batch", None, None),
        P("batch", None),
        P("batch", None, None),
        P("batch", None),
        P("batch", "feat", None),
        P("batch", "feat"),
        P("batch", "feat", None),
        P("feat", None),
        P("feat", None),
        P(),
        P(),
        P(),
        P(),
    )
    out_specs = (P("batch", "feat", None), P(), P(), P("feat", None), P("feat", None))
    return jax.shard_map(local, mesh=mesh, in_specs=in_specs, out_specs=out_specs, check_vma=False)
```

```python
import functools
import math

import jax
import jax.numpy as jnp
from jax import lax
from jax.experimental import pallas as pl
from jax.experimental.pallas import tpu as pltpu
from jax.sharding import PartitionSpec as P

TILE = 256
LANES = 128
SLOTS = 16
WIDE = 2
FEW = 16
TILE_BITS, LANE_BITS, SLOT_BITS = 8, 7, 4
VMEM_BYTES = 56 * 1024 * 1024
VMEM = pl.BlockSpec(memory_space=pltpu.VMEM)
SMEM = pl.BlockSpec(memory_space=pltpu.SMEM)
ANY = pl.BlockSpec(memory_space=pl.ANY)


def silu_grad(values):
    sig = jax.nn.sigmoid(values)
    return sig * (1.0 + values * (1.0 - sig))


def contract_rows(left_side, right_side):
    return lax.dot_general(
        left_side, right_side, (((0,), (0,)), ((), ())), preferred_element_type=jnp.float32
    )


def contract_cols(left_side, right_side):
    return lax.dot_general(
        left_side, right_side, (((1,), (1,)), ((), ())), preferred_element_type=jnp.float32
    )


def params(**more):
    return pltpu.CompilerParams(vmem_limit_bytes=VMEM_BYTES, **more)


def cost(flops, moved):
    return pl.CostEstimate(flops=int(flops), bytes_accessed=int(moved), transcendentals=0)


def requests_body(batch_count, capacity, owner_ref, row_ref, slot_ref, count_ref, request_ref):
    blocks, width = owner_ref.shape[0] // 2, TILE
    places = request_ref.shape[0]
    line = lambda ref, b: jnp.concatenate([ref[2 * b : 2 * b + 1], ref[2 * b + 1 : 2 * b + 2]], axis=1)
    owner_id = lax.broadcasted_iota(jnp.int32, (batch_count, width), 0)
    earlier = lax.broadcasted_iota(jnp.int32, (width, width), 0)
    later = lax.broadcasted_iota(jnp.int32, (width, width), 1)
    upper = jnp.where(earlier <= later, 1.0, 0.0).astype(jnp.bfloat16)
    high_id = lax.broadcasted_iota(jnp.int32, (places, width), 0)
    low_id = lax.broadcasted_iota(jnp.int32, (LANES, width), 0)
    marks = [
        jnp.where(line(owner_ref, b) == owner_id, 1.0, 0.0) for b in range(blocks)
    ]
    stacked = jnp.concatenate(marks, axis=0).astype(jnp.bfloat16)
    prefix = jnp.dot(stacked, upper, preferred_element_type=jnp.float32)
    running = jnp.zeros((batch_count, 1), jnp.float32)
    total = jnp.zeros((2 * places, LANES), jnp.float32)
    for b in range(blocks):
        part = prefix[b * batch_count : (b + 1) * batch_count]
        slots = jnp.sum(marks[b] * (part + running - 1.0), axis=0, keepdims=True)
        slots = slots.astype(jnp.int32)
        slot_ref[2 * b : 2 * b + 1, :] = slots[:, :LANES]
        slot_ref[2 * b + 1 : 2 * b + 2, :] = slots[:, LANES:]
        running = running + part[:, width - 1 : width]
        bucket = line(owner_ref, b) * capacity + slots
        rows = line(row_ref, b)
        hit = (bucket >> LANE_BITS) == high_id
        left = jnp.concatenate(
            [
                jnp.where(hit, (rows >> TILE_BITS).astype(jnp.float32), 0.0),
                jnp.where(hit, (rows & (TILE - 1)).astype(jnp.float32), 0.0),
            ],
            axis=0,
        ).astype(jnp.bfloat16)
        right = jnp.where((bucket & (LANES - 1)) == low_id, 1.0, 0.0).astype(jnp.bfloat16)
        total = total + contract_cols(left, right)
    count_ref[...] = jnp.broadcast_to(running, count_ref.shape).astype(jnp.int32)
    request_ref[...] = (total[:places] * TILE + total[places:]).astype(jnp.int32)


def make_requests(batch_count, capacity, owners, wanted):
    total = owners.shape[0] * LANES
    places = batch_count * capacity // LANES
    return pl.pallas_call(
        functools.partial(requests_body, batch_count, capacity),
        out_shape=(
            jax.ShapeDtypeStruct(owners.shape, jnp.int32),
            jax.ShapeDtypeStruct((batch_count, LANES), jnp.int32),
            jax.ShapeDtypeStruct((places, LANES), jnp.int32),
        ),
        in_specs=[VMEM, VMEM],
        out_specs=(VMEM, VMEM, VMEM),
        compiler_params=params(),
        cost_estimate=cost(4 * total * places * LANES, 24 * total),
        name="requests",
    )(owners, wanted)


def joined_body(first, width, want_ref, store_ref, out_ref, table):
    group = pl.program_id(0)
    rows_all = store_ref.shape[0]

    @pl.when(group == 0)
    def _():
        @pl.loop(0, rows_all // TILE)
        def _(j):
            part = pl.ds(pl.multiple_of(j * TILE, TILE), TILE)
            table[part, :] = store_ref[part, :].astype(jnp.float32)

    @pl.loop(0, width // SLOTS, unroll=2)
    def _(j):
        at = [want_ref[group, first + j * SLOTS + u] for u in range(SLOTS)]
        rows = jnp.concatenate([table[pl.ds(a, 1), :] for a in at], axis=0)
        out_ref[0, pl.ds(pl.multiple_of(j * SLOTS, SLOTS), SLOTS), :] = rows.astype(jnp.bfloat16)


def paired_body(first, width, want_ref, store_ref, out_ref, table, lines):
    group = pl.program_id(0)
    rows_all = store_ref.shape[0]
    halves = store_ref.shape[1] // LANES
    lane = lambda h: pl.ds(h * LANES, LANES)

    @pl.when(group == 0)
    def _():
        @pl.loop(0, rows_all // TILE)
        def _(j):
            part = pl.ds(pl.multiple_of(j * TILE, TILE), TILE)
            for h in range(halves):
                spot = pl.ds(pl.multiple_of(j * TILE * halves, TILE) + h, TILE, stride=halves)
                table[spot, :] = store_ref[part, lane(h)].astype(jnp.float32)

    @pl.loop(0, width // SLOTS)
    def _(j):
        at = [want_ref[group, first + j * SLOTS + u] for u in range(SLOTS)]
        spot = lambda a: pl.ds(pl.multiple_of(a * halves, halves), halves)
        rows = [table[spot(a), :] for a in at]
        for u in range(SLOTS):
            lines[spot(j * SLOTS + u), :] = rows[u]

    for h in range(halves):
        out_ref[0, :, lane(h)] = lines[pl.ds(h, width, stride=halves), :].astype(jnp.bfloat16)


def lookup(store, received, first, width, paired):
    groups = received.shape[0]
    rows_all, features = store.shape
    halves = features // LANES
    apart = lambda rows: pltpu.VMEM((rows * halves, LANES), jnp.float32)
    return pl.pallas_call(
        functools.partial(paired_body if paired else joined_body, first, width),
        out_shape=jax.ShapeDtypeStruct((groups, width, features), jnp.bfloat16),
        grid=(groups,),
        in_specs=[SMEM, pl.BlockSpec((rows_all, features), lambda g: (0, 0))],
        out_specs=pl.BlockSpec((1, width, features), lambda g: (g, 0, 0)),
        scratch_shapes=[apart(rows_all), apart(width)]
        if paired
        else [pltpu.VMEM((rows_all, features), jnp.float32)],
        compiler_params=params(),
        cost_estimate=cost(groups * width * features * 40, 2 * rows_all * features),
        name="lookup",
    )(received, store)


def adjacency_body(tiles, near_ref, table_ref, out_ref):
    groups = near_ref.shape[0]
    node_high = lax.broadcasted_iota(jnp.int32, (LANES, TILE), 0)
    own_row = (
        lax.shift_right_logical(lax.broadcasted_iota(jnp.int32, (SLOTS, TILE), 1), SLOT_BITS)
        == lax.broadcasted_iota(jnp.int32, (SLOTS, TILE), 0)
    )
    low_id = lax.broadcasted_iota(jnp.int32, (TILE, TILE), 0).astype(jnp.float32)

    def one_group(g):
        near = near_ref[pl.ds(g, 1), :]
        pick = jnp.where((near >> LANE_BITS) == node_high, 1.0, 0.0).astype(jnp.bfloat16)
        found = jnp.dot(table_ref[...], pick, preferred_element_type=jnp.float32)
        here = (near & (LANES - 1)) == node_high
        high = jnp.sum(jnp.where(here, found[:LANES], 0.0), axis=0, keepdims=True)
        low = jnp.sum(jnp.where(here, found[LANES:], 0.0), axis=0, keepdims=True)
        high = jnp.where(near < 0, -1.0, high)
        rows = jnp.where(own_row, high, -1.0)
        left = jnp.concatenate(
            [jnp.where(rows == float(t), 1.0, 0.0) for t in range(tiles)], axis=0
        ).astype(jnp.bfloat16)
        right = jnp.where(low == low_id, 1.0, 0.0).astype(jnp.bfloat16)
        return contract_cols(left, right).reshape(tiles, SLOTS, TILE)

    @pl.loop(0, groups // 2, unroll=2)
    def _(j):
        pair = jnp.concatenate([one_group(2 * j), one_group(2 * j + 1)], axis=1)
        out_ref[:, pl.ds(pl.multiple_of(j * 2 * SLOTS, 2 * SLOTS), 2 * SLOTS), :] = pair.astype(
            out_ref.dtype
        )


def adjacency(near, table, tiles):
    groups = near.shape[0]
    nodes = groups * SLOTS
    step = TILE // SLOTS
    return pl.pallas_call(
        functools.partial(adjacency_body, tiles),
        out_shape=jax.ShapeDtypeStruct((tiles, nodes, TILE), jnp.float8_e4m3fn),
        grid=(groups // step,),
        in_specs=[
            pl.BlockSpec((step, TILE), lambda r: (r, 0)),
            pl.BlockSpec(table.shape, lambda r: (0, 0)),
        ],
        out_specs=pl.BlockSpec((tiles, TILE, TILE), lambda r: (0, r, 0)),
        compiler_params=params(),
        cost_estimate=cost(2 * nodes * TILE * TILE * tiles * 2, nodes * TILE * tiles),
        name="adjacency",
    )(near, table)


def collect(piece, counts_ref, starts_ref, answer_ref, landed, arrived, packed):
    batch_count = answer_ref.shape[0]

    def bring(o):
        return pltpu.make_async_copy(answer_ref.at[o], landed.at[o], arrived.at[o])

    @pl.loop(0, batch_count)
    def _(o):
        bring(o).start()

    @pl.loop(0, batch_count)
    def _(o):
        bring(o).wait()
        base = starts_ref[o]

        @pl.loop(0, pl.cdiv(counts_ref[o], piece))
        def _(c):
            source = pl.ds(pl.multiple_of(c * piece, piece), piece)
            target = pl.ds(pl.multiple_of(base + c * piece, SLOTS), piece)
            packed[target, :] = landed[o, source, :]

    end = starts_ref[batch_count]
    packed[pl.ds(pl.multiple_of(end, SLOTS), WIDE * TILE), :] = jnp.zeros(
        (WIDE * TILE, packed.shape[1]), packed.dtype
    )


def gather_sum_body(
    piece, last, spans_ref, counts_ref, starts_ref, answer_ref, column_ref, adj_ref, *refs
):
    if last:
        (total_in, own_in, deg_ref, wself_ref, wneigh_ref, own_ref, mean_ref, share_ref) = refs[:8]
        packed, tiles_ref, ready, found_ref, landed, arrived, total_ref = refs[8:]
    else:
        total_ref, own_ref, packed, tiles_ref, ready, found_ref, landed, arrived = refs
    nodes = own_ref.shape[0]
    rows = math.gcd(nodes, 3 * TILE)
    begin, count = spans_ref[0], spans_ref[1]

    def fetch(step, slot):
        return pltpu.make_async_copy(
            adj_ref.at[pl.ds(begin + step * WIDE, WIDE)], tiles_ref.at[slot], ready.at[slot]
        )

    @pl.when(count > 0)
    def _():
        fetch(0, 0).start()

    collect(piece, counts_ref, starts_ref, answer_ref, landed, arrived, packed)

    @pl.loop(0, nodes // TILE)
    def _(r):
        part = pl.ds(pl.multiple_of(r * TILE, TILE), TILE)
        if last:
            total_ref[part, :] = total_in[part, :]
            found_ref[part, :] = own_in[part, :].astype(jnp.float32)
        else:
            total_ref[part, :] = jnp.zeros((TILE, total_ref.shape[1]), jnp.float32)
            found_ref[part, :] = jnp.zeros((TILE, found_ref.shape[1]), jnp.float32)

    @pl.loop(0, count)
    def _(step):
        slot = step & 1

        @pl.when(step + 1 < count)
        def _():
            fetch(step + 1, 1 - slot).start()

        fetch(step, slot).wait()
        depth = WIDE * TILE
        block = packed[pl.ds(pl.multiple_of(step * depth, depth), depth), :]
        lane = lax.broadcasted_iota(jnp.int32, (rows, depth), 1) + (begin * TILE + step * depth)

        @pl.loop(0, nodes // rows)
        def _(r):
            part = pl.ds(pl.multiple_of(r * rows, rows), rows)
            near = jnp.concatenate(
                [tiles_ref[slot, w, part, :].astype(jnp.bfloat16) for w in range(WIDE)], axis=1
            )
            own = jnp.where(column_ref[part, :] == lane, 1.0, 0.0).astype(jnp.bfloat16)
            both = jnp.dot(
                jnp.concatenate([near, own], axis=0), block, preferred_element_type=jnp.float32
            )
            total_ref[part, :] += both[:rows]
            found_ref[part, :] += both[rows:]

    @pl.loop(0, nodes // TILE)
    def _(r):
        part = pl.ds(pl.multiple_of(r * TILE, TILE), TILE)
        own_ref[part, :] = found_ref[part, :].astype(jnp.bfloat16)

    if last:

        @pl.loop(0, nodes // TILE)
        def _(r):
            part = pl.ds(pl.multiple_of(r * TILE, TILE), TILE)
            mean = (total_ref[part, :] / deg_ref[part, :]).astype(jnp.bfloat16)
            mean_ref[part, :] = mean
            share_ref[part, :] = (
                jnp.dot(own_ref[part, :], wself_ref[...], preferred_element_type=jnp.float32)
                + jnp.dot(mean, wneigh_ref[...], preferred_element_type=jnp.float32)
            ).astype(share_ref.dtype)


def gather_sum(inputs, spans, counts, starts, answer, column, adj, rest, share_type=jnp.bfloat16):
    batch_count, width, features = answer.shape
    tiles, nodes, _ = adj.shape
    piece = LANES if width % LANES == 0 else SLOTS
    last = rest is not None
    room = min(batch_count * width, inputs) + SLOTS * batch_count + 2 * WIDE * TILE
    in_specs = [SMEM, SMEM, SMEM, ANY, VMEM, ANY]
    rows = lambda dtype: jax.ShapeDtypeStruct((nodes, features), dtype)
    scratch = [
        pltpu.VMEM((room, features), jnp.bfloat16),
        pltpu.VMEM((2, WIDE, nodes, TILE), adj.dtype),
        pltpu.SemaphoreType.DMA((2,)),
        pltpu.VMEM((nodes, features), jnp.float32),
        pltpu.VMEM(answer.shape, answer.dtype),
        pltpu.SemaphoreType.DMA((batch_count,)),
    ]
    operands = [answer, column, adj]
    if last:
        operands += list(rest)
        in_specs += [VMEM] * len(rest)
        out_shape = (
            rows(jnp.bfloat16),
            rows(jnp.bfloat16),
            jax.ShapeDtypeStruct((nodes, rest[3].shape[1]), share_type),
        )
        scratch += [pltpu.VMEM((nodes, features), jnp.float32)]
    else:
        out_shape = (rows(jnp.float32), rows(jnp.bfloat16))
    return pl.pallas_call(
        functools.partial(gather_sum_body, piece, last),
        out_shape=out_shape,
        in_specs=in_specs,
        out_specs=(VMEM,) * len(out_shape),
        scratch_shapes=scratch,
        compiler_params=params(),
        cost_estimate=cost(2 * nodes * features * TILE * tiles, nodes * TILE * tiles // 2),
        name="gather_sum",
    )(spans, counts, starts, *operands)


def share_order(array, parts, seeds):
    others = array.shape[0] - seeds
    own, rest = seeds // parts, others // parts
    tail = array.shape[1:]
    blocks = jnp.concatenate(
        [array[:seeds].reshape(parts, own, *tail), array[seeds:].reshape(parts, rest, *tail)],
        axis=1,
    )
    return ahead(blocks).reshape(array.shape)


def spread(part, axis, count):
    return lax.all_to_all(
        jnp.broadcast_to(part[None], (count,) + part.shape), axis, 0, 0, tiled=True
    )


def passed(part, shift, axis="feat"):
    parts = lax.axis_size(axis)
    return lax.ppermute(part, axis, [((i + shift) % parts, i) for i in range(parts)])


def turned(array, by):
    twice = jnp.concatenate([array, array], axis=0)
    return lax.dynamic_slice_in_dim(twice, by, array.shape[0], 0)


def ahead(array, axis="feat"):
    return turned(array, lax.axis_index(axis))


def spread_parts(part, axis="feat"):
    return [part] + [passed(part, j, axis) for j in range(1, lax.axis_size(axis))]


def sum_parts(blocks, axis="feat"):
    parts = lax.axis_size(axis)
    came = [blocks[0]] + [passed(blocks[j], -j, axis) for j in range(1, parts)]
    return sum(x.astype(jnp.float32) for x in came)


def total_over_batch(one, two):
    count = lax.axis_size("batch")
    both = jnp.concatenate([one, two]).astype(jnp.bfloat16)
    pieces = both.reshape(count, both.shape[0] // count, both.shape[1])
    pieces = lax.all_to_all(pieces, "batch", 0, 0, tiled=True)
    total = spread(jnp.sum(pieces.astype(jnp.float32), axis=0), "batch", count)
    total = total.reshape(both.shape)
    return total[: one.shape[0]], total[one.shape[0] :]


def total_by_permutes(one, two):
    count = lax.axis_size("batch")
    if count > FEW:
        return total_over_batch(one, two)
    both = jnp.concatenate([one, two]).astype(jnp.bfloat16)
    pieces = ahead(both.reshape(count, both.shape[0] // count, both.shape[1]), "batch")
    came = spread_parts(sum_parts(pieces, "batch"), "batch")
    total = jnp.zeros(pieces.shape, jnp.float32)
    for j, piece in enumerate(came):
        spot = (lax.axis_index("batch") + j) % count
        total = lax.dynamic_update_index_in_dim(total, piece, spot, 0)
    total = total.reshape(both.shape)
    return total[: one.shape[0]], total[one.shape[0] :]


def local(
    store,
    input_owner,
    input_row,
    nbr_one,
    deg_one,
    nbr_two,
    deg_two,
    cotangent,
    w1_self,
    w1_neigh,
    bias_one,
    w2_self,
    w2_neigh,
    bias_two,
):
    batch_count = lax.axis_size("batch")
    parts = lax.axis_size("feat")
    feat_index = lax.axis_index("feat")
    input_count = input_owner.shape[1]
    capacity = 2 * input_count // batch_count
    nodes = nbr_one.shape[1]
    seed_rows = nbr_two.shape[1]
    seeds = seed_rows * parts
    share = nodes // parts
    hidden_width = w1_self.shape[1]

    owners = input_owner.reshape(input_count // LANES, LANES)
    wanted = input_row.reshape(input_count // LANES, LANES)
    slots, counts, requests = make_requests(batch_count, capacity, owners, wanted)
    owners = owners.reshape(1, input_count)
    received = lax.all_to_all(
        requests.reshape(batch_count, capacity), "batch", split_axis=0, concat_axis=0, tiled=True
    )
    first = capacity // 2
    looked_a = lookup(store, received, 0, first, False)
    near_first, looked_a = lax.optimization_barrier((nbr_one[0], looked_a))
    answer_a = lax.all_to_all(looked_a, "batch", split_axis=0, concat_axis=0, tiled=True)
    looked = lookup(store, received, first, capacity - first, True)

    depth = WIDE * TILE
    steps = -(-(input_count + 2 * (SLOTS - 1) * batch_count + depth - 1) // depth)
    tally = counts[:, 0]
    tally_a = jnp.minimum(tally, first)
    tally_b = tally - tally_a
    padded = lambda n: (n + SLOTS - 1) // SLOTS * SLOTS
    ends = lambda n: jnp.concatenate([jnp.zeros((1,), jnp.int32), jnp.cumsum(padded(n))])
    starts_a, starts_b = ends(tally_a), ends(tally_b)
    steps_a = (starts_a[batch_count] + depth - 1) // depth
    steps_b = (starts_b[batch_count] + depth - 1) // depth
    spans_a = jnp.stack([jnp.zeros_like(steps_a), steps_a])
    spans_b = jnp.stack([steps_a * WIDE, steps_b])
    slot = slots.reshape(1, input_count)
    shifted = jnp.where(
        slot < first,
        slot + starts_a[:batch_count, None],
        slot - first + steps_a * depth + starts_b[:batch_count, None],
    )
    mine = owners == jnp.arange(batch_count)[:, None]
    column = jnp.sum(jnp.where(mine, shifted, 0), axis=0)
    grid = jnp.pad(column.reshape(-1, LANES), ((0, LANES - input_count // LANES), (0, 0))).T
    table = jnp.concatenate([grid // TILE, grid % TILE], axis=0).astype(jnp.bfloat16)
    own_column = share_order(column[:nodes], parts, seeds).reshape(nodes, 1)

    fanout_two = nbr_two.shape[2]
    used_two = jnp.arange(fanout_two)[:, None] < deg_two
    lists = jnp.concatenate([jnp.where(used_two, nbr_two[0].T, -1), deg_two], axis=0)
    lists = jnp.stack(spread_parts(lists))

    fanout = nbr_one.shape[2]
    used = jnp.arange(fanout)[None, :] < deg_one[0][:, None]
    near = share_order(jnp.where(used, near_first, -1), parts, seeds)
    near = jnp.pad(near, ((0, 0), (0, SLOTS - fanout)), constant_values=-1)
    near, lists = lax.optimization_barrier((near, lists))
    adj = adjacency(near.reshape(nodes // SLOTS, TILE), table, steps * WIDE)
    looked, answer_a, adj = lax.optimization_barrier((looked, answer_a, adj))
    answer_b = lax.all_to_all(looked, "batch", split_axis=0, concat_axis=0, tiled=True)
    deg_first = share_order(deg_one[0], parts, seeds).astype(jnp.float32).reshape(nodes, 1)

    near_two = lists[:, :fanout_two].transpose(1, 0, 2).reshape(fanout_two, seeds)
    deg_all = lists[:, fanout_two].reshape(seeds)
    rest = share - seed_rows
    after = near_two - seeds
    place = jnp.where(
        near_two < seeds,
        near_two // seed_rows * share + near_two % seed_rows,
        after // rest * share + seed_rows + after % rest,
    )
    place = jnp.where(near_two < 0, -1, place - feat_index * share)
    adj_two = jnp.sum(
        place[:, :, None] == jnp.arange(share)[None, None, :], axis=0, dtype=jnp.float32
    ).astype(jnp.bfloat16)

    total, own = gather_sum(input_count, spans_a, tally_a, starts_a, answer_a, own_column, adj, None)
    self_one, agg_one, z_part = gather_sum(
        input_count,
        spans_b,
        tally_b,
        starts_b,
        answer_b,
        own_column,
        adj,
        (total, own, deg_first, w1_self, w1_neigh),
    )
    z_share = sum_parts(z_part.reshape(parts, share, hidden_width)) + bias_one
    hidden = jax.nn.silu(z_share).astype(jnp.bfloat16)

    agg_parts = jnp.dot(adj_two, hidden, preferred_element_type=jnp.float32)
    agg_total = sum_parts(agg_parts.reshape(parts, seed_rows, hidden_width))
    deg_second = deg_two[0].astype(jnp.float32)[:, None]
    agg_two = (agg_total / deg_second).astype(jnp.bfloat16)
    self_two = hidden[:seed_rows]
    z_two = (
        jnp.dot(self_two, w2_self, preferred_element_type=jnp.float32)
        + jnp.dot(agg_two, w2_neigh, preferred_element_type=jnp.float32)
        + bias_two
    )
    activations = jax.nn.silu(z_two).astype(jnp.bfloat16)[None]
    dz_two = (cotangent[0].astype(jnp.float32) * silu_grad(z_two)).astype(jnp.bfloat16)
    group = jnp.stack(spread_parts(jnp.stack([self_two, agg_two, dz_two])), axis=1)
    self_all, agg_all, dz_two_all = (x.reshape(seeds, hidden_width) for x in group)
    gw2 = total_by_permutes(contract_rows(self_all, dz_two_all), contract_rows(agg_all, dz_two_all))

    back = contract_cols(dz_two_all, w2_neigh) / deg_all.astype(jnp.float32)[:, None]
    back_high = back.astype(jnp.bfloat16)
    back_low = (back - back_high.astype(jnp.float32)).astype(jnp.bfloat16)
    dh_share = contract_rows(adj_two, back_high) + contract_rows(adj_two, back_low)
    dh_share = dh_share + jnp.pad(contract_cols(dz_two, w2_self), ((0, rest), (0, 0)))
    dz_share = (dh_share * silu_grad(z_share)).astype(jnp.bfloat16)
    dz_one = jnp.concatenate(spread_parts(dz_share))
    gw1 = total_over_batch(contract_rows(self_one, dz_one), contract_rows(agg_one, dz_one))
    return (activations, *gw2, *gw1)


def solution(mesh):
    in_specs = (
        P("batch", "feat"),
        P("batch", None, None),
        P("batch", None),
        P("batch", None, None),
        P("batch", None),
        P("batch", "feat", None),
        P("batch", "feat"),
        P("batch", "feat", None),
        P("feat", None),
        P("feat", None),
        P(),
        P(),
        P(),
        P(),
    )
    out_specs = (P("batch", "feat", None), P(), P(), P("feat", None), P("feat", None))
    return jax.shard_map(local, mesh=mesh, in_specs=in_specs, out_specs=out_specs, check_vma=False)
```

```python
import functools
import math

import jax
import jax.numpy as jnp
from jax import lax
from jax.experimental import pallas as pl
from jax.experimental.pallas import tpu as pltpu
from jax.sharding import PartitionSpec as P

TILE = 256
LANES = 128
SLOTS = 16
WIDE = 2
FEW = 16
TILE_BITS, LANE_BITS, SLOT_BITS = 8, 7, 4
MIB = 1024 * 1024
VMEM = pl.BlockSpec(memory_space=pltpu.VMEM)
SMEM = pl.BlockSpec(memory_space=pltpu.SMEM)
ANY = pl.BlockSpec(memory_space=pl.ANY)


def silu_grad(values):
    sig = jax.nn.sigmoid(values)
    return sig * (1.0 + values * (1.0 - sig))


def contract_rows(left_side, right_side):
    return lax.dot_general(
        left_side, right_side, (((0,), (0,)), ((), ())), preferred_element_type=jnp.float32
    )


def contract_cols(left_side, right_side):
    return lax.dot_general(
        left_side, right_side, (((1,), (1,)), ((), ())), preferred_element_type=jnp.float32
    )


def params(mib):
    return pltpu.CompilerParams(vmem_limit_bytes=mib * MIB)


def cost(flops, moved):
    return pl.CostEstimate(flops=int(flops), bytes_accessed=int(moved), transcendentals=0)


def requests_body(batch_count, capacity, owner_ref, row_ref, slot_ref, count_ref, request_ref):
    blocks, width = owner_ref.shape[0] // 2, TILE
    places = request_ref.shape[0]
    line = lambda ref, b: jnp.concatenate([ref[2 * b : 2 * b + 1], ref[2 * b + 1 : 2 * b + 2]], axis=1)
    owner_id = lax.broadcasted_iota(jnp.int32, (batch_count, width), 0)
    earlier = lax.broadcasted_iota(jnp.int32, (width, width), 0)
    later = lax.broadcasted_iota(jnp.int32, (width, width), 1)
    upper = jnp.where(earlier <= later, 1.0, 0.0).astype(jnp.bfloat16)
    high_id = lax.broadcasted_iota(jnp.int32, (places, width), 0)
    low_id = lax.broadcasted_iota(jnp.int32, (LANES, width), 0)
    marks = [
        jnp.where(line(owner_ref, b) == owner_id, 1.0, 0.0) for b in range(blocks)
    ]
    stacked = jnp.concatenate(marks, axis=0).astype(jnp.bfloat16)
    prefix = jnp.dot(stacked, upper, preferred_element_type=jnp.float32)
    running = jnp.zeros((batch_count, 1), jnp.float32)
    total = jnp.zeros((2 * places, LANES), jnp.float32)
    for b in range(blocks):
        part = prefix[b * batch_count : (b + 1) * batch_count]
        slots = jnp.sum(marks[b] * (part + running - 1.0), axis=0, keepdims=True)
        slots = slots.astype(jnp.int32)
        slot_ref[2 * b : 2 * b + 1, :] = slots[:, :LANES]
        slot_ref[2 * b + 1 : 2 * b + 2, :] = slots[:, LANES:]
        running = running + part[:, width - 1 : width]
        bucket = line(owner_ref, b) * capacity + slots
        rows = line(row_ref, b)
        hit = (bucket >> LANE_BITS) == high_id
        left = jnp.concatenate(
            [
                jnp.where(hit, (rows >> TILE_BITS).astype(jnp.float32), 0.0),
                jnp.where(hit, (rows & (TILE - 1)).astype(jnp.float32), 0.0),
            ],
            axis=0,
        ).astype(jnp.bfloat16)
        right = jnp.where((bucket & (LANES - 1)) == low_id, 1.0, 0.0).astype(jnp.bfloat16)
        total = total + contract_cols(left, right)
    count_ref[...] = jnp.broadcast_to(running, count_ref.shape).astype(jnp.int32)
    request_ref[...] = (total[:places] * TILE + total[places:]).astype(jnp.int32)


def make_requests(batch_count, capacity, owners, wanted):
    total = owners.shape[0] * LANES
    places = batch_count * capacity // LANES
    return pl.pallas_call(
        functools.partial(requests_body, batch_count, capacity),
        out_shape=(
            jax.ShapeDtypeStruct(owners.shape, jnp.int32),
            jax.ShapeDtypeStruct((batch_count, LANES), jnp.int32),
            jax.ShapeDtypeStruct((places, LANES), jnp.int32),
        ),
        in_specs=[VMEM, VMEM],
        out_specs=(VMEM, VMEM, VMEM),
        compiler_params=params(16),
        cost_estimate=cost(4 * total * places * LANES, 24 * total),
        name="requests",
    )(owners, wanted)


def lookup_body(stride, first, width, want_ref, store_ref, out_ref, table, lines):
    rows_all = store_ref.shape[0]
    halves = store_ref.shape[1] // LANES
    lane = lambda h: pl.ds(h * LANES, LANES)
    begin = pl.program_id(0) * stride + first

    @pl.when(pl.program_id(0) == 0)
    def _():
        @pl.loop(0, rows_all // TILE)
        def _(j):
            part = pl.ds(pl.multiple_of(j * TILE, TILE), TILE)
            for h in range(halves):
                spot = pl.ds(pl.multiple_of(j * TILE * halves, TILE) + h, TILE, stride=halves)
                table[spot, :] = store_ref[part, lane(h)].astype(jnp.float32)

    @pl.loop(0, width // SLOTS, unroll=2)
    def _(j):
        at = [want_ref[begin + j * SLOTS + u] for u in range(SLOTS)]
        rows = [table[pl.ds(pl.multiple_of(a, halves), halves), :] for a in at]
        block = lines.at[pl.ds(pl.multiple_of(j * SLOTS * halves, SLOTS * halves), SLOTS * halves)]
        for u in range(SLOTS):
            block[pl.ds(u * halves, halves), :] = rows[u]

    for h in range(halves):
        out_ref[0, :, lane(h)] = lines[pl.ds(h, width, stride=halves), :].astype(jnp.bfloat16)


def lookup(store, places, groups, first, width):
    rows_all, features = store.shape
    halves = features // LANES
    apart = lambda rows: pltpu.VMEM((rows * halves, LANES), jnp.float32)
    return pl.pallas_call(
        functools.partial(lookup_body, places.shape[0] // groups, first, width),
        out_shape=jax.ShapeDtypeStruct((groups, width, features), jnp.bfloat16),
        grid=(groups,),
        in_specs=[SMEM, pl.BlockSpec((rows_all, features), lambda g: (0, 0))],
        out_specs=pl.BlockSpec((1, width, features), lambda g: (g, 0, 0)),
        scratch_shapes=[apart(rows_all), apart(width)],
        compiler_params=params(24),
        cost_estimate=cost(groups * width * features * 40, 2 * rows_all * features),
        name="lookup",
    )(places, store)


def adjacency_body(tiles, near_ref, table_ref, out_ref):
    groups = near_ref.shape[0]
    node_high = lax.broadcasted_iota(jnp.int32, (LANES, TILE), 0)
    own_row = (
        lax.shift_right_logical(lax.broadcasted_iota(jnp.int32, (SLOTS, TILE), 1), SLOT_BITS)
        == lax.broadcasted_iota(jnp.int32, (SLOTS, TILE), 0)
    )
    low_id = lax.broadcasted_iota(jnp.int32, (TILE, TILE), 0).astype(jnp.float32)

    def one_group(g):
        near = near_ref[pl.ds(g, 1), :]
        pick = jnp.where((near >> LANE_BITS) == node_high, 1.0, 0.0).astype(jnp.bfloat16)
        found = jnp.dot(table_ref[...], pick, preferred_element_type=jnp.float32)
        here = (near & (LANES - 1)) == node_high
        high = jnp.sum(jnp.where(here, found[:LANES], 0.0), axis=0, keepdims=True)
        low = jnp.sum(jnp.where(here, found[LANES:], 0.0), axis=0, keepdims=True)
        high = jnp.where(near < 0, -1.0, high)
        rows = jnp.where(own_row, high, -1.0)
        left = jnp.concatenate(
            [jnp.where(rows == float(t), 1.0, 0.0) for t in range(tiles)], axis=0
        ).astype(jnp.bfloat16)
        right = jnp.where(low == low_id, 1.0, 0.0).astype(jnp.bfloat16)
        return contract_cols(left, right).reshape(tiles, SLOTS, TILE)

    @pl.loop(0, groups // 2, unroll=2)
    def _(j):
        pair = jnp.concatenate([one_group(2 * j), one_group(2 * j + 1)], axis=1)
        out_ref[:, pl.ds(pl.multiple_of(j * 2 * SLOTS, 2 * SLOTS), 2 * SLOTS), :] = pair.astype(
            out_ref.dtype
        )


def adjacency(near, table, tiles):
    groups = near.shape[0]
    nodes = groups * SLOTS
    step = TILE // SLOTS
    return pl.pallas_call(
        functools.partial(adjacency_body, tiles),
        out_shape=jax.ShapeDtypeStruct((tiles, nodes, TILE), jnp.float8_e4m3fn),
        grid=(groups // step,),
        in_specs=[
            pl.BlockSpec((step, TILE), lambda r: (r, 0)),
            pl.BlockSpec(table.shape, lambda r: (0, 0)),
        ],
        out_specs=pl.BlockSpec((tiles, TILE, TILE), lambda r: (0, r, 0)),
        compiler_params=params(16),
        cost_estimate=cost(2 * nodes * TILE * TILE * tiles * 2, nodes * TILE * tiles),
        name="adjacency",
    )(near, table)


def collect(piece, counts_ref, starts_ref, answer_ref, landed, arrived, packed):
    batch_count = answer_ref.shape[0]

    def bring(o):
        return pltpu.make_async_copy(answer_ref.at[o], landed.at[o], arrived.at[o])

    @pl.loop(0, batch_count)
    def _(o):
        bring(o).start()

    @pl.loop(0, batch_count)
    def _(o):
        bring(o).wait()
        base = starts_ref[o]

        @pl.loop(0, pl.cdiv(counts_ref[o], piece))
        def _(c):
            source = pl.ds(pl.multiple_of(c * piece, piece), piece)
            target = pl.ds(pl.multiple_of(base + c * piece, SLOTS), piece)
            packed[target, :] = landed[o, source, :]

    end = starts_ref[batch_count]
    packed[pl.ds(pl.multiple_of(end, SLOTS), WIDE * TILE), :] = jnp.zeros(
        (WIDE * TILE, packed.shape[1]), packed.dtype
    )


def gather_sum_body(
    piece, last, spans_ref, counts_ref, starts_ref, answer_ref, column_ref, adj_ref, *refs
):
    if last:
        (total_in, found_in, deg_ref, wself_ref, wneigh_ref, own_ref, mean_ref) = refs[:7]
        share_refs = refs[7:-8]
        packed, tiles_ref, ready, landed, arrived, total_ref, found_ref, carried = refs[-8:]
        carry = [
            pltpu.make_async_copy(total_in, total_ref, carried.at[0]),
            pltpu.make_async_copy(found_in, found_ref, carried.at[1]),
        ]
    else:
        total_ref, found_ref, packed, tiles_ref, ready, landed, arrived = refs
        carry = []
    nodes = total_ref.shape[0]
    rows = math.gcd(nodes, 3 * TILE)
    begin, count = spans_ref[0], spans_ref[1]

    def fetch(step, slot):
        return pltpu.make_async_copy(
            adj_ref.at[pl.ds(begin + step * WIDE, WIDE)], tiles_ref.at[slot], ready.at[slot]
        )

    @pl.when(count > 0)
    def _():
        fetch(0, 0).start()

    for copy in carry:
        copy.start()
    collect(piece, counts_ref, starts_ref, answer_ref, landed, arrived, packed)
    for copy in carry:
        copy.wait()
    if not last:
        total_ref[...] = jnp.zeros(total_ref.shape, jnp.float32)
        found_ref[...] = jnp.zeros(found_ref.shape, jnp.float32)

    @pl.loop(0, count)
    def _(step):
        slot = step & 1

        @pl.when(step + 1 < count)
        def _():
            fetch(step + 1, 1 - slot).start()

        fetch(step, slot).wait()
        depth = WIDE * TILE
        block = packed[pl.ds(pl.multiple_of(step * depth, depth), depth), :]
        lane = lax.broadcasted_iota(jnp.int32, (rows, depth), 1) + (begin * TILE + step * depth)

        @pl.loop(0, nodes // rows)
        def _(r):
            part = pl.ds(pl.multiple_of(r * rows, rows), rows)
            near = jnp.concatenate(
                [tiles_ref[slot, w, part, :].astype(jnp.bfloat16) for w in range(WIDE)], axis=1
            )
            own = jnp.where(column_ref[part, :] == lane, 1.0, 0.0).astype(jnp.bfloat16)
            both = jnp.dot(
                jnp.concatenate([near, own], axis=0), block, preferred_element_type=jnp.float32
            )
            total_ref[part, :] += both[:rows]
            found_ref[part, :] += both[rows:]

    if last:
        share = share_refs[0].shape[0]
        step_rows = math.gcd(share, 3 * TILE)
        for p, share_ref in enumerate(share_refs):
            for r in range(share // step_rows):
                part = pl.ds(p * share + r * step_rows, step_rows)
                own = found_ref[part, :].astype(jnp.bfloat16)
                mean = (total_ref[part, :] / deg_ref[part, :]).astype(jnp.bfloat16)
                own_ref[part, :] = own
                mean_ref[part, :] = mean
                share_ref[pl.ds(r * step_rows, step_rows), :] = (
                    jnp.dot(own, wself_ref[...], preferred_element_type=jnp.float32)
                    + jnp.dot(mean, wneigh_ref[...], preferred_element_type=jnp.float32)
                ).astype(share_ref.dtype)


def gather_sum(inputs, parts, spans, counts, starts, answer, column, adj, rest):
    batch_count, width, features = answer.shape
    tiles, nodes, _ = adj.shape
    piece = LANES if width % LANES == 0 else SLOTS
    last = rest is not None
    room = min(batch_count * width, inputs) + SLOTS * batch_count + 2 * WIDE * TILE
    in_specs = [SMEM, SMEM, SMEM, ANY, VMEM, ANY]
    rows = lambda dtype: jax.ShapeDtypeStruct((nodes, features), dtype)
    scratch = [
        pltpu.VMEM((room, features), jnp.bfloat16),
        pltpu.VMEM((2, WIDE, nodes, TILE), adj.dtype),
        pltpu.SemaphoreType.DMA((2,)),
        pltpu.VMEM(answer.shape, answer.dtype),
        pltpu.SemaphoreType.DMA((batch_count,)),
    ]
    operands = [answer, column, adj]
    if last:
        operands += list(rest)
        in_specs += [ANY, ANY, VMEM, VMEM, VMEM]
        share = jax.ShapeDtypeStruct((nodes // parts, rest[3].shape[1]), jnp.bfloat16)
        out_shape = (rows(jnp.bfloat16), rows(jnp.bfloat16)) + (share,) * parts
        scratch += [pltpu.VMEM((nodes, features), jnp.float32)] * 2
        scratch += [pltpu.SemaphoreType.DMA((2,))]
    else:
        out_shape = (rows(jnp.float32), rows(jnp.float32))
    return pl.pallas_call(
        functools.partial(gather_sum_body, piece, last),
        out_shape=out_shape,
        in_specs=in_specs,
        out_specs=(VMEM,) * len(out_shape),
        scratch_shapes=scratch,
        compiler_params=params(40),
        cost_estimate=cost(2 * nodes * features * TILE * tiles, nodes * TILE * tiles // 2),
        name="gather_sum",
    )(spans, counts, starts, *operands)


def share_order(array, parts, seeds):
    others = array.shape[0] - seeds
    own, rest = seeds // parts, others // parts
    tail = array.shape[1:]
    blocks = jnp.concatenate(
        [array[:seeds].reshape(parts, own, *tail), array[seeds:].reshape(parts, rest, *tail)],
        axis=1,
    )
    return ahead(blocks).reshape(array.shape)


def spread(part, axis, count):
    return lax.all_to_all(
        jnp.broadcast_to(part[None], (count,) + part.shape), axis, 0, 0, tiled=True
    )


def passed(part, shift, axis="feat"):
    parts = lax.axis_size(axis)
    return lax.ppermute(part, axis, [((i + shift) % parts, i) for i in range(parts)])


def turned(array, by):
    twice = jnp.concatenate([array, array], axis=0)
    return lax.dynamic_slice_in_dim(twice, by, array.shape[0], 0)


def ahead(array, axis="feat"):
    return turned(array, lax.axis_index(axis))


def spread_parts(part, axis="feat"):
    return [part] + [passed(part, j, axis) for j in range(1, lax.axis_size(axis))]


def sum_parts(blocks, axis="feat"):
    parts = lax.axis_size(axis)
    came = [blocks[0]] + [passed(blocks[j], -j, axis) for j in range(1, parts)]
    return sum(x.astype(jnp.float32) for x in came)


def batch_pieces(one, two):
    both = jnp.concatenate([one, two]).astype(jnp.bfloat16)
    count = lax.axis_size("batch")
    return both.reshape(count, both.shape[0] // count, both.shape[1])


def halves_of(total):
    total = total.reshape(-1, total.shape[-1])
    return total[: total.shape[0] // 2], total[total.shape[0] // 2 :]


def reduce_pieces(pieces):
    pieces = lax.all_to_all(pieces, "batch", 0, 0, tiled=True)
    return jnp.sum(pieces.astype(jnp.float32), axis=0)


def placed(blocks, axis):
    count = lax.axis_size(axis)
    total = jnp.zeros((count,) + blocks[0].shape, blocks[0].dtype)
    for j, block in enumerate(blocks):
        spot = (lax.axis_index(axis) + j) % count
        total = lax.dynamic_update_index_in_dim(total, block, spot, 0)
    return total


def local(
    store,
    input_owner,
    input_row,
    nbr_one,
    deg_one,
    nbr_two,
    deg_two,
    cotangent,
    w1_self,
    w1_neigh,
    bias_one,
    w2_self,
    w2_neigh,
    bias_two,
):
    batch_count = lax.axis_size("batch")
    parts = lax.axis_size("feat")
    feat_index = lax.axis_index("feat")
    input_count = input_owner.shape[1]
    capacity = 2 * input_count // batch_count
    nodes = nbr_one.shape[1]
    seed_rows = nbr_two.shape[1]
    seeds = seed_rows * parts
    share = nodes // parts
    hidden_width = w1_self.shape[1]

    owners = input_owner.reshape(input_count // LANES, LANES)
    wanted = input_row.reshape(input_count // LANES, LANES)
    slots, counts, requests = make_requests(batch_count, capacity, owners, wanted)
    owners = owners.reshape(1, input_count)
    received = lax.all_to_all(
        requests.reshape(batch_count, capacity), "batch", split_axis=0, concat_axis=0, tiled=True
    )
    first = capacity // 2
    places = received.reshape(batch_count * capacity) * (store.shape[1] // LANES)
    looked_a = lookup(store, places, batch_count, 0, first)
    near_first, looked_a = lax.optimization_barrier((nbr_one[0], looked_a))
    answer_a = lax.all_to_all(looked_a, "batch", split_axis=0, concat_axis=0, tiled=True)
    looked = lookup(store, places, batch_count, first, capacity - first)

    depth = WIDE * TILE
    steps = -(-(input_count + 2 * (SLOTS - 1) * batch_count + depth - 1) // depth)
    tally = counts[:, 0]
    tally_a = jnp.minimum(tally, first)
    tally_b = tally - tally_a
    padded = lambda n: (n + SLOTS - 1) // SLOTS * SLOTS
    ends = lambda n: jnp.concatenate([jnp.zeros((1,), jnp.int32), jnp.cumsum(padded(n))])
    starts_a, starts_b = ends(tally_a), ends(tally_b)
    steps_a = (starts_a[batch_count] + depth - 1) // depth
    steps_b = (starts_b[batch_count] + depth - 1) // depth
    spans_a = jnp.stack([jnp.zeros_like(steps_a), steps_a])
    spans_b = jnp.stack([steps_a * WIDE, steps_b])
    slot = slots.reshape(1, input_count)
    shifted = jnp.where(
        slot < first,
        slot + starts_a[:batch_count, None],
        slot - first + steps_a * depth + starts_b[:batch_count, None],
    )
    mine = owners == jnp.arange(batch_count)[:, None]
    column = jnp.sum(jnp.where(mine, shifted, 0), axis=0)
    grid = jnp.pad(column.reshape(-1, LANES), ((0, LANES - input_count // LANES), (0, 0))).T
    table = jnp.concatenate([grid // TILE, grid % TILE], axis=0).astype(jnp.bfloat16)
    own_column = share_order(column[:nodes], parts, seeds).reshape(nodes, 1)

    fanout_two = nbr_two.shape[2]
    used_two = jnp.arange(fanout_two)[:, None] < deg_two
    lists = jnp.concatenate([jnp.where(used_two, nbr_two[0].T, -1), deg_two], axis=0)
    lists = jnp.stack(spread_parts(lists))

    fanout = nbr_one.shape[2]
    used = jnp.arange(fanout)[None, :] < deg_one[0][:, None]
    near = share_order(jnp.where(used, near_first, -1), parts, seeds)
    near = jnp.pad(near, ((0, 0), (0, SLOTS - fanout)), constant_values=-1)
    near, lists = lax.optimization_barrier((near, lists))
    adj = adjacency(near.reshape(nodes // SLOTS, TILE), table, steps * WIDE)
    looked, answer_a, adj = lax.optimization_barrier((looked, answer_a, adj))
    answer_b = lax.all_to_all(looked, "batch", split_axis=0, concat_axis=0, tiled=True)
    deg_first = share_order(deg_one[0], parts, seeds).astype(jnp.float32).reshape(nodes, 1)

    near_two = lists[:, :fanout_two].transpose(1, 0, 2).reshape(fanout_two, seeds)
    deg_all = lists[:, fanout_two].reshape(seeds)
    rest = share - seed_rows
    after = near_two - seeds
    place = jnp.where(
        near_two < seeds,
        near_two // seed_rows * share + near_two % seed_rows,
        after // rest * share + seed_rows + after % rest,
    )
    place = jnp.where(near_two < 0, -1, place - feat_index * share)
    adj_two = jnp.sum(
        place[:, :, None] == jnp.arange(share)[None, None, :], axis=0, dtype=jnp.float32
    ).astype(jnp.bfloat16)

    total, found = gather_sum(
        input_count, parts, spans_a, tally_a, starts_a, answer_a, own_column, adj, None
    )
    self_one, agg_one, *z_blocks = gather_sum(
        input_count,
        parts,
        spans_b,
        tally_b,
        starts_b,
        answer_b,
        own_column,
        adj,
        (total, found, deg_first, w1_self, w1_neigh),
    )
    z_share = sum_parts(z_blocks) + bias_one
    hidden = jax.nn.silu(z_share).astype(jnp.bfloat16)

    agg_parts = jnp.dot(adj_two, hidden, preferred_element_type=jnp.float32)
    agg_total = sum_parts(agg_parts.reshape(parts, seed_rows, hidden_width))
    deg_second = deg_two[0].astype(jnp.float32)[:, None]
    agg_two = (agg_total / deg_second).astype(jnp.bfloat16)
    self_two = hidden[:seed_rows]
    z_two = (
        jnp.dot(self_two, w2_self, preferred_element_type=jnp.float32)
        + jnp.dot(agg_two, w2_neigh, preferred_element_type=jnp.float32)
        + bias_two
    )
    activations = jax.nn.silu(z_two).astype(jnp.bfloat16)[None]
    dz_two = (cotangent[0].astype(jnp.float32) * silu_grad(z_two)).astype(jnp.bfloat16)
    dz_two_all = jnp.concatenate(spread_parts(dz_two))

    back = contract_cols(dz_two_all, w2_neigh) / deg_all.astype(jnp.float32)[:, None]
    back_high = back.astype(jnp.bfloat16)
    back_low = (back - back_high.astype(jnp.float32)).astype(jnp.bfloat16)
    dh_share = contract_rows(adj_two, back_high) + contract_rows(adj_two, back_low)
    dh_share = dh_share + jnp.pad(contract_cols(dz_two, w2_self), ((0, rest), (0, 0)))
    dz_share = (dh_share * silu_grad(z_share)).astype(jnp.bfloat16)
    dz_blocks = spread_parts(dz_share)

    pair = jnp.stack(spread_parts(jnp.stack([self_two, agg_two])), axis=1)
    pair = pair.reshape(2, seeds, hidden_width)
    gw2 = batch_pieces(contract_rows(pair[0], dz_two_all), contract_rows(pair[1], dz_two_all))
    few = batch_count <= FEW
    gw2 = sum_parts(ahead(gw2, "batch"), "batch") if few else reduce_pieces(gw2)
    dz_blocks[-1], gw2 = lax.optimization_barrier((dz_blocks[-1], gw2))
    dz_one = jnp.concatenate(dz_blocks)
    gw1 = batch_pieces(contract_rows(self_one, dz_one), contract_rows(agg_one, dz_one))
    gw1 = reduce_pieces(gw1).astype(jnp.bfloat16)
    gw2 = spread_parts(gw2, "batch") if few else spread(gw2, "batch", batch_count)
    gw1, gw2 = lax.optimization_barrier((gw1, gw2))
    gw1 = spread(gw1, "batch", batch_count).astype(jnp.float32)
    gw2 = placed(gw2, "batch") if few else gw2
    return (activations, *halves_of(gw2), *halves_of(gw1))


def solution(mesh):
    in_specs = (
        P("batch", "feat"),
        P("batch", None, None),
        P("batch", None),
        P("batch", None, None),
        P("batch", None),
        P("batch", "feat", None),
        P("batch", "feat"),
        P("batch", "feat", None),
        P("feat", None),
        P("feat", None),
        P(),
        P(),
        P(),
        P(),
    )
    out_specs = (P("batch", "feat", None), P(), P(), P("feat", None), P("feat", None))
    return jax.shard_map(local, mesh=mesh, in_specs=in_specs, out_specs=out_specs, check_vma=False)
```

```python
import functools
import math

import jax
import jax.numpy as jnp
from jax import lax
from jax.experimental import pallas as pl
from jax.experimental.pallas import tpu as pltpu
from jax.sharding import PartitionSpec as P

TILE = 256
LANES = 128
SLOTS = 16
WIDE = 2
FEW = 16
TILE_BITS, LANE_BITS, SLOT_BITS = 8, 7, 4
MIB = 1024 * 1024
VMEM = pl.BlockSpec(memory_space=pltpu.VMEM)
SMEM = pl.BlockSpec(memory_space=pltpu.SMEM)
ANY = pl.BlockSpec(memory_space=pl.ANY)
HBM = pl.BlockSpec(memory_space=pltpu.HBM)


def silu_grad(values):
    sig = jax.nn.sigmoid(values)
    return sig * (1.0 + values * (1.0 - sig))


def contract_rows(left_side, right_side):
    return lax.dot_general(
        left_side, right_side, (((0,), (0,)), ((), ())), preferred_element_type=jnp.float32
    )


def contract_cols(left_side, right_side):
    return lax.dot_general(
        left_side, right_side, (((1,), (1,)), ((), ())), preferred_element_type=jnp.float32
    )


def params(mib):
    return pltpu.CompilerParams(vmem_limit_bytes=mib * MIB)


def cost(flops, moved):
    return pl.CostEstimate(flops=int(flops), bytes_accessed=int(moved), transcendentals=0)


def requests_body(batch_count, capacity, owner_ref, row_ref, slot_ref, count_ref, request_ref):
    blocks, width = owner_ref.shape[0] // 2, TILE
    places = request_ref.shape[0]
    line = lambda ref, b: jnp.concatenate([ref[2 * b : 2 * b + 1], ref[2 * b + 1 : 2 * b + 2]], axis=1)
    owner_id = lax.broadcasted_iota(jnp.int32, (batch_count, width), 0)
    earlier = lax.broadcasted_iota(jnp.int32, (width, width), 0)
    later = lax.broadcasted_iota(jnp.int32, (width, width), 1)
    upper = jnp.where(earlier <= later, 1.0, 0.0).astype(jnp.bfloat16)
    high_id = lax.broadcasted_iota(jnp.int32, (places, width), 0)
    low_id = lax.broadcasted_iota(jnp.int32, (LANES, width), 0)
    marks = [
        jnp.where(line(owner_ref, b) == owner_id, 1.0, 0.0) for b in range(blocks)
    ]
    stacked = jnp.concatenate(marks, axis=0).astype(jnp.bfloat16)
    prefix = jnp.dot(stacked, upper, preferred_element_type=jnp.float32)
    running = jnp.zeros((batch_count, 1), jnp.float32)
    total = jnp.zeros((2 * places, LANES), jnp.float32)
    for b in range(blocks):
        part = prefix[b * batch_count : (b + 1) * batch_count]
        slots = jnp.sum(marks[b] * (part + running - 1.0), axis=0, keepdims=True)
        slots = slots.astype(jnp.int32)
        slot_ref[2 * b : 2 * b + 1, :] = slots[:, :LANES]
        slot_ref[2 * b + 1 : 2 * b + 2, :] = slots[:, LANES:]
        running = running + part[:, width - 1 : width]
        bucket = line(owner_ref, b) * capacity + slots
        rows = line(row_ref, b)
        hit = (bucket >> LANE_BITS) == high_id
        left = jnp.concatenate(
            [
                jnp.where(hit, (rows >> TILE_BITS).astype(jnp.float32), 0.0),
                jnp.where(hit, (rows & (TILE - 1)).astype(jnp.float32), 0.0),
            ],
            axis=0,
        ).astype(jnp.bfloat16)
        right = jnp.where((bucket & (LANES - 1)) == low_id, 1.0, 0.0).astype(jnp.bfloat16)
        total = total + contract_cols(left, right)
    count_ref[...] = jnp.broadcast_to(running, count_ref.shape).astype(jnp.int32)
    request_ref[...] = (total[:places] * TILE + total[places:]).astype(jnp.int32)


def make_requests(batch_count, capacity, owners, wanted):
    total = owners.shape[0] * LANES
    places = batch_count * capacity // LANES
    return pl.pallas_call(
        functools.partial(requests_body, batch_count, capacity),
        out_shape=(
            jax.ShapeDtypeStruct(owners.shape, jnp.int32),
            jax.ShapeDtypeStruct((batch_count, LANES), jnp.int32),
            jax.ShapeDtypeStruct((places, LANES), jnp.int32),
        ),
        in_specs=[VMEM, VMEM],
        out_specs=(VMEM, VMEM, VMEM),
        compiler_params=params(16),
        cost_estimate=cost(4 * total * places * LANES, 24 * total),
        name="requests",
    )(owners, wanted)


def lookup_body(stride, first, width, want_ref, store_ref, out_ref, table, lines):
    rows_all = store_ref.shape[0]
    halves = store_ref.shape[1] // LANES
    lane = lambda h: pl.ds(h * LANES, LANES)
    begin = pl.program_id(0) * stride + first

    @pl.when(pl.program_id(0) == 0)
    def _():
        @pl.loop(0, rows_all // TILE)
        def _(j):
            part = pl.ds(pl.multiple_of(j * TILE, TILE), TILE)
            for h in range(halves):
                spot = pl.ds(pl.multiple_of(j * TILE * halves, TILE) + h, TILE, stride=halves)
                table[spot, :] = store_ref[part, lane(h)].astype(jnp.float32)

    @pl.loop(0, width // SLOTS, unroll=2)
    def _(j):
        at = [want_ref[begin + j * SLOTS + u] for u in range(SLOTS)]
        rows = [table[pl.ds(pl.multiple_of(a, halves), halves), :] for a in at]
        block = lines.at[pl.ds(pl.multiple_of(j * SLOTS * halves, SLOTS * halves), SLOTS * halves)]
        for u in range(SLOTS):
            block[pl.ds(u * halves, halves), :] = rows[u]

    for h in range(halves):
        out_ref[0, :, lane(h)] = lines[pl.ds(h, width, stride=halves), :].astype(jnp.bfloat16)


def lookup(store, places, groups, first, width):
    rows_all, features = store.shape
    halves = features // LANES
    apart = lambda rows: pltpu.VMEM((rows * halves, LANES), jnp.float32)
    return pl.pallas_call(
        functools.partial(lookup_body, places.shape[0] // groups, first, width),
        out_shape=jax.ShapeDtypeStruct((groups, width, features), jnp.bfloat16),
        grid=(groups,),
        in_specs=[SMEM, pl.BlockSpec((rows_all, features), lambda g: (0, 0))],
        out_specs=pl.BlockSpec((1, width, features), lambda g: (g, 0, 0)),
        scratch_shapes=[apart(rows_all), apart(width)],
        compiler_params=params(24),
        cost_estimate=cost(groups * width * features * 40, 2 * rows_all * features),
        name="lookup",
    )(places, store)


def adjacency_body(tiles, me_ref, near_ref, table_ref, out_ref):
    groups = near_ref.shape[0]
    node_high = lax.broadcasted_iota(jnp.int32, (LANES, TILE), 0)
    own_row = (
        lax.shift_right_logical(lax.broadcasted_iota(jnp.int32, (SLOTS, TILE), 1), SLOT_BITS)
        == lax.broadcasted_iota(jnp.int32, (SLOTS, TILE), 0)
    )
    low_id = lax.broadcasted_iota(jnp.int32, (TILE, TILE), 0).astype(jnp.float32)

    def one_group(g):
        near = near_ref[pl.ds(g, 1), :]
        pick = jnp.where((near >> LANE_BITS) == node_high, 1.0, 0.0).astype(jnp.bfloat16)
        found = jnp.dot(table_ref[...], pick, preferred_element_type=jnp.float32)
        here = (near & (LANES - 1)) == node_high
        high = jnp.sum(jnp.where(here, found[:LANES], 0.0), axis=0, keepdims=True)
        low = jnp.sum(jnp.where(here, found[LANES:], 0.0), axis=0, keepdims=True)
        high = jnp.where(near < 0, -1.0, high)
        rows = jnp.where(own_row, high, -1.0)
        left = jnp.concatenate(
            [jnp.where(rows == float(t), 1.0, 0.0) for t in range(tiles)], axis=0
        ).astype(jnp.bfloat16)
        right = jnp.where(low == low_id, 1.0, 0.0).astype(jnp.bfloat16)
        return contract_cols(left, right).reshape(tiles, SLOTS, TILE)

    @pl.loop(0, groups // 2, unroll=2)
    def _(j):
        pair = jnp.concatenate([one_group(2 * j), one_group(2 * j + 1)], axis=1)
        out_ref[:, pl.ds(pl.multiple_of(j * 2 * SLOTS, 2 * SLOTS), 2 * SLOTS), :] = pair.astype(
            out_ref.dtype
        )


def adjacency(me, near, table, tiles, parts, seeds):
    groups = near.shape[0]
    nodes = groups * SLOTS
    step = LANES // SLOTS
    own, rest, share = (n // parts // LANES for n in (seeds, nodes - seeds, nodes))

    def place(block, me_ref):
        after = block - own * parts
        is_own = after < 0
        part = jnp.where(is_own, lax.div(block, own), lax.div(after, rest))
        at = jnp.where(is_own, lax.rem(block, own), own + lax.rem(after, rest))
        return (0, lax.rem(part - me_ref[0] + parts, parts) * share + at, 0)

    return pl.pallas_call(
        functools.partial(adjacency_body, tiles),
        out_shape=jax.ShapeDtypeStruct((tiles, nodes, TILE), jnp.float8_e4m3fn),
        grid_spec=pltpu.PrefetchScalarGridSpec(
            num_scalar_prefetch=1,
            grid=(groups // step,),
            in_specs=[
                pl.BlockSpec((step, TILE), lambda r, me: (r, 0)),
                pl.BlockSpec(table.shape, lambda r, me: (0, 0)),
            ],
            out_specs=pl.BlockSpec((tiles, LANES, TILE), place),
        ),
        compiler_params=params(48),
        cost_estimate=cost(2 * nodes * TILE * TILE * tiles * 2, nodes * TILE * tiles),
        name="adjacency",
    )(me, near, table)


def collect(piece, counts_ref, starts_ref, answer_ref, landed, arrived, packed):
    batch_count = answer_ref.shape[0]

    def bring(o):
        return pltpu.make_async_copy(answer_ref.at[o], landed.at[o], arrived.at[o])

    @pl.loop(0, batch_count)
    def _(o):
        bring(o).start()

    @pl.loop(0, batch_count)
    def _(o):
        bring(o).wait()
        base = starts_ref[o]

        @pl.loop(0, pl.cdiv(counts_ref[o], piece))
        def _(c):
            source = pl.ds(pl.multiple_of(c * piece, piece), piece)
            target = pl.ds(pl.multiple_of(base + c * piece, SLOTS), piece)
            packed[target, :] = landed[o, source, :]

    end = starts_ref[batch_count]
    packed[pl.ds(pl.multiple_of(end, SLOTS), WIDE * TILE), :] = jnp.zeros(
        (WIDE * TILE, packed.shape[1]), packed.dtype
    )


def gather_sum_body(
    piece, last, spans_ref, counts_ref, starts_ref, answer_ref, notes_in, adj_ref, *refs
):
    if last:
        (total_in, found_in, wself_in, wneigh_in, own_ref, mean_ref) = refs[:6]
        share_refs = refs[6:-11]
        packed, tiles_ref, ready, landed, arrived, notes_ref, carried = refs[-11:-4]
        total_ref, found_ref, wself_ref, wneigh_ref = refs[-4:]
        pairs = ((notes_in, notes_ref), (total_in, total_ref), (found_in, found_ref))
        pairs += ((wself_in, wself_ref), (wneigh_in, wneigh_ref))
    else:
        total_ref, found_ref, packed, tiles_ref, ready, landed, arrived, notes_ref, carried = refs
        pairs = ((notes_in, notes_ref),)
    carry = [pltpu.make_async_copy(*pair, carried.at[n]) for n, pair in enumerate(pairs)]
    nodes = total_ref.shape[0]
    rows = math.gcd(nodes, 3 * TILE)
    begin, count = spans_ref[0], spans_ref[1]

    def fetch(step, slot):
        return pltpu.make_async_copy(
            adj_ref.at[pl.ds(begin + step * WIDE, WIDE)], tiles_ref.at[slot], ready.at[slot]
        )

    @pl.when(count > 0)
    def _():
        fetch(0, 0).start()

    for copy in carry:
        copy.start()
    collect(piece, counts_ref, starts_ref, answer_ref, landed, arrived, packed)
    for copy in carry:
        copy.wait()
    if not last:
        total_ref[...] = jnp.zeros(total_ref.shape, jnp.float32)
        found_ref[...] = jnp.zeros(found_ref.shape, jnp.float32)

    @pl.loop(0, count)
    def _(step):
        slot = step & 1

        @pl.when(step + 1 < count)
        def _():
            fetch(step + 1, 1 - slot).start()

        fetch(step, slot).wait()
        depth = WIDE * TILE
        block = packed[pl.ds(pl.multiple_of(step * depth, depth), depth), :]
        lane = lax.broadcasted_iota(jnp.int32, (rows, depth), 1) + (begin * TILE + step * depth)
        lane = lane.astype(jnp.float32)

        @pl.loop(0, nodes // rows)
        def _(r):
            part = pl.ds(pl.multiple_of(r * rows, rows), rows)
            near = jnp.concatenate(
                [tiles_ref[slot, w, part, :].astype(jnp.bfloat16) for w in range(WIDE)], axis=1
            )
            own = jnp.where(notes_ref[part, 0:1] == lane, 1.0, 0.0).astype(jnp.bfloat16)
            both = jnp.dot(
                jnp.concatenate([near, own], axis=0), block, preferred_element_type=jnp.float32
            )
            total_ref[part, :] += both[:rows]
            found_ref[part, :] += both[rows:]

    if last:
        share = share_refs[0].shape[0]
        step_rows = math.gcd(share, 3 * TILE)
        for p, share_ref in enumerate(share_refs):
            for r in range(share // step_rows):
                part = pl.ds(p * share + r * step_rows, step_rows)
                own = found_ref[part, :].astype(jnp.bfloat16)
                mean = (total_ref[part, :] / notes_ref[part, 1:2]).astype(jnp.bfloat16)
                own_ref[part, :] = own
                mean_ref[part, :] = mean
                share_ref[pl.ds(r * step_rows, step_rows), :] = (
                    jnp.dot(own, wself_ref[...], preferred_element_type=jnp.float32)
                    + jnp.dot(mean, wneigh_ref[...], preferred_element_type=jnp.float32)
                ).astype(share_ref.dtype)


def gather_sum(inputs, parts, spans, counts, starts, answer, notes, adj, rest):
    batch_count, width, features = answer.shape
    tiles, nodes, _ = adj.shape
    piece = LANES if width % LANES == 0 else SLOTS
    last = rest is not None
    room = min(batch_count * width, inputs) + SLOTS * batch_count + 2 * WIDE * TILE
    in_specs = [SMEM, SMEM, SMEM, ANY, HBM, HBM]
    rows = lambda dtype: jax.ShapeDtypeStruct((nodes, features), dtype)
    scratch = [
        pltpu.VMEM((room, features), jnp.bfloat16),
        pltpu.VMEM((2, WIDE, nodes, TILE), adj.dtype),
        pltpu.SemaphoreType.DMA((2,)),
        pltpu.VMEM(answer.shape, answer.dtype),
        pltpu.SemaphoreType.DMA((batch_count,)),
        pltpu.VMEM(notes.shape, notes.dtype),
        pltpu.SemaphoreType.DMA((5,)),
    ]
    operands = [answer, notes, adj]
    if last:
        operands += list(rest)
        in_specs += [HBM] * len(rest)
        share = jax.ShapeDtypeStruct((nodes // parts, rest[3].shape[1]), jnp.bfloat16)
        out_shape = (rows(jnp.bfloat16), rows(jnp.bfloat16)) + (share,) * parts
        scratch += [pltpu.VMEM(x.shape, x.dtype) for x in rest]
    else:
        out_shape = (rows(jnp.float32), rows(jnp.float32))
    return pl.pallas_call(
        functools.partial(gather_sum_body, piece, last),
        out_shape=out_shape,
        in_specs=in_specs,
        out_specs=(VMEM,) * len(out_shape),
        scratch_shapes=scratch,
        compiler_params=params(50),
        cost_estimate=cost(2 * nodes * features * TILE * tiles, nodes * TILE * tiles // 2),
        name="gather_sum",
    )(spans, counts, starts, *operands)


def share_order(array, parts, seeds):
    others = array.shape[0] - seeds
    own, rest = seeds // parts, others // parts
    tail = array.shape[1:]
    blocks = jnp.concatenate(
        [array[:seeds].reshape(parts, own, *tail), array[seeds:].reshape(parts, rest, *tail)],
        axis=1,
    )
    return ahead(blocks).reshape(array.shape)


def spread(part, axis, count):
    return lax.all_to_all(
        jnp.broadcast_to(part[None], (count,) + part.shape), axis, 0, 0, tiled=True
    )


def passed(part, shift, axis="feat"):
    parts = lax.axis_size(axis)
    return lax.ppermute(part, axis, [((i + shift) % parts, i) for i in range(parts)])


def turned(array, by):
    twice = jnp.concatenate([array, array], axis=0)
    return lax.dynamic_slice_in_dim(twice, by, array.shape[0], 0)


def ahead(array, axis="feat"):
    return turned(array, lax.axis_index(axis))


def spread_parts(part, axis="feat"):
    return [part] + [passed(part, j, axis) for j in range(1, lax.axis_size(axis))]


def sum_parts(blocks, axis="feat"):
    parts = lax.axis_size(axis)
    came = [blocks[0]] + [passed(blocks[j], -j, axis) for j in range(1, parts)]
    return sum(x.astype(jnp.float32) for x in came)


def swapped(part):
    return lax.ppermute(part, "batch", [(i, i ^ 1) for i in range(lax.axis_size("batch"))])


def total_over_batch(terms):
    count = lax.axis_size("batch")
    rows, width = terms.shape
    if count > FEW:
        pieces = terms.astype(jnp.bfloat16).reshape(count, rows // count, width)
        pieces = lax.all_to_all(pieces, "batch", 0, 0, tiled=True)
        total = jnp.sum(pieces.astype(jnp.float32), axis=0).astype(jnp.bfloat16)
        return spread(total, "batch", count).reshape(rows, width)
    chips = count // 2
    index = lax.axis_index("batch")
    first, chip = index % 2 == 0, index // 2
    upper, lower = terms[: rows // 2], terms[rows // 2 :]
    came = swapped(jnp.where(first, lower, upper).astype(jnp.bfloat16))
    mine = jnp.where(first, upper, lower) + came.astype(jnp.float32)
    pieces = turned(mine.reshape(chips, rows // count, width), chip)
    total = pieces[0]
    for j in range(1, chips):
        total = total + passed(pieces[j].astype(jnp.bfloat16), -2 * j, "batch").astype(jnp.float32)
    total = total.astype(jnp.bfloat16)
    mine = jnp.stack([total] + [passed(total, 2 * j, "batch") for j in range(1, chips)])
    other = swapped(mine)
    both = jnp.stack([jnp.where(first, mine, other), jnp.where(first, other, mine)], axis=1)
    return turned(both, (chips - chip) % chips).transpose(1, 0, 2, 3).reshape(rows, width)


def local(
    store,
    input_owner,
    input_row,
    nbr_one,
    deg_one,
    nbr_two,
    deg_two,
    cotangent,
    w1_self,
    w1_neigh,
    bias_one,
    w2_self,
    w2_neigh,
    bias_two,
):
    batch_count = lax.axis_size("batch")
    parts = lax.axis_size("feat")
    feat_index = lax.axis_index("feat")
    input_count = input_owner.shape[1]
    capacity = 2 * input_count // batch_count
    nodes = nbr_one.shape[1]
    seed_rows = nbr_two.shape[1]
    seeds = seed_rows * parts
    share = nodes // parts
    hidden_width = w1_self.shape[1]

    owners = input_owner.reshape(input_count // LANES, LANES)
    wanted = input_row.reshape(input_count // LANES, LANES)
    slots, counts, requests = make_requests(batch_count, capacity, owners, wanted)
    owners = owners.reshape(1, input_count)
    received = lax.all_to_all(
        requests.reshape(batch_count, capacity), "batch", split_axis=0, concat_axis=0, tiled=True
    )
    first = capacity // 2
    places = received.reshape(batch_count * capacity) * (store.shape[1] // LANES)
    looked_a = lookup(store, places, batch_count, 0, first)
    near_first, looked_a = lax.optimization_barrier((nbr_one[0], looked_a))
    answer_a = lax.all_to_all(looked_a, "batch", split_axis=0, concat_axis=0, tiled=True)
    looked = lookup(store, places, batch_count, first, capacity - first)

    depth = WIDE * TILE
    steps = -(-(input_count + 2 * (SLOTS - 1) * batch_count + depth - 1) // depth)
    tally = counts[:, 0]
    tally_a = jnp.minimum(tally, first)
    tally_b = tally - tally_a
    padded = lambda n: (n + SLOTS - 1) // SLOTS * SLOTS
    ends = lambda n: jnp.concatenate([jnp.zeros((1,), jnp.int32), jnp.cumsum(padded(n))])
    starts_a, starts_b = ends(tally_a), ends(tally_b)
    steps_a = (starts_a[batch_count] + depth - 1) // depth
    steps_b = (starts_b[batch_count] + depth - 1) // depth
    spans_a = jnp.stack([jnp.zeros_like(steps_a), steps_a])
    spans_b = jnp.stack([steps_a * WIDE, steps_b])
    slot = slots.reshape(1, input_count)
    shifted = jnp.where(
        slot < first,
        slot + starts_a[:batch_count, None],
        slot - first + steps_a * depth + starts_b[:batch_count, None],
    )
    mine = owners == jnp.arange(batch_count)[:, None]
    column = jnp.sum(jnp.where(mine, shifted, 0), axis=0)
    grid = jnp.pad(column.reshape(-1, LANES), ((0, LANES - input_count // LANES), (0, 0))).T
    table = jnp.concatenate([grid // TILE, grid % TILE], axis=0).astype(jnp.bfloat16)
    notes = jnp.stack([column[:nodes], deg_one[0]], axis=1).astype(jnp.float32)
    notes = share_order(notes, parts, seeds)

    fanout_two = nbr_two.shape[2]
    used_two = jnp.arange(fanout_two)[:, None] < deg_two
    lists = jnp.concatenate([jnp.where(used_two, nbr_two[0].T, -1), deg_two], axis=0)
    lists = jnp.stack(spread_parts(lists))

    fanout = nbr_one.shape[2]
    used = jnp.arange(fanout)[None, :] < deg_one[0][:, None]
    near = jnp.pad(jnp.where(used, near_first, -1), ((0, 0), (0, SLOTS - fanout)), constant_values=-1)
    near, lists = lax.optimization_barrier((near, lists))
    me = feat_index.astype(jnp.int32).reshape(1)
    near = near.reshape(nodes // SLOTS, TILE)
    adj = adjacency(me, near, table, steps * WIDE, parts, seeds)
    looked, answer_a, adj = lax.optimization_barrier((looked, answer_a, adj))
    answer_b = lax.all_to_all(looked, "batch", split_axis=0, concat_axis=0, tiled=True)

    near_two = lists[:, :fanout_two].transpose(1, 0, 2).reshape(fanout_two, seeds)
    deg_all = lists[:, fanout_two].reshape(seeds)
    rest = share - seed_rows
    after = near_two - seeds
    place = jnp.where(
        near_two < seeds,
        near_two // seed_rows * share + near_two % seed_rows,
        after // rest * share + seed_rows + after % rest,
    )
    place = jnp.where(near_two < 0, -1, place - feat_index * share)
    adj_two = jnp.sum(
        place[:, :, None] == jnp.arange(share)[None, None, :], axis=0, dtype=jnp.float32
    ).astype(jnp.bfloat16)

    total, found = gather_sum(
        input_count, parts, spans_a, tally_a, starts_a, answer_a, notes, adj, None
    )
    self_one, agg_one, *z_blocks = gather_sum(
        input_count,
        parts,
        spans_b,
        tally_b,
        starts_b,
        answer_b,
        notes,
        adj,
        (total, found, w1_self, w1_neigh),
    )
    z_share = sum_parts(z_blocks) + bias_one
    hidden = jax.nn.silu(z_share).astype(jnp.bfloat16)

    agg_parts = jnp.dot(adj_two, hidden, preferred_element_type=jnp.float32)
    agg_total = sum_parts(agg_parts.reshape(parts, seed_rows, hidden_width))
    deg_second = deg_two[0].astype(jnp.float32)[:, None]
    agg_two = (agg_total / deg_second).astype(jnp.bfloat16)
    self_two = hidden[:seed_rows]
    z_two = (
        jnp.dot(self_two, w2_self, preferred_element_type=jnp.float32)
        + jnp.dot(agg_two, w2_neigh, preferred_element_type=jnp.float32)
        + bias_two
    )
    activations = jax.nn.silu(z_two).astype(jnp.bfloat16)[None]
    dz_two = (cotangent[0].astype(jnp.float32) * silu_grad(z_two)).astype(jnp.bfloat16)
    group = jnp.stack(spread_parts(jnp.stack([self_two, agg_two, dz_two])))
    dz_two_all = group[:, 2].reshape(seeds, hidden_width)

    back = contract_cols(dz_two_all, w2_neigh) / deg_all.astype(jnp.float32)[:, None]
    back_high = back.astype(jnp.bfloat16)
    back_low = (back - back_high.astype(jnp.float32)).astype(jnp.bfloat16)
    dh_share = contract_rows(adj_two, back_high) + contract_rows(adj_two, back_low)
    dh_share = dh_share + jnp.pad(contract_cols(dz_two, w2_self), ((0, rest), (0, 0)))
    dz_share = (dh_share * silu_grad(z_share)).astype(jnp.bfloat16)
    dz_one = jnp.concatenate(spread_parts(dz_share))
    group = turned(group, (parts - feat_index) % parts).transpose(1, 0, 2, 3)
    self_all, agg_all, dz_all = (x.reshape(seeds, hidden_width) for x in group)
    grads = [contract_rows(self_all, dz_all), contract_rows(agg_all, dz_all)]
    grads += [contract_rows(self_one, dz_one), contract_rows(agg_one, dz_one)]
    total = total_over_batch(jnp.concatenate(grads)).astype(jnp.float32)
    return (activations, *total.reshape(len(grads), -1, hidden_width))


def solution(mesh):
    in_specs = (
        P("batch", "feat"),
        P("batch", None, None),
        P("batch", None),
        P("batch", None, None),
        P("batch", None),
        P("batch", "feat", None),
        P("batch", "feat"),
        P("batch", "feat", None),
        P("feat", None),
        P("feat", None),
        P(),
        P(),
        P(),
        P(),
    )
    out_specs = (P("batch", "feat", None), P(), P(), P("feat", None), P("feat", None))
    return jax.shard_map(local, mesh=mesh, in_specs=in_specs, out_specs=out_specs, check_vma=False)
```

```python
import functools
import math

import jax
import jax.numpy as jnp
from jax import lax
from jax.experimental import pallas as pl
from jax.experimental.pallas import tpu as pltpu
from jax.sharding import PartitionSpec as P

TILE = 256
LANES = 128
SLOTS = 16
WIDE = 2
FEW = 16
TILE_BITS, LANE_BITS, SLOT_BITS = 8, 7, 4
MIB = 1024 * 1024
VMEM = pl.BlockSpec(memory_space=pltpu.VMEM)
SMEM = pl.BlockSpec(memory_space=pltpu.SMEM)
ANY = pl.BlockSpec(memory_space=pl.ANY)
HBM = pl.BlockSpec(memory_space=pltpu.HBM)


def silu_grad(values):
    sig = jax.nn.sigmoid(values)
    return sig * (1.0 + values * (1.0 - sig))


def contract_rows(left_side, right_side):
    return lax.dot_general(
        left_side, right_side, (((0,), (0,)), ((), ())), preferred_element_type=jnp.float32
    )


def contract_cols(left_side, right_side):
    return lax.dot_general(
        left_side, right_side, (((1,), (1,)), ((), ())), preferred_element_type=jnp.float32
    )


def params(mib):
    return pltpu.CompilerParams(vmem_limit_bytes=mib * MIB)


def cost(flops, moved):
    return pl.CostEstimate(flops=int(flops), bytes_accessed=int(moved), transcendentals=0)


def requests_body(batch_count, capacity, owner_ref, row_ref, slot_ref, count_ref, request_ref):
    blocks, width = owner_ref.shape[0] // 2, TILE
    places = request_ref.shape[0]
    line = lambda ref, b: jnp.concatenate([ref[2 * b : 2 * b + 1], ref[2 * b + 1 : 2 * b + 2]], axis=1)
    owner_id = lax.broadcasted_iota(jnp.int32, (batch_count, width), 0)
    earlier = lax.broadcasted_iota(jnp.int32, (width, width), 0)
    later = lax.broadcasted_iota(jnp.int32, (width, width), 1)
    upper = jnp.where(earlier <= later, 1.0, 0.0).astype(jnp.bfloat16)
    high_id = lax.broadcasted_iota(jnp.int32, (places, width), 0)
    low_id = lax.broadcasted_iota(jnp.int32, (LANES, width), 0)
    marks = [
        jnp.where(line(owner_ref, b) == owner_id, 1.0, 0.0) for b in range(blocks)
    ]
    stacked = jnp.concatenate(marks, axis=0).astype(jnp.bfloat16)
    prefix = jnp.dot(stacked, upper, preferred_element_type=jnp.float32)
    running = jnp.zeros((batch_count, 1), jnp.float32)
    total = jnp.zeros((2 * places, LANES), jnp.float32)
    for b in range(blocks):
        part = prefix[b * batch_count : (b + 1) * batch_count]
        slots = jnp.sum(marks[b] * (part + running - 1.0), axis=0, keepdims=True)
        slots = slots.astype(jnp.int32)
        slot_ref[2 * b : 2 * b + 1, :] = slots[:, :LANES]
        slot_ref[2 * b + 1 : 2 * b + 2, :] = slots[:, LANES:]
        running = running + part[:, width - 1 : width]
        bucket = line(owner_ref, b) * capacity + slots
        rows = line(row_ref, b)
        hit = (bucket >> LANE_BITS) == high_id
        left = jnp.concatenate(
            [
                jnp.where(hit, (rows >> TILE_BITS).astype(jnp.float32), 0.0),
                jnp.where(hit, (rows & (TILE - 1)).astype(jnp.float32), 0.0),
            ],
            axis=0,
        ).astype(jnp.bfloat16)
        right = jnp.where((bucket & (LANES - 1)) == low_id, 1.0, 0.0).astype(jnp.bfloat16)
        total = total + contract_cols(left, right)
    count_ref[...] = jnp.broadcast_to(running, count_ref.shape).astype(jnp.int32)
    request_ref[...] = (total[:places] * TILE + total[places:]).astype(jnp.int32)


def make_requests(batch_count, capacity, owners, wanted):
    total = owners.shape[0] * LANES
    places = batch_count * capacity // LANES
    return pl.pallas_call(
        functools.partial(requests_body, batch_count, capacity),
        out_shape=(
            jax.ShapeDtypeStruct(owners.shape, jnp.int32),
            jax.ShapeDtypeStruct((batch_count, LANES), jnp.int32),
            jax.ShapeDtypeStruct((places, LANES), jnp.int32),
        ),
        in_specs=[VMEM, VMEM],
        out_specs=(VMEM, VMEM, VMEM),
        compiler_params=params(16),
        cost_estimate=cost(4 * total * places * LANES, 24 * total),
        name="requests",
    )(owners, wanted)


def lookup_body(stride, first, width, want_ref, store_ref, *refs):
    *out_refs, table, lines = refs
    rows_all = store_ref.shape[0]
    halves = store_ref.shape[1] // LANES
    lane = lambda h: pl.ds(h * LANES, LANES)

    @pl.loop(0, rows_all // TILE)
    def _(j):
        part = pl.ds(pl.multiple_of(j * TILE, TILE), TILE)
        for h in range(halves):
            spot = pl.ds(pl.multiple_of(j * TILE * halves, TILE) + h, TILE, stride=halves)
            table[spot, :] = store_ref[part, lane(h)].astype(jnp.float32)

    group = 0
    for out_ref in out_refs:

        @pl.loop(0, out_ref.shape[0])
        def _(k, out_ref=out_ref, group=group):
            begin = (group + k) * stride + first

            @pl.loop(0, width // SLOTS, unroll=2)
            def _(j):
                at = [want_ref[begin + j * SLOTS + u] for u in range(SLOTS)]
                rows = [table[pl.ds(pl.multiple_of(a, halves), halves), :] for a in at]
                depth = SLOTS * halves
                block = lines.at[pl.ds(pl.multiple_of(j * depth, depth), depth)]
                for u in range(SLOTS):
                    block[pl.ds(u * halves, halves), :] = rows[u]

            for h in range(halves):
                out_ref[k, :, lane(h)] = lines[pl.ds(h, width, stride=halves), :].astype(
                    jnp.bfloat16
                )

        group += out_ref.shape[0]


def lookup(store, places, sizes, first, width):
    rows_all, features = store.shape
    halves = features // LANES
    apart = lambda rows: pltpu.VMEM((rows * halves, LANES), jnp.float32)
    return pl.pallas_call(
        functools.partial(lookup_body, places.shape[0] // sum(sizes), first, width),
        out_shape=[jax.ShapeDtypeStruct((n, width, features), jnp.bfloat16) for n in sizes],
        in_specs=[SMEM, VMEM],
        out_specs=[VMEM] * len(sizes),
        scratch_shapes=[apart(rows_all), apart(width)],
        compiler_params=params(24),
        cost_estimate=cost(sum(sizes) * width * features * 40, 2 * rows_all * features),
        name="lookup",
    )(places, store)


def adjacency_body(tiles, me_ref, near_ref, table_ref, out_ref):
    groups = near_ref.shape[0]
    node_high = lax.broadcasted_iota(jnp.int32, (LANES, TILE), 0)
    own_row = (
        lax.shift_right_logical(lax.broadcasted_iota(jnp.int32, (SLOTS, TILE), 1), SLOT_BITS)
        == lax.broadcasted_iota(jnp.int32, (SLOTS, TILE), 0)
    )
    low_id = lax.broadcasted_iota(jnp.int32, (TILE, TILE), 0).astype(jnp.float32)

    def one_group(g):
        near = near_ref[pl.ds(g, 1), :]
        pick = jnp.where((near >> LANE_BITS) == node_high, 1.0, 0.0).astype(jnp.bfloat16)
        found = jnp.dot(table_ref[...], pick, preferred_element_type=jnp.float32)
        here = (near & (LANES - 1)) == node_high
        high = jnp.sum(jnp.where(here, found[:LANES], 0.0), axis=0, keepdims=True)
        low = jnp.sum(jnp.where(here, found[LANES:], 0.0), axis=0, keepdims=True)
        high = jnp.where(near < 0, -1.0, high)
        rows = jnp.where(own_row, high, -1.0)
        left = jnp.concatenate(
            [jnp.where(rows == float(t), 1.0, 0.0) for t in range(tiles)], axis=0
        ).astype(jnp.bfloat16)
        right = jnp.where(low == low_id, 1.0, 0.0).astype(jnp.bfloat16)
        return contract_cols(left, right).reshape(tiles, SLOTS, TILE)

    @pl.loop(0, groups // 2, unroll=2)
    def _(j):
        pair = jnp.concatenate([one_group(2 * j), one_group(2 * j + 1)], axis=1)
        out_ref[:, pl.ds(pl.multiple_of(j * 2 * SLOTS, 2 * SLOTS), 2 * SLOTS), :] = pair.astype(
            out_ref.dtype
        )


def adjacency(me, near, table, tiles, parts, seeds):
    groups = near.shape[0]
    nodes = groups * SLOTS
    step = LANES // SLOTS
    own, rest, share = (n // parts // LANES for n in (seeds, nodes - seeds, nodes))

    def place(block, me_ref):
        after = block - own * parts
        is_own = after < 0
        part = jnp.where(is_own, lax.div(block, own), lax.div(after, rest))
        at = jnp.where(is_own, lax.rem(block, own), own + lax.rem(after, rest))
        return (0, lax.rem(part - me_ref[0] + parts, parts) * share + at, 0)

    return pl.pallas_call(
        functools.partial(adjacency_body, tiles),
        out_shape=jax.ShapeDtypeStruct((tiles, nodes, TILE), jnp.float8_e4m3fn),
        grid_spec=pltpu.PrefetchScalarGridSpec(
            num_scalar_prefetch=1,
            grid=(groups // step,),
            in_specs=[
                pl.BlockSpec((step, TILE), lambda r, me: (r, 0)),
                pl.BlockSpec(table.shape, lambda r, me: (0, 0)),
            ],
            out_specs=pl.BlockSpec((tiles, LANES, TILE), place),
        ),
        compiler_params=params(48),
        cost_estimate=cost(2 * nodes * TILE * TILE * tiles * 2, nodes * TILE * tiles),
        name="adjacency",
    )(me, near, table)


def collect(piece, counts_ref, starts_ref, answer_refs, landed, arrived, packed):
    batch_count = landed.shape[0]
    each = batch_count // len(answer_refs)

    def bring(n):
        return pltpu.make_async_copy(
            answer_refs[n], landed.at[pl.ds(n * each, each)], arrived.at[n]
        )

    for n in range(len(answer_refs)):
        bring(n).start()
    for n in range(len(answer_refs)):
        bring(n).wait()

    @pl.loop(0, batch_count)
    def _(o):
        base = starts_ref[o]

        @pl.loop(0, pl.cdiv(counts_ref[o], piece))
        def _(c):
            source = pl.ds(pl.multiple_of(c * piece, piece), piece)
            target = pl.ds(pl.multiple_of(base + c * piece, SLOTS), piece)
            packed[target, :] = landed[o, source, :]

    end = starts_ref[batch_count]
    packed[pl.ds(pl.multiple_of(end, SLOTS), WIDE * TILE), :] = jnp.zeros(
        (WIDE * TILE, packed.shape[1]), packed.dtype
    )


def gather_sum_body(
    piece, last, answers, spans_ref, counts_ref, starts_ref, notes_in, adj_ref, *refs
):
    answer_refs, refs = refs[:answers], refs[answers:]
    if last:
        (total_in, found_in, wself_in, wneigh_in, own_ref, mean_ref) = refs[:6]
        share_refs = refs[6:-11]
        packed, tiles_ref, ready, landed, arrived, notes_ref, carried = refs[-11:-4]
        total_ref, found_ref, wself_ref, wneigh_ref = refs[-4:]
        pairs = ((notes_in, notes_ref), (total_in, total_ref), (found_in, found_ref))
        pairs += ((wself_in, wself_ref), (wneigh_in, wneigh_ref))
    else:
        total_ref, found_ref, packed, tiles_ref, ready, landed, arrived, notes_ref, carried = refs
        pairs = ((notes_in, notes_ref),)
    carry = [pltpu.make_async_copy(*pair, carried.at[n]) for n, pair in enumerate(pairs)]
    nodes = total_ref.shape[0]
    rows = math.gcd(nodes, 3 * TILE)
    begin, count = spans_ref[0], spans_ref[1]

    def fetch(step, slot):
        return pltpu.make_async_copy(
            adj_ref.at[pl.ds(begin + step * WIDE, WIDE)], tiles_ref.at[slot], ready.at[slot]
        )

    @pl.when(count > 0)
    def _():
        fetch(0, 0).start()

    for copy in carry:
        copy.start()
    collect(piece, counts_ref, starts_ref, answer_refs, landed, arrived, packed)
    for copy in carry:
        copy.wait()
    if not last:
        total_ref[...] = jnp.zeros(total_ref.shape, jnp.float32)
        found_ref[...] = jnp.zeros(found_ref.shape, jnp.float32)

    @pl.loop(0, count)
    def _(step):
        slot = step & 1

        @pl.when(step + 1 < count)
        def _():
            fetch(step + 1, 1 - slot).start()

        fetch(step, slot).wait()
        depth = WIDE * TILE
        block = packed[pl.ds(pl.multiple_of(step * depth, depth), depth), :]
        lane = lax.broadcasted_iota(jnp.int32, (rows, depth), 1) + (begin * TILE + step * depth)
        lane = lane.astype(jnp.float32)

        @pl.loop(0, nodes // rows)
        def _(r):
            part = pl.ds(pl.multiple_of(r * rows, rows), rows)
            near = jnp.concatenate(
                [tiles_ref[slot, w, part, :].astype(jnp.bfloat16) for w in range(WIDE)], axis=1
            )
            own = jnp.where(notes_ref[part, 0:1] == lane, 1.0, 0.0).astype(jnp.bfloat16)
            both = jnp.dot(
                jnp.concatenate([near, own], axis=0), block, preferred_element_type=jnp.float32
            )
            total_ref[part, :] += both[:rows]
            found_ref[part, :] += both[rows:]

    if last:
        share = share_refs[0].shape[0]
        step_rows = math.gcd(share, 3 * TILE)
        for p, share_ref in enumerate(share_refs):
            for r in range(share // step_rows):
                part = pl.ds(p * share + r * step_rows, step_rows)
                own = found_ref[part, :].astype(jnp.bfloat16)
                mean = (total_ref[part, :] / notes_ref[part, 1:2]).astype(jnp.bfloat16)
                own_ref[part, :] = own
                mean_ref[part, :] = mean
                share_ref[pl.ds(r * step_rows, step_rows), :] = (
                    jnp.dot(own, wself_ref[...], preferred_element_type=jnp.float32)
                    + jnp.dot(mean, wneigh_ref[...], preferred_element_type=jnp.float32)
                ).astype(share_ref.dtype)


def gather_sum(inputs, parts, spans, counts, starts, answers, notes, adj, rest):
    batch_count = sum(a.shape[0] for a in answers)
    _, width, features = answers[0].shape
    tiles, nodes, _ = adj.shape
    piece = LANES if width % LANES == 0 else SLOTS
    last = rest is not None
    room = min(batch_count * width, inputs) + SLOTS * batch_count + 2 * WIDE * TILE
    in_specs = [SMEM, SMEM, SMEM, HBM, HBM] + [ANY] * len(answers)
    rows = lambda dtype: jax.ShapeDtypeStruct((nodes, features), dtype)
    scratch = [
        pltpu.VMEM((room, features), jnp.bfloat16),
        pltpu.VMEM((2, WIDE, nodes, TILE), adj.dtype),
        pltpu.SemaphoreType.DMA((2,)),
        pltpu.VMEM((batch_count, width, features), jnp.bfloat16),
        pltpu.SemaphoreType.DMA((len(answers),)),
        pltpu.VMEM(notes.shape, notes.dtype),
        pltpu.SemaphoreType.DMA((5,)),
    ]
    operands = [notes, adj, *answers]
    if last:
        operands += list(rest)
        in_specs += [HBM] * len(rest)
        share = jax.ShapeDtypeStruct((nodes // parts, rest[3].shape[1]), jnp.bfloat16)
        out_shape = (rows(jnp.bfloat16), rows(jnp.bfloat16)) + (share,) * parts
        scratch += [pltpu.VMEM(x.shape, x.dtype) for x in rest]
    else:
        out_shape = (rows(jnp.float32), rows(jnp.float32))
    return pl.pallas_call(
        functools.partial(gather_sum_body, piece, last, len(answers)),
        out_shape=out_shape,
        in_specs=in_specs,
        out_specs=(VMEM,) * len(out_shape),
        scratch_shapes=scratch,
        compiler_params=params(50),
        cost_estimate=cost(2 * nodes * features * TILE * tiles, nodes * TILE * tiles // 2),
        name="gather_sum",
    )(spans, counts, starts, *operands)


def share_order(array, parts, seeds):
    others = array.shape[0] - seeds
    own, rest = seeds // parts, others // parts
    tail = array.shape[1:]
    blocks = jnp.concatenate(
        [array[:seeds].reshape(parts, own, *tail), array[seeds:].reshape(parts, rest, *tail)],
        axis=1,
    )
    return ahead(blocks).reshape(array.shape)


def spread(part, axis, count):
    return lax.all_to_all(
        jnp.broadcast_to(part[None], (count,) + part.shape), axis, 0, 0, tiled=True
    )


def passed(part, shift, axis="feat"):
    parts = lax.axis_size(axis)
    return lax.ppermute(part, axis, [((i + shift) % parts, i) for i in range(parts)])


def turned(array, by):
    twice = jnp.concatenate([array, array], axis=0)
    return lax.dynamic_slice_in_dim(twice, by, array.shape[0], 0)


def ahead(array, axis="feat"):
    return turned(array, lax.axis_index(axis))


def spread_parts(part, axis="feat"):
    return [part] + [passed(part, j, axis) for j in range(1, lax.axis_size(axis))]


def pushed(blocks, axis):
    return [blocks[0]] + [passed(x, -j, axis) for j, x in enumerate(blocks) if j]


def sum_parts(blocks, axis="feat"):
    return sum(x.astype(jnp.float32) for x in pushed(blocks, axis))


def swapped(part):
    return lax.ppermute(part, "batch", [(i, i ^ 1) for i in range(lax.axis_size("batch"))])


def total_over_batch(terms):
    count = lax.axis_size("batch")
    rows, width = terms.shape
    if count > FEW:
        pieces = terms.astype(jnp.bfloat16).reshape(count, rows // count, width)
        pieces = lax.all_to_all(pieces, "batch", 0, 0, tiled=True)
        total = jnp.sum(pieces.astype(jnp.float32), axis=0).astype(jnp.bfloat16)
        return spread(total, "batch", count).reshape(rows, width)
    chips = count // 2
    index = lax.axis_index("batch")
    first, chip = index % 2 == 0, index // 2
    upper, lower = terms[: rows // 2], terms[rows // 2 :]
    came = swapped(jnp.where(first, lower, upper).astype(jnp.bfloat16))
    mine = jnp.where(first, upper, lower) + came.astype(jnp.float32)
    pieces = turned(mine.reshape(chips, rows // count, width), chip)
    total = pieces[0]
    for j in range(1, chips):
        total = total + passed(pieces[j].astype(jnp.bfloat16), -2 * j, "batch").astype(jnp.float32)
    total = total.astype(jnp.bfloat16)
    mine = jnp.stack([total] + [passed(total, 2 * j, "batch") for j in range(1, chips)])
    other = swapped(mine)
    both = jnp.stack([jnp.where(first, mine, other), jnp.where(first, other, mine)], axis=1)
    return turned(both, (chips - chip) % chips).transpose(1, 0, 2, 3).reshape(rows, width)


def local(
    store,
    input_owner,
    input_row,
    nbr_one,
    deg_one,
    nbr_two,
    deg_two,
    cotangent,
    w1_self,
    w1_neigh,
    bias_one,
    w2_self,
    w2_neigh,
    bias_two,
):
    batch_count = lax.axis_size("batch")
    parts = lax.axis_size("feat")
    feat_index = lax.axis_index("feat")
    input_count = input_owner.shape[1]
    capacity = 2 * input_count // batch_count
    nodes = nbr_one.shape[1]
    seed_rows = nbr_two.shape[1]
    seeds = seed_rows * parts
    share = nodes // parts
    hidden_width = w1_self.shape[1]

    owners = input_owner.reshape(input_count // LANES, LANES)
    wanted = input_row.reshape(input_count // LANES, LANES)
    slots, counts, requests = make_requests(batch_count, capacity, owners, wanted)
    owners = owners.reshape(1, input_count)
    requests = requests.reshape(batch_count, capacity)
    few = batch_count <= FEW
    if few:
        blocks = ahead(requests.reshape(batch_count, -1, LANES), "batch")
        received = jnp.stack(pushed(list(blocks), "batch"))
        sizes = (1,) * batch_count
    else:
        received = lax.all_to_all(requests, "batch", split_axis=0, concat_axis=0, tiled=True)
        sizes = (batch_count,)

    def answers(looked):
        if few:
            return [looked[0]] + [passed(x, j, "batch") for j, x in enumerate(looked) if j]
        return [lax.all_to_all(looked[0], "batch", split_axis=0, concat_axis=0, tiled=True)]

    first = capacity // 2
    places = received.reshape(batch_count * capacity) * (store.shape[1] // LANES)
    looked_a = lookup(store, places, sizes, 0, first)
    near_first, looked_a = lax.optimization_barrier((nbr_one[0], looked_a))
    answer_a = answers(looked_a)
    looked = lookup(store, places, sizes, first, capacity - first)

    depth = WIDE * TILE
    steps = -(-(input_count + 2 * (SLOTS - 1) * batch_count + depth - 1) // depth)
    tally = counts[:, 0]
    near_owner = owners
    if few:
        tally = ahead(tally, "batch")
        near_owner = (owners - lax.axis_index("batch")) & (batch_count - 1)
    tally_a = jnp.minimum(tally, first)
    tally_b = tally - tally_a
    padded = lambda n: (n + SLOTS - 1) // SLOTS * SLOTS
    ends = lambda n: jnp.concatenate([jnp.zeros((1,), jnp.int32), jnp.cumsum(padded(n))])
    starts_a, starts_b = ends(tally_a), ends(tally_b)
    steps_a = (starts_a[batch_count] + depth - 1) // depth
    steps_b = (starts_b[batch_count] + depth - 1) // depth
    spans_a = jnp.stack([jnp.zeros_like(steps_a), steps_a])
    spans_b = jnp.stack([steps_a * WIDE, steps_b])
    slot = slots.reshape(1, input_count)
    shifted = jnp.where(
        slot < first,
        slot + starts_a[:batch_count, None],
        slot - first + steps_a * depth + starts_b[:batch_count, None],
    )
    mine = near_owner == jnp.arange(batch_count)[:, None]
    column = jnp.sum(jnp.where(mine, shifted, 0), axis=0)
    grid = jnp.pad(column.reshape(-1, LANES), ((0, LANES - input_count // LANES), (0, 0))).T
    table = jnp.concatenate([grid // TILE, grid % TILE], axis=0).astype(jnp.bfloat16)
    notes = jnp.stack([column[:nodes], deg_one[0]], axis=1).astype(jnp.float32)
    notes = share_order(notes, parts, seeds)

    fanout_two = nbr_two.shape[2]
    used_two = jnp.arange(fanout_two)[:, None] < deg_two
    lists = jnp.concatenate([jnp.where(used_two, nbr_two[0].T, -1), deg_two], axis=0)
    lists = jnp.stack(spread_parts(lists))

    fanout = nbr_one.shape[2]
    used = jnp.arange(fanout)[None, :] < deg_one[0][:, None]
    near = jnp.pad(jnp.where(used, near_first, -1), ((0, 0), (0, SLOTS - fanout)), constant_values=-1)
    near, lists = lax.optimization_barrier((near, lists))
    me = feat_index.astype(jnp.int32).reshape(1)
    near = near.reshape(nodes // SLOTS, TILE)
    adj = adjacency(me, near, table, steps * WIDE, parts, seeds)
    looked, answer_a, adj = lax.optimization_barrier((looked, answer_a, adj))
    answer_b = answers(looked)

    near_two = lists[:, :fanout_two].transpose(1, 0, 2).reshape(fanout_two, seeds)
    deg_all = lists[:, fanout_two].reshape(seeds)
    rest = share - seed_rows
    after = near_two - seeds
    place = jnp.where(
        near_two < seeds,
        near_two // seed_rows * share + near_two % seed_rows,
        after // rest * share + seed_rows + after % rest,
    )
    place = jnp.where(near_two < 0, -1, place - feat_index * share)
    adj_two = jnp.sum(
        place[:, :, None] == jnp.arange(share)[None, None, :], axis=0, dtype=jnp.float32
    ).astype(jnp.bfloat16)

    total, found = gather_sum(
        input_count, parts, spans_a, tally_a, starts_a, answer_a, notes, adj, None
    )
    self_one, agg_one, *z_blocks = gather_sum(
        input_count,
        parts,
        spans_b,
        tally_b,
        starts_b,
        answer_b,
        notes,
        adj,
        (total, found, w1_self, w1_neigh),
    )
    z_share = sum_parts(z_blocks) + bias_one
    hidden = jax.nn.silu(z_share).astype(jnp.bfloat16)

    agg_parts = jnp.dot(adj_two, hidden, preferred_element_type=jnp.float32)
    agg_total = sum_parts(agg_parts.reshape(parts, seed_rows, hidden_width))
    deg_second = deg_two[0].astype(jnp.float32)[:, None]
    agg_two = (agg_total / deg_second).astype(jnp.bfloat16)
    self_two = hidden[:seed_rows]
    z_two = (
        jnp.dot(self_two, w2_self, preferred_element_type=jnp.float32)
        + jnp.dot(agg_two, w2_neigh, preferred_element_type=jnp.float32)
        + bias_two
    )
    activations = jax.nn.silu(z_two).astype(jnp.bfloat16)[None]
    dz_two = (cotangent[0].astype(jnp.float32) * silu_grad(z_two)).astype(jnp.bfloat16)
    group = jnp.stack(spread_parts(jnp.stack([self_two, agg_two, dz_two])))
    dz_two_all = group[:, 2].reshape(seeds, hidden_width)

    back = contract_cols(dz_two_all, w2_neigh) / deg_all.astype(jnp.float32)[:, None]
    back_high = back.astype(jnp.bfloat16)
    back_low = (back - back_high.astype(jnp.float32)).astype(jnp.bfloat16)
    dh_share = contract_rows(adj_two, back_high) + contract_rows(adj_two, back_low)
    dh_share = dh_share + jnp.pad(contract_cols(dz_two, w2_self), ((0, rest), (0, 0)))
    dz_share = (dh_share * silu_grad(z_share)).astype(jnp.bfloat16)
    dz_one = jnp.concatenate(spread_parts(dz_share))
    group = turned(group, (parts - feat_index) % parts).transpose(1, 0, 2, 3)
    self_all, agg_all, dz_all = (x.reshape(seeds, hidden_width) for x in group)
    grads = [contract_rows(self_all, dz_all), contract_rows(agg_all, dz_all)]
    grads += [contract_rows(self_one, dz_one), contract_rows(agg_one, dz_one)]
    total = total_over_batch(jnp.concatenate(grads)).astype(jnp.float32)
    return (activations, *total.reshape(len(grads), -1, hidden_width))


def solution(mesh):
    in_specs = (
        P("batch", "feat"),
        P("batch", None, None),
        P("batch", None),
        P("batch", None, None),
        P("batch", None),
        P("batch", "feat", None),
        P("batch", "feat"),
        P("batch", "feat", None),
        P("feat", None),
        P("feat", None),
        P(),
        P(),
        P(),
        P(),
    )
    out_specs = (P("batch", "feat", None), P(), P(), P("feat", None), P("feat", None))
    return jax.shard_map(local, mesh=mesh, in_specs=in_specs, out_specs=out_specs, check_vma=False)
```

```python
import functools
import math

import jax
import jax.numpy as jnp
from jax import lax
from jax.experimental import pallas as pl
from jax.experimental.pallas import tpu as pltpu
from jax.sharding import PartitionSpec as P

TILE = 256
LANES = 128
SLOTS = 16
WIDE = 2
FEW = 16
TILE_BITS, LANE_BITS, SLOT_BITS = 8, 7, 4
MIB = 1024 * 1024
VMEM = pl.BlockSpec(memory_space=pltpu.VMEM)
SMEM = pl.BlockSpec(memory_space=pltpu.SMEM)
ANY = pl.BlockSpec(memory_space=pl.ANY)
HBM = pl.BlockSpec(memory_space=pltpu.HBM)


def silu_grad(values):
    sig = jax.nn.sigmoid(values)
    return sig * (1.0 + values * (1.0 - sig))


def contract_rows(left_side, right_side):
    return lax.dot_general(
        left_side, right_side, (((0,), (0,)), ((), ())), preferred_element_type=jnp.float32
    )


def contract_cols(left_side, right_side):
    return lax.dot_general(
        left_side, right_side, (((1,), (1,)), ((), ())), preferred_element_type=jnp.float32
    )


def params(mib):
    return pltpu.CompilerParams(vmem_limit_bytes=mib * MIB)


def cost(flops, moved):
    return pl.CostEstimate(flops=int(flops), bytes_accessed=int(moved), transcendentals=0)


def requests_body(batch_count, capacity, owner_ref, row_ref, slot_ref, count_ref, request_ref):
    blocks, width = owner_ref.shape[0] // 2, TILE
    places = request_ref.shape[0]
    line = lambda ref, b: jnp.concatenate([ref[2 * b : 2 * b + 1], ref[2 * b + 1 : 2 * b + 2]], axis=1)
    owner_id = lax.broadcasted_iota(jnp.int32, (batch_count, width), 0)
    earlier = lax.broadcasted_iota(jnp.int32, (width, width), 0)
    later = lax.broadcasted_iota(jnp.int32, (width, width), 1)
    upper = jnp.where(earlier <= later, 1.0, 0.0).astype(jnp.bfloat16)
    high_id = lax.broadcasted_iota(jnp.int32, (places, width), 0)
    low_id = lax.broadcasted_iota(jnp.int32, (LANES, width), 0)
    marks = [
        jnp.where(line(owner_ref, b) == owner_id, 1.0, 0.0) for b in range(blocks)
    ]
    stacked = jnp.concatenate(marks, axis=0).astype(jnp.bfloat16)
    prefix = jnp.dot(stacked, upper, preferred_element_type=jnp.float32)
    running = jnp.zeros((batch_count, 1), jnp.float32)
    total = jnp.zeros((2 * places, LANES), jnp.float32)
    for b in range(blocks):
        part = prefix[b * batch_count : (b + 1) * batch_count]
        slots = jnp.sum(marks[b] * (part + running - 1.0), axis=0, keepdims=True)
        slots = slots.astype(jnp.int32)
        slot_ref[2 * b : 2 * b + 1, :] = slots[:, :LANES]
        slot_ref[2 * b + 1 : 2 * b + 2, :] = slots[:, LANES:]
        running = running + part[:, width - 1 : width]
        bucket = line(owner_ref, b) * capacity + slots
        rows = line(row_ref, b)
        hit = (bucket >> LANE_BITS) == high_id
        left = jnp.concatenate(
            [
                jnp.where(hit, (rows >> TILE_BITS).astype(jnp.float32), 0.0),
                jnp.where(hit, (rows & (TILE - 1)).astype(jnp.float32), 0.0),
            ],
            axis=0,
        ).astype(jnp.bfloat16)
        right = jnp.where((bucket & (LANES - 1)) == low_id, 1.0, 0.0).astype(jnp.bfloat16)
        total = total + contract_cols(left, right)
    count_ref[...] = jnp.broadcast_to(running, count_ref.shape).astype(jnp.int32)
    request_ref[...] = (total[:places] * TILE + total[places:]).astype(jnp.int32)


def make_requests(batch_count, capacity, owners, wanted):
    total = owners.shape[0] * LANES
    places = batch_count * capacity // LANES
    return pl.pallas_call(
        functools.partial(requests_body, batch_count, capacity),
        out_shape=(
            jax.ShapeDtypeStruct(owners.shape, jnp.int32),
            jax.ShapeDtypeStruct((batch_count, LANES), jnp.int32),
            jax.ShapeDtypeStruct((places, LANES), jnp.int32),
        ),
        in_specs=[VMEM, VMEM],
        out_specs=(VMEM, VMEM, VMEM),
        compiler_params=params(16),
        cost_estimate=cost(4 * total * places * LANES, 24 * total),
        name="requests",
    )(owners, wanted)


def lookup_body(stride, first, width, want_ref, store_in, out_ref, table, lines, store_ref, came):
    rows_all = store_ref.shape[0]
    halves = store_ref.shape[1] // LANES
    lane = lambda h: pl.ds(h * LANES, LANES)
    begin = pl.program_id(0) * stride + first

    @pl.when(pl.program_id(0) == 0)
    def _():
        pieces = came.shape[0]
        depth = rows_all // pieces
        copies = [
            pltpu.make_async_copy(
                store_in.at[pl.ds(n * depth, depth)], store_ref.at[pl.ds(n * depth, depth)], came.at[n]
            )
            for n in range(pieces)
        ]
        for copy in copies:
            copy.start()
        for n, copy in enumerate(copies):
            copy.wait()

            @pl.loop(n * depth // TILE, (n + 1) * depth // TILE)
            def _(j):
                part = pl.ds(pl.multiple_of(j * TILE, TILE), TILE)
                for h in range(halves):
                    spot = pl.ds(pl.multiple_of(j * TILE * halves, TILE) + h, TILE, stride=halves)
                    table[spot, :] = store_ref[part, lane(h)].astype(jnp.float32)

    @pl.loop(0, width // SLOTS, unroll=2)
    def _(j):
        at = [want_ref[begin + j * SLOTS + u] for u in range(SLOTS)]
        rows = [table[pl.ds(pl.multiple_of(a, halves), halves), :] for a in at]
        block = lines.at[pl.ds(pl.multiple_of(j * SLOTS * halves, SLOTS * halves), SLOTS * halves)]
        for u in range(SLOTS):
            block[pl.ds(u * halves, halves), :] = rows[u]

    for h in range(halves):
        out_ref[0, :, lane(h)] = lines[pl.ds(h, width, stride=halves), :].astype(jnp.bfloat16)


def lookup(store, places, groups, first, width):
    rows_all, features = store.shape
    halves = features // LANES
    apart = lambda rows: pltpu.VMEM((rows * halves, LANES), jnp.float32)
    return pl.pallas_call(
        functools.partial(lookup_body, places.shape[0] // groups, first, width),
        out_shape=jax.ShapeDtypeStruct((groups, width, features), jnp.bfloat16),
        grid=(groups,),
        in_specs=[SMEM, HBM],
        out_specs=pl.BlockSpec((1, width, features), lambda g: (g, 0, 0)),
        scratch_shapes=[
            apart(rows_all),
            apart(width),
            pltpu.VMEM((rows_all, features), store.dtype),
            pltpu.SemaphoreType.DMA((4,)),
        ],
        compiler_params=params(24),
        cost_estimate=cost(groups * width * features * 40, 2 * rows_all * features),
        name="lookup",
    )(places, store)


def adjacency_body(tiles, me_ref, near_ref, table_ref, out_ref):
    groups = near_ref.shape[0]
    node_high = lax.broadcasted_iota(jnp.int32, (LANES, TILE), 0)
    own_row = (
        lax.shift_right_logical(lax.broadcasted_iota(jnp.int32, (SLOTS, TILE), 1), SLOT_BITS)
        == lax.broadcasted_iota(jnp.int32, (SLOTS, TILE), 0)
    )
    low_id = lax.broadcasted_iota(jnp.int32, (TILE, TILE), 0).astype(jnp.float32)

    def one_group(g):
        near = near_ref[pl.ds(g, 1), :]
        pick = jnp.where((near >> LANE_BITS) == node_high, 1.0, 0.0).astype(jnp.bfloat16)
        found = jnp.dot(table_ref[...], pick, preferred_element_type=jnp.float32)
        here = (near & (LANES - 1)) == node_high
        high = jnp.sum(jnp.where(here, found[:LANES], 0.0), axis=0, keepdims=True)
        low = jnp.sum(jnp.where(here, found[LANES:], 0.0), axis=0, keepdims=True)
        high = jnp.where(near < 0, -1.0, high)
        rows = jnp.where(own_row, high, -1.0)
        left = jnp.concatenate(
            [jnp.where(rows == float(t), 1.0, 0.0) for t in range(tiles)], axis=0
        ).astype(jnp.bfloat16)
        right = jnp.where(low == low_id, 1.0, 0.0).astype(jnp.bfloat16)
        return contract_cols(left, right).reshape(tiles, SLOTS, TILE)

    @pl.loop(0, groups // 2, unroll=2)
    def _(j):
        pair = jnp.concatenate([one_group(2 * j), one_group(2 * j + 1)], axis=1)
        out_ref[:, pl.ds(pl.multiple_of(j * 2 * SLOTS, 2 * SLOTS), 2 * SLOTS), :] = pair.astype(
            out_ref.dtype
        )


def adjacency(me, near, table, tiles, parts, seeds):
    groups = near.shape[0]
    nodes = groups * SLOTS
    step = LANES // SLOTS
    own, rest, share = (n // parts // LANES for n in (seeds, nodes - seeds, nodes))

    def place(block, me_ref):
        after = block - own * parts
        is_own = after < 0
        part = jnp.where(is_own, lax.div(block, own), lax.div(after, rest))
        at = jnp.where(is_own, lax.rem(block, own), own + lax.rem(after, rest))
        return (0, lax.rem(part - me_ref[0] + parts, parts) * share + at, 0)

    return pl.pallas_call(
        functools.partial(adjacency_body, tiles),
        out_shape=jax.ShapeDtypeStruct((tiles, nodes, TILE), jnp.float8_e4m3fn),
        grid_spec=pltpu.PrefetchScalarGridSpec(
            num_scalar_prefetch=1,
            grid=(groups // step,),
            in_specs=[
                pl.BlockSpec((step, TILE), lambda r, me: (r, 0)),
                pl.BlockSpec(table.shape, lambda r, me: (0, 0)),
            ],
            out_specs=pl.BlockSpec((tiles, LANES, TILE), place),
        ),
        compiler_params=params(48),
        cost_estimate=cost(2 * nodes * TILE * TILE * tiles * 2, nodes * TILE * tiles),
        name="adjacency",
    )(me, near, table)


def collect(piece, counts_ref, starts_ref, answer_ref, landed, arrived, packed):
    batch_count, width, _ = answer_ref.shape
    pieces = width // piece

    def each_used(what):
        @pl.loop(0, batch_count)
        def _(o):
            for c in range(pieces):

                @pl.when(c * piece < counts_ref[o])
                def _(c=c):
                    part = pl.ds(c * piece, piece)
                    what(
                        o,
                        c,
                        part,
                        pltpu.make_async_copy(
                            answer_ref.at[o, part], landed.at[o, part], arrived.at[o, c]
                        ),
                    )

    def lay(o, c, part, copy):
        copy.wait()
        packed[pl.ds(pl.multiple_of(starts_ref[o] + c * piece, SLOTS), piece), :] = landed[o, part]

    each_used(lambda o, c, part, copy: copy.start())
    each_used(lay)
    end = starts_ref[batch_count]
    packed[pl.ds(pl.multiple_of(end, SLOTS), WIDE * TILE), :] = jnp.zeros(
        (WIDE * TILE, packed.shape[1]), packed.dtype
    )


def gather_sum_body(
    piece, last, row0, spans_ref, counts_ref, starts_ref, answer_ref, notes_in, adj_ref, *refs
):
    if last:
        (total_in, found_in, wself_in, wneigh_in, own_ref, mean_ref) = refs[:6]
        share_refs = refs[6:-11]
        packed, tiles_ref, ready, landed, arrived, notes_ref, carried = refs[-11:-4]
        total_ref, found_ref, wself_ref, wneigh_ref = refs[-4:]
        mine = pl.ds(row0, total_ref.shape[0])
        pairs = ((notes_in.at[mine], notes_ref), (total_in.at[mine], total_ref))
        pairs += ((found_in.at[mine], found_ref),)
        pairs += ((wself_in, wself_ref), (wneigh_in, wneigh_ref))
    else:
        total_ref, found_ref, packed, tiles_ref, ready, landed, arrived, notes_ref, carried = refs
        pairs = ((notes_in, notes_ref),)
    carry = [pltpu.make_async_copy(*pair, carried.at[n]) for n, pair in enumerate(pairs)]
    nodes = total_ref.shape[0]
    rows = math.gcd(nodes, 3 * TILE)
    begin, count = spans_ref[0], spans_ref[1]

    def fetch(step, slot):
        return pltpu.make_async_copy(
            adj_ref.at[pl.ds(begin + step * WIDE, WIDE), pl.ds(row0, nodes)],
            tiles_ref.at[slot],
            ready.at[slot],
        )

    @pl.when(count > 0)
    def _():
        fetch(0, 0).start()

    for copy in carry:
        copy.start()
    collect(piece, counts_ref, starts_ref, answer_ref, landed, arrived, packed)
    for copy in carry:
        copy.wait()
    if not last:
        total_ref[...] = jnp.zeros(total_ref.shape, jnp.float32)
        found_ref[...] = jnp.zeros(found_ref.shape, jnp.float32)

    @pl.loop(0, count)
    def _(step):
        slot = step & 1

        @pl.when(step + 1 < count)
        def _():
            fetch(step + 1, 1 - slot).start()

        fetch(step, slot).wait()
        depth = WIDE * TILE
        block = packed[pl.ds(pl.multiple_of(step * depth, depth), depth), :]
        lane = lax.broadcasted_iota(jnp.int32, (rows, depth), 1) + (begin * TILE + step * depth)
        lane = lane.astype(jnp.float32)

        @pl.loop(0, nodes // rows)
        def _(r):
            part = pl.ds(pl.multiple_of(r * rows, rows), rows)
            near = jnp.concatenate(
                [tiles_ref[slot, w, part, :].astype(jnp.bfloat16) for w in range(WIDE)], axis=1
            )
            own = jnp.where(notes_ref[part, 0:1] == lane, 1.0, 0.0).astype(jnp.bfloat16)
            both = jnp.dot(
                jnp.concatenate([near, own], axis=0), block, preferred_element_type=jnp.float32
            )
            total_ref[part, :] += both[:rows]
            found_ref[part, :] += both[rows:]

    if last:
        share = share_refs[0].shape[0]
        step_rows = math.gcd(share, 3 * TILE)
        for p, share_ref in enumerate(share_refs):
            for r in range(share // step_rows):
                part = pl.ds(p * share + r * step_rows, step_rows)
                own = found_ref[part, :].astype(jnp.bfloat16)
                mean = (total_ref[part, :] / notes_ref[part, 1:2]).astype(jnp.bfloat16)
                own_ref[part, :] = own
                mean_ref[part, :] = mean
                share_ref[pl.ds(r * step_rows, step_rows), :] = (
                    jnp.dot(own, wself_ref[...], preferred_element_type=jnp.float32)
                    + jnp.dot(mean, wneigh_ref[...], preferred_element_type=jnp.float32)
                ).astype(share_ref.dtype)


def gather_sum(inputs, spans, counts, starts, answer, notes, adj, rest=None, row0=0, shares=()):
    batch_count, width, features = answer.shape
    tiles, nodes, _ = adj.shape
    nodes = sum(shares) or nodes
    piece = LANES if width % LANES == 0 else SLOTS
    last = rest is not None
    room = min(batch_count * width, inputs) + SLOTS * batch_count + 2 * WIDE * TILE
    in_specs = [SMEM, SMEM, SMEM, ANY, HBM, HBM]
    rows = lambda dtype: jax.ShapeDtypeStruct((nodes, features), dtype)
    scratch = [
        pltpu.VMEM((room, features), jnp.bfloat16),
        pltpu.VMEM((2, WIDE, nodes, TILE), adj.dtype),
        pltpu.SemaphoreType.DMA((2,)),
        pltpu.VMEM(answer.shape, answer.dtype),
        pltpu.SemaphoreType.DMA((batch_count, width // piece)),
        pltpu.VMEM((nodes, notes.shape[1]), notes.dtype),
        pltpu.SemaphoreType.DMA((5,)),
    ]
    operands = [answer, notes, adj]
    if last:
        operands += list(rest)
        in_specs += [HBM] * len(rest)
        out_shape = (rows(jnp.bfloat16), rows(jnp.bfloat16))
        out_shape += tuple(
            jax.ShapeDtypeStruct((n, rest[3].shape[1]), jnp.bfloat16) for n in shares
        )
        scratch += [pltpu.VMEM((nodes, features), jnp.float32)] * 2
        scratch += [pltpu.VMEM(x.shape, x.dtype) for x in rest[2:]]
    else:
        out_shape = (rows(jnp.float32), rows(jnp.float32))
    return pl.pallas_call(
        functools.partial(gather_sum_body, piece, last, row0),
        out_shape=out_shape,
        in_specs=in_specs,
        out_specs=(VMEM,) * len(out_shape),
        scratch_shapes=scratch,
        compiler_params=params(50),
        cost_estimate=cost(2 * nodes * features * TILE * tiles, nodes * TILE * tiles // 2),
        name="gather_sum",
    )(spans, counts, starts, *operands)


def share_order(array, parts, seeds):
    others = array.shape[0] - seeds
    own, rest = seeds // parts, others // parts
    tail = array.shape[1:]
    blocks = jnp.concatenate(
        [array[:seeds].reshape(parts, own, *tail), array[seeds:].reshape(parts, rest, *tail)],
        axis=1,
    )
    return ahead(blocks).reshape(array.shape)


def spread(part, axis, count):
    return lax.all_to_all(
        jnp.broadcast_to(part[None], (count,) + part.shape), axis, 0, 0, tiled=True
    )


def passed(part, shift, axis="feat"):
    parts = lax.axis_size(axis)
    return lax.ppermute(part, axis, [((i + shift) % parts, i) for i in range(parts)])


def turned(array, by):
    twice = jnp.concatenate([array, array], axis=0)
    return lax.dynamic_slice_in_dim(twice, by, array.shape[0], 0)


def ahead(array, axis="feat"):
    return turned(array, lax.axis_index(axis))


def spread_parts(part, axis="feat"):
    return [part] + [passed(part, j, axis) for j in range(1, lax.axis_size(axis))]


def sum_parts(blocks, axis="feat"):
    parts = lax.axis_size(axis)
    came = [blocks[0]] + [passed(blocks[j], -j, axis) for j in range(1, parts)]
    return sum(x.astype(jnp.float32) for x in came)


def swapped(part):
    return lax.ppermute(part, "batch", [(i, i ^ 1) for i in range(lax.axis_size("batch"))])


def total_over_batch(terms):
    count = lax.axis_size("batch")
    rows, width = terms.shape
    if count > FEW:
        pieces = terms.astype(jnp.bfloat16).reshape(count, rows // count, width)
        pieces = lax.all_to_all(pieces, "batch", 0, 0, tiled=True)
        total = jnp.sum(pieces.astype(jnp.float32), axis=0).astype(jnp.bfloat16)
        return spread(total, "batch", count).reshape(rows, width)
    chips = count // 2
    index = lax.axis_index("batch")
    first, chip = index % 2 == 0, index // 2
    upper, lower = terms[: rows // 2], terms[rows // 2 :]
    came = swapped(jnp.where(first, lower, upper).astype(jnp.bfloat16))
    mine = jnp.where(first, upper, lower) + came.astype(jnp.float32)
    pieces = turned(mine.reshape(chips, rows // count, width), chip)
    total = pieces[0]
    for j in range(1, chips):
        total = total + passed(pieces[j].astype(jnp.bfloat16), -2 * j, "batch").astype(jnp.float32)
    total = total.astype(jnp.bfloat16)
    mine = jnp.stack([total] + [passed(total, 2 * j, "batch") for j in range(1, chips)])
    other = swapped(mine)
    both = jnp.stack([jnp.where(first, mine, other), jnp.where(first, other, mine)], axis=1)
    return turned(both, (chips - chip) % chips).transpose(1, 0, 2, 3).reshape(rows, width)


def local(
    store,
    input_owner,
    input_row,
    nbr_one,
    deg_one,
    nbr_two,
    deg_two,
    cotangent,
    w1_self,
    w1_neigh,
    bias_one,
    w2_self,
    w2_neigh,
    bias_two,
):
    batch_count = lax.axis_size("batch")
    parts = lax.axis_size("feat")
    feat_index = lax.axis_index("feat")
    input_count = input_owner.shape[1]
    capacity = 2 * input_count // batch_count
    nodes = nbr_one.shape[1]
    seed_rows = nbr_two.shape[1]
    seeds = seed_rows * parts
    share = nodes // parts
    hidden_width = w1_self.shape[1]

    owners = input_owner.reshape(input_count // LANES, LANES)
    wanted = input_row.reshape(input_count // LANES, LANES)
    slots, counts, requests = make_requests(batch_count, capacity, owners, wanted)
    owners = owners.reshape(1, input_count)
    received = lax.all_to_all(
        requests.reshape(batch_count, capacity), "batch", split_axis=0, concat_axis=0, tiled=True
    )
    first = capacity // 2
    places = received.reshape(batch_count * capacity) * (store.shape[1] // LANES)
    looked_a = lookup(store, places, batch_count, 0, first)
    near_first, looked_a = lax.optimization_barrier((nbr_one[0], looked_a))
    answer_a = lax.all_to_all(looked_a, "batch", split_axis=0, concat_axis=0, tiled=True)
    looked = lookup(store, places, batch_count, first, capacity - first)

    depth = WIDE * TILE
    steps = -(-(input_count + 2 * (SLOTS - 1) * batch_count + depth - 1) // depth)
    tally = counts[:, 0]
    tally_a = jnp.minimum(tally, first)
    tally_b = tally - tally_a
    padded = lambda n: (n + SLOTS - 1) // SLOTS * SLOTS
    ends = lambda n: jnp.concatenate([jnp.zeros((1,), jnp.int32), jnp.cumsum(padded(n))])
    starts_a, starts_b = ends(tally_a), ends(tally_b)
    steps_a = (starts_a[batch_count] + depth - 1) // depth
    steps_b = (starts_b[batch_count] + depth - 1) // depth
    spans_a = jnp.stack([jnp.zeros_like(steps_a), steps_a])
    spans_b = jnp.stack([steps_a * WIDE, steps_b])
    slot = slots.reshape(1, input_count)
    shifted = jnp.where(
        slot < first,
        slot + starts_a[:batch_count, None],
        slot - first + steps_a * depth + starts_b[:batch_count, None],
    )
    mine = owners == jnp.arange(batch_count)[:, None]
    column = jnp.sum(jnp.where(mine, shifted, 0), axis=0)
    grid = jnp.pad(column.reshape(-1, LANES), ((0, LANES - input_count // LANES), (0, 0))).T
    table = jnp.concatenate([grid // TILE, grid % TILE], axis=0).astype(jnp.bfloat16)
    notes = jnp.stack([column[:nodes], deg_one[0]], axis=1).astype(jnp.float32)
    notes = share_order(notes, parts, seeds)

    fanout_two = nbr_two.shape[2]
    used_two = jnp.arange(fanout_two)[:, None] < deg_two
    lists = jnp.concatenate([jnp.where(used_two, nbr_two[0].T, -1), deg_two], axis=0)
    lists = jnp.stack(spread_parts(lists))

    fanout = nbr_one.shape[2]
    used = jnp.arange(fanout)[None, :] < deg_one[0][:, None]
    near = jnp.pad(jnp.where(used, near_first, -1), ((0, 0), (0, SLOTS - fanout)), constant_values=-1)
    near, lists = lax.optimization_barrier((near, lists))
    me = feat_index.astype(jnp.int32).reshape(1)
    near = near.reshape(nodes // SLOTS, TILE)
    adj = adjacency(me, near, table, steps * WIDE, parts, seeds)
    looked, answer_a, adj = lax.optimization_barrier((looked, answer_a, adj))
    answer_b = lax.all_to_all(looked, "batch", split_axis=0, concat_axis=0, tiled=True)

    near_two = lists[:, :fanout_two].transpose(1, 0, 2).reshape(fanout_two, seeds)
    deg_all = lists[:, fanout_two].reshape(seeds)
    rest = share - seed_rows
    after = near_two - seeds
    place = jnp.where(
        near_two < seeds,
        near_two // seed_rows * share + near_two % seed_rows,
        after // rest * share + seed_rows + after % rest,
    )
    place = jnp.where(near_two < 0, -1, place - feat_index * share)
    adj_two = jnp.sum(
        place[:, :, None] == jnp.arange(share)[None, None, :], axis=0, dtype=jnp.float32
    ).astype(jnp.bfloat16)

    total, found = gather_sum(input_count, spans_a, tally_a, starts_a, answer_a, notes, adj)

    def finish(begin, end):
        return gather_sum(
            input_count,
            spans_b,
            tally_b,
            starts_b,
            answer_b,
            notes,
            adj,
            (total, found, w1_self, w1_neigh),
            begin * share,
            (share,) * (end - begin),
        )

    self_far, agg_far, *z_far = finish(1, parts)
    total, z_far = lax.optimization_barrier((total, z_far))
    self_near, agg_near, *z_near = finish(0, 1)
    z_share = sum_parts(z_near + z_far) + bias_one
    hidden = jax.nn.silu(z_share).astype(jnp.bfloat16)

    agg_parts = jnp.dot(adj_two, hidden, preferred_element_type=jnp.float32)
    agg_total = sum_parts(agg_parts.reshape(parts, seed_rows, hidden_width))
    deg_second = deg_two[0].astype(jnp.float32)[:, None]
    agg_two = (agg_total / deg_second).astype(jnp.bfloat16)
    self_two = hidden[:seed_rows]
    z_two = (
        jnp.dot(self_two, w2_self, preferred_element_type=jnp.float32)
        + jnp.dot(agg_two, w2_neigh, preferred_element_type=jnp.float32)
        + bias_two
    )
    activations = jax.nn.silu(z_two).astype(jnp.bfloat16)[None]
    dz_two = (cotangent[0].astype(jnp.float32) * silu_grad(z_two)).astype(jnp.bfloat16)
    group = jnp.stack(spread_parts(jnp.stack([self_two, agg_two, dz_two])))
    dz_two_all = group[:, 2].reshape(seeds, hidden_width)

    back = contract_cols(dz_two_all, w2_neigh) / deg_all.astype(jnp.float32)[:, None]
    back_high = back.astype(jnp.bfloat16)
    back_low = (back - back_high.astype(jnp.float32)).astype(jnp.bfloat16)
    dh_share = contract_rows(adj_two, back_high) + contract_rows(adj_two, back_low)
    dh_share = dh_share + jnp.pad(contract_cols(dz_two, w2_self), ((0, rest), (0, 0)))
    dz_share = (dh_share * silu_grad(z_share)).astype(jnp.bfloat16)
    dz_blocks = spread_parts(dz_share)
    dz_near, dz_far = dz_blocks[0], jnp.concatenate(dz_blocks[1:])
    group = turned(group, (parts - feat_index) % parts).transpose(1, 0, 2, 3)
    self_all, agg_all, dz_all = (x.reshape(seeds, hidden_width) for x in group)
    grads = [contract_rows(self_all, dz_all), contract_rows(agg_all, dz_all)]
    grads.append(contract_rows(self_near, dz_near) + contract_rows(self_far, dz_far))
    grads.append(contract_rows(agg_near, dz_near) + contract_rows(agg_far, dz_far))
    total = total_over_batch(jnp.concatenate(grads)).astype(jnp.float32)
    return (activations, *total.reshape(len(grads), -1, hidden_width))


def solution(mesh):
    in_specs = (
        P("batch", "feat"),
        P("batch", None, None),
        P("batch", None),
        P("batch", None, None),
        P("batch", None),
        P("batch", "feat", None),
        P("batch", "feat"),
        P("batch", "feat", None),
        P("feat", None),
        P("feat", None),
        P(),
        P(),
        P(),
        P(),
    )
    out_specs = (P("batch", "feat", None), P(), P(), P("feat", None), P("feat", None))
    return jax.shard_map(local, mesh=mesh, in_specs=in_specs, out_specs=out_specs, check_vma=False)
```

```python
import functools
import math

import jax
import jax.numpy as jnp
from jax import lax
from jax.experimental import pallas as pl
from jax.experimental.pallas import tpu as pltpu
from jax.sharding import PartitionSpec as P

TILE = 256
LANES = 128
SLOTS = 16
WIDE = 2
FEW = 16
TILE_BITS, LANE_BITS, SLOT_BITS = 8, 7, 4
MIB = 1024 * 1024
VMEM = pl.BlockSpec(memory_space=pltpu.VMEM)
SMEM = pl.BlockSpec(memory_space=pltpu.SMEM)
ANY = pl.BlockSpec(memory_space=pl.ANY)
HBM = pl.BlockSpec(memory_space=pltpu.HBM)


def silu_grad(values):
    sig = jax.nn.sigmoid(values)
    return sig * (1.0 + values * (1.0 - sig))


def contract_rows(left_side, right_side):
    return lax.dot_general(
        left_side, right_side, (((0,), (0,)), ((), ())), preferred_element_type=jnp.float32
    )


def contract_cols(left_side, right_side):
    return lax.dot_general(
        left_side, right_side, (((1,), (1,)), ((), ())), preferred_element_type=jnp.float32
    )


def params(mib):
    return pltpu.CompilerParams(vmem_limit_bytes=mib * MIB)


def cost(flops, moved):
    return pl.CostEstimate(flops=int(flops), bytes_accessed=int(moved), transcendentals=0)


def requests_body(batch_count, capacity, owner_ref, row_ref, slot_ref, count_ref, request_ref):
    blocks, width = owner_ref.shape[0] // 2, TILE
    places = request_ref.shape[0]
    line = lambda ref, b: jnp.concatenate([ref[2 * b : 2 * b + 1], ref[2 * b + 1 : 2 * b + 2]], axis=1)
    owner_id = lax.broadcasted_iota(jnp.int32, (batch_count, width), 0)
    earlier = lax.broadcasted_iota(jnp.int32, (width, width), 0)
    later = lax.broadcasted_iota(jnp.int32, (width, width), 1)
    upper = jnp.where(earlier <= later, 1.0, 0.0).astype(jnp.bfloat16)
    high_id = lax.broadcasted_iota(jnp.int32, (places, width), 0)
    low_id = lax.broadcasted_iota(jnp.int32, (LANES, width), 0)
    marks = [
        jnp.where(line(owner_ref, b) == owner_id, 1.0, 0.0) for b in range(blocks)
    ]
    stacked = jnp.concatenate(marks, axis=0).astype(jnp.bfloat16)
    prefix = jnp.dot(stacked, upper, preferred_element_type=jnp.float32)
    running = jnp.zeros((batch_count, 1), jnp.float32)
    total = jnp.zeros((2 * places, LANES), jnp.float32)
    for b in range(blocks):
        part = prefix[b * batch_count : (b + 1) * batch_count]
        slots = jnp.sum(marks[b] * (part + running - 1.0), axis=0, keepdims=True)
        slots = slots.astype(jnp.int32)
        slot_ref[2 * b : 2 * b + 1, :] = slots[:, :LANES]
        slot_ref[2 * b + 1 : 2 * b + 2, :] = slots[:, LANES:]
        running = running + part[:, width - 1 : width]
        bucket = line(owner_ref, b) * capacity + slots
        rows = line(row_ref, b)
        hit = (bucket >> LANE_BITS) == high_id
        left = jnp.concatenate(
            [
                jnp.where(hit, (rows >> TILE_BITS).astype(jnp.float32), 0.0),
                jnp.where(hit, (rows & (TILE - 1)).astype(jnp.float32), 0.0),
            ],
            axis=0,
        ).astype(jnp.bfloat16)
        right = jnp.where((bucket & (LANES - 1)) == low_id, 1.0, 0.0).astype(jnp.bfloat16)
        total = total + contract_cols(left, right)
    count_ref[...] = jnp.broadcast_to(running, count_ref.shape).astype(jnp.int32)
    request_ref[...] = (total[:places] * TILE + total[places:]).astype(jnp.int32)


def make_requests(batch_count, capacity, owners, wanted):
    total = owners.shape[0] * LANES
    places = batch_count * capacity // LANES
    return pl.pallas_call(
        functools.partial(requests_body, batch_count, capacity),
        out_shape=(
            jax.ShapeDtypeStruct(owners.shape, jnp.int32),
            jax.ShapeDtypeStruct((batch_count, LANES), jnp.int32),
            jax.ShapeDtypeStruct((places, LANES), jnp.int32),
        ),
        in_specs=[VMEM, VMEM],
        out_specs=(VMEM, VMEM, VMEM),
        compiler_params=params(16),
        cost_estimate=cost(4 * total * places * LANES, 24 * total),
        name="requests",
    )(owners, wanted)


def lookup_body(stride, first, width, want_ref, store_in, out_ref, table, lines, store_ref, came):
    rows_all = store_ref.shape[0]
    halves = store_ref.shape[1] // LANES
    lane = lambda h: pl.ds(h * LANES, LANES)
    begin = pl.program_id(0) * stride + first

    @pl.when(pl.program_id(0) == 0)
    def _():
        pieces = came.shape[0]
        depth = rows_all // pieces
        copies = [
            pltpu.make_async_copy(
                store_in.at[pl.ds(n * depth, depth)], store_ref.at[pl.ds(n * depth, depth)], came.at[n]
            )
            for n in range(pieces)
        ]
        for copy in copies:
            copy.start()
        for n, copy in enumerate(copies):
            copy.wait()

            @pl.loop(n * depth // TILE, (n + 1) * depth // TILE)
            def _(j):
                part = pl.ds(pl.multiple_of(j * TILE, TILE), TILE)
                for h in range(halves):
                    spot = pl.ds(pl.multiple_of(j * TILE * halves, TILE) + h, TILE, stride=halves)
                    table[spot, :] = store_ref[part, lane(h)].astype(jnp.float32)

    @pl.loop(0, width // SLOTS, unroll=2)
    def _(j):
        at = [want_ref[begin + j * SLOTS + u] for u in range(SLOTS)]
        rows = [table[pl.ds(pl.multiple_of(a, halves), halves), :] for a in at]
        block = lines.at[pl.ds(pl.multiple_of(j * SLOTS * halves, SLOTS * halves), SLOTS * halves)]
        for u in range(SLOTS):
            block[pl.ds(u * halves, halves), :] = rows[u]

    for h in range(halves):
        out_ref[0, :, lane(h)] = lines[pl.ds(h, width, stride=halves), :].astype(jnp.bfloat16)


def lookup(store, places, groups, first, width, mib):
    rows_all, features = store.shape
    halves = features // LANES
    apart = lambda rows: pltpu.VMEM((rows * halves, LANES), jnp.float32)
    return pl.pallas_call(
        functools.partial(lookup_body, places.shape[0] // groups, first, width),
        out_shape=jax.ShapeDtypeStruct((groups, width, features), jnp.bfloat16),
        grid=(groups,),
        in_specs=[SMEM, HBM],
        out_specs=pl.BlockSpec((1, width, features), lambda g: (g, 0, 0)),
        scratch_shapes=[
            apart(rows_all),
            apart(width),
            pltpu.VMEM((rows_all, features), store.dtype),
            pltpu.SemaphoreType.DMA((4,)),
        ],
        compiler_params=params(mib),
        cost_estimate=cost(groups * width * features * 40, 2 * rows_all * features),
        name="lookup",
    )(places, store)


def adjacency_body(tiles, me_ref, near_ref, table_ref, out_ref):
    groups = near_ref.shape[0]
    node_high = lax.broadcasted_iota(jnp.int32, (LANES, TILE), 0)
    own_row = (
        lax.shift_right_logical(lax.broadcasted_iota(jnp.int32, (SLOTS, TILE), 1), SLOT_BITS)
        == lax.broadcasted_iota(jnp.int32, (SLOTS, TILE), 0)
    )
    low_id = lax.broadcasted_iota(jnp.int32, (TILE, TILE), 0).astype(jnp.float32)

    def one_group(g):
        near = near_ref[pl.ds(g, 1), :]
        pick = jnp.where((near >> LANE_BITS) == node_high, 1.0, 0.0).astype(jnp.bfloat16)
        found = jnp.dot(table_ref[...], pick, preferred_element_type=jnp.float32)
        here = (near & (LANES - 1)) == node_high
        high = jnp.sum(jnp.where(here, found[:LANES], 0.0), axis=0, keepdims=True)
        low = jnp.sum(jnp.where(here, found[LANES:], 0.0), axis=0, keepdims=True)
        high = jnp.where(near < 0, -1.0, high)
        rows = jnp.where(own_row, high, -1.0)
        left = jnp.concatenate(
            [jnp.where(rows == float(t), 1.0, 0.0) for t in range(tiles)], axis=0
        ).astype(jnp.bfloat16)
        right = jnp.where(low == low_id, 1.0, 0.0).astype(jnp.bfloat16)
        return contract_cols(left, right).reshape(tiles, SLOTS, TILE)

    @pl.loop(0, groups // 2, unroll=2)
    def _(j):
        pair = jnp.concatenate([one_group(2 * j), one_group(2 * j + 1)], axis=1)
        out_ref[:, pl.ds(pl.multiple_of(j * 2 * SLOTS, 2 * SLOTS), 2 * SLOTS), :] = pair.astype(
            out_ref.dtype
        )


def adjacency(me, near, table, tiles, parts, seeds):
    groups = near.shape[0]
    nodes = groups * SLOTS
    step = LANES // SLOTS
    own, rest, share = (n // parts // LANES for n in (seeds, nodes - seeds, nodes))

    def place(block, me_ref):
        after = block - own * parts
        is_own = after < 0
        part = jnp.where(is_own, lax.div(block, own), lax.div(after, rest))
        at = jnp.where(is_own, lax.rem(block, own), own + lax.rem(after, rest))
        return (0, lax.rem(part - me_ref[0] + parts, parts) * share + at, 0)

    return pl.pallas_call(
        functools.partial(adjacency_body, tiles),
        out_shape=jax.ShapeDtypeStruct((tiles, nodes, TILE), jnp.float8_e4m3fn),
        grid_spec=pltpu.PrefetchScalarGridSpec(
            num_scalar_prefetch=1,
            grid=(groups // step,),
            in_specs=[
                pl.BlockSpec((step, TILE), lambda r, me: (r, 0)),
                pl.BlockSpec(table.shape, lambda r, me: (0, 0)),
            ],
            out_specs=pl.BlockSpec((tiles, LANES, TILE), place),
        ),
        compiler_params=params(48),
        cost_estimate=cost(2 * nodes * TILE * TILE * tiles * 2, nodes * TILE * tiles),
        name="adjacency",
    )(me, near, table)


def collect(piece, counts_ref, starts_ref, answer_ref, landed, arrived, packed):
    batch_count, width, _ = answer_ref.shape
    pieces = width // piece

    def each_used(what):
        @pl.loop(0, batch_count)
        def _(o):
            for c in range(pieces):

                @pl.when(c * piece < counts_ref[o])
                def _(c=c):
                    part = pl.ds(c * piece, piece)
                    what(
                        o,
                        c,
                        part,
                        pltpu.make_async_copy(
                            answer_ref.at[o, part], landed.at[o, part], arrived.at[o, c]
                        ),
                    )

    def lay(o, c, part, copy):
        copy.wait()
        packed[pl.ds(pl.multiple_of(starts_ref[o] + c * piece, SLOTS), piece), :] = landed[o, part]

    each_used(lambda o, c, part, copy: copy.start())
    each_used(lay)
    end = starts_ref[batch_count]
    packed[pl.ds(pl.multiple_of(end, SLOTS), WIDE * TILE), :] = jnp.zeros(
        (WIDE * TILE, packed.shape[1]), packed.dtype
    )


def gather_sum_body(
    piece,
    last,
    row0,
    spans_ref,
    counts_ref,
    starts_ref,
    own_here_ref,
    answer_ref,
    notes_in,
    adj_ref,
    *refs,
):
    if last:
        (total_in, found_in, wself_in, wneigh_in, own_ref, mean_ref) = refs[:6]
        share_refs = refs[6:-11]
        packed, tiles_ref, ready, landed, arrived, notes_ref, carried = refs[-11:-4]
        total_ref, found_ref, wself_ref, wneigh_ref = refs[-4:]
        mine = pl.ds(row0, total_ref.shape[0])
        pairs = ((notes_in.at[mine], notes_ref), (total_in.at[mine], total_ref))
        pairs += ((found_in.at[mine], found_ref),)
        pairs += ((wself_in, wself_ref), (wneigh_in, wneigh_ref))
    else:
        total_ref, found_ref, packed, tiles_ref, ready, landed, arrived, notes_ref, carried = refs
        pairs = ((notes_in, notes_ref),)
    carry = [pltpu.make_async_copy(*pair, carried.at[n]) for n, pair in enumerate(pairs)]
    nodes = total_ref.shape[0]
    rows = math.gcd(adj_ref.shape[1], 3 * TILE)
    begin, count = spans_ref[0], spans_ref[1]

    def fetch(step, slot):
        return pltpu.make_async_copy(
            adj_ref.at[pl.ds(begin + step * WIDE, WIDE), pl.ds(row0, nodes)],
            tiles_ref.at[slot],
            ready.at[slot],
        )

    @pl.when(count > 0)
    def _():
        fetch(0, 0).start()

    for copy in carry:
        copy.start()
    collect(piece, counts_ref, starts_ref, answer_ref, landed, arrived, packed)
    for copy in carry:
        copy.wait()
    if not last:
        total_ref[...] = jnp.zeros(total_ref.shape, jnp.float32)
        found_ref[...] = jnp.zeros(found_ref.shape, jnp.float32)

    @pl.loop(0, count)
    def _(step):
        slot = step & 1

        @pl.when(step + 1 < count)
        def _():
            fetch(step + 1, 1 - slot).start()

        fetch(step, slot).wait()
        depth = WIDE * TILE
        block = packed[pl.ds(pl.multiple_of(step * depth, depth), depth), :]
        lane = lax.broadcasted_iota(jnp.int32, (rows, depth), 1) + (begin * TILE + step * depth)
        lane = lane.astype(jnp.float32)

        @pl.loop(0, nodes // rows)
        def _(r):
            part = pl.ds(pl.multiple_of(r * rows, rows), rows)
            near = jnp.concatenate(
                [tiles_ref[slot, w, part, :].astype(jnp.bfloat16) for w in range(WIDE)], axis=1
            )
            flag = (lax.div(begin, WIDE) + step) * (adj_ref.shape[1] // rows) + row0 // rows + r

            @pl.when(own_here_ref[flag] == 0)
            def _():
                total_ref[part, :] += jnp.dot(near, block, preferred_element_type=jnp.float32)

            @pl.when(own_here_ref[flag] != 0)
            def _():
                own = jnp.where(notes_ref[part, 0:1] == lane, 1.0, 0.0).astype(jnp.bfloat16)
                both = jnp.dot(
                    jnp.concatenate([near, own], axis=0), block, preferred_element_type=jnp.float32
                )
                total_ref[part, :] += both[:rows]
                found_ref[part, :] += both[rows:]

    if last:
        share = share_refs[0].shape[0]
        step_rows = math.gcd(share, 3 * TILE)
        for p, share_ref in enumerate(share_refs):
            for r in range(share // step_rows):
                part = pl.ds(p * share + r * step_rows, step_rows)
                own = found_ref[part, :].astype(jnp.bfloat16)
                mean = (total_ref[part, :] / notes_ref[part, 1:2]).astype(jnp.bfloat16)
                own_ref[part, :] = own
                mean_ref[part, :] = mean
                share_ref[pl.ds(r * step_rows, step_rows), :] = (
                    jnp.dot(own, wself_ref[...], preferred_element_type=jnp.float32)
                    + jnp.dot(mean, wneigh_ref[...], preferred_element_type=jnp.float32)
                ).astype(share_ref.dtype)


def gather_sum(inputs, scalars, answer, notes, adj, rest=None, row0=0, shares=()):
    batch_count, width, features = answer.shape
    tiles, nodes, _ = adj.shape
    nodes = sum(shares) or nodes
    piece = LANES if width % LANES == 0 else SLOTS
    last = rest is not None
    room = min(batch_count * width, inputs) + SLOTS * batch_count + 2 * WIDE * TILE
    in_specs = [SMEM, SMEM, SMEM, SMEM, ANY, HBM, HBM]
    rows = lambda dtype: jax.ShapeDtypeStruct((nodes, features), dtype)
    scratch = [
        pltpu.VMEM((room, features), jnp.bfloat16),
        pltpu.VMEM((2, WIDE, nodes, TILE), adj.dtype),
        pltpu.SemaphoreType.DMA((2,)),
        pltpu.VMEM(answer.shape, answer.dtype),
        pltpu.SemaphoreType.DMA((batch_count, width // piece)),
        pltpu.VMEM((nodes, notes.shape[1]), notes.dtype),
        pltpu.SemaphoreType.DMA((5,)),
    ]
    operands = [answer, notes, adj]
    if last:
        operands += list(rest)
        in_specs += [HBM] * len(rest)
        out_shape = (rows(jnp.bfloat16), rows(jnp.bfloat16))
        out_shape += tuple(
            jax.ShapeDtypeStruct((n, rest[3].shape[1]), jnp.bfloat16) for n in shares
        )
        scratch += [pltpu.VMEM((nodes, features), jnp.float32)] * 2
        scratch += [pltpu.VMEM(x.shape, x.dtype) for x in rest[2:]]
    else:
        out_shape = (rows(jnp.float32), rows(jnp.float32))
    return pl.pallas_call(
        functools.partial(gather_sum_body, piece, last, row0),
        out_shape=out_shape,
        in_specs=in_specs,
        out_specs=(VMEM,) * len(out_shape),
        scratch_shapes=scratch,
        compiler_params=params(50),
        cost_estimate=cost(2 * nodes * features * TILE * tiles, nodes * TILE * tiles // 2),
        name="gather_sum",
    )(*scalars, *operands)


def share_order(array, parts, seeds):
    others = array.shape[0] - seeds
    own, rest = seeds // parts, others // parts
    tail = array.shape[1:]
    blocks = jnp.concatenate(
        [array[:seeds].reshape(parts, own, *tail), array[seeds:].reshape(parts, rest, *tail)],
        axis=1,
    )
    return ahead(blocks).reshape(array.shape)


def spread(part, axis, count):
    return lax.all_to_all(
        jnp.broadcast_to(part[None], (count,) + part.shape), axis, 0, 0, tiled=True
    )


def passed(part, shift, axis="feat"):
    parts = lax.axis_size(axis)
    return lax.ppermute(part, axis, [((i + shift) % parts, i) for i in range(parts)])


def turned(array, by):
    twice = jnp.concatenate([array, array], axis=0)
    return lax.dynamic_slice_in_dim(twice, by, array.shape[0], 0)


def ahead(array, axis="feat"):
    return turned(array, lax.axis_index(axis))


def spread_parts(part, axis="feat"):
    return [part] + [passed(part, j, axis) for j in range(1, lax.axis_size(axis))]


def sum_parts(blocks, axis="feat"):
    parts = lax.axis_size(axis)
    came = [blocks[0]] + [passed(blocks[j], -j, axis) for j in range(1, parts)]
    return sum(x.astype(jnp.float32) for x in came)


def swapped(part):
    return lax.ppermute(part, "batch", [(i, i ^ 1) for i in range(lax.axis_size("batch"))])


def total_over_batch(terms):
    count = lax.axis_size("batch")
    rows, width = terms.shape
    if count > FEW:
        pieces = terms.astype(jnp.bfloat16).reshape(count, rows // count, width)
        pieces = lax.all_to_all(pieces, "batch", 0, 0, tiled=True)
        total = jnp.sum(pieces.astype(jnp.float32), axis=0).astype(jnp.bfloat16)
        return spread(total, "batch", count).reshape(rows, width)
    chips = count // 2
    index = lax.axis_index("batch")
    first, chip = index % 2 == 0, index // 2
    upper, lower = terms[: rows // 2], terms[rows // 2 :]
    came = swapped(jnp.where(first, lower, upper).astype(jnp.bfloat16))
    mine = jnp.where(first, upper, lower) + came.astype(jnp.float32)
    pieces = turned(mine.reshape(chips, rows // count, width), chip)
    total = pieces[0]
    for j in range(1, chips):
        total = total + passed(pieces[j].astype(jnp.bfloat16), -2 * j, "batch").astype(jnp.float32)
    total = total.astype(jnp.bfloat16)
    mine = jnp.stack([total] + [passed(total, 2 * j, "batch") for j in range(1, chips)])
    other = swapped(mine)
    both = jnp.stack([jnp.where(first, mine, other), jnp.where(first, other, mine)], axis=1)
    return turned(both, (chips - chip) % chips).transpose(1, 0, 2, 3).reshape(rows, width)


def local(
    store,
    input_owner,
    input_row,
    nbr_one,
    deg_one,
    nbr_two,
    deg_two,
    cotangent,
    w1_self,
    w1_neigh,
    bias_one,
    w2_self,
    w2_neigh,
    bias_two,
):
    batch_count = lax.axis_size("batch")
    parts = lax.axis_size("feat")
    feat_index = lax.axis_index("feat")
    input_count = input_owner.shape[1]
    capacity = 2 * input_count // batch_count
    nodes = nbr_one.shape[1]
    seed_rows = nbr_two.shape[1]
    seeds = seed_rows * parts
    share = nodes // parts
    hidden_width = w1_self.shape[1]

    owners = input_owner.reshape(input_count // LANES, LANES)
    wanted = input_row.reshape(input_count // LANES, LANES)
    slots, counts, requests = make_requests(batch_count, capacity, owners, wanted)
    owners = owners.reshape(1, input_count)
    received = lax.all_to_all(
        requests.reshape(batch_count, capacity), "batch", split_axis=0, concat_axis=0, tiled=True
    )
    first = capacity // 2
    places = received.reshape(batch_count * capacity) * (store.shape[1] // LANES)
    looked_a = lookup(store, places, batch_count, 0, first, 60)
    near_first, looked_a = lax.optimization_barrier((nbr_one[0], looked_a))
    answer_a = lax.all_to_all(looked_a, "batch", split_axis=0, concat_axis=0, tiled=True)
    looked = lookup(store, places, batch_count, first, capacity - first, 24)

    depth = WIDE * TILE
    steps = -(-(input_count + 2 * (SLOTS - 1) * batch_count + depth - 1) // depth)
    tally = counts[:, 0]
    tally_a = jnp.minimum(tally, first)
    tally_b = tally - tally_a
    padded = lambda n: (n + SLOTS - 1) // SLOTS * SLOTS
    ends = lambda n: jnp.concatenate([jnp.zeros((1,), jnp.int32), jnp.cumsum(padded(n))])
    starts_a, starts_b = ends(tally_a), ends(tally_b)
    steps_a = (starts_a[batch_count] + depth - 1) // depth
    steps_b = (starts_b[batch_count] + depth - 1) // depth
    spans_a = jnp.stack([jnp.zeros_like(steps_a), steps_a])
    spans_b = jnp.stack([steps_a * WIDE, steps_b])
    slot = slots.reshape(1, input_count)
    shifted = jnp.where(
        slot < first,
        slot + starts_a[:batch_count, None],
        slot - first + steps_a * depth + starts_b[:batch_count, None],
    )
    mine = owners == jnp.arange(batch_count)[:, None]
    column = jnp.sum(jnp.where(mine, shifted, 0), axis=0)
    grid = jnp.pad(column.reshape(-1, LANES), ((0, LANES - input_count // LANES), (0, 0))).T
    table = jnp.concatenate([grid // TILE, grid % TILE], axis=0).astype(jnp.bfloat16)
    notes = jnp.stack([column[:nodes], deg_one[0]], axis=1).astype(jnp.float32)
    notes = share_order(notes, parts, seeds)
    block = math.gcd(nodes, 3 * TILE)
    met = notes[:, 0].reshape(1, nodes // block, block) // depth
    met = met.astype(jnp.int32) == jnp.arange(steps)[:, None, None]
    own_here = jnp.any(met, axis=2).astype(jnp.int32).reshape(-1)

    fanout_two = nbr_two.shape[2]
    used_two = jnp.arange(fanout_two)[:, None] < deg_two
    lists = jnp.concatenate([jnp.where(used_two, nbr_two[0].T, -1), deg_two], axis=0)
    lists = jnp.stack(spread_parts(lists))

    fanout = nbr_one.shape[2]
    used = jnp.arange(fanout)[None, :] < deg_one[0][:, None]
    near = jnp.pad(jnp.where(used, near_first, -1), ((0, 0), (0, SLOTS - fanout)), constant_values=-1)
    near, lists = lax.optimization_barrier((near, lists))
    me = feat_index.astype(jnp.int32).reshape(1)
    near = near.reshape(nodes // SLOTS, TILE)
    adj = adjacency(me, near, table, steps * WIDE, parts, seeds)
    looked, answer_a, adj = lax.optimization_barrier((looked, answer_a, adj))
    answer_b = lax.all_to_all(looked, "batch", split_axis=0, concat_axis=0, tiled=True)

    near_two = lists[:, :fanout_two].transpose(1, 0, 2).reshape(fanout_two, seeds)
    deg_all = lists[:, fanout_two].reshape(seeds)
    rest = share - seed_rows
    after = near_two - seeds
    place = jnp.where(
        near_two < seeds,
        near_two // seed_rows * share + near_two % seed_rows,
        after // rest * share + seed_rows + after % rest,
    )
    place = jnp.where(near_two < 0, -1, place - feat_index * share)
    adj_two = jnp.sum(
        place[:, :, None] == jnp.arange(share)[None, None, :], axis=0, dtype=jnp.float32
    ).astype(jnp.bfloat16)

    scalars = (spans_a, tally_a, starts_a, own_here)
    total, found = gather_sum(input_count, scalars, answer_a, notes, adj)

    def finish(begin, end):
        return gather_sum(
            input_count,
            (spans_b, tally_b, starts_b, own_here),
            answer_b,
            notes,
            adj,
            (total, found, w1_self, w1_neigh),
            begin * share,
            (share,) * (end - begin),
        )

    self_far, agg_far, *z_far = finish(1, parts)
    total, z_far = lax.optimization_barrier((total, z_far))
    self_near, agg_near, *z_near = finish(0, 1)
    z_share = sum_parts(z_near + z_far) + bias_one
    hidden = jax.nn.silu(z_share).astype(jnp.bfloat16)

    agg_parts = jnp.dot(adj_two, hidden, preferred_element_type=jnp.float32)
    agg_total = sum_parts(agg_parts.reshape(parts, seed_rows, hidden_width))
    deg_second = deg_two[0].astype(jnp.float32)[:, None]
    agg_two = (agg_total / deg_second).astype(jnp.bfloat16)
    self_two = hidden[:seed_rows]
    z_two = (
        jnp.dot(self_two, w2_self, preferred_element_type=jnp.float32)
        + jnp.dot(agg_two, w2_neigh, preferred_element_type=jnp.float32)
        + bias_two
    )
    activations = jax.nn.silu(z_two).astype(jnp.bfloat16)[None]
    dz_two = (cotangent[0].astype(jnp.float32) * silu_grad(z_two)).astype(jnp.bfloat16)
    group = jnp.stack(spread_parts(jnp.stack([self_two, agg_two, dz_two])))
    dz_two_all = group[:, 2].reshape(seeds, hidden_width)

    back = contract_cols(dz_two_all, w2_neigh) / deg_all.astype(jnp.float32)[:, None]
    back_high = back.astype(jnp.bfloat16)
    back_low = (back - back_high.astype(jnp.float32)).astype(jnp.bfloat16)
    dh_share = contract_rows(adj_two, back_high) + contract_rows(adj_two, back_low)
    dh_share = dh_share + jnp.pad(contract_cols(dz_two, w2_self), ((0, rest), (0, 0)))
    dz_share = (dh_share * silu_grad(z_share)).astype(jnp.bfloat16)
    dz_blocks = spread_parts(dz_share)
    dz_near, dz_far = dz_blocks[0], jnp.concatenate(dz_blocks[1:])
    group = turned(group, (parts - feat_index) % parts).transpose(1, 0, 2, 3)
    self_all, agg_all, dz_all = (x.reshape(seeds, hidden_width) for x in group)
    grads = [contract_rows(self_all, dz_all), contract_rows(agg_all, dz_all)]
    grads.append(contract_rows(self_near, dz_near) + contract_rows(self_far, dz_far))
    grads.append(contract_rows(agg_near, dz_near) + contract_rows(agg_far, dz_far))
    total = total_over_batch(jnp.concatenate(grads)).astype(jnp.float32)
    return (activations, *total.reshape(len(grads), -1, hidden_width))


def solution(mesh):
    in_specs = (
        P("batch", "feat"),
        P("batch", None, None),
        P("batch", None),
        P("batch", None, None),
        P("batch", None),
        P("batch", "feat", None),
        P("batch", "feat"),
        P("batch", "feat", None),
        P("feat", None),
        P("feat", None),
        P(),
        P(),
        P(),
        P(),
    )
    out_specs = (P("batch", "feat", None), P(), P(), P("feat", None), P("feat", None))
    return jax.shard_map(local, mesh=mesh, in_specs=in_specs, out_specs=out_specs, check_vma=False)
```

```python
import functools
import math

import jax
import jax.numpy as jnp
from jax import lax
from jax.experimental import pallas as pl
from jax.experimental.pallas import tpu as pltpu
from jax.sharding import PartitionSpec as P

TILE = 256
LANES = 128
SLOTS = 16
WIDE = 2
FEW = 16
TILE_BITS, LANE_BITS, SLOT_BITS = 8, 7, 4
MIB = 1024 * 1024
VMEM = pl.BlockSpec(memory_space=pltpu.VMEM)
SMEM = pl.BlockSpec(memory_space=pltpu.SMEM)
ANY = pl.BlockSpec(memory_space=pl.ANY)
HBM = pl.BlockSpec(memory_space=pltpu.HBM)


def silu_grad(values):
    sig = jax.nn.sigmoid(values)
    return sig * (1.0 + values * (1.0 - sig))


def contract_rows(left_side, right_side):
    return lax.dot_general(
        left_side, right_side, (((0,), (0,)), ((), ())), preferred_element_type=jnp.float32
    )


def contract_cols(left_side, right_side):
    return lax.dot_general(
        left_side, right_side, (((1,), (1,)), ((), ())), preferred_element_type=jnp.float32
    )


def params(mib):
    return pltpu.CompilerParams(vmem_limit_bytes=mib * MIB)


def cost(flops, moved):
    return pl.CostEstimate(flops=int(flops), bytes_accessed=int(moved), transcendentals=0)


def requests_body(batch_count, capacity, scale, owner_ref, row_ref, slot_ref, count_ref, request_ref):
    blocks, width = owner_ref.shape[0] // 2, TILE
    places = request_ref.shape[0]
    line = lambda ref, b: jnp.concatenate([ref[2 * b : 2 * b + 1], ref[2 * b + 1 : 2 * b + 2]], axis=1)
    owner_id = lax.broadcasted_iota(jnp.int32, (batch_count, width), 0)
    earlier = lax.broadcasted_iota(jnp.int32, (width, width), 0)
    later = lax.broadcasted_iota(jnp.int32, (width, width), 1)
    upper = jnp.where(earlier <= later, 1.0, 0.0).astype(jnp.bfloat16)
    high_id = lax.broadcasted_iota(jnp.int32, (places, width), 0)
    low_id = lax.broadcasted_iota(jnp.int32, (LANES, width), 0)
    marks = [
        jnp.where(line(owner_ref, b) == owner_id, 1.0, 0.0) for b in range(blocks)
    ]
    stacked = jnp.concatenate(marks, axis=0).astype(jnp.bfloat16)
    prefix = jnp.dot(stacked, upper, preferred_element_type=jnp.float32)
    running = jnp.zeros((batch_count, 1), jnp.float32)
    total = jnp.zeros((2 * places, LANES), jnp.float32)
    for b in range(blocks):
        part = prefix[b * batch_count : (b + 1) * batch_count]
        slots = jnp.sum(marks[b] * (part + running - 1.0), axis=0, keepdims=True)
        slots = slots.astype(jnp.int32)
        slot_ref[2 * b : 2 * b + 1, :] = slots[:, :LANES]
        slot_ref[2 * b + 1 : 2 * b + 2, :] = slots[:, LANES:]
        running = running + part[:, width - 1 : width]
        bucket = line(owner_ref, b) * capacity + slots
        rows = line(row_ref, b)
        hit = (bucket >> LANE_BITS) == high_id
        left = jnp.concatenate(
            [
                jnp.where(hit, (rows >> TILE_BITS).astype(jnp.float32), 0.0),
                jnp.where(hit, (rows & (TILE - 1)).astype(jnp.float32), 0.0),
            ],
            axis=0,
        ).astype(jnp.bfloat16)
        right = jnp.where((bucket & (LANES - 1)) == low_id, 1.0, 0.0).astype(jnp.bfloat16)
        total = total + contract_cols(left, right)
    count_ref[...] = jnp.broadcast_to(running, count_ref.shape).astype(jnp.int32)
    request_ref[...] = (total[:places] * TILE + total[places:]).astype(jnp.int32) * scale


def make_requests(batch_count, capacity, scale, owners, wanted):
    total = owners.shape[0] * LANES
    places = batch_count * capacity // LANES
    return pl.pallas_call(
        functools.partial(requests_body, batch_count, capacity, scale),
        out_shape=(
            jax.ShapeDtypeStruct(owners.shape, jnp.int32),
            jax.ShapeDtypeStruct((batch_count, LANES), jnp.int32),
            jax.ShapeDtypeStruct((places, LANES), jnp.int32),
        ),
        in_specs=[VMEM, VMEM],
        out_specs=(VMEM, VMEM, VMEM),
        compiler_params=params(16),
        cost_estimate=cost(4 * total * places * LANES, 24 * total),
        name="requests",
    )(owners, wanted)


def table_body(store_ref, table_ref):
    halves = store_ref.shape[1] // LANES

    @pl.loop(0, store_ref.shape[0] // TILE)
    def _(j):
        part = pl.ds(pl.multiple_of(j * TILE, TILE), TILE)
        for h in range(halves):
            spot = pl.ds(pl.multiple_of(j * TILE * halves, TILE) + h, TILE, stride=halves)
            table_ref[spot, :] = store_ref[part, pl.ds(h * LANES, LANES)].astype(jnp.float32)


def make_table(store):
    rows_all, features = store.shape
    return pl.pallas_call(
        table_body,
        out_shape=jax.ShapeDtypeStruct((rows_all * features // LANES, LANES), jnp.float32),
        in_specs=[VMEM],
        out_specs=VMEM,
        compiler_params=params(24),
        cost_estimate=cost(rows_all * features, 6 * rows_all * features),
        name="table",
    )(store)


def lookup_body(stride, first, want_ref, table_ref, out_ref, lines):
    groups, width, features = out_ref.shape
    halves = features // LANES

    @pl.loop(0, groups)
    def _(g):
        begin = g * stride + first

        @pl.loop(0, width // SLOTS, unroll=2)
        def _(j):
            at = [want_ref[begin + j * SLOTS + u] for u in range(SLOTS)]
            rows = [table_ref[pl.ds(pl.multiple_of(a, halves), halves), :] for a in at]
            depth = SLOTS * halves
            block = lines.at[pl.ds(pl.multiple_of(j * depth, depth), depth)]
            for u in range(SLOTS):
                block[pl.ds(u * halves, halves), :] = rows[u]

        for h in range(halves):
            out_ref[g, :, pl.ds(h * LANES, LANES)] = lines[
                pl.ds(h, width, stride=halves), :
            ].astype(jnp.bfloat16)


def lookup(table, places, groups, features, first, width):
    return pl.pallas_call(
        functools.partial(lookup_body, places.shape[0] // groups, first),
        out_shape=jax.ShapeDtypeStruct((groups, width, features), jnp.bfloat16),
        in_specs=[SMEM, VMEM],
        out_specs=VMEM,
        scratch_shapes=[pltpu.VMEM((width * features // LANES, LANES), jnp.float32)],
        compiler_params=params(24),
        cost_estimate=cost(groups * width * features * 40, 4 * table.size),
        name="lookup",
    )(places, table)


def adjacency_body(tiles, me_ref, near_ref, table_ref, out_ref):
    groups = near_ref.shape[0]
    node_high = lax.broadcasted_iota(jnp.int32, (LANES, TILE), 0)
    own_row = (
        lax.shift_right_logical(lax.broadcasted_iota(jnp.int32, (SLOTS, TILE), 1), SLOT_BITS)
        == lax.broadcasted_iota(jnp.int32, (SLOTS, TILE), 0)
    )
    low_id = lax.broadcasted_iota(jnp.int32, (TILE, TILE), 0).astype(jnp.float32)

    def one_group(g):
        near = near_ref[pl.ds(g, 1), :]
        pick = jnp.where((near >> LANE_BITS) == node_high, 1.0, 0.0).astype(jnp.bfloat16)
        found = jnp.dot(table_ref[...], pick, preferred_element_type=jnp.float32)
        here = (near & (LANES - 1)) == node_high
        high = jnp.sum(jnp.where(here, found[:LANES], 0.0), axis=0, keepdims=True)
        low = jnp.sum(jnp.where(here, found[LANES:], 0.0), axis=0, keepdims=True)
        high = jnp.where(near < 0, -1.0, high)
        rows = jnp.where(own_row, high, -1.0)
        left = jnp.concatenate(
            [jnp.where(rows == float(t), 1.0, 0.0) for t in range(tiles)], axis=0
        ).astype(jnp.bfloat16)
        right = jnp.where(low == low_id, 1.0, 0.0).astype(jnp.bfloat16)
        return contract_cols(left, right).reshape(tiles, SLOTS, TILE)

    @pl.loop(0, groups // 2, unroll=2)
    def _(j):
        pair = jnp.concatenate([one_group(2 * j), one_group(2 * j + 1)], axis=1)
        out_ref[:, pl.ds(pl.multiple_of(j * 2 * SLOTS, 2 * SLOTS), 2 * SLOTS), :] = pair.astype(
            out_ref.dtype
        )


def adjacency(me, near, table, tiles, parts, seeds):
    groups = near.shape[0]
    nodes = groups * SLOTS
    step = LANES // SLOTS
    own, rest, share = (n // parts // LANES for n in (seeds, nodes - seeds, nodes))

    def place(block, me_ref):
        after = block - own * parts
        is_own = after < 0
        part = jnp.where(is_own, lax.div(block, own), lax.div(after, rest))
        at = jnp.where(is_own, lax.rem(block, own), own + lax.rem(after, rest))
        return (0, lax.rem(part - me_ref[0] + parts, parts) * share + at, 0)

    return pl.pallas_call(
        functools.partial(adjacency_body, tiles),
        out_shape=jax.ShapeDtypeStruct((tiles, nodes, TILE), jnp.float8_e4m3fn),
        grid_spec=pltpu.PrefetchScalarGridSpec(
            num_scalar_prefetch=1,
            grid=(groups // step,),
            in_specs=[
                pl.BlockSpec((step, TILE), lambda r, me: (r, 0)),
                pl.BlockSpec(table.shape, lambda r, me: (0, 0)),
            ],
            out_specs=pl.BlockSpec((tiles, LANES, TILE), place),
        ),
        compiler_params=params(48),
        cost_estimate=cost(2 * nodes * TILE * TILE * tiles * 2, nodes * TILE * tiles),
        name="adjacency",
    )(me, near, table)


def collect(piece, counts_ref, starts_ref, answer_ref, landed, arrived, packed):
    batch_count = answer_ref.shape[0]

    def each_used(what):
        @pl.loop(0, batch_count)
        def _(o):
            @pl.loop(0, pl.cdiv(counts_ref[o], piece))
            def _(c):
                part = pl.ds(pl.multiple_of(c * piece, piece), piece)
                what(
                    o,
                    c,
                    part,
                    pltpu.make_async_copy(
                        answer_ref.at[o, part], landed.at[o, part], arrived.at[o, c]
                    ),
                )

    def lay(o, c, part, copy):
        copy.wait()
        packed[pl.ds(pl.multiple_of(starts_ref[o] + c * piece, SLOTS), piece), :] = landed[o, part]

    each_used(lambda o, c, part, copy: copy.start())
    each_used(lay)
    end = starts_ref[batch_count]
    packed[pl.ds(pl.multiple_of(end, SLOTS), WIDE * TILE), :] = jnp.zeros(
        (WIDE * TILE, packed.shape[1]), packed.dtype
    )


def gather_sum_body(
    piece,
    last,
    row0,
    spans_ref,
    counts_ref,
    starts_ref,
    own_here_ref,
    answer_ref,
    notes_in,
    adj_ref,
    *refs,
):
    if last:
        (total_in, found_in, wself_in, wneigh_in, own_ref, mean_ref) = refs[:6]
        share_refs = refs[6:-11]
        packed, tiles_ref, ready, landed, arrived, notes_ref, carried = refs[-11:-4]
        total_ref, found_ref, wself_ref, wneigh_ref = refs[-4:]
        mine = pl.ds(row0, total_ref.shape[0])
        pairs = ((notes_in.at[mine], notes_ref), (total_in.at[mine], total_ref))
        pairs += ((found_in.at[mine], found_ref),)
        pairs += ((wself_in, wself_ref), (wneigh_in, wneigh_ref))
    else:
        total_ref, found_ref, packed, tiles_ref, ready, landed, arrived, notes_ref, carried = refs
        pairs = ((notes_in, notes_ref),)
    carry = [pltpu.make_async_copy(*pair, carried.at[n]) for n, pair in enumerate(pairs)]
    nodes = total_ref.shape[0]
    rows = math.gcd(adj_ref.shape[1], 3 * TILE)
    begin, count = spans_ref[0], spans_ref[1]

    def fetch(step, slot):
        return pltpu.make_async_copy(
            adj_ref.at[pl.ds(begin + step * WIDE, WIDE), pl.ds(row0, nodes)],
            tiles_ref.at[slot],
            ready.at[slot],
        )

    @pl.when(count > 0)
    def _():
        fetch(0, 0).start()

    for copy in carry:
        copy.start()
    collect(piece, counts_ref, starts_ref, answer_ref, landed, arrived, packed)
    for copy in carry:
        copy.wait()
    if not last:
        total_ref[...] = jnp.zeros(total_ref.shape, jnp.float32)
        found_ref[...] = jnp.zeros(found_ref.shape, jnp.float32)

    @pl.loop(0, count)
    def _(step):
        slot = step & 1

        @pl.when(step + 1 < count)
        def _():
            fetch(step + 1, 1 - slot).start()

        fetch(step, slot).wait()
        depth = WIDE * TILE
        block = packed[pl.ds(pl.multiple_of(step * depth, depth), depth), :]
        lane = lax.broadcasted_iota(jnp.int32, (rows, depth), 1) + (begin * TILE + step * depth)
        lane = lane.astype(jnp.float32)

        @pl.loop(0, nodes // rows)
        def _(r):
            part = pl.ds(pl.multiple_of(r * rows, rows), rows)
            near = jnp.concatenate(
                [tiles_ref[slot, w, part, :].astype(jnp.bfloat16) for w in range(WIDE)], axis=1
            )
            flag = (lax.div(begin, WIDE) + step) * (adj_ref.shape[1] // rows) + row0 // rows + r

            @pl.when(own_here_ref[flag] == 0)
            def _():
                total_ref[part, :] += jnp.dot(near, block, preferred_element_type=jnp.float32)

            @pl.when(own_here_ref[flag] != 0)
            def _():
                own = jnp.where(notes_ref[part, 0:1] == lane, 1.0, 0.0).astype(jnp.bfloat16)
                both = jnp.dot(
                    jnp.concatenate([near, own], axis=0), block, preferred_element_type=jnp.float32
                )
                total_ref[part, :] += both[:rows]
                found_ref[part, :] += both[rows:]

    if last:
        share = share_refs[0].shape[0]
        step_rows = math.gcd(share, 3 * TILE)
        for p, share_ref in enumerate(share_refs):
            for r in range(share // step_rows):
                part = pl.ds(p * share + r * step_rows, step_rows)
                own = found_ref[part, :].astype(jnp.bfloat16)
                mean = (total_ref[part, :] / notes_ref[part, 1:2]).astype(jnp.bfloat16)
                own_ref[part, :] = own
                mean_ref[part, :] = mean
                share_ref[pl.ds(r * step_rows, step_rows), :] = (
                    jnp.dot(own, wself_ref[...], preferred_element_type=jnp.float32)
                    + jnp.dot(mean, wneigh_ref[...], preferred_element_type=jnp.float32)
                ).astype(share_ref.dtype)


def gather_sum(inputs, scalars, answer, notes, adj, rest=None, row0=0, shares=()):
    batch_count, width, features = answer.shape
    tiles, nodes, _ = adj.shape
    nodes = sum(shares) or nodes
    piece = LANES if width % LANES == 0 else SLOTS
    last = rest is not None
    room = min(batch_count * width, inputs) + SLOTS * batch_count + 2 * WIDE * TILE
    in_specs = [SMEM, SMEM, SMEM, SMEM, ANY, HBM, HBM]
    rows = lambda dtype: jax.ShapeDtypeStruct((nodes, features), dtype)
    scratch = [
        pltpu.VMEM((room, features), jnp.bfloat16),
        pltpu.VMEM((2, WIDE, nodes, TILE), adj.dtype),
        pltpu.SemaphoreType.DMA((2,)),
        pltpu.VMEM(answer.shape, answer.dtype),
        pltpu.SemaphoreType.DMA((batch_count, width // piece)),
        pltpu.VMEM((nodes, notes.shape[1]), notes.dtype),
        pltpu.SemaphoreType.DMA((5,)),
    ]
    operands = [answer, notes, adj]
    if last:
        operands += list(rest)
        in_specs += [HBM] * len(rest)
        out_shape = (rows(jnp.bfloat16), rows(jnp.bfloat16))
        out_shape += tuple(
            jax.ShapeDtypeStruct((n, rest[3].shape[1]), jnp.bfloat16) for n in shares
        )
        scratch += [pltpu.VMEM((nodes, features), jnp.float32)] * 2
        scratch += [pltpu.VMEM(x.shape, x.dtype) for x in rest[2:]]
    else:
        out_shape = (rows(jnp.float32), rows(jnp.float32))
    return pl.pallas_call(
        functools.partial(gather_sum_body, piece, last, row0),
        out_shape=out_shape,
        in_specs=in_specs,
        out_specs=(VMEM,) * len(out_shape),
        scratch_shapes=scratch,
        compiler_params=params(50),
        cost_estimate=cost(2 * nodes * features * TILE * tiles, nodes * TILE * tiles // 2),
        name="gather_sum",
    )(*scalars, *operands)


def share_order(array, parts, seeds):
    others = array.shape[0] - seeds
    own, rest = seeds // parts, others // parts
    tail = array.shape[1:]
    blocks = jnp.concatenate(
        [array[:seeds].reshape(parts, own, *tail), array[seeds:].reshape(parts, rest, *tail)],
        axis=1,
    )
    return ahead(blocks).reshape(array.shape)


def spread(part, axis, count):
    return lax.all_to_all(
        jnp.broadcast_to(part[None], (count,) + part.shape), axis, 0, 0, tiled=True
    )


def passed(part, shift, axis="feat"):
    parts = lax.axis_size(axis)
    return lax.ppermute(part, axis, [((i + shift) % parts, i) for i in range(parts)])


def turned(array, by):
    twice = jnp.concatenate([array, array], axis=0)
    return lax.dynamic_slice_in_dim(twice, by, array.shape[0], 0)


def ahead(array, axis="feat"):
    return turned(array, lax.axis_index(axis))


def spread_parts(part, axis="feat"):
    return [part] + [passed(part, j, axis) for j in range(1, lax.axis_size(axis))]


def sum_parts(blocks, axis="feat"):
    parts = lax.axis_size(axis)
    came = [blocks[0]] + [passed(blocks[j], -j, axis) for j in range(1, parts)]
    return sum(x.astype(jnp.float32) for x in came)


def swapped(part):
    return lax.ppermute(part, "batch", [(i, i ^ 1) for i in range(lax.axis_size("batch"))])


def total_over_batch(terms):
    count = lax.axis_size("batch")
    rows, width = terms.shape
    if count > FEW:
        pieces = terms.astype(jnp.bfloat16).reshape(count, rows // count, width)
        pieces = lax.all_to_all(pieces, "batch", 0, 0, tiled=True)
        total = jnp.sum(pieces.astype(jnp.float32), axis=0).astype(jnp.bfloat16)
        return spread(total, "batch", count).reshape(rows, width)
    chips = count // 2
    index = lax.axis_index("batch")
    first, chip = index % 2 == 0, index // 2
    upper, lower = terms[: rows // 2], terms[rows // 2 :]
    came = swapped(jnp.where(first, lower, upper).astype(jnp.bfloat16))
    mine = jnp.where(first, upper, lower) + came.astype(jnp.float32)
    pieces = turned(mine.reshape(chips, rows // count, width), chip)
    total = pieces[0]
    for j in range(1, chips):
        total = total + passed(pieces[j].astype(jnp.bfloat16), -2 * j, "batch").astype(jnp.float32)
    total = total.astype(jnp.bfloat16)
    mine = jnp.stack([total] + [passed(total, 2 * j, "batch") for j in range(1, chips)])
    other = swapped(mine)
    both = jnp.stack([jnp.where(first, mine, other), jnp.where(first, other, mine)], axis=1)
    return turned(both, (chips - chip) % chips).transpose(1, 0, 2, 3).reshape(rows, width)


def local(
    store,
    input_owner,
    input_row,
    nbr_one,
    deg_one,
    nbr_two,
    deg_two,
    cotangent,
    w1_self,
    w1_neigh,
    bias_one,
    w2_self,
    w2_neigh,
    bias_two,
):
    batch_count = lax.axis_size("batch")
    parts = lax.axis_size("feat")
    feat_index = lax.axis_index("feat")
    input_count = input_owner.shape[1]
    capacity = 2 * input_count // batch_count
    nodes = nbr_one.shape[1]
    seed_rows = nbr_two.shape[1]
    seeds = seed_rows * parts
    share = nodes // parts
    hidden_width = w1_self.shape[1]

    owners = input_owner.reshape(input_count // LANES, LANES)
    wanted = input_row.reshape(input_count // LANES, LANES)
    slots, counts, requests = make_requests(
        batch_count, capacity, store.shape[1] // LANES, owners, wanted
    )
    owners = owners.reshape(1, input_count)
    received = lax.all_to_all(
        requests.reshape(batch_count, capacity), "batch", split_axis=0, concat_axis=0, tiled=True
    )
    first = capacity // 2
    places = received.reshape(batch_count * capacity)
    table = make_table(store)
    features = store.shape[1]
    looked_a = lookup(table, places, batch_count, features, 0, first)
    near_first, looked_a = lax.optimization_barrier((nbr_one[0], looked_a))
    answer_a = lax.all_to_all(looked_a, "batch", split_axis=0, concat_axis=0, tiled=True)
    looked = lookup(table, places, batch_count, features, first, capacity - first)

    depth = WIDE * TILE
    steps = -(-(input_count + 2 * (SLOTS - 1) * batch_count + depth - 1) // depth)
    tally = counts[:, 0]
    tally_a = jnp.minimum(tally, first)
    tally_b = tally - tally_a
    padded = lambda n: (n + SLOTS - 1) // SLOTS * SLOTS
    ends = lambda n: jnp.concatenate([jnp.zeros((1,), jnp.int32), jnp.cumsum(padded(n))])
    starts_a, starts_b = ends(tally_a), ends(tally_b)
    steps_a = (starts_a[batch_count] + depth - 1) // depth
    steps_b = (starts_b[batch_count] + depth - 1) // depth
    spans_a = jnp.stack([jnp.zeros_like(steps_a), steps_a])
    spans_b = jnp.stack([steps_a * WIDE, steps_b])
    slot = slots.reshape(1, input_count)
    shifted = jnp.where(
        slot < first,
        slot + starts_a[:batch_count, None],
        slot - first + steps_a * depth + starts_b[:batch_count, None],
    )
    mine = owners == jnp.arange(batch_count)[:, None]
    column = jnp.sum(jnp.where(mine, shifted, 0), axis=0)
    grid = jnp.pad(column.reshape(-1, LANES), ((0, LANES - input_count // LANES), (0, 0))).T
    finder = jnp.concatenate([grid // TILE, grid % TILE], axis=0).astype(jnp.bfloat16)
    notes = jnp.stack([column[:nodes], deg_one[0]], axis=1).astype(jnp.float32)
    notes = share_order(notes, parts, seeds)
    block = math.gcd(nodes, 3 * TILE)
    met = notes[:, 0].reshape(1, nodes // block, block) // depth
    met = met.astype(jnp.int32) == jnp.arange(steps)[:, None, None]
    own_here = jnp.any(met, axis=2).astype(jnp.int32).reshape(-1)

    fanout_two = nbr_two.shape[2]
    used_two = jnp.arange(fanout_two)[:, None] < deg_two
    lists = jnp.concatenate([jnp.where(used_two, nbr_two[0].T, -1), deg_two], axis=0)
    lists = jnp.stack(spread_parts(lists))

    fanout = nbr_one.shape[2]
    used = jnp.arange(fanout)[None, :] < deg_one[0][:, None]
    near = jnp.pad(jnp.where(used, near_first, -1), ((0, 0), (0, SLOTS - fanout)), constant_values=-1)
    near, lists = lax.optimization_barrier((near, lists))
    me = feat_index.astype(jnp.int32).reshape(1)
    near = near.reshape(nodes // SLOTS, TILE)
    adj = adjacency(me, near, finder, steps * WIDE, parts, seeds)
    looked, answer_a, adj = lax.optimization_barrier((looked, answer_a, adj))
    answer_b = lax.all_to_all(looked, "batch", split_axis=0, concat_axis=0, tiled=True)

    near_two = lists[:, :fanout_two].transpose(1, 0, 2).reshape(fanout_two, seeds)
    deg_all = lists[:, fanout_two].reshape(seeds)
    rest = share - seed_rows
    after = near_two - seeds
    place = jnp.where(
        near_two < seeds,
        near_two // seed_rows * share + near_two % seed_rows,
        after // rest * share + seed_rows + after % rest,
    )
    place = jnp.where(near_two < 0, -1, place - feat_index * share)
    adj_two = jnp.sum(
        place[:, :, None] == jnp.arange(share)[None, None, :], axis=0, dtype=jnp.float32
    ).astype(jnp.bfloat16)

    scalars = (spans_a, tally_a, starts_a, own_here)
    total, found = gather_sum(input_count, scalars, answer_a, notes, adj)

    def finish(begin, end):
        return gather_sum(
            input_count,
            (spans_b, tally_b, starts_b, own_here),
            answer_b,
            notes,
            adj,
            (total, found, w1_self, w1_neigh),
            begin * share,
            (share,) * (end - begin),
        )

    self_far, agg_far, *z_far = finish(1, parts)
    total, z_far = lax.optimization_barrier((total, z_far))
    self_near, agg_near, *z_near = finish(0, 1)
    z_share = sum_parts(z_near + z_far) + bias_one
    hidden = jax.nn.silu(z_share).astype(jnp.bfloat16)

    agg_parts = jnp.dot(adj_two, hidden, preferred_element_type=jnp.float32)
    agg_total = sum_parts(agg_parts.reshape(parts, seed_rows, hidden_width))
    deg_second = deg_two[0].astype(jnp.float32)[:, None]
    agg_two = (agg_total / deg_second).astype(jnp.bfloat16)
    self_two = hidden[:seed_rows]
    z_two = (
        jnp.dot(self_two, w2_self, preferred_element_type=jnp.float32)
        + jnp.dot(agg_two, w2_neigh, preferred_element_type=jnp.float32)
        + bias_two
    )
    activations = jax.nn.silu(z_two).astype(jnp.bfloat16)[None]
    dz_two = (cotangent[0].astype(jnp.float32) * silu_grad(z_two)).astype(jnp.bfloat16)
    group = jnp.stack(spread_parts(jnp.stack([self_two, agg_two, dz_two])))
    dz_two_all = group[:, 2].reshape(seeds, hidden_width)

    back = contract_cols(dz_two_all, w2_neigh) / deg_all.astype(jnp.float32)[:, None]
    back_high = back.astype(jnp.bfloat16)
    back_low = (back - back_high.astype(jnp.float32)).astype(jnp.bfloat16)
    dh_share = contract_rows(adj_two, back_high) + contract_rows(adj_two, back_low)
    dh_share = dh_share + jnp.pad(contract_cols(dz_two, w2_self), ((0, rest), (0, 0)))
    dz_share = (dh_share * silu_grad(z_share)).astype(jnp.bfloat16)
    dz_blocks = spread_parts(dz_share)
    dz_near, dz_far = dz_blocks[0], jnp.concatenate(dz_blocks[1:])
    group = turned(group, (parts - feat_index) % parts).transpose(1, 0, 2, 3)
    self_all, agg_all, dz_all = (x.reshape(seeds, hidden_width) for x in group)
    grads = [contract_rows(self_all, dz_all), contract_rows(agg_all, dz_all)]
    grads.append(contract_rows(self_near, dz_near) + contract_rows(self_far, dz_far))
    grads.append(contract_rows(agg_near, dz_near) + contract_rows(agg_far, dz_far))
    total = total_over_batch(jnp.concatenate(grads)).astype(jnp.float32)
    return (activations, *total.reshape(len(grads), -1, hidden_width))


def solution(mesh):
    in_specs = (
        P("batch", "feat"),
        P("batch", None, None),
        P("batch", None),
        P("batch", None, None),
        P("batch", None),
        P("batch", "feat", None),
        P("batch", "feat"),
        P("batch", "feat", None),
        P("feat", None),
        P("feat", None),
        P(),
        P(),
        P(),
        P(),
    )
    out_specs = (P("batch", "feat", None), P(), P(), P("feat", None), P("feat", None))
    return jax.shard_map(local, mesh=mesh, in_specs=in_specs, out_specs=out_specs, check_vma=False)
```

```python
import functools
import math

import jax
import jax.numpy as jnp
from jax import lax
from jax.experimental import pallas as pl
from jax.experimental.pallas import tpu as pltpu
from jax.sharding import PartitionSpec as P

TILE = 256
LANES = 128
SLOTS = 16
WIDE = 2
FEW = 16
TILE_BITS, LANE_BITS, SLOT_BITS = 8, 7, 4
MIB = 1024 * 1024
VMEM = pl.BlockSpec(memory_space=pltpu.VMEM)
SMEM = pl.BlockSpec(memory_space=pltpu.SMEM)
ANY = pl.BlockSpec(memory_space=pl.ANY)
HBM = pl.BlockSpec(memory_space=pltpu.HBM)


def silu_grad(values):
    sig = jax.nn.sigmoid(values)
    return sig * (1.0 + values * (1.0 - sig))


def contract_rows(left_side, right_side):
    return lax.dot_general(
        left_side, right_side, (((0,), (0,)), ((), ())), preferred_element_type=jnp.float32
    )


def contract_cols(left_side, right_side):
    return lax.dot_general(
        left_side, right_side, (((1,), (1,)), ((), ())), preferred_element_type=jnp.float32
    )


def params(mib):
    return pltpu.CompilerParams(vmem_limit_bytes=mib * MIB)


def cost(flops, moved):
    return pl.CostEstimate(flops=int(flops), bytes_accessed=int(moved), transcendentals=0)


def requests_body(batch_count, capacity, scale, owner_ref, row_ref, slot_ref, count_ref, request_ref):
    blocks, width = owner_ref.shape[0] // 2, TILE
    places = request_ref.shape[0]
    line = lambda ref, b: jnp.concatenate([ref[2 * b : 2 * b + 1], ref[2 * b + 1 : 2 * b + 2]], axis=1)
    owner_id = lax.broadcasted_iota(jnp.int32, (batch_count, width), 0)
    earlier = lax.broadcasted_iota(jnp.int32, (width, width), 0)
    later = lax.broadcasted_iota(jnp.int32, (width, width), 1)
    upper = jnp.where(earlier <= later, 1.0, 0.0).astype(jnp.bfloat16)
    high_id = lax.broadcasted_iota(jnp.int32, (places, width), 0)
    low_id = lax.broadcasted_iota(jnp.int32, (LANES, width), 0)
    marks = [
        jnp.where(line(owner_ref, b) == owner_id, 1.0, 0.0) for b in range(blocks)
    ]
    stacked = jnp.concatenate(marks, axis=0).astype(jnp.bfloat16)
    prefix = jnp.dot(stacked, upper, preferred_element_type=jnp.float32)
    running = jnp.zeros((batch_count, 1), jnp.float32)
    total = jnp.zeros((2 * places, LANES), jnp.float32)
    for b in range(blocks):
        part = prefix[b * batch_count : (b + 1) * batch_count]
        slots = jnp.sum(marks[b] * (part + running - 1.0), axis=0, keepdims=True)
        slots = slots.astype(jnp.int32)
        slot_ref[2 * b : 2 * b + 1, :] = slots[:, :LANES]
        slot_ref[2 * b + 1 : 2 * b + 2, :] = slots[:, LANES:]
        running = running + part[:, width - 1 : width]
        bucket = line(owner_ref, b) * capacity + slots
        rows = line(row_ref, b)
        hit = (bucket >> LANE_BITS) == high_id
        left = jnp.concatenate(
            [
                jnp.where(hit, (rows >> TILE_BITS).astype(jnp.float32), 0.0),
                jnp.where(hit, (rows & (TILE - 1)).astype(jnp.float32), 0.0),
            ],
            axis=0,
        ).astype(jnp.bfloat16)
        right = jnp.where((bucket & (LANES - 1)) == low_id, 1.0, 0.0).astype(jnp.bfloat16)
        total = total + contract_cols(left, right)
    count_ref[...] = jnp.broadcast_to(running, count_ref.shape).astype(jnp.int32)
    request_ref[...] = (total[:places] * TILE + total[places:]).astype(jnp.int32) * scale


def make_requests(batch_count, capacity, scale, owners, wanted):
    total = owners.shape[0] * LANES
    places = batch_count * capacity // LANES
    return pl.pallas_call(
        functools.partial(requests_body, batch_count, capacity, scale),
        out_shape=(
            jax.ShapeDtypeStruct(owners.shape, jnp.int32),
            jax.ShapeDtypeStruct((batch_count, LANES), jnp.int32),
            jax.ShapeDtypeStruct((places, LANES), jnp.int32),
        ),
        in_specs=[VMEM, VMEM],
        out_specs=(VMEM, VMEM, VMEM),
        compiler_params=params(16),
        cost_estimate=cost(4 * total * places * LANES, 24 * total),
        name="requests",
    )(owners, wanted)


def lookup_body(stride, first, width, want_ref, store_in, out_ref, table, lines, store_ref, came):
    rows_all = store_ref.shape[0]
    halves = store_ref.shape[1] // LANES
    lane = lambda h: pl.ds(h * LANES, LANES)
    begin = pl.program_id(0) * stride + first

    @pl.when(pl.program_id(0) == 0)
    def _():
        pieces = came.shape[0]
        depth = rows_all // pieces
        copies = [
            pltpu.make_async_copy(
                store_in.at[pl.ds(n * depth, depth)], store_ref.at[pl.ds(n * depth, depth)], came.at[n]
            )
            for n in range(pieces)
        ]
        for copy in copies:
            copy.start()
        for n, copy in enumerate(copies):
            copy.wait()

            @pl.loop(n * depth // TILE, (n + 1) * depth // TILE)
            def _(j):
                part = pl.ds(pl.multiple_of(j * TILE, TILE), TILE)
                for h in range(halves):
                    spot = pl.ds(pl.multiple_of(j * TILE * halves, TILE) + h, TILE, stride=halves)
                    table[spot, :] = store_ref[part, lane(h)].astype(jnp.float32)

    @pl.loop(0, width // SLOTS, unroll=2)
    def _(j):
        at = [want_ref[begin + j * SLOTS + u] for u in range(SLOTS)]
        rows = [table[pl.ds(pl.multiple_of(a, halves), halves), :] for a in at]
        block = lines.at[pl.ds(pl.multiple_of(j * SLOTS * halves, SLOTS * halves), SLOTS * halves)]
        for u in range(SLOTS):
            block[pl.ds(u * halves, halves), :] = rows[u]

    for h in range(halves):
        out_ref[0, :, lane(h)] = lines[pl.ds(h, width, stride=halves), :].astype(jnp.bfloat16)


def lookup(store, places, groups, first, width, mib):
    rows_all, features = store.shape
    halves = features // LANES
    apart = lambda rows: pltpu.VMEM((rows * halves, LANES), jnp.float32)
    return pl.pallas_call(
        functools.partial(lookup_body, places.shape[0] // groups, first, width),
        out_shape=jax.ShapeDtypeStruct((groups, width, features), jnp.bfloat16),
        grid=(groups,),
        in_specs=[SMEM, HBM],
        out_specs=pl.BlockSpec((1, width, features), lambda g: (g, 0, 0)),
        scratch_shapes=[
            apart(rows_all),
            apart(width),
            pltpu.VMEM((rows_all, features), store.dtype),
            pltpu.SemaphoreType.DMA((4,)),
        ],
        compiler_params=params(mib),
        cost_estimate=cost(groups * width * features * 40, 2 * rows_all * features),
        name="lookup",
    )(places, store)


def adjacency_body(tiles, me_ref, near_ref, table_ref, out_ref):
    groups = near_ref.shape[0]
    node_high = lax.broadcasted_iota(jnp.int32, (LANES, TILE), 0)
    own_row = (
        lax.shift_right_logical(lax.broadcasted_iota(jnp.int32, (SLOTS, TILE), 1), SLOT_BITS)
        == lax.broadcasted_iota(jnp.int32, (SLOTS, TILE), 0)
    )
    low_id = lax.broadcasted_iota(jnp.int32, (TILE, TILE), 0).astype(jnp.float32)

    def one_group(g):
        near = near_ref[pl.ds(g, 1), :]
        pick = jnp.where((near >> LANE_BITS) == node_high, 1.0, 0.0).astype(jnp.bfloat16)
        found = jnp.dot(table_ref[...], pick, preferred_element_type=jnp.float32)
        here = (near & (LANES - 1)) == node_high
        high = jnp.sum(jnp.where(here, found[:LANES], 0.0), axis=0, keepdims=True)
        low = jnp.sum(jnp.where(here, found[LANES:], 0.0), axis=0, keepdims=True)
        high = jnp.where(near < 0, -1.0, high)
        rows = jnp.where(own_row, high, -1.0)
        left = jnp.concatenate(
            [jnp.where(rows == float(t), 1.0, 0.0) for t in range(tiles)], axis=0
        ).astype(jnp.bfloat16)
        right = jnp.where(low == low_id, 1.0, 0.0).astype(jnp.bfloat16)
        return contract_cols(left, right).reshape(tiles, SLOTS, TILE)

    @pl.loop(0, groups // 2, unroll=2)
    def _(j):
        pair = jnp.concatenate([one_group(2 * j), one_group(2 * j + 1)], axis=1)
        out_ref[:, pl.ds(pl.multiple_of(j * 2 * SLOTS, 2 * SLOTS), 2 * SLOTS), :] = pair.astype(
            out_ref.dtype
        )


def adjacency(me, near, table, tiles, parts, seeds):
    groups = near.shape[0]
    nodes = groups * SLOTS
    step = LANES // SLOTS
    own, rest, share = (n // parts // LANES for n in (seeds, nodes - seeds, nodes))

    def place(block, me_ref):
        after = block - own * parts
        is_own = after < 0
        part = jnp.where(is_own, lax.div(block, own), lax.div(after, rest))
        at = jnp.where(is_own, lax.rem(block, own), own + lax.rem(after, rest))
        return (0, lax.rem(part - me_ref[0] + parts, parts) * share + at, 0)

    return pl.pallas_call(
        functools.partial(adjacency_body, tiles),
        out_shape=jax.ShapeDtypeStruct((tiles, nodes, TILE), jnp.float8_e4m3fn),
        grid_spec=pltpu.PrefetchScalarGridSpec(
            num_scalar_prefetch=1,
            grid=(groups // step,),
            in_specs=[
                pl.BlockSpec((step, TILE), lambda r, me: (r, 0)),
                pl.BlockSpec(table.shape, lambda r, me: (0, 0)),
            ],
            out_specs=pl.BlockSpec((tiles, LANES, TILE), place),
        ),
        compiler_params=params(48),
        cost_estimate=cost(2 * nodes * TILE * TILE * tiles * 2, nodes * TILE * tiles),
        name="adjacency",
    )(me, near, table)


def collect(piece, counts_ref, starts_ref, answer_ref, landed, arrived, packed):
    batch_count = answer_ref.shape[0]

    def each_used(what):
        @pl.loop(0, batch_count)
        def _(o):
            @pl.loop(0, pl.cdiv(counts_ref[o], piece))
            def _(c):
                part = pl.ds(pl.multiple_of(c * piece, piece), piece)
                what(
                    o,
                    c,
                    part,
                    pltpu.make_async_copy(
                        answer_ref.at[o, part], landed.at[o, part], arrived.at[o, c]
                    ),
                )

    def lay(o, c, part, copy):
        copy.wait()
        packed[pl.ds(pl.multiple_of(starts_ref[o] + c * piece, SLOTS), piece), :] = landed[o, part]

    each_used(lambda o, c, part, copy: copy.start())
    each_used(lay)
    end = starts_ref[batch_count]
    packed[pl.ds(pl.multiple_of(end, SLOTS), WIDE * TILE), :] = jnp.zeros(
        (WIDE * TILE, packed.shape[1]), packed.dtype
    )


def gather_sum_body(
    piece,
    last,
    row0,
    spans_ref,
    counts_ref,
    starts_ref,
    own_here_ref,
    answer_ref,
    notes_in,
    adj_ref,
    *refs,
):
    if last:
        (total_in, found_in, wself_in, wneigh_in, own_ref, mean_ref) = refs[:6]
        share_refs = refs[6:-11]
        packed, tiles_ref, ready, landed, arrived, notes_ref, carried = refs[-11:-4]
        total_ref, found_ref, wself_ref, wneigh_ref = refs[-4:]
        mine = pl.ds(row0, total_ref.shape[0])
        pairs = ((notes_in.at[mine], notes_ref), (total_in.at[mine], total_ref))
        pairs += ((found_in.at[mine], found_ref),)
        pairs += ((wself_in, wself_ref), (wneigh_in, wneigh_ref))
    else:
        total_ref, found_ref, packed, tiles_ref, ready, landed, arrived, notes_ref, carried = refs
        pairs = ((notes_in, notes_ref),)
    carry = [pltpu.make_async_copy(*pair, carried.at[n]) for n, pair in enumerate(pairs)]
    nodes = total_ref.shape[0]
    rows = math.gcd(adj_ref.shape[1], 3 * TILE)
    begin, count = spans_ref[0], spans_ref[1]

    def fetch(step, slot):
        return pltpu.make_async_copy(
            adj_ref.at[pl.ds(begin + step * WIDE, WIDE), pl.ds(row0, nodes)],
            tiles_ref.at[slot],
            ready.at[slot],
        )

    @pl.when(count > 0)
    def _():
        fetch(0, 0).start()

    for copy in carry:
        copy.start()
    collect(piece, counts_ref, starts_ref, answer_ref, landed, arrived, packed)
    for copy in carry:
        copy.wait()
    if not last:
        total_ref[...] = jnp.zeros(total_ref.shape, jnp.float32)
        found_ref[...] = jnp.zeros(found_ref.shape, jnp.float32)

    @pl.loop(0, count)
    def _(step):
        slot = step & 1

        @pl.when(step + 1 < count)
        def _():
            fetch(step + 1, 1 - slot).start()

        fetch(step, slot).wait()
        depth = WIDE * TILE
        block = packed[pl.ds(pl.multiple_of(step * depth, depth), depth), :]
        lane = lax.broadcasted_iota(jnp.int32, (rows, depth), 1) + (begin * TILE + step * depth)
        lane = lane.astype(jnp.float32)

        @pl.loop(0, nodes // rows)
        def _(r):
            part = pl.ds(pl.multiple_of(r * rows, rows), rows)
            near = jnp.concatenate(
                [tiles_ref[slot, w, part, :].astype(jnp.bfloat16) for w in range(WIDE)], axis=1
            )
            flag = (lax.div(begin, WIDE) + step) * (adj_ref.shape[1] // rows) + row0 // rows + r

            @pl.when(own_here_ref[flag] == 0)
            def _():
                total_ref[part, :] += jnp.dot(near, block, preferred_element_type=jnp.float32)

            @pl.when(own_here_ref[flag] != 0)
            def _():
                own = jnp.where(notes_ref[part, 0:1] == lane, 1.0, 0.0).astype(jnp.bfloat16)
                both = jnp.dot(
                    jnp.concatenate([near, own], axis=0), block, preferred_element_type=jnp.float32
                )
                total_ref[part, :] += both[:rows]
                found_ref[part, :] += both[rows:]

    if last:
        share = share_refs[0].shape[0]
        step_rows = math.gcd(share, 3 * TILE)
        for p, share_ref in enumerate(share_refs):
            for r in range(share // step_rows):
                part = pl.ds(p * share + r * step_rows, step_rows)
                own = found_ref[part, :].astype(jnp.bfloat16)
                mean = (total_ref[part, :] / notes_ref[part, 1:2]).astype(jnp.bfloat16)
                own_ref[part, :] = own
                mean_ref[part, :] = mean
                share_ref[pl.ds(r * step_rows, step_rows), :] = (
                    jnp.dot(own, wself_ref[...], preferred_element_type=jnp.float32)
                    + jnp.dot(mean, wneigh_ref[...], preferred_element_type=jnp.float32)
                ).astype(share_ref.dtype)


def gather_sum(inputs, scalars, answer, notes, adj, rest=None, row0=0, shares=()):
    batch_count, width, features = answer.shape
    tiles, nodes, _ = adj.shape
    nodes = sum(shares) or nodes
    piece = LANES if width % LANES == 0 else SLOTS
    last = rest is not None
    room = min(batch_count * width, inputs) + SLOTS * batch_count + 2 * WIDE * TILE
    in_specs = [SMEM, SMEM, SMEM, SMEM, ANY, HBM, HBM]
    rows = lambda dtype: jax.ShapeDtypeStruct((nodes, features), dtype)
    scratch = [
        pltpu.VMEM((room, features), jnp.bfloat16),
        pltpu.VMEM((2, WIDE, nodes, TILE), adj.dtype),
        pltpu.SemaphoreType.DMA((2,)),
        pltpu.VMEM(answer.shape, answer.dtype),
        pltpu.SemaphoreType.DMA((batch_count, width // piece)),
        pltpu.VMEM((nodes, notes.shape[1]), notes.dtype),
        pltpu.SemaphoreType.DMA((5,)),
    ]
    operands = [answer, notes, adj]
    if last:
        operands += list(rest)
        in_specs += [HBM] * len(rest)
        out_shape = (rows(jnp.bfloat16), rows(jnp.bfloat16))
        out_shape += tuple(
            jax.ShapeDtypeStruct((n, rest[3].shape[1]), jnp.bfloat16) for n in shares
        )
        scratch += [pltpu.VMEM((nodes, features), jnp.float32)] * 2
        scratch += [pltpu.VMEM(x.shape, x.dtype) for x in rest[2:]]
    else:
        out_shape = (rows(jnp.float32), rows(jnp.float32))
    return pl.pallas_call(
        functools.partial(gather_sum_body, piece, last, row0),
        out_shape=out_shape,
        in_specs=in_specs,
        out_specs=(VMEM,) * len(out_shape),
        scratch_shapes=scratch,
        compiler_params=params(50),
        cost_estimate=cost(2 * nodes * features * TILE * tiles // (4 if last else 1), nodes * TILE),
        name="gather_sum",
    )(*scalars, *operands)


def share_order(array, parts, seeds):
    others = array.shape[0] - seeds
    own, rest = seeds // parts, others // parts
    tail = array.shape[1:]
    blocks = jnp.concatenate(
        [array[:seeds].reshape(parts, own, *tail), array[seeds:].reshape(parts, rest, *tail)],
        axis=1,
    )
    return ahead(blocks).reshape(array.shape)


def spread(part, axis, count):
    return lax.all_to_all(
        jnp.broadcast_to(part[None], (count,) + part.shape), axis, 0, 0, tiled=True
    )


def passed(part, shift, axis="feat"):
    parts = lax.axis_size(axis)
    return lax.ppermute(part, axis, [((i + shift) % parts, i) for i in range(parts)])


def turned(array, by):
    twice = jnp.concatenate([array, array], axis=0)
    return lax.dynamic_slice_in_dim(twice, by, array.shape[0], 0)


def ahead(array, axis="feat"):
    return turned(array, lax.axis_index(axis))


def spread_parts(part, axis="feat"):
    return [part] + [passed(part, j, axis) for j in range(1, lax.axis_size(axis))]


def sum_parts(blocks, axis="feat"):
    parts = lax.axis_size(axis)
    came = [blocks[0]] + [passed(blocks[j], -j, axis) for j in range(1, parts)]
    return sum(x.astype(jnp.float32) for x in came)


def swapped(part):
    return lax.ppermute(part, "batch", [(i, i ^ 1) for i in range(lax.axis_size("batch"))])


def total_over_batch(terms):
    count = lax.axis_size("batch")
    rows, width = terms.shape
    if count > FEW:
        pieces = terms.astype(jnp.bfloat16).reshape(count, rows // count, width)
        pieces = lax.all_to_all(pieces, "batch", 0, 0, tiled=True)
        total = jnp.sum(pieces.astype(jnp.float32), axis=0).astype(jnp.bfloat16)
        return spread(total, "batch", count).reshape(rows, width)
    chips = count // 2
    index = lax.axis_index("batch")
    first, chip = index % 2 == 0, index // 2
    upper, lower = terms[: rows // 2], terms[rows // 2 :]
    came = swapped(jnp.where(first, lower, upper).astype(jnp.bfloat16))
    mine = jnp.where(first, upper, lower) + came.astype(jnp.float32)
    pieces = turned(mine.reshape(chips, rows // count, width), chip)
    total = pieces[0]
    for j in range(1, chips):
        total = total + passed(pieces[j].astype(jnp.bfloat16), -2 * j, "batch").astype(jnp.float32)
    total = total.astype(jnp.bfloat16)
    mine = jnp.stack([total] + [passed(total, 2 * j, "batch") for j in range(1, chips)])
    other = swapped(mine)
    both = jnp.stack([jnp.where(first, mine, other), jnp.where(first, other, mine)], axis=1)
    return turned(both, (chips - chip) % chips).transpose(1, 0, 2, 3).reshape(rows, width)


def local(
    store,
    input_owner,
    input_row,
    nbr_one,
    deg_one,
    nbr_two,
    deg_two,
    cotangent,
    w1_self,
    w1_neigh,
    bias_one,
    w2_self,
    w2_neigh,
    bias_two,
):
    batch_count = lax.axis_size("batch")
    parts = lax.axis_size("feat")
    feat_index = lax.axis_index("feat")
    input_count = input_owner.shape[1]
    capacity = 2 * input_count // batch_count
    nodes = nbr_one.shape[1]
    seed_rows = nbr_two.shape[1]
    seeds = seed_rows * parts
    share = nodes // parts
    hidden_width = w1_self.shape[1]

    owners = input_owner.reshape(input_count // LANES, LANES)
    wanted = input_row.reshape(input_count // LANES, LANES)
    slots, counts, requests = make_requests(
        batch_count, capacity, store.shape[1] // LANES, owners, wanted
    )
    owners = owners.reshape(1, input_count)
    received = lax.all_to_all(
        requests.reshape(batch_count, capacity), "batch", split_axis=0, concat_axis=0, tiled=True
    )
    first = capacity // 2
    places = received.reshape(batch_count * capacity)
    looked_a = lookup(store, places, batch_count, 0, first, 60)
    near_first, looked_a = lax.optimization_barrier((nbr_one[0], looked_a))
    answer_a = lax.all_to_all(looked_a, "batch", split_axis=0, concat_axis=0, tiled=True)
    looked = lookup(store, places, batch_count, first, capacity - first, 24)

    depth = WIDE * TILE
    steps = -(-(input_count + 2 * (SLOTS - 1) * batch_count + depth - 1) // depth)
    tally = counts[:, 0]
    tally_a = jnp.minimum(tally, first)
    tally_b = tally - tally_a
    padded = lambda n: (n + SLOTS - 1) // SLOTS * SLOTS
    ends = lambda n: jnp.concatenate([jnp.zeros((1,), jnp.int32), jnp.cumsum(padded(n))])
    starts_a, starts_b = ends(tally_a), ends(tally_b)
    steps_a = (starts_a[batch_count] + depth - 1) // depth
    steps_b = (starts_b[batch_count] + depth - 1) // depth
    spans_a = jnp.stack([jnp.zeros_like(steps_a), steps_a])
    spans_b = jnp.stack([steps_a * WIDE, steps_b])
    slot = slots.reshape(1, input_count)
    shifted = jnp.where(
        slot < first,
        slot + starts_a[:batch_count, None],
        slot - first + steps_a * depth + starts_b[:batch_count, None],
    )
    mine = owners == jnp.arange(batch_count)[:, None]
    column = jnp.sum(jnp.where(mine, shifted, 0), axis=0)
    grid = jnp.pad(column.reshape(-1, LANES), ((0, LANES - input_count // LANES), (0, 0))).T
    finder = jnp.concatenate([grid // TILE, grid % TILE], axis=0).astype(jnp.bfloat16)
    notes = jnp.stack([column[:nodes], deg_one[0]], axis=1).astype(jnp.float32)
    notes = share_order(notes, parts, seeds)
    block = math.gcd(nodes, 3 * TILE)
    met = notes[:, 0].reshape(1, nodes // block, block) // depth
    met = met.astype(jnp.int32) == jnp.arange(steps)[:, None, None]
    own_here = jnp.any(met, axis=2).astype(jnp.int32).reshape(-1)

    fanout_two = nbr_two.shape[2]
    used_two = jnp.arange(fanout_two)[:, None] < deg_two
    lists = jnp.concatenate([jnp.where(used_two, nbr_two[0].T, -1), deg_two], axis=0)
    lists = jnp.stack(spread_parts(lists))

    fanout = nbr_one.shape[2]
    used = jnp.arange(fanout)[None, :] < deg_one[0][:, None]
    near = jnp.pad(jnp.where(used, near_first, -1), ((0, 0), (0, SLOTS - fanout)), constant_values=-1)
    near, lists = lax.optimization_barrier((near, lists))
    me = feat_index.astype(jnp.int32).reshape(1)
    near = near.reshape(nodes // SLOTS, TILE)
    adj = adjacency(me, near, finder, steps * WIDE, parts, seeds)
    looked, answer_a, adj = lax.optimization_barrier((looked, answer_a, adj))
    answer_b = lax.all_to_all(looked, "batch", split_axis=0, concat_axis=0, tiled=True)

    near_two = lists[:, :fanout_two].transpose(1, 0, 2).reshape(fanout_two, seeds)
    deg_all = lists[:, fanout_two].reshape(seeds)
    rest = share - seed_rows
    after = near_two - seeds
    place = jnp.where(
        near_two < seeds,
        near_two // seed_rows * share + near_two % seed_rows,
        after // rest * share + seed_rows + after % rest,
    )
    place = jnp.where(near_two < 0, -1, place - feat_index * share)
    adj_two = jnp.sum(
        place[:, :, None] == jnp.arange(share)[None, None, :], axis=0, dtype=jnp.float32
    ).astype(jnp.bfloat16)

    scalars = (spans_a, tally_a, starts_a, own_here)
    total, found = gather_sum(input_count, scalars, answer_a, notes, adj)

    def finish(begin, end):
        return gather_sum(
            input_count,
            (spans_b, tally_b, starts_b, own_here),
            answer_b,
            notes,
            adj,
            (total, found, w1_self, w1_neigh),
            begin * share,
            (share,) * (end - begin),
        )

    half = parts // 2
    cuts = [(half, parts), (1, half), (0, 1)]
    own_rows, mean_rows, z_blocks = [], [], []
    for begin, end in cuts:
        own, mean, *blocks = finish(begin, end)
        total, blocks = lax.optimization_barrier((total, blocks))
        own_rows.append(own)
        mean_rows.append(mean)
        z_blocks = blocks + z_blocks
    z_share = sum_parts(z_blocks) + bias_one
    hidden = jax.nn.silu(z_share).astype(jnp.bfloat16)

    agg_parts = jnp.dot(adj_two, hidden, preferred_element_type=jnp.float32)
    agg_total = sum_parts(agg_parts.reshape(parts, seed_rows, hidden_width))
    deg_second = deg_two[0].astype(jnp.float32)[:, None]
    agg_two = (agg_total / deg_second).astype(jnp.bfloat16)
    self_two = hidden[:seed_rows]
    z_two = (
        jnp.dot(self_two, w2_self, preferred_element_type=jnp.float32)
        + jnp.dot(agg_two, w2_neigh, preferred_element_type=jnp.float32)
        + bias_two
    )
    activations = jax.nn.silu(z_two).astype(jnp.bfloat16)[None]
    dz_two = (cotangent[0].astype(jnp.float32) * silu_grad(z_two)).astype(jnp.bfloat16)
    group = jnp.stack(spread_parts(jnp.stack([self_two, agg_two, dz_two])))
    dz_two_all = group[:, 2].reshape(seeds, hidden_width)

    back = contract_cols(dz_two_all, w2_neigh) / deg_all.astype(jnp.float32)[:, None]
    back_high = back.astype(jnp.bfloat16)
    back_low = (back - back_high.astype(jnp.float32)).astype(jnp.bfloat16)
    dh_share = contract_rows(adj_two, back_high) + contract_rows(adj_two, back_low)
    dh_share = dh_share + jnp.pad(contract_cols(dz_two, w2_self), ((0, rest), (0, 0)))
    dz_share = (dh_share * silu_grad(z_share)).astype(jnp.bfloat16)
    dz_blocks = spread_parts(dz_share)
    dz_rows = [jnp.concatenate(dz_blocks[begin:end]) for begin, end in cuts]
    group = turned(group, (parts - feat_index) % parts).transpose(1, 0, 2, 3)
    self_all, agg_all, dz_all = (x.reshape(seeds, hidden_width) for x in group)
    grads = [contract_rows(self_all, dz_all), contract_rows(agg_all, dz_all)]
    for rows in (own_rows, mean_rows):
        grads.append(sum(contract_rows(x, y) for x, y in zip(rows, dz_rows)))
    total = total_over_batch(jnp.concatenate(grads)).astype(jnp.float32)
    return (activations, *total.reshape(len(grads), -1, hidden_width))


def solution(mesh):
    in_specs = (
        P("batch", "feat"),
        P("batch", None, None),
        P("batch", None),
        P("batch", None, None),
        P("batch", None),
        P("batch", "feat", None),
        P("batch", "feat"),
        P("batch", "feat", None),
        P("feat", None),
        P("feat", None),
        P(),
        P(),
        P(),
        P(),
    )
    out_specs = (P("batch", "feat", None), P(), P(), P("feat", None), P("feat", None))
    return jax.shard_map(local, mesh=mesh, in_specs=in_specs, out_specs=out_specs, check_vma=False)
```

```python
import functools
import math

import jax
import jax.numpy as jnp
from jax import lax
from jax.experimental import pallas as pl
from jax.experimental.pallas import tpu as pltpu
from jax.sharding import PartitionSpec as P

TILE = 256
LANES = 128
SLOTS = 16
WIDE = 2
FEW = 16
TILE_BITS, LANE_BITS, SLOT_BITS = 8, 7, 4
MIB = 1024 * 1024
VMEM = pl.BlockSpec(memory_space=pltpu.VMEM)
SMEM = pl.BlockSpec(memory_space=pltpu.SMEM)
ANY = pl.BlockSpec(memory_space=pl.ANY)
HBM = pl.BlockSpec(memory_space=pltpu.HBM)


def silu_grad(values):
    sig = jax.nn.sigmoid(values)
    return sig * (1.0 + values * (1.0 - sig))


def contract_rows(left_side, right_side):
    return lax.dot_general(
        left_side, right_side, (((0,), (0,)), ((), ())), preferred_element_type=jnp.float32
    )


def contract_cols(left_side, right_side):
    return lax.dot_general(
        left_side, right_side, (((1,), (1,)), ((), ())), preferred_element_type=jnp.float32
    )


def params(mib):
    return pltpu.CompilerParams(vmem_limit_bytes=mib * MIB)


def cost(flops, moved):
    return pl.CostEstimate(flops=int(flops), bytes_accessed=int(moved), transcendentals=0)


def requests_body(batch_count, capacity, scale, owner_ref, row_ref, slot_ref, count_ref, request_ref):
    blocks, width = owner_ref.shape[0] // 2, TILE
    places = request_ref.shape[0]
    line = lambda ref, b: jnp.concatenate([ref[2 * b : 2 * b + 1], ref[2 * b + 1 : 2 * b + 2]], axis=1)
    owner_id = lax.broadcasted_iota(jnp.int32, (batch_count, width), 0)
    earlier = lax.broadcasted_iota(jnp.int32, (width, width), 0)
    later = lax.broadcasted_iota(jnp.int32, (width, width), 1)
    upper = jnp.where(earlier <= later, 1.0, 0.0).astype(jnp.bfloat16)
    high_id = lax.broadcasted_iota(jnp.int32, (places, width), 0)
    low_id = lax.broadcasted_iota(jnp.int32, (LANES, width), 0)
    marks = [
        jnp.where(line(owner_ref, b) == owner_id, 1.0, 0.0) for b in range(blocks)
    ]
    stacked = jnp.concatenate(marks, axis=0).astype(jnp.bfloat16)
    prefix = jnp.dot(stacked, upper, preferred_element_type=jnp.float32)
    running = jnp.zeros((batch_count, 1), jnp.float32)
    total = jnp.zeros((2 * places, LANES), jnp.float32)
    for b in range(blocks):
        part = prefix[b * batch_count : (b + 1) * batch_count]
        slots = jnp.sum(marks[b] * (part + running - 1.0), axis=0, keepdims=True)
        slots = slots.astype(jnp.int32)
        slot_ref[2 * b : 2 * b + 1, :] = slots[:, :LANES]
        slot_ref[2 * b + 1 : 2 * b + 2, :] = slots[:, LANES:]
        running = running + part[:, width - 1 : width]
        bucket = line(owner_ref, b) * capacity + slots
        rows = line(row_ref, b)
        hit = (bucket >> LANE_BITS) == high_id
        left = jnp.concatenate(
            [
                jnp.where(hit, (rows >> TILE_BITS).astype(jnp.float32), 0.0),
                jnp.where(hit, (rows & (TILE - 1)).astype(jnp.float32), 0.0),
            ],
            axis=0,
        ).astype(jnp.bfloat16)
        right = jnp.where((bucket & (LANES - 1)) == low_id, 1.0, 0.0).astype(jnp.bfloat16)
        total = total + contract_cols(left, right)
    count_ref[...] = jnp.broadcast_to(running, count_ref.shape).astype(jnp.int32)
    request_ref[...] = (total[:places] * TILE + total[places:]).astype(jnp.int32) * scale


def make_requests(batch_count, capacity, scale, owners, wanted):
    total = owners.shape[0] * LANES
    places = batch_count * capacity // LANES
    return pl.pallas_call(
        functools.partial(requests_body, batch_count, capacity, scale),
        out_shape=(
            jax.ShapeDtypeStruct(owners.shape, jnp.int32),
            jax.ShapeDtypeStruct((batch_count, LANES), jnp.int32),
            jax.ShapeDtypeStruct((places, LANES), jnp.int32),
        ),
        in_specs=[VMEM, VMEM],
        out_specs=(VMEM, VMEM, VMEM),
        compiler_params=params(16),
        cost_estimate=cost(4 * total * places * LANES, 24 * total),
        name="requests",
    )(owners, wanted)


def lookup_body(stride, first, width, want_ref, store_in, out_ref, table, lines, store_ref, came):
    rows_all = store_ref.shape[0]
    halves = store_ref.shape[1] // LANES
    lane = lambda h: pl.ds(h * LANES, LANES)
    begin = pl.program_id(0) * stride + first

    @pl.when(pl.program_id(0) == 0)
    def _():
        pieces = came.shape[0]
        depth = rows_all // pieces
        copies = [
            pltpu.make_async_copy(
                store_in.at[pl.ds(n * depth, depth)], store_ref.at[pl.ds(n * depth, depth)], came.at[n]
            )
            for n in range(pieces)
        ]
        for copy in copies:
            copy.start()
        for n, copy in enumerate(copies):
            copy.wait()

            @pl.loop(n * depth // TILE, (n + 1) * depth // TILE)
            def _(j):
                part = pl.ds(pl.multiple_of(j * TILE, TILE), TILE)
                for h in range(halves):
                    spot = pl.ds(pl.multiple_of(j * TILE * halves, TILE) + h, TILE, stride=halves)
                    table[spot, :] = store_ref[part, lane(h)].astype(jnp.float32)

    @pl.loop(0, width // SLOTS, unroll=2)
    def _(j):
        at = [want_ref[begin + j * SLOTS + u] for u in range(SLOTS)]
        rows = [table[pl.ds(pl.multiple_of(a, halves), halves), :] for a in at]
        block = lines.at[pl.ds(pl.multiple_of(j * SLOTS * halves, SLOTS * halves), SLOTS * halves)]
        for u in range(SLOTS):
            block[pl.ds(u * halves, halves), :] = rows[u]

    for h in range(halves):
        out_ref[0, :, lane(h)] = lines[pl.ds(h, width, stride=halves), :].astype(jnp.bfloat16)


def lookup(store, places, groups, first, width, mib):
    rows_all, features = store.shape
    halves = features // LANES
    apart = lambda rows: pltpu.VMEM((rows * halves, LANES), jnp.float32)
    return pl.pallas_call(
        functools.partial(lookup_body, places.shape[0] // groups, first, width),
        out_shape=jax.ShapeDtypeStruct((groups, width, features), jnp.bfloat16),
        grid=(groups,),
        in_specs=[SMEM, HBM],
        out_specs=pl.BlockSpec((1, width, features), lambda g: (g, 0, 0)),
        scratch_shapes=[
            apart(rows_all),
            apart(width),
            pltpu.VMEM((rows_all, features), store.dtype),
            pltpu.SemaphoreType.DMA((4,)),
        ],
        compiler_params=params(mib),
        cost_estimate=cost(groups * width * features * 40, 2 * rows_all * features),
        name="lookup",
    )(places, store)


def adjacency_body(tiles, me_ref, near_ref, table_ref, out_ref):
    groups = near_ref.shape[0]
    node_high = lax.broadcasted_iota(jnp.int32, (LANES, TILE), 0)
    own_row = (
        lax.shift_right_logical(lax.broadcasted_iota(jnp.int32, (SLOTS, TILE), 1), SLOT_BITS)
        == lax.broadcasted_iota(jnp.int32, (SLOTS, TILE), 0)
    )
    low_id = lax.broadcasted_iota(jnp.int32, (TILE, TILE), 0).astype(jnp.float32)

    def one_group(g):
        near = near_ref[pl.ds(g, 1), :]
        pick = jnp.where((near >> LANE_BITS) == node_high, 1.0, 0.0).astype(jnp.bfloat16)
        found = jnp.dot(table_ref[...], pick, preferred_element_type=jnp.float32)
        here = (near & (LANES - 1)) == node_high
        high = jnp.sum(jnp.where(here, found[:LANES], 0.0), axis=0, keepdims=True)
        low = jnp.sum(jnp.where(here, found[LANES:], 0.0), axis=0, keepdims=True)
        high = jnp.where(near < 0, -1.0, high)
        rows = jnp.where(own_row, high, -1.0)
        left = jnp.concatenate(
            [jnp.where(rows == float(t), 1.0, 0.0) for t in range(tiles)], axis=0
        ).astype(jnp.bfloat16)
        right = jnp.where(low == low_id, 1.0, 0.0).astype(jnp.bfloat16)
        return contract_cols(left, right).reshape(tiles, SLOTS, TILE)

    @pl.loop(0, groups // 2, unroll=2)
    def _(j):
        pair = jnp.concatenate([one_group(2 * j), one_group(2 * j + 1)], axis=1)
        out_ref[:, pl.ds(pl.multiple_of(j * 2 * SLOTS, 2 * SLOTS), 2 * SLOTS), :] = pair.astype(
            out_ref.dtype
        )


def adjacency(me, near, table, tiles, parts, seeds):
    groups = near.shape[0]
    nodes = groups * SLOTS
    step = LANES // SLOTS
    own, rest, share = (n // parts // LANES for n in (seeds, nodes - seeds, nodes))

    def place(block, me_ref):
        after = block - own * parts
        is_own = after < 0
        part = jnp.where(is_own, lax.div(block, own), lax.div(after, rest))
        at = jnp.where(is_own, lax.rem(block, own), own + lax.rem(after, rest))
        return (0, lax.rem(part - me_ref[0] + parts, parts) * share + at, 0)

    return pl.pallas_call(
        functools.partial(adjacency_body, tiles),
        out_shape=jax.ShapeDtypeStruct((tiles, nodes, TILE), jnp.float8_e4m3fn),
        grid_spec=pltpu.PrefetchScalarGridSpec(
            num_scalar_prefetch=1,
            grid=(groups // step,),
            in_specs=[
                pl.BlockSpec((step, TILE), lambda r, me: (r, 0)),
                pl.BlockSpec(table.shape, lambda r, me: (0, 0)),
            ],
            out_specs=pl.BlockSpec((tiles, LANES, TILE), place),
        ),
        compiler_params=params(48),
        cost_estimate=cost(2 * nodes * TILE * TILE * tiles * 2, nodes * TILE * tiles),
        name="adjacency",
    )(me, near, table)


def collect(piece, counts_ref, starts_ref, answer_ref, landed, arrived, packed):
    batch_count = answer_ref.shape[0]

    def each_used(what):
        @pl.loop(0, batch_count)
        def _(o):
            @pl.loop(0, pl.cdiv(counts_ref[o], piece))
            def _(c):
                part = pl.ds(pl.multiple_of(c * piece, piece), piece)
                what(
                    o,
                    c,
                    part,
                    pltpu.make_async_copy(
                        answer_ref.at[o, part], landed.at[o, part], arrived.at[o, c]
                    ),
                )

    def lay(o, c, part, copy):
        copy.wait()
        packed[pl.ds(pl.multiple_of(starts_ref[o] + c * piece, SLOTS), piece), :] = landed[o, part]

    each_used(lambda o, c, part, copy: copy.start())
    each_used(lay)
    end = starts_ref[batch_count]
    packed[pl.ds(pl.multiple_of(end, SLOTS), WIDE * TILE), :] = jnp.zeros(
        (WIDE * TILE, packed.shape[1]), packed.dtype
    )


def gather_sum_body(
    piece,
    last,
    row0,
    spans_ref,
    counts_ref,
    starts_ref,
    own_here_ref,
    answer_ref,
    notes_in,
    adj_ref,
    *refs,
):
    if last:
        (total_in, found_in, wself_in, wneigh_in, own_ref, mean_ref) = refs[:6]
        share_refs = refs[6:-11]
        packed, tiles_ref, ready, landed, arrived, notes_ref, carried = refs[-11:-4]
        total_ref, found_ref, wself_ref, wneigh_ref = refs[-4:]
        mine = pl.ds(row0, total_ref.shape[0])
        pairs = ((notes_in.at[mine], notes_ref), (total_in.at[mine], total_ref))
        pairs += ((found_in.at[mine], found_ref),)
        pairs += ((wself_in, wself_ref), (wneigh_in, wneigh_ref))
    else:
        total_ref, found_ref, packed, tiles_ref, ready, landed, arrived, notes_ref, carried = refs
        pairs = ((notes_in, notes_ref),)
    carry = [pltpu.make_async_copy(*pair, carried.at[n]) for n, pair in enumerate(pairs)]
    nodes = total_ref.shape[0]
    rows = math.gcd(adj_ref.shape[1], 3 * TILE)
    begin, count = spans_ref[0], spans_ref[1]

    def fetch(step, slot):
        return pltpu.make_async_copy(
            adj_ref.at[pl.ds(begin + step * WIDE, WIDE), pl.ds(row0, nodes)],
            tiles_ref.at[slot],
            ready.at[slot],
        )

    @pl.when(count > 0)
    def _():
        fetch(0, 0).start()

    for copy in carry:
        copy.start()
    collect(piece, counts_ref, starts_ref, answer_ref, landed, arrived, packed)
    for copy in carry:
        copy.wait()
    if not last:
        total_ref[...] = jnp.zeros(total_ref.shape, jnp.float32)
        found_ref[...] = jnp.zeros(found_ref.shape, jnp.float32)

    @pl.loop(0, count)
    def _(step):
        slot = step & 1

        @pl.when(step + 1 < count)
        def _():
            fetch(step + 1, 1 - slot).start()

        fetch(step, slot).wait()
        depth = WIDE * TILE
        block = packed[pl.ds(pl.multiple_of(step * depth, depth), depth), :]
        lane = lax.broadcasted_iota(jnp.int32, (rows, depth), 1) + (begin * TILE + step * depth)
        lane = lane.astype(jnp.float32)

        @pl.loop(0, nodes // rows)
        def _(r):
            part = pl.ds(pl.multiple_of(r * rows, rows), rows)
            near = jnp.concatenate(
                [tiles_ref[slot, w, part, :].astype(jnp.bfloat16) for w in range(WIDE)], axis=1
            )
            flag = (lax.div(begin, WIDE) + step) * (adj_ref.shape[1] // rows) + row0 // rows + r

            @pl.when(own_here_ref[flag] == 0)
            def _():
                total_ref[part, :] += jnp.dot(near, block, preferred_element_type=jnp.float32)

            @pl.when(own_here_ref[flag] != 0)
            def _():
                own = jnp.where(notes_ref[part, 0:1] == lane, 1.0, 0.0).astype(jnp.bfloat16)
                both = jnp.dot(
                    jnp.concatenate([near, own], axis=0), block, preferred_element_type=jnp.float32
                )
                total_ref[part, :] += both[:rows]
                found_ref[part, :] += both[rows:]

    if last:
        share = share_refs[0].shape[0]
        step_rows = math.gcd(share, 3 * TILE)
        for p, share_ref in enumerate(share_refs):
            for r in range(share // step_rows):
                part = pl.ds(p * share + r * step_rows, step_rows)
                own = found_ref[part, :].astype(jnp.bfloat16)
                mean = (total_ref[part, :] / notes_ref[part, 1:2]).astype(jnp.bfloat16)
                own_ref[part, :] = own
                mean_ref[part, :] = mean
                share_ref[pl.ds(r * step_rows, step_rows), :] = (
                    jnp.dot(own, wself_ref[...], preferred_element_type=jnp.float32)
                    + jnp.dot(mean, wneigh_ref[...], preferred_element_type=jnp.float32)
                ).astype(share_ref.dtype)


def gather_sum(inputs, scalars, answer, notes, adj, rest=None, row0=0, shares=()):
    batch_count, width, features = answer.shape
    tiles, nodes, _ = adj.shape
    nodes = sum(shares) or nodes
    piece = LANES if width % LANES == 0 else SLOTS
    last = rest is not None
    room = min(batch_count * width, inputs) + SLOTS * batch_count + 2 * WIDE * TILE
    in_specs = [SMEM, SMEM, SMEM, SMEM, ANY, HBM, HBM]
    rows = lambda dtype: jax.ShapeDtypeStruct((nodes, features), dtype)
    scratch = [
        pltpu.VMEM((room, features), jnp.bfloat16),
        pltpu.VMEM((2, WIDE, nodes, TILE), adj.dtype),
        pltpu.SemaphoreType.DMA((2,)),
        pltpu.VMEM(answer.shape, answer.dtype),
        pltpu.SemaphoreType.DMA((batch_count, width // piece)),
        pltpu.VMEM((nodes, notes.shape[1]), notes.dtype),
        pltpu.SemaphoreType.DMA((5,)),
    ]
    operands = [answer, notes, adj]
    if last:
        operands += list(rest)
        in_specs += [HBM] * len(rest)
        out_shape = (rows(jnp.bfloat16), rows(jnp.bfloat16))
        out_shape += tuple(
            jax.ShapeDtypeStruct((n, rest[3].shape[1]), jnp.bfloat16) for n in shares
        )
        scratch += [pltpu.VMEM((nodes, features), jnp.float32)] * 2
        scratch += [pltpu.VMEM(x.shape, x.dtype) for x in rest[2:]]
    else:
        out_shape = (rows(jnp.float32), rows(jnp.float32))
    return pl.pallas_call(
        functools.partial(gather_sum_body, piece, last, row0),
        out_shape=out_shape,
        in_specs=in_specs,
        out_specs=(VMEM,) * len(out_shape),
        scratch_shapes=scratch,
        compiler_params=params(50),
        cost_estimate=cost(2 * nodes * features * TILE * tiles // (4 if last else 1), nodes * TILE),
        name="gather_sum",
    )(*scalars, *operands)


def share_order(array, parts, seeds):
    others = array.shape[0] - seeds
    own, rest = seeds // parts, others // parts
    tail = array.shape[1:]
    blocks = jnp.concatenate(
        [array[:seeds].reshape(parts, own, *tail), array[seeds:].reshape(parts, rest, *tail)],
        axis=1,
    )
    return ahead(blocks).reshape(array.shape)


def spread(part, axis, count):
    return lax.all_to_all(
        jnp.broadcast_to(part[None], (count,) + part.shape), axis, 0, 0, tiled=True
    )


def passed(part, shift, axis="feat"):
    parts = lax.axis_size(axis)
    return lax.ppermute(part, axis, [((i + shift) % parts, i) for i in range(parts)])


def turned(array, by):
    twice = jnp.concatenate([array, array], axis=0)
    return lax.dynamic_slice_in_dim(twice, by, array.shape[0], 0)


def ahead(array, axis="feat"):
    return turned(array, lax.axis_index(axis))


def in_order(blocks):
    parts = lax.axis_size("feat")
    total = jnp.zeros((parts,) + blocks[0].shape, blocks[0].dtype)
    for j, block in enumerate(blocks):
        spot = (lax.axis_index("feat") + j) % parts
        total = lax.dynamic_update_index_in_dim(total, block, spot, 0)
    return total


def spread_parts(part, axis="feat"):
    return [part] + [passed(part, j, axis) for j in range(1, lax.axis_size(axis))]


def sum_parts(blocks, axis="feat"):
    parts = lax.axis_size(axis)
    came = [blocks[0]] + [passed(blocks[j], -j, axis) for j in range(1, parts)]
    return sum(x.astype(jnp.float32) for x in came)


def swapped(part):
    return lax.ppermute(part, "batch", [(i, i ^ 1) for i in range(lax.axis_size("batch"))])


def total_over_batch(terms):
    count = lax.axis_size("batch")
    rows, width = terms.shape
    if count > FEW:
        pieces = terms.astype(jnp.bfloat16).reshape(count, rows // count, width)
        pieces = lax.all_to_all(pieces, "batch", 0, 0, tiled=True)
        total = jnp.sum(pieces.astype(jnp.float32), axis=0).astype(jnp.bfloat16)
        return spread(total, "batch", count).reshape(rows, width)
    chips = count // 2
    index = lax.axis_index("batch")
    first, chip = index % 2 == 0, index // 2
    upper, lower = terms[: rows // 2], terms[rows // 2 :]
    came = swapped(jnp.where(first, lower, upper).astype(jnp.bfloat16))
    mine = jnp.where(first, upper, lower) + came.astype(jnp.float32)
    pieces = turned(mine.reshape(chips, rows // count, width), chip)
    total = pieces[0]
    for j in range(1, chips):
        total = total + passed(pieces[j].astype(jnp.bfloat16), -2 * j, "batch").astype(jnp.float32)
    total = total.astype(jnp.bfloat16)
    mine = jnp.stack([total] + [passed(total, 2 * j, "batch") for j in range(1, chips)])
    other = swapped(mine)
    both = jnp.stack([jnp.where(first, mine, other), jnp.where(first, other, mine)], axis=1)
    return turned(both, (chips - chip) % chips).transpose(1, 0, 2, 3).reshape(rows, width)


def local(
    store,
    input_owner,
    input_row,
    nbr_one,
    deg_one,
    nbr_two,
    deg_two,
    cotangent,
    w1_self,
    w1_neigh,
    bias_one,
    w2_self,
    w2_neigh,
    bias_two,
):
    batch_count = lax.axis_size("batch")
    parts = lax.axis_size("feat")
    feat_index = lax.axis_index("feat")
    input_count = input_owner.shape[1]
    capacity = 2 * input_count // batch_count
    nodes = nbr_one.shape[1]
    seed_rows = nbr_two.shape[1]
    seeds = seed_rows * parts
    share = nodes // parts
    hidden_width = w1_self.shape[1]

    owners = input_owner.reshape(input_count // LANES, LANES)
    wanted = input_row.reshape(input_count // LANES, LANES)
    slots, counts, requests = make_requests(
        batch_count, capacity, store.shape[1] // LANES, owners, wanted
    )
    owners = owners.reshape(1, input_count)
    received = lax.all_to_all(
        requests.reshape(batch_count, capacity), "batch", split_axis=0, concat_axis=0, tiled=True
    )
    first = capacity // 2
    places = received.reshape(batch_count * capacity)
    looked_a = lookup(store, places, batch_count, 0, first, 60)
    near_first, looked_a = lax.optimization_barrier((nbr_one[0], looked_a))
    answer_a = lax.all_to_all(looked_a, "batch", split_axis=0, concat_axis=0, tiled=True)
    looked = lookup(store, places, batch_count, first, capacity - first, 24)

    depth = WIDE * TILE
    steps = -(-(input_count + 2 * (SLOTS - 1) * batch_count + depth - 1) // depth)
    tally = counts[:, 0]
    tally_a = jnp.minimum(tally, first)
    tally_b = tally - tally_a
    padded = lambda n: (n + SLOTS - 1) // SLOTS * SLOTS
    ends = lambda n: jnp.concatenate([jnp.zeros((1,), jnp.int32), jnp.cumsum(padded(n))])
    starts_a, starts_b = ends(tally_a), ends(tally_b)
    steps_a = (starts_a[batch_count] + depth - 1) // depth
    steps_b = (starts_b[batch_count] + depth - 1) // depth
    spans_a = jnp.stack([jnp.zeros_like(steps_a), steps_a])
    spans_b = jnp.stack([steps_a * WIDE, steps_b])
    slot = slots.reshape(1, input_count)
    shifted = jnp.where(
        slot < first,
        slot + starts_a[:batch_count, None],
        slot - first + steps_a * depth + starts_b[:batch_count, None],
    )
    mine = owners == jnp.arange(batch_count)[:, None]
    column = jnp.sum(jnp.where(mine, shifted, 0), axis=0)
    grid = jnp.pad(column.reshape(-1, LANES), ((0, LANES - input_count // LANES), (0, 0))).T
    finder = jnp.concatenate([grid // TILE, grid % TILE], axis=0).astype(jnp.bfloat16)
    notes = jnp.stack([column[:nodes], deg_one[0]], axis=1).astype(jnp.float32)
    notes = share_order(notes, parts, seeds)
    block = math.gcd(nodes, 3 * TILE)
    met = notes[:, 0].reshape(1, nodes // block, block) // depth
    met = met.astype(jnp.int32) == jnp.arange(steps)[:, None, None]
    own_here = jnp.any(met, axis=2).astype(jnp.int32).reshape(-1)

    fanout_two = nbr_two.shape[2]
    used_two = jnp.arange(fanout_two)[:, None] < deg_two
    lists = jnp.concatenate([jnp.where(used_two, nbr_two[0].T, -1), deg_two], axis=0)
    lists = in_order(spread_parts(lists))
    upstream = in_order(spread_parts(cotangent[0])).reshape(seeds, hidden_width)

    fanout = nbr_one.shape[2]
    used = jnp.arange(fanout)[None, :] < deg_one[0][:, None]
    near = jnp.pad(jnp.where(used, near_first, -1), ((0, 0), (0, SLOTS - fanout)), constant_values=-1)
    near, lists, upstream = lax.optimization_barrier((near, lists, upstream))
    me = feat_index.astype(jnp.int32).reshape(1)
    near = near.reshape(nodes // SLOTS, TILE)
    adj = adjacency(me, near, finder, steps * WIDE, parts, seeds)
    looked, answer_a, adj = lax.optimization_barrier((looked, answer_a, adj))
    answer_b = lax.all_to_all(looked, "batch", split_axis=0, concat_axis=0, tiled=True)

    near_two = lists[:, :fanout_two].transpose(1, 0, 2).reshape(fanout_two, seeds)
    deg_all = lists[:, fanout_two].reshape(seeds)
    rest = share - seed_rows
    after = near_two - seeds
    place = jnp.where(
        near_two < seeds,
        near_two // seed_rows * share + near_two % seed_rows,
        after // rest * share + seed_rows + after % rest,
    )
    place = jnp.where(near_two < 0, -1, place - feat_index * share)
    adj_two = jnp.sum(
        place[:, :, None] == jnp.arange(share)[None, None, :], axis=0, dtype=jnp.float32
    ).astype(jnp.bfloat16)

    scalars = (spans_a, tally_a, starts_a, own_here)
    total, found = gather_sum(input_count, scalars, answer_a, notes, adj)

    def finish(begin, end):
        return gather_sum(
            input_count,
            (spans_b, tally_b, starts_b, own_here),
            answer_b,
            notes,
            adj,
            (total, found, w1_self, w1_neigh),
            begin * share,
            (share,) * (end - begin),
        )

    half = parts // 2
    cuts = [(half, parts), (1, half), (0, 1)]
    own_rows, mean_rows, z_blocks = [], [], []
    for begin, end in cuts:
        own, mean, *blocks = finish(begin, end)
        total, blocks = lax.optimization_barrier((total, blocks))
        own_rows.append(own)
        mean_rows.append(mean)
        z_blocks = blocks + z_blocks
    z_share = sum_parts(z_blocks) + bias_one
    hidden = jax.nn.silu(z_share).astype(jnp.bfloat16)

    agg_part = jnp.dot(adj_two, hidden, preferred_element_type=jnp.float32).astype(jnp.bfloat16)
    blocks = spread_parts(jnp.concatenate([agg_part, hidden[:seed_rows]]))
    deg_second = deg_all.astype(jnp.float32)[:, None]
    agg_two = sum(x[:seeds].astype(jnp.float32) for x in blocks) / deg_second
    agg_two = agg_two.astype(jnp.bfloat16)
    self_two = in_order([x[seeds:] for x in blocks]).reshape(seeds, hidden_width)
    z_two = (
        jnp.dot(self_two, w2_self, preferred_element_type=jnp.float32)
        + jnp.dot(agg_two, w2_neigh, preferred_element_type=jnp.float32)
        + bias_two
    )
    dz_two = (upstream.astype(jnp.float32) * silu_grad(z_two)).astype(jnp.bfloat16)
    mine = lambda x: lax.dynamic_slice_in_dim(x, feat_index * seed_rows, seed_rows, 0)
    activations = jax.nn.silu(mine(z_two)).astype(jnp.bfloat16)[None]

    back = contract_cols(dz_two, w2_neigh) / deg_second
    back_high = back.astype(jnp.bfloat16)
    back_low = (back - back_high.astype(jnp.float32)).astype(jnp.bfloat16)
    dh_share = contract_rows(adj_two, back_high) + contract_rows(adj_two, back_low)
    dh_share = dh_share + jnp.pad(contract_cols(mine(dz_two), w2_self), ((0, rest), (0, 0)))
    dz_share = (dh_share * silu_grad(z_share)).astype(jnp.bfloat16)
    dz_blocks = spread_parts(dz_share)
    dz_rows = [jnp.concatenate(dz_blocks[begin:end]) for begin, end in cuts]
    grads = [contract_rows(self_two, dz_two), contract_rows(agg_two, dz_two)]
    for rows in (own_rows, mean_rows):
        grads.append(sum(contract_rows(x, y) for x, y in zip(rows, dz_rows)))
    total = total_over_batch(jnp.concatenate(grads)).astype(jnp.float32)
    return (activations, *total.reshape(len(grads), -1, hidden_width))


def solution(mesh):
    in_specs = (
        P("batch", "feat"),
        P("batch", None, None),
        P("batch", None),
        P("batch", None, None),
        P("batch", None),
        P("batch", "feat", None),
        P("batch", "feat"),
        P("batch", "feat", None),
        P("feat", None),
        P("feat", None),
        P(),
        P(),
        P(),
        P(),
    )
    out_specs = (P("batch", "feat", None), P(), P(), P("feat", None), P("feat", None))
    return jax.shard_map(local, mesh=mesh, in_specs=in_specs, out_specs=out_specs, check_vma=False)
```

```python
import functools
import math

import jax
import jax.numpy as jnp
from jax import lax
from jax.experimental import pallas as pl
from jax.experimental.pallas import tpu as pltpu
from jax.sharding import PartitionSpec as P

TILE = 256
LANES = 128
SLOTS = 16
WIDE = 2
FEW = 16
TILE_BITS, LANE_BITS, SLOT_BITS = 8, 7, 4
MIB = 1024 * 1024
VMEM = pl.BlockSpec(memory_space=pltpu.VMEM)
SMEM = pl.BlockSpec(memory_space=pltpu.SMEM)
ANY = pl.BlockSpec(memory_space=pl.ANY)
HBM = pl.BlockSpec(memory_space=pltpu.HBM)


def silu_grad(values):
    sig = jax.nn.sigmoid(values)
    return sig * (1.0 + values * (1.0 - sig))


def contract_rows(left_side, right_side):
    return lax.dot_general(
        left_side, right_side, (((0,), (0,)), ((), ())), preferred_element_type=jnp.float32
    )


def contract_cols(left_side, right_side):
    return lax.dot_general(
        left_side, right_side, (((1,), (1,)), ((), ())), preferred_element_type=jnp.float32
    )


def params(mib):
    return pltpu.CompilerParams(vmem_limit_bytes=mib * MIB)


def cost(flops, moved):
    return pl.CostEstimate(flops=int(flops), bytes_accessed=int(moved), transcendentals=0)


def requests_body(batch_count, capacity, scale, owner_ref, row_ref, slot_ref, count_ref, request_ref):
    blocks, width = owner_ref.shape[0] // 2, TILE
    places = request_ref.shape[0]
    line = lambda ref, b: jnp.concatenate([ref[2 * b : 2 * b + 1], ref[2 * b + 1 : 2 * b + 2]], axis=1)
    owner_id = lax.broadcasted_iota(jnp.int32, (batch_count, width), 0)
    earlier = lax.broadcasted_iota(jnp.int32, (width, width), 0)
    later = lax.broadcasted_iota(jnp.int32, (width, width), 1)
    upper = jnp.where(earlier <= later, 1.0, 0.0).astype(jnp.bfloat16)
    high_id = lax.broadcasted_iota(jnp.int32, (places, width), 0)
    low_id = lax.broadcasted_iota(jnp.int32, (LANES, width), 0)
    marks = [
        jnp.where(line(owner_ref, b) == owner_id, 1.0, 0.0) for b in range(blocks)
    ]
    stacked = jnp.concatenate(marks, axis=0).astype(jnp.bfloat16)
    prefix = jnp.dot(stacked, upper, preferred_element_type=jnp.float32)
    running = jnp.zeros((batch_count, 1), jnp.float32)
    total = jnp.zeros((2 * places, LANES), jnp.float32)
    for b in range(blocks):
        part = prefix[b * batch_count : (b + 1) * batch_count]
        slots = jnp.sum(marks[b] * (part + running - 1.0), axis=0, keepdims=True)
        slots = slots.astype(jnp.int32)
        slot_ref[2 * b : 2 * b + 1, :] = slots[:, :LANES]
        slot_ref[2 * b + 1 : 2 * b + 2, :] = slots[:, LANES:]
        running = running + part[:, width - 1 : width]
        bucket = line(owner_ref, b) * capacity + slots
        rows = line(row_ref, b)
        hit = (bucket >> LANE_BITS) == high_id
        left = jnp.concatenate(
            [
                jnp.where(hit, (rows >> TILE_BITS).astype(jnp.float32), 0.0),
                jnp.where(hit, (rows & (TILE - 1)).astype(jnp.float32), 0.0),
            ],
            axis=0,
        ).astype(jnp.bfloat16)
        right = jnp.where((bucket & (LANES - 1)) == low_id, 1.0, 0.0).astype(jnp.bfloat16)
        total = total + contract_cols(left, right)
    count_ref[...] = jnp.broadcast_to(running, count_ref.shape).astype(jnp.int32)
    request_ref[...] = (total[:places] * TILE + total[places:]).astype(jnp.int32) * scale


def make_requests(batch_count, capacity, scale, owners, wanted):
    total = owners.shape[0] * LANES
    places = batch_count * capacity // LANES
    return pl.pallas_call(
        functools.partial(requests_body, batch_count, capacity, scale),
        out_shape=(
            jax.ShapeDtypeStruct(owners.shape, jnp.int32),
            jax.ShapeDtypeStruct((batch_count, LANES), jnp.int32),
            jax.ShapeDtypeStruct((places, LANES), jnp.int32),
        ),
        in_specs=[VMEM, VMEM],
        out_specs=(VMEM, VMEM, VMEM),
        compiler_params=params(16),
        cost_estimate=cost(4 * total * places * LANES, 24 * total),
        name="requests",
    )(owners, wanted)


def lookup_body(stride, first, width, want_ref, store_in, out_ref, table, lines, store_ref, came):
    rows_all = store_ref.shape[0]
    halves = store_ref.shape[1] // LANES
    lane = lambda h: pl.ds(h * LANES, LANES)
    begin = pl.program_id(0) * stride + first

    @pl.when(pl.program_id(0) == 0)
    def _():
        pieces = came.shape[0]
        depth = rows_all // pieces
        copies = [
            pltpu.make_async_copy(
                store_in.at[pl.ds(n * depth, depth)], store_ref.at[pl.ds(n * depth, depth)], came.at[n]
            )
            for n in range(pieces)
        ]
        for copy in copies:
            copy.start()
        for n, copy in enumerate(copies):
            copy.wait()

            @pl.loop(n * depth // TILE, (n + 1) * depth // TILE)
            def _(j):
                part = pl.ds(pl.multiple_of(j * TILE, TILE), TILE)
                for h in range(halves):
                    spot = pl.ds(pl.multiple_of(j * TILE * halves, TILE) + h, TILE, stride=halves)
                    table[spot, :] = store_ref[part, lane(h)].astype(jnp.float32)

    @pl.loop(0, width // SLOTS, unroll=2)
    def _(j):
        at = [want_ref[begin + j * SLOTS + u] for u in range(SLOTS)]
        rows = [table[pl.ds(pl.multiple_of(a, halves), halves), :] for a in at]
        block = lines.at[pl.ds(pl.multiple_of(j * SLOTS * halves, SLOTS * halves), SLOTS * halves)]
        for u in range(SLOTS):
            block[pl.ds(u * halves, halves), :] = rows[u]

    for h in range(halves):
        out_ref[0, :, lane(h)] = lines[pl.ds(h, width, stride=halves), :].astype(jnp.bfloat16)


def lookup(store, places, groups, first, width, mib):
    rows_all, features = store.shape
    halves = features // LANES
    apart = lambda rows: pltpu.VMEM((rows * halves, LANES), jnp.float32)
    return pl.pallas_call(
        functools.partial(lookup_body, places.shape[0] // groups, first, width),
        out_shape=jax.ShapeDtypeStruct((groups, width, features), jnp.bfloat16),
        grid=(groups,),
        in_specs=[SMEM, HBM],
        out_specs=pl.BlockSpec((1, width, features), lambda g: (g, 0, 0)),
        scratch_shapes=[
            apart(rows_all),
            apart(width),
            pltpu.VMEM((rows_all, features), store.dtype),
            pltpu.SemaphoreType.DMA((4,)),
        ],
        compiler_params=params(mib),
        cost_estimate=cost(groups * width * features * 40, 2 * rows_all * features),
        name="lookup",
    )(places, store)


def adjacency_body(tiles, me_ref, near_ref, table_ref, out_ref):
    groups = near_ref.shape[0]
    node_high = lax.broadcasted_iota(jnp.int32, (LANES, TILE), 0)
    own_row = (
        lax.shift_right_logical(lax.broadcasted_iota(jnp.int32, (SLOTS, TILE), 1), SLOT_BITS)
        == lax.broadcasted_iota(jnp.int32, (SLOTS, TILE), 0)
    )
    low_id = lax.broadcasted_iota(jnp.int32, (TILE, TILE), 0).astype(jnp.float32)

    def one_group(g):
        near = near_ref[pl.ds(g, 1), :]
        pick = jnp.where((near >> LANE_BITS) == node_high, 1.0, 0.0).astype(jnp.bfloat16)
        found = jnp.dot(table_ref[...], pick, preferred_element_type=jnp.float32)
        here = (near & (LANES - 1)) == node_high
        high = jnp.sum(jnp.where(here, found[:LANES], 0.0), axis=0, keepdims=True)
        low = jnp.sum(jnp.where(here, found[LANES:], 0.0), axis=0, keepdims=True)
        high = jnp.where(near < 0, -1.0, high)
        rows = jnp.where(own_row, high, -1.0)
        left = jnp.concatenate(
            [jnp.where(rows == float(t), 1.0, 0.0) for t in range(tiles)], axis=0
        ).astype(jnp.bfloat16)
        right = jnp.where(low == low_id, 1.0, 0.0).astype(jnp.bfloat16)
        return contract_cols(left, right).reshape(tiles, SLOTS, TILE)

    @pl.loop(0, groups // 2, unroll=2)
    def _(j):
        pair = jnp.concatenate([one_group(2 * j), one_group(2 * j + 1)], axis=1)
        out_ref[:, pl.ds(pl.multiple_of(j * 2 * SLOTS, 2 * SLOTS), 2 * SLOTS), :] = pair.astype(
            out_ref.dtype
        )


def adjacency(me, near, table, tiles, parts, seeds):
    groups = near.shape[0]
    nodes = groups * SLOTS
    step = LANES // SLOTS
    own, rest, share = (n // parts // LANES for n in (seeds, nodes - seeds, nodes))

    def place(block, me_ref):
        after = block - own * parts
        is_own = after < 0
        part = jnp.where(is_own, lax.div(block, own), lax.div(after, rest))
        at = jnp.where(is_own, lax.rem(block, own), own + lax.rem(after, rest))
        return (0, lax.rem(part - me_ref[0] + parts, parts) * share + at, 0)

    return pl.pallas_call(
        functools.partial(adjacency_body, tiles),
        out_shape=jax.ShapeDtypeStruct((tiles, nodes, TILE), jnp.float8_e4m3fn),
        grid_spec=pltpu.PrefetchScalarGridSpec(
            num_scalar_prefetch=1,
            grid=(groups // step,),
            in_specs=[
                pl.BlockSpec((step, TILE), lambda r, me: (r, 0)),
                pl.BlockSpec(table.shape, lambda r, me: (0, 0)),
            ],
            out_specs=pl.BlockSpec((tiles, LANES, TILE), place),
        ),
        compiler_params=params(48),
        cost_estimate=cost(2 * nodes * TILE * TILE * tiles * 2, nodes * TILE * tiles),
        name="adjacency",
    )(me, near, table)


def collect(piece, counts_ref, starts_ref, answer_ref, landed, arrived, packed):
    batch_count = answer_ref.shape[0]

    def each_used(what):
        @pl.loop(0, batch_count)
        def _(o):
            @pl.loop(0, pl.cdiv(counts_ref[o], piece))
            def _(c):
                part = pl.ds(pl.multiple_of(c * piece, piece), piece)
                what(
                    o,
                    c,
                    part,
                    pltpu.make_async_copy(
                        answer_ref.at[o, part], landed.at[o, part], arrived.at[o, c]
                    ),
                )

    def lay(o, c, part, copy):
        copy.wait()
        packed[pl.ds(pl.multiple_of(starts_ref[o] + c * piece, SLOTS), piece), :] = landed[o, part]

    each_used(lambda o, c, part, copy: copy.start())
    each_used(lay)
    end = starts_ref[batch_count]
    packed[pl.ds(pl.multiple_of(end, SLOTS), WIDE * TILE), :] = jnp.zeros(
        (WIDE * TILE, packed.shape[1]), packed.dtype
    )


def gather_sum_body(
    piece,
    last,
    row0,
    spans_ref,
    counts_ref,
    starts_ref,
    own_here_ref,
    answer_ref,
    notes_in,
    adj_ref,
    *refs,
):
    if last:
        (total_in, found_in, wself_in, wneigh_in, own_ref, mean_ref) = refs[:6]
        share_refs = refs[6:-11]
        packed, tiles_ref, ready, landed, arrived, notes_ref, carried = refs[-11:-4]
        total_ref, found_ref, wself_ref, wneigh_ref = refs[-4:]
        mine = pl.ds(row0, total_ref.shape[0])
        pairs = ((notes_in.at[mine], notes_ref), (total_in.at[mine], total_ref))
        pairs += ((found_in.at[mine], found_ref),)
        pairs += ((wself_in, wself_ref), (wneigh_in, wneigh_ref))
    else:
        total_ref, found_ref, packed, tiles_ref, ready, landed, arrived, notes_ref, carried = refs
        pairs = ((notes_in, notes_ref),)
    carry = [pltpu.make_async_copy(*pair, carried.at[n]) for n, pair in enumerate(pairs)]
    nodes = total_ref.shape[0]
    rows = math.gcd(adj_ref.shape[1], 3 * TILE)
    begin, count = spans_ref[0], spans_ref[1]

    def fetch(step, slot):
        return pltpu.make_async_copy(
            adj_ref.at[pl.ds(begin + step * WIDE, WIDE), pl.ds(row0, nodes)],
            tiles_ref.at[slot],
            ready.at[slot],
        )

    @pl.when(count > 0)
    def _():
        fetch(0, 0).start()

    for copy in carry:
        copy.start()
    collect(piece, counts_ref, starts_ref, answer_ref, landed, arrived, packed)
    for copy in carry:
        copy.wait()
    if not last:
        total_ref[...] = jnp.zeros(total_ref.shape, jnp.float32)
        found_ref[...] = jnp.zeros(found_ref.shape, jnp.float32)

    @pl.loop(0, count)
    def _(step):
        slot = step & 1

        @pl.when(step + 1 < count)
        def _():
            fetch(step + 1, 1 - slot).start()

        fetch(step, slot).wait()
        depth = WIDE * TILE
        block = packed[pl.ds(pl.multiple_of(step * depth, depth), depth), :]
        lane = lax.broadcasted_iota(jnp.int32, (rows, depth), 1) + (begin * TILE + step * depth)
        lane = lane.astype(jnp.float32)

        @pl.loop(0, nodes // rows)
        def _(r):
            part = pl.ds(pl.multiple_of(r * rows, rows), rows)
            near = jnp.concatenate(
                [tiles_ref[slot, w, part, :].astype(jnp.bfloat16) for w in range(WIDE)], axis=1
            )
            flag = (lax.div(begin, WIDE) + step) * (adj_ref.shape[1] // rows) + row0 // rows + r

            @pl.when(own_here_ref[flag] == 0)
            def _():
                total_ref[part, :] += jnp.dot(near, block, preferred_element_type=jnp.float32)

            @pl.when(own_here_ref[flag] != 0)
            def _():
                own = jnp.where(notes_ref[part, 0:1] == lane, 1.0, 0.0).astype(jnp.bfloat16)
                both = jnp.dot(
                    jnp.concatenate([near, own], axis=0), block, preferred_element_type=jnp.float32
                )
                total_ref[part, :] += both[:rows]
                found_ref[part, :] += both[rows:]

    if last:
        share = share_refs[0].shape[0]
        step_rows = math.gcd(share, 3 * TILE)
        for p, share_ref in enumerate(share_refs):
            for r in range(share // step_rows):
                part = pl.ds(p * share + r * step_rows, step_rows)
                own = found_ref[part, :].astype(jnp.bfloat16)
                mean = (total_ref[part, :] / notes_ref[part, 1:2]).astype(jnp.bfloat16)
                own_ref[part, :] = own
                mean_ref[part, :] = mean
                share_ref[pl.ds(r * step_rows, step_rows), :] = (
                    jnp.dot(own, wself_ref[...], preferred_element_type=jnp.float32)
                    + jnp.dot(mean, wneigh_ref[...], preferred_element_type=jnp.float32)
                ).astype(share_ref.dtype)


def gather_sum(inputs, scalars, answer, notes, adj, rest=None, row0=0, shares=()):
    batch_count, width, features = answer.shape
    tiles, nodes, _ = adj.shape
    nodes = sum(shares) or nodes
    piece = LANES if width % LANES == 0 else SLOTS
    last = rest is not None
    room = min(batch_count * width, inputs) + SLOTS * batch_count + 2 * WIDE * TILE
    in_specs = [SMEM, SMEM, SMEM, SMEM, ANY, HBM, HBM]
    rows = lambda dtype: jax.ShapeDtypeStruct((nodes, features), dtype)
    scratch = [
        pltpu.VMEM((room, features), jnp.bfloat16),
        pltpu.VMEM((2, WIDE, nodes, TILE), adj.dtype),
        pltpu.SemaphoreType.DMA((2,)),
        pltpu.VMEM(answer.shape, answer.dtype),
        pltpu.SemaphoreType.DMA((batch_count, width // piece)),
        pltpu.VMEM((nodes, notes.shape[1]), notes.dtype),
        pltpu.SemaphoreType.DMA((5,)),
    ]
    operands = [answer, notes, adj]
    if last:
        operands += list(rest)
        in_specs += [HBM] * len(rest)
        out_shape = (rows(jnp.bfloat16), rows(jnp.bfloat16))
        out_shape += tuple(
            jax.ShapeDtypeStruct((n, rest[3].shape[1]), jnp.bfloat16) for n in shares
        )
        scratch += [pltpu.VMEM((nodes, features), jnp.float32)] * 2
        scratch += [pltpu.VMEM(x.shape, x.dtype) for x in rest[2:]]
    else:
        out_shape = (rows(jnp.float32), rows(jnp.float32))
    return pl.pallas_call(
        functools.partial(gather_sum_body, piece, last, row0),
        out_shape=out_shape,
        in_specs=in_specs,
        out_specs=(VMEM,) * len(out_shape),
        scratch_shapes=scratch,
        compiler_params=params(50),
        cost_estimate=cost(2 * nodes * features * TILE * tiles // (4 if last else 1), nodes * TILE),
        name="gather_sum",
    )(*scalars, *operands)


def share_order(array, parts, seeds):
    others = array.shape[0] - seeds
    own, rest = seeds // parts, others // parts
    tail = array.shape[1:]
    blocks = jnp.concatenate(
        [array[:seeds].reshape(parts, own, *tail), array[seeds:].reshape(parts, rest, *tail)],
        axis=1,
    )
    return ahead(blocks).reshape(array.shape)


def spread(part, axis, count):
    return lax.all_to_all(
        jnp.broadcast_to(part[None], (count,) + part.shape), axis, 0, 0, tiled=True
    )


def passed(part, shift, axis="feat"):
    parts = lax.axis_size(axis)
    return lax.ppermute(part, axis, [((i + shift) % parts, i) for i in range(parts)])


def turned(array, by):
    twice = jnp.concatenate([array, array], axis=0)
    return lax.dynamic_slice_in_dim(twice, by, array.shape[0], 0)


def ahead(array, axis="feat"):
    return turned(array, lax.axis_index(axis))


def in_order(blocks):
    parts = lax.axis_size("feat")
    total = jnp.zeros((parts,) + blocks[0].shape, blocks[0].dtype)
    for j, block in enumerate(blocks):
        spot = (lax.axis_index("feat") + j) % parts
        total = lax.dynamic_update_index_in_dim(total, block, spot, 0)
    return total


def spread_parts(part, axis="feat"):
    return [part] + [passed(part, j, axis) for j in range(1, lax.axis_size(axis))]


def sum_parts(blocks, axis="feat"):
    parts = lax.axis_size(axis)
    came = [blocks[0]] + [passed(blocks[j], -j, axis) for j in range(1, parts)]
    return sum(x.astype(jnp.float32) for x in came)


def swapped(part):
    return lax.ppermute(part, "batch", [(i, i ^ 1) for i in range(lax.axis_size("batch"))])


def total_over_batch(terms):
    count = lax.axis_size("batch")
    rows, width = terms.shape
    if count > FEW:
        pieces = terms.astype(jnp.bfloat16).reshape(count, rows // count, width)
        pieces = lax.all_to_all(pieces, "batch", 0, 0, tiled=True)
        total = jnp.sum(pieces.astype(jnp.float32), axis=0).astype(jnp.bfloat16)
        return spread(total, "batch", count).reshape(rows, width)
    chips = count // 2
    index = lax.axis_index("batch")
    first, chip = index % 2 == 0, index // 2
    upper, lower = terms[: rows // 2], terms[rows // 2 :]
    came = swapped(jnp.where(first, lower, upper).astype(jnp.bfloat16))
    mine = jnp.where(first, upper, lower) + came.astype(jnp.float32)
    pieces = turned(mine.reshape(chips, rows // count, width), chip)
    total = pieces[0]
    for j in range(1, chips):
        total = total + passed(pieces[j].astype(jnp.bfloat16), -2 * j, "batch").astype(jnp.float32)
    total = total.astype(jnp.bfloat16)
    mine = jnp.stack([total] + [passed(total, 2 * j, "batch") for j in range(1, chips)])
    other = swapped(mine)
    both = jnp.stack([jnp.where(first, mine, other), jnp.where(first, other, mine)], axis=1)
    return turned(both, (chips - chip) % chips).transpose(1, 0, 2, 3).reshape(rows, width)


def local(
    store,
    input_owner,
    input_row,
    nbr_one,
    deg_one,
    nbr_two,
    deg_two,
    cotangent,
    w1_self,
    w1_neigh,
    bias_one,
    w2_self,
    w2_neigh,
    bias_two,
):
    batch_count = lax.axis_size("batch")
    parts = lax.axis_size("feat")
    feat_index = lax.axis_index("feat")
    input_count = input_owner.shape[1]
    capacity = 2 * input_count // batch_count
    nodes = nbr_one.shape[1]
    seed_rows = nbr_two.shape[1]
    seeds = seed_rows * parts
    share = nodes // parts
    hidden_width = w1_self.shape[1]

    owners = input_owner.reshape(input_count // LANES, LANES)
    wanted = input_row.reshape(input_count // LANES, LANES)
    slots, counts, requests = make_requests(
        batch_count, capacity, store.shape[1] // LANES, owners, wanted
    )
    owners = owners.reshape(1, input_count)
    received = lax.all_to_all(
        requests.reshape(batch_count, capacity), "batch", split_axis=0, concat_axis=0, tiled=True
    )
    first = capacity // 2
    places = received.reshape(batch_count * capacity)
    looked_a = lookup(store, places, batch_count, 0, first, 60)
    near_first, looked_a = lax.optimization_barrier((nbr_one[0], looked_a))
    answer_a = lax.all_to_all(looked_a, "batch", split_axis=0, concat_axis=0, tiled=True)
    looked = lookup(store, places, batch_count, first, capacity - first, 24)

    depth = WIDE * TILE
    steps = -(-(input_count + 2 * (SLOTS - 1) * batch_count + depth - 1) // depth)
    tally = counts[:, 0]
    tally_a = jnp.minimum(tally, first)
    tally_b = tally - tally_a
    padded = lambda n: (n + SLOTS - 1) // SLOTS * SLOTS
    ends = lambda n: jnp.concatenate([jnp.zeros((1,), jnp.int32), jnp.cumsum(padded(n))])
    starts_a, starts_b = ends(tally_a), ends(tally_b)
    steps_a = (starts_a[batch_count] + depth - 1) // depth
    steps_b = (starts_b[batch_count] + depth - 1) // depth
    spans_a = jnp.stack([jnp.zeros_like(steps_a), steps_a])
    spans_b = jnp.stack([steps_a * WIDE, steps_b])
    slot = slots.reshape(1, input_count)
    shifted = jnp.where(
        slot < first,
        slot + starts_a[:batch_count, None],
        slot - first + steps_a * depth + starts_b[:batch_count, None],
    )
    mine = owners == jnp.arange(batch_count)[:, None]
    column = jnp.sum(jnp.where(mine, shifted, 0), axis=0)
    grid = jnp.pad(column.reshape(-1, LANES), ((0, LANES - input_count // LANES), (0, 0))).T
    finder = jnp.concatenate([grid // TILE, grid % TILE], axis=0).astype(jnp.bfloat16)
    notes = jnp.stack([column[:nodes], deg_one[0]], axis=1).astype(jnp.float32)
    notes = share_order(notes, parts, seeds)
    block = math.gcd(nodes, 3 * TILE)
    met = notes[:, 0].reshape(1, nodes // block, block) // depth
    met = met.astype(jnp.int32) == jnp.arange(steps)[:, None, None]
    own_here = jnp.any(met, axis=2).astype(jnp.int32).reshape(-1)

    fanout = nbr_one.shape[2]
    used = jnp.arange(fanout)[None, :] < deg_one[0][:, None]
    near = jnp.pad(jnp.where(used, near_first, -1), ((0, 0), (0, SLOTS - fanout)), constant_values=-1)
    me = feat_index.astype(jnp.int32).reshape(1)
    near = near.reshape(nodes // SLOTS, TILE)
    adj = adjacency(me, near, finder, steps * WIDE, parts, seeds)
    looked, answer_a, adj = lax.optimization_barrier((looked, answer_a, adj))
    answer_b = lax.all_to_all(looked, "batch", split_axis=0, concat_axis=0, tiled=True)

    scalars = (spans_a, tally_a, starts_a, own_here)
    total, found = gather_sum(input_count, scalars, answer_a, notes, adj)
    second = (nbr_two[0], deg_two, cotangent[0])
    total, second = lax.optimization_barrier((total, second))

    fanout_two = nbr_two.shape[2]
    used_two = jnp.arange(fanout_two)[:, None] < second[1]
    lists = jnp.concatenate([jnp.where(used_two, second[0].T, -1), second[1]], axis=0)
    lists = in_order(spread_parts(lists))
    upstream = in_order(spread_parts(second[2])).reshape(seeds, hidden_width)

    near_two = lists[:, :fanout_two].transpose(1, 0, 2).reshape(fanout_two, seeds)
    deg_all = lists[:, fanout_two].reshape(seeds)
    rest = share - seed_rows
    after = near_two - seeds
    place = jnp.where(
        near_two < seeds,
        near_two // seed_rows * share + near_two % seed_rows,
        after // rest * share + seed_rows + after % rest,
    )
    place = jnp.where(near_two < 0, -1, place - feat_index * share)
    adj_two = jnp.sum(
        place[:, :, None] == jnp.arange(share)[None, None, :], axis=0, dtype=jnp.float32
    ).astype(jnp.bfloat16)
    total, adj_two, upstream = lax.optimization_barrier((total, adj_two, upstream))

    def finish(begin, end):
        return gather_sum(
            input_count,
            (spans_b, tally_b, starts_b, own_here),
            answer_b,
            notes,
            adj,
            (total, found, w1_self, w1_neigh),
            begin * share,
            (share,) * (end - begin),
        )

    half = parts // 2
    cuts = [(half, parts), (1, half), (0, 1)]
    own_rows, mean_rows, z_blocks = [], [], []
    for begin, end in cuts:
        own, mean, *blocks = finish(begin, end)
        total, blocks = lax.optimization_barrier((total, blocks))
        own_rows.append(own)
        mean_rows.append(mean)
        z_blocks = blocks + z_blocks
    z_share = sum_parts(z_blocks) + bias_one
    hidden = jax.nn.silu(z_share).astype(jnp.bfloat16)

    agg_part = jnp.dot(adj_two, hidden, preferred_element_type=jnp.float32).astype(jnp.bfloat16)
    blocks = spread_parts(jnp.concatenate([agg_part, hidden[:seed_rows]]))
    deg_second = deg_all.astype(jnp.float32)[:, None]
    agg_two = sum(x[:seeds].astype(jnp.float32) for x in blocks) / deg_second
    agg_two = agg_two.astype(jnp.bfloat16)
    self_two = in_order([x[seeds:] for x in blocks]).reshape(seeds, hidden_width)
    z_two = (
        jnp.dot(self_two, w2_self, preferred_element_type=jnp.float32)
        + jnp.dot(agg_two, w2_neigh, preferred_element_type=jnp.float32)
        + bias_two
    )
    dz_two = (upstream.astype(jnp.float32) * silu_grad(z_two)).astype(jnp.bfloat16)
    mine = lambda x: lax.dynamic_slice_in_dim(x, feat_index * seed_rows, seed_rows, 0)
    activations = jax.nn.silu(mine(z_two)).astype(jnp.bfloat16)[None]

    back = contract_cols(dz_two, w2_neigh) / deg_second
    back_high = back.astype(jnp.bfloat16)
    back_low = (back - back_high.astype(jnp.float32)).astype(jnp.bfloat16)
    dh_share = contract_rows(adj_two, back_high) + contract_rows(adj_two, back_low)
    dh_share = dh_share + jnp.pad(contract_cols(mine(dz_two), w2_self), ((0, rest), (0, 0)))
    dz_share = (dh_share * silu_grad(z_share)).astype(jnp.bfloat16)
    dz_blocks = spread_parts(dz_share)
    dz_rows = [jnp.concatenate(dz_blocks[begin:end]) for begin, end in cuts]
    grads = [contract_rows(self_two, dz_two), contract_rows(agg_two, dz_two)]
    for rows in (own_rows, mean_rows):
        grads.append(sum(contract_rows(x, y) for x, y in zip(rows, dz_rows)))
    total = total_over_batch(jnp.concatenate(grads)).astype(jnp.float32)
    return (activations, *total.reshape(len(grads), -1, hidden_width))


def solution(mesh):
    in_specs = (
        P("batch", "feat"),
        P("batch", None, None),
        P("batch", None),
        P("batch", None, None),
        P("batch", None),
        P("batch", "feat", None),
        P("batch", "feat"),
        P("batch", "feat", None),
        P("feat", None),
        P("feat", None),
        P(),
        P(),
        P(),
        P(),
    )
    out_specs = (P("batch", "feat", None), P(), P(), P("feat", None), P("feat", None))
    return jax.shard_map(local, mesh=mesh, in_specs=in_specs, out_specs=out_specs, check_vma=False)
```

```python
import functools
import math

import jax
import jax.numpy as jnp
from jax import lax
from jax.experimental import pallas as pl
from jax.experimental.pallas import tpu as pltpu
from jax.sharding import PartitionSpec as P

TILE = 256
LANES = 128
SLOTS = 16
WIDE = 2
FEW = 16
TILE_BITS, LANE_BITS, SLOT_BITS = 8, 7, 4
MIB = 1024 * 1024
VMEM = pl.BlockSpec(memory_space=pltpu.VMEM)
SMEM = pl.BlockSpec(memory_space=pltpu.SMEM)
ANY = pl.BlockSpec(memory_space=pl.ANY)
HBM = pl.BlockSpec(memory_space=pltpu.HBM)


def silu_grad(values):
    sig = jax.nn.sigmoid(values)
    return sig * (1.0 + values * (1.0 - sig))


def contract_rows(left_side, right_side):
    return lax.dot_general(
        left_side, right_side, (((0,), (0,)), ((), ())), preferred_element_type=jnp.float32
    )


def contract_cols(left_side, right_side):
    return lax.dot_general(
        left_side, right_side, (((1,), (1,)), ((), ())), preferred_element_type=jnp.float32
    )


def params(mib):
    return pltpu.CompilerParams(vmem_limit_bytes=mib * MIB)


def cost(flops, moved):
    return pl.CostEstimate(flops=int(flops), bytes_accessed=int(moved), transcendentals=0)


def requests_body(batch_count, capacity, scale, owner_ref, row_ref, slot_ref, count_ref, request_ref):
    blocks, width = owner_ref.shape[0] // 2, TILE
    places = request_ref.shape[0]
    line = lambda ref, b: jnp.concatenate([ref[2 * b : 2 * b + 1], ref[2 * b + 1 : 2 * b + 2]], axis=1)
    owner_id = lax.broadcasted_iota(jnp.int32, (batch_count, width), 0)
    earlier = lax.broadcasted_iota(jnp.int32, (width, width), 0)
    later = lax.broadcasted_iota(jnp.int32, (width, width), 1)
    upper = jnp.where(earlier <= later, 1.0, 0.0).astype(jnp.bfloat16)
    high_id = lax.broadcasted_iota(jnp.int32, (places, width), 0)
    low_id = lax.broadcasted_iota(jnp.int32, (LANES, width), 0)
    marks = [
        jnp.where(line(owner_ref, b) == owner_id, 1.0, 0.0) for b in range(blocks)
    ]
    stacked = jnp.concatenate(marks, axis=0).astype(jnp.bfloat16)
    prefix = jnp.dot(stacked, upper, preferred_element_type=jnp.float32)
    running = jnp.zeros((batch_count, 1), jnp.float32)
    total = jnp.zeros((2 * places, LANES), jnp.float32)
    for b in range(blocks):
        part = prefix[b * batch_count : (b + 1) * batch_count]
        slots = jnp.sum(marks[b] * (part + running - 1.0), axis=0, keepdims=True)
        slots = slots.astype(jnp.int32)
        slot_ref[2 * b : 2 * b + 1, :] = slots[:, :LANES]
        slot_ref[2 * b + 1 : 2 * b + 2, :] = slots[:, LANES:]
        running = running + part[:, width - 1 : width]
        bucket = line(owner_ref, b) * capacity + slots
        rows = line(row_ref, b)
        hit = (bucket >> LANE_BITS) == high_id
        left = jnp.concatenate(
            [
                jnp.where(hit, (rows >> TILE_BITS).astype(jnp.float32), 0.0),
                jnp.where(hit, (rows & (TILE - 1)).astype(jnp.float32), 0.0),
            ],
            axis=0,
        ).astype(jnp.bfloat16)
        right = jnp.where((bucket & (LANES - 1)) == low_id, 1.0, 0.0).astype(jnp.bfloat16)
        total = total + contract_cols(left, right)
    count_ref[...] = jnp.broadcast_to(running, count_ref.shape).astype(jnp.int32)
    request_ref[...] = (total[:places] * TILE + total[places:]).astype(jnp.int32) * scale


def make_requests(batch_count, capacity, scale, owners, wanted):
    total = owners.shape[0] * LANES
    places = batch_count * capacity // LANES
    return pl.pallas_call(
        functools.partial(requests_body, batch_count, capacity, scale),
        out_shape=(
            jax.ShapeDtypeStruct(owners.shape, jnp.int32),
            jax.ShapeDtypeStruct((batch_count, LANES), jnp.int32),
            jax.ShapeDtypeStruct((places, LANES), jnp.int32),
        ),
        in_specs=[VMEM, VMEM],
        out_specs=(VMEM, VMEM, VMEM),
        compiler_params=params(16),
        cost_estimate=cost(4 * total * places * LANES, 24 * total),
        name="requests",
    )(owners, wanted)


def lookup_body(stride, first, width, want_ref, store_in, out_ref, table, lines, store_ref, came):
    rows_all = store_ref.shape[0]
    halves = store_ref.shape[1] // LANES
    lane = lambda h: pl.ds(h * LANES, LANES)
    begin = pl.program_id(0) * stride + first

    @pl.when(pl.program_id(0) == 0)
    def _():
        pieces = came.shape[0]
        depth = rows_all // pieces
        copies = [
            pltpu.make_async_copy(
                store_in.at[pl.ds(n * depth, depth)], store_ref.at[pl.ds(n * depth, depth)], came.at[n]
            )
            for n in range(pieces)
        ]
        for copy in copies:
            copy.start()
        for n, copy in enumerate(copies):
            copy.wait()

            @pl.loop(n * depth // TILE, (n + 1) * depth // TILE)
            def _(j):
                part = pl.ds(pl.multiple_of(j * TILE, TILE), TILE)
                for h in range(halves):
                    spot = pl.ds(pl.multiple_of(j * TILE * halves, TILE) + h, TILE, stride=halves)
                    table[spot, :] = store_ref[part, lane(h)].astype(jnp.float32)

    @pl.loop(0, width // SLOTS, unroll=2)
    def _(j):
        at = [want_ref[begin + j * SLOTS + u] for u in range(SLOTS)]
        rows = [table[pl.ds(pl.multiple_of(a, halves), halves), :] for a in at]
        block = lines.at[pl.ds(pl.multiple_of(j * SLOTS * halves, SLOTS * halves), SLOTS * halves)]
        for u in range(SLOTS):
            block[pl.ds(u * halves, halves), :] = rows[u]

    for h in range(halves):
        out_ref[0, :, lane(h)] = lines[pl.ds(h, width, stride=halves), :].astype(jnp.bfloat16)


def lookup(store, places, groups, first, width, mib):
    rows_all, features = store.shape
    halves = features // LANES
    apart = lambda rows: pltpu.VMEM((rows * halves, LANES), jnp.float32)
    return pl.pallas_call(
        functools.partial(lookup_body, places.shape[0] // groups, first, width),
        out_shape=jax.ShapeDtypeStruct((groups, width, features), jnp.bfloat16),
        grid=(groups,),
        in_specs=[SMEM, HBM],
        out_specs=pl.BlockSpec((1, width, features), lambda g: (g, 0, 0)),
        scratch_shapes=[
            apart(rows_all),
            apart(width),
            pltpu.VMEM((rows_all, features), store.dtype),
            pltpu.SemaphoreType.DMA((4,)),
        ],
        compiler_params=params(mib),
        cost_estimate=cost(groups * width * features * 40, 2 * rows_all * features),
        name="lookup",
    )(places, store)


def adjacency_body(tiles, me_ref, near_ref, table_ref, out_ref):
    groups = near_ref.shape[0]
    node_high = lax.broadcasted_iota(jnp.int32, (LANES, TILE), 0)
    own_row = (
        lax.shift_right_logical(lax.broadcasted_iota(jnp.int32, (SLOTS, TILE), 1), SLOT_BITS)
        == lax.broadcasted_iota(jnp.int32, (SLOTS, TILE), 0)
    )
    low_id = lax.broadcasted_iota(jnp.int32, (TILE, TILE), 0).astype(jnp.float32)

    def one_group(g):
        near = near_ref[pl.ds(g, 1), :]
        pick = jnp.where((near >> LANE_BITS) == node_high, 1.0, 0.0).astype(jnp.bfloat16)
        found = jnp.dot(table_ref[...], pick, preferred_element_type=jnp.float32)
        here = (near & (LANES - 1)) == node_high
        high = jnp.sum(jnp.where(here, found[:LANES], 0.0), axis=0, keepdims=True)
        low = jnp.sum(jnp.where(here, found[LANES:], 0.0), axis=0, keepdims=True)
        high = jnp.where(near < 0, -1.0, high)
        rows = jnp.where(own_row, high, -1.0)
        left = jnp.concatenate(
            [jnp.where(rows == float(t), 1.0, 0.0) for t in range(tiles)], axis=0
        ).astype(jnp.bfloat16)
        right = jnp.where(low == low_id, 1.0, 0.0).astype(jnp.bfloat16)
        return contract_cols(left, right).reshape(tiles, SLOTS, TILE)

    @pl.loop(0, groups // 2, unroll=2)
    def _(j):
        pair = jnp.concatenate([one_group(2 * j), one_group(2 * j + 1)], axis=1)
        out_ref[:, pl.ds(pl.multiple_of(j * 2 * SLOTS, 2 * SLOTS), 2 * SLOTS), :] = pair.astype(
            out_ref.dtype
        )


def adjacency(me, near, table, tiles, parts, seeds):
    groups = near.shape[0]
    nodes = groups * SLOTS
    step = LANES // SLOTS
    own, rest, share = (n // parts // LANES for n in (seeds, nodes - seeds, nodes))

    def place(block, me_ref):
        after = block - own * parts
        is_own = after < 0
        part = jnp.where(is_own, lax.div(block, own), lax.div(after, rest))
        at = jnp.where(is_own, lax.rem(block, own), own + lax.rem(after, rest))
        return (0, lax.rem(part - me_ref[0] + parts, parts) * share + at, 0)

    return pl.pallas_call(
        functools.partial(adjacency_body, tiles),
        out_shape=jax.ShapeDtypeStruct((tiles, nodes, TILE), jnp.float8_e4m3fn),
        grid_spec=pltpu.PrefetchScalarGridSpec(
            num_scalar_prefetch=1,
            grid=(groups // step,),
            in_specs=[
                pl.BlockSpec((step, TILE), lambda r, me: (r, 0)),
                pl.BlockSpec(table.shape, lambda r, me: (0, 0)),
            ],
            out_specs=pl.BlockSpec((tiles, LANES, TILE), place),
        ),
        compiler_params=params(48),
        cost_estimate=cost(2 * nodes * TILE * TILE * tiles * 2, nodes * TILE * tiles),
        name="adjacency",
    )(me, near, table)


def collect(piece, counts_ref, starts_ref, answer_ref, landed, arrived, packed):
    batch_count = answer_ref.shape[0]

    def each_used(what):
        @pl.loop(0, batch_count)
        def _(o):
            @pl.loop(0, pl.cdiv(counts_ref[o], piece))
            def _(c):
                part = pl.ds(pl.multiple_of(c * piece, piece), piece)
                what(
                    o,
                    c,
                    part,
                    pltpu.make_async_copy(
                        answer_ref.at[o, part], landed.at[o, part], arrived.at[o, c]
                    ),
                )

    def lay(o, c, part, copy):
        copy.wait()
        packed[pl.ds(pl.multiple_of(starts_ref[o] + c * piece, SLOTS), piece), :] = landed[o, part]

    each_used(lambda o, c, part, copy: copy.start())
    each_used(lay)
    end = starts_ref[batch_count]
    packed[pl.ds(pl.multiple_of(end, SLOTS), WIDE * TILE), :] = jnp.zeros(
        (WIDE * TILE, packed.shape[1]), packed.dtype
    )


def gather_sum_body(
    piece,
    last,
    row0,
    spans_ref,
    counts_ref,
    starts_ref,
    own_here_ref,
    answer_ref,
    notes_in,
    adj_ref,
    *refs,
):
    if last:
        (total_in, found_in, wself_in, wneigh_in, own_ref, mean_ref) = refs[:6]
        share_refs = refs[6:-11]
        packed, tiles_ref, ready, landed, arrived, notes_ref, carried = refs[-11:-4]
        total_ref, found_ref, wself_ref, wneigh_ref = refs[-4:]
        mine = pl.ds(row0, total_ref.shape[0])
        pairs = ((notes_in.at[mine], notes_ref), (total_in.at[mine], total_ref))
        pairs += ((found_in.at[mine], found_ref),)
        pairs += ((wself_in, wself_ref), (wneigh_in, wneigh_ref))
    else:
        total_ref, found_ref, packed, tiles_ref, ready, landed, arrived, notes_ref, carried = refs
        pairs = ((notes_in, notes_ref),)
    carry = [pltpu.make_async_copy(*pair, carried.at[n]) for n, pair in enumerate(pairs)]
    nodes = total_ref.shape[0]
    rows = math.gcd(adj_ref.shape[1], 3 * TILE)
    begin, count = spans_ref[0], spans_ref[1]

    def fetch(step, slot):
        return pltpu.make_async_copy(
            adj_ref.at[pl.ds(begin + step * WIDE, WIDE), pl.ds(row0, nodes)],
            tiles_ref.at[slot],
            ready.at[slot],
        )

    @pl.when(count > 0)
    def _():
        fetch(0, 0).start()

    for copy in carry:
        copy.start()
    collect(piece, counts_ref, starts_ref, answer_ref, landed, arrived, packed)
    for copy in carry:
        copy.wait()
    if not last:
        total_ref[...] = jnp.zeros(total_ref.shape, jnp.float32)
        found_ref[...] = jnp.zeros(found_ref.shape, jnp.float32)

    @pl.loop(0, count)
    def _(step):
        slot = step & 1

        @pl.when(step + 1 < count)
        def _():
            fetch(step + 1, 1 - slot).start()

        fetch(step, slot).wait()
        depth = WIDE * TILE
        block = packed[pl.ds(pl.multiple_of(step * depth, depth), depth), :]
        lane = lax.broadcasted_iota(jnp.int32, (rows, depth), 1) + (begin * TILE + step * depth)
        lane = lane.astype(jnp.float32)

        @pl.loop(0, nodes // rows)
        def _(r):
            part = pl.ds(pl.multiple_of(r * rows, rows), rows)
            near = jnp.concatenate(
                [tiles_ref[slot, w, part, :].astype(jnp.bfloat16) for w in range(WIDE)], axis=1
            )
            flag = (lax.div(begin, WIDE) + step) * (adj_ref.shape[1] // rows) + row0 // rows + r

            @pl.when(own_here_ref[flag] == 0)
            def _():
                total_ref[part, :] += jnp.dot(near, block, preferred_element_type=jnp.float32)

            @pl.when(own_here_ref[flag] != 0)
            def _():
                own = jnp.where(notes_ref[part, 0:1] == lane, 1.0, 0.0).astype(jnp.bfloat16)
                both = jnp.dot(
                    jnp.concatenate([near, own], axis=0), block, preferred_element_type=jnp.float32
                )
                total_ref[part, :] += both[:rows]
                found_ref[part, :] += both[rows:]

    if last:
        share = share_refs[0].shape[0]
        step_rows = math.gcd(share, 3 * TILE)
        for p, share_ref in enumerate(share_refs):
            for r in range(share // step_rows):
                part = pl.ds(p * share + r * step_rows, step_rows)
                own = found_ref[part, :].astype(jnp.bfloat16)
                mean = (total_ref[part, :] / notes_ref[part, 1:2]).astype(jnp.bfloat16)
                own_ref[part, :] = own
                mean_ref[part, :] = mean
                share_ref[pl.ds(r * step_rows, step_rows), :] = (
                    jnp.dot(own, wself_ref[...], preferred_element_type=jnp.float32)
                    + jnp.dot(mean, wneigh_ref[...], preferred_element_type=jnp.float32)
                ).astype(share_ref.dtype)


def gather_sum(inputs, scalars, answer, notes, adj, rest=None, row0=0, shares=()):
    batch_count, width, features = answer.shape
    tiles, nodes, _ = adj.shape
    nodes = sum(shares) or nodes
    piece = LANES if width % LANES == 0 else SLOTS
    last = rest is not None
    room = min(batch_count * width, inputs) + SLOTS * batch_count + 2 * WIDE * TILE
    in_specs = [SMEM, SMEM, SMEM, SMEM, ANY, HBM, HBM]
    rows = lambda dtype: jax.ShapeDtypeStruct((nodes, features), dtype)
    scratch = [
        pltpu.VMEM((room, features), jnp.bfloat16),
        pltpu.VMEM((2, WIDE, nodes, TILE), adj.dtype),
        pltpu.SemaphoreType.DMA((2,)),
        pltpu.VMEM(answer.shape, answer.dtype),
        pltpu.SemaphoreType.DMA((batch_count, width // piece)),
        pltpu.VMEM((nodes, notes.shape[1]), notes.dtype),
        pltpu.SemaphoreType.DMA((5,)),
    ]
    operands = [answer, notes, adj]
    if last:
        operands += list(rest)
        in_specs += [HBM] * len(rest)
        out_shape = (rows(jnp.bfloat16), rows(jnp.bfloat16))
        out_shape += tuple(
            jax.ShapeDtypeStruct((n, rest[3].shape[1]), jnp.bfloat16) for n in shares
        )
        scratch += [pltpu.VMEM((nodes, features), jnp.float32)] * 2
        scratch += [pltpu.VMEM(x.shape, x.dtype) for x in rest[2:]]
    else:
        out_shape = (rows(jnp.float32), rows(jnp.float32))
    return pl.pallas_call(
        functools.partial(gather_sum_body, piece, last, row0),
        out_shape=out_shape,
        in_specs=in_specs,
        out_specs=(VMEM,) * len(out_shape),
        scratch_shapes=scratch,
        compiler_params=params(50),
        cost_estimate=cost(2 * nodes * features * TILE * tiles // (4 if last else 1), nodes * TILE),
        name="gather_sum",
    )(*scalars, *operands)


def share_order(array, parts, seeds):
    others = array.shape[0] - seeds
    own, rest = seeds // parts, others // parts
    tail = array.shape[1:]
    blocks = jnp.concatenate(
        [array[:seeds].reshape(parts, own, *tail), array[seeds:].reshape(parts, rest, *tail)],
        axis=1,
    )
    return ahead(blocks).reshape(array.shape)


def spread(part, axis, count):
    return lax.all_to_all(
        jnp.broadcast_to(part[None], (count,) + part.shape), axis, 0, 0, tiled=True
    )


def passed(part, shift, axis="feat"):
    parts = lax.axis_size(axis)
    return lax.ppermute(part, axis, [((i + shift) % parts, i) for i in range(parts)])


def turned(array, by):
    twice = jnp.concatenate([array, array], axis=0)
    return lax.dynamic_slice_in_dim(twice, by, array.shape[0], 0)


def ahead(array, axis="feat"):
    return turned(array, lax.axis_index(axis))


def in_order(blocks):
    parts = lax.axis_size("feat")
    total = jnp.zeros((parts,) + blocks[0].shape, blocks[0].dtype)
    for j, block in enumerate(blocks):
        spot = (lax.axis_index("feat") + j) % parts
        total = lax.dynamic_update_index_in_dim(total, block, spot, 0)
    return total


def spread_parts(part, axis="feat"):
    return [part] + [passed(part, j, axis) for j in range(1, lax.axis_size(axis))]


def sum_parts(blocks, axis="feat"):
    parts = lax.axis_size(axis)
    came = [blocks[0]] + [passed(blocks[j], -j, axis) for j in range(1, parts)]
    return sum(x.astype(jnp.float32) for x in came)


def swapped(part):
    return lax.ppermute(part, "batch", [(i, i ^ 1) for i in range(lax.axis_size("batch"))])


def total_over_batch(terms):
    count = lax.axis_size("batch")
    rows, width = terms.shape
    if count > FEW:
        pieces = terms.astype(jnp.bfloat16).reshape(count, rows // count, width)
        pieces = lax.all_to_all(pieces, "batch", 0, 0, tiled=True)
        total = jnp.sum(pieces.astype(jnp.float32), axis=0).astype(jnp.bfloat16)
        return spread(total, "batch", count).reshape(rows, width)
    chips = count // 2
    index = lax.axis_index("batch")
    first, chip = index % 2 == 0, index // 2
    upper, lower = terms[: rows // 2], terms[rows // 2 :]
    came = swapped(jnp.where(first, lower, upper).astype(jnp.bfloat16))
    mine = jnp.where(first, upper, lower) + came.astype(jnp.float32)
    pieces = turned(mine.reshape(chips, rows // count, width), chip)
    total = pieces[0]
    for j in range(1, chips):
        total = total + passed(pieces[j].astype(jnp.bfloat16), -2 * j, "batch").astype(jnp.float32)
    total = total.astype(jnp.bfloat16)
    mine = jnp.stack([total] + [passed(total, 2 * j, "batch") for j in range(1, chips)])
    other = swapped(mine)
    both = jnp.stack([jnp.where(first, mine, other), jnp.where(first, other, mine)], axis=1)
    return turned(both, (chips - chip) % chips).transpose(1, 0, 2, 3).reshape(rows, width)


def local(
    store,
    input_owner,
    input_row,
    nbr_one,
    deg_one,
    nbr_two,
    deg_two,
    cotangent,
    w1_self,
    w1_neigh,
    bias_one,
    w2_self,
    w2_neigh,
    bias_two,
):
    batch_count = lax.axis_size("batch")
    parts = lax.axis_size("feat")
    feat_index = lax.axis_index("feat")
    input_count = input_owner.shape[1]
    capacity = 2 * input_count // batch_count
    nodes = nbr_one.shape[1]
    seed_rows = nbr_two.shape[1]
    seeds = seed_rows * parts
    share = nodes // parts
    hidden_width = w1_self.shape[1]

    owners = input_owner.reshape(input_count // LANES, LANES)
    wanted = input_row.reshape(input_count // LANES, LANES)
    slots, counts, requests = make_requests(
        batch_count, capacity, store.shape[1] // LANES, owners, wanted
    )
    owners = owners.reshape(1, input_count)
    received = lax.all_to_all(
        requests.reshape(batch_count, capacity), "batch", split_axis=0, concat_axis=0, tiled=True
    )
    first = capacity // 2
    places = received.reshape(batch_count * capacity)
    looked_a = lookup(store, places, batch_count, 0, first, 60)
    near_first, looked_a = lax.optimization_barrier((nbr_one[0], looked_a))
    answer_a = lax.all_to_all(looked_a, "batch", split_axis=0, concat_axis=0, tiled=True)
    looked = lookup(store, places, batch_count, first, capacity - first, 24)

    depth = WIDE * TILE
    steps = -(-(input_count + 2 * (SLOTS - 1) * batch_count + depth - 1) // depth)
    tally = counts[:, 0]
    tally_a = jnp.minimum(tally, first)
    tally_b = tally - tally_a
    padded = lambda n: (n + SLOTS - 1) // SLOTS * SLOTS
    ends = lambda n: jnp.concatenate([jnp.zeros((1,), jnp.int32), jnp.cumsum(padded(n))])
    starts_a, starts_b = ends(tally_a), ends(tally_b)
    steps_a = (starts_a[batch_count] + depth - 1) // depth
    steps_b = (starts_b[batch_count] + depth - 1) // depth
    spans_a = jnp.stack([jnp.zeros_like(steps_a), steps_a])
    spans_b = jnp.stack([steps_a * WIDE, steps_b])
    slot = slots.reshape(1, input_count)
    shifted = jnp.where(
        slot < first,
        slot + starts_a[:batch_count, None],
        slot - first + steps_a * depth + starts_b[:batch_count, None],
    )
    mine = owners == jnp.arange(batch_count)[:, None]
    column = jnp.sum(jnp.where(mine, shifted, 0), axis=0)
    grid = jnp.pad(column.reshape(-1, LANES), ((0, LANES - input_count // LANES), (0, 0))).T
    finder = jnp.concatenate([grid // TILE, grid % TILE], axis=0).astype(jnp.bfloat16)
    notes = jnp.stack([column[:nodes], deg_one[0]], axis=1).astype(jnp.float32)
    notes = share_order(notes, parts, seeds)
    block = math.gcd(nodes, 3 * TILE)
    met = notes[:, 0].reshape(1, nodes // block, block) // depth
    met = met.astype(jnp.int32) == jnp.arange(steps)[:, None, None]
    own_here = jnp.any(met, axis=2).astype(jnp.int32).reshape(-1)

    fanout = nbr_one.shape[2]
    used = jnp.arange(fanout)[None, :] < deg_one[0][:, None]
    near = jnp.pad(jnp.where(used, near_first, -1), ((0, 0), (0, SLOTS - fanout)), constant_values=-1)
    me = feat_index.astype(jnp.int32).reshape(1)
    near = near.reshape(nodes // SLOTS, TILE)
    adj = adjacency(me, near, finder, steps * WIDE, parts, seeds)
    looked, answer_a, adj = lax.optimization_barrier((looked, answer_a, adj))
    answer_b = lax.all_to_all(looked, "batch", split_axis=0, concat_axis=0, tiled=True)

    scalars = (spans_a, tally_a, starts_a, own_here)
    total, found = gather_sum(input_count, scalars, answer_a, notes, adj)
    second = (nbr_two[0], deg_two, cotangent[0])
    total, second = lax.optimization_barrier((total, second))

    fanout_two = nbr_two.shape[2]
    used_two = jnp.arange(fanout_two)[:, None] < second[1]
    lists = jnp.concatenate([jnp.where(used_two, second[0].T, -1), second[1]], axis=0)
    lists = in_order(spread_parts(lists))
    upstream = in_order(spread_parts(second[2])).reshape(seeds, hidden_width)
    total, lists, upstream = lax.optimization_barrier((total, lists, upstream))

    near_two = lists[:, :fanout_two].transpose(1, 0, 2).reshape(fanout_two, seeds)
    deg_all = lists[:, fanout_two].reshape(seeds)
    rest = share - seed_rows
    after = near_two - seeds
    place = jnp.where(
        near_two < seeds,
        near_two // seed_rows * share + near_two % seed_rows,
        after // rest * share + seed_rows + after % rest,
    )
    place = jnp.where(near_two < 0, -1, place - feat_index * share)
    adj_two = jnp.sum(
        place[:, :, None] == jnp.arange(share)[None, None, :], axis=0, dtype=jnp.float32
    ).astype(jnp.bfloat16)

    def finish(begin, end):
        return gather_sum(
            input_count,
            (spans_b, tally_b, starts_b, own_here),
            answer_b,
            notes,
            adj,
            (total, found, w1_self, w1_neigh),
            begin * share,
            (share,) * (end - begin),
        )

    half = parts // 2
    cuts = [(half, parts), (1, half), (0, 1)]
    own_rows, mean_rows, z_blocks = [], [], []
    for begin, end in cuts:
        own, mean, *blocks = finish(begin, end)
        total, blocks = lax.optimization_barrier((total, blocks))
        own_rows.append(own)
        mean_rows.append(mean)
        z_blocks = blocks + z_blocks
    z_share = sum_parts(z_blocks) + bias_one
    hidden = jax.nn.silu(z_share).astype(jnp.bfloat16)

    agg_part = jnp.dot(adj_two, hidden, preferred_element_type=jnp.float32).astype(jnp.bfloat16)
    blocks = spread_parts(jnp.concatenate([agg_part, hidden[:seed_rows]]))
    deg_second = deg_all.astype(jnp.float32)[:, None]
    agg_two = sum(x[:seeds].astype(jnp.float32) for x in blocks) / deg_second
    agg_two = agg_two.astype(jnp.bfloat16)
    self_two = in_order([x[seeds:] for x in blocks]).reshape(seeds, hidden_width)
    z_two = (
        jnp.dot(self_two, w2_self, preferred_element_type=jnp.float32)
        + jnp.dot(agg_two, w2_neigh, preferred_element_type=jnp.float32)
        + bias_two
    )
    dz_two = (upstream.astype(jnp.float32) * silu_grad(z_two)).astype(jnp.bfloat16)
    mine = lambda x: lax.dynamic_slice_in_dim(x, feat_index * seed_rows, seed_rows, 0)
    activations = jax.nn.silu(mine(z_two)).astype(jnp.bfloat16)[None]

    back = contract_cols(dz_two, w2_neigh) / deg_second
    back_high = back.astype(jnp.bfloat16)
    back_low = (back - back_high.astype(jnp.float32)).astype(jnp.bfloat16)
    dh_share = contract_rows(adj_two, back_high) + contract_rows(adj_two, back_low)
    dh_share = dh_share + jnp.pad(contract_cols(mine(dz_two), w2_self), ((0, rest), (0, 0)))
    dz_share = (dh_share * silu_grad(z_share)).astype(jnp.bfloat16)
    dz_blocks = spread_parts(dz_share)
    dz_rows = [jnp.concatenate(dz_blocks[begin:end]) for begin, end in cuts]
    grads = [contract_rows(self_two, dz_two), contract_rows(agg_two, dz_two)]
    for rows in (own_rows, mean_rows):
        grads.append(sum(contract_rows(x, y) for x, y in zip(rows, dz_rows)))
    total = total_over_batch(jnp.concatenate(grads)).astype(jnp.float32)
    return (activations, *total.reshape(len(grads), -1, hidden_width))


def solution(mesh):
    in_specs = (
        P("batch", "feat"),
        P("batch", None, None),
        P("batch", None),
        P("batch", None, None),
        P("batch", None),
        P("batch", "feat", None),
        P("batch", "feat"),
        P("batch", "feat", None),
        P("feat", None),
        P("feat", None),
        P(),
        P(),
        P(),
        P(),
    )
    out_specs = (P("batch", "feat", None), P(), P(), P("feat", None), P("feat", None))
    return jax.shard_map(local, mesh=mesh, in_specs=in_specs, out_specs=out_specs, check_vma=False)
```

```python
import functools
import math

import jax
import jax.numpy as jnp
from jax import lax
from jax.experimental import pallas as pl
from jax.experimental.pallas import tpu as pltpu
from jax.sharding import PartitionSpec as P

TILE = 256
LANES = 128
SLOTS = 16
WIDE = 2
FEW = 16
TILE_BITS, LANE_BITS, SLOT_BITS = 8, 7, 4
MIB = 1024 * 1024
VMEM = pl.BlockSpec(memory_space=pltpu.VMEM)
SMEM = pl.BlockSpec(memory_space=pltpu.SMEM)
ANY = pl.BlockSpec(memory_space=pl.ANY)
HBM = pl.BlockSpec(memory_space=pltpu.HBM)


def silu_grad(values):
    sig = jax.nn.sigmoid(values)
    return sig * (1.0 + values * (1.0 - sig))


def contract_rows(left_side, right_side):
    return lax.dot_general(
        left_side, right_side, (((0,), (0,)), ((), ())), preferred_element_type=jnp.float32
    )


def contract_cols(left_side, right_side):
    return lax.dot_general(
        left_side, right_side, (((1,), (1,)), ((), ())), preferred_element_type=jnp.float32
    )


def params(mib):
    return pltpu.CompilerParams(vmem_limit_bytes=mib * MIB)


def cost(flops, moved):
    return pl.CostEstimate(flops=int(flops), bytes_accessed=int(moved), transcendentals=0)


def requests_body(
    batch_count,
    capacity,
    scale,
    owner_in,
    row_in,
    slot_ref,
    count_ref,
    request_ref,
    owner_ref,
    row_ref,
    came,
):
    copies = [
        pltpu.make_async_copy(owner_in, owner_ref, came.at[0]),
        pltpu.make_async_copy(row_in, row_ref, came.at[1]),
    ]
    for copy in copies:
        copy.start()
    for copy in copies:
        copy.wait()
    blocks, width = owner_ref.shape[0] // 2, TILE
    places = request_ref.shape[0]
    line = lambda ref, b: jnp.concatenate([ref[2 * b : 2 * b + 1], ref[2 * b + 1 : 2 * b + 2]], axis=1)
    owner_id = lax.broadcasted_iota(jnp.int32, (batch_count, width), 0)
    earlier = lax.broadcasted_iota(jnp.int32, (width, width), 0)
    later = lax.broadcasted_iota(jnp.int32, (width, width), 1)
    upper = jnp.where(earlier <= later, 1.0, 0.0).astype(jnp.bfloat16)
    high_id = lax.broadcasted_iota(jnp.int32, (places, width), 0)
    low_id = lax.broadcasted_iota(jnp.int32, (LANES, width), 0)
    marks = [
        jnp.where(line(owner_ref, b) == owner_id, 1.0, 0.0) for b in range(blocks)
    ]
    stacked = jnp.concatenate(marks, axis=0).astype(jnp.bfloat16)
    prefix = jnp.dot(stacked, upper, preferred_element_type=jnp.float32)
    running = jnp.zeros((batch_count, 1), jnp.float32)
    total = jnp.zeros((2 * places, LANES), jnp.float32)
    for b in range(blocks):
        part = prefix[b * batch_count : (b + 1) * batch_count]
        slots = jnp.sum(marks[b] * (part + running - 1.0), axis=0, keepdims=True)
        slots = slots.astype(jnp.int32)
        slot_ref[2 * b : 2 * b + 1, :] = slots[:, :LANES]
        slot_ref[2 * b + 1 : 2 * b + 2, :] = slots[:, LANES:]
        running = running + part[:, width - 1 : width]
        bucket = line(owner_ref, b) * capacity + slots
        rows = line(row_ref, b)
        hit = (bucket >> LANE_BITS) == high_id
        left = jnp.concatenate(
            [
                jnp.where(hit, (rows >> TILE_BITS).astype(jnp.float32), 0.0),
                jnp.where(hit, (rows & (TILE - 1)).astype(jnp.float32), 0.0),
            ],
            axis=0,
        ).astype(jnp.bfloat16)
        right = jnp.where((bucket & (LANES - 1)) == low_id, 1.0, 0.0).astype(jnp.bfloat16)
        total = total + contract_cols(left, right)
    count_ref[...] = jnp.broadcast_to(running, count_ref.shape).astype(jnp.int32)
    request_ref[...] = (total[:places] * TILE + total[places:]).astype(jnp.int32) * scale


def make_requests(batch_count, capacity, scale, owners, wanted):
    total = owners.shape[0] * LANES
    places = batch_count * capacity // LANES
    return pl.pallas_call(
        functools.partial(requests_body, batch_count, capacity, scale),
        out_shape=(
            jax.ShapeDtypeStruct(owners.shape, jnp.int32),
            jax.ShapeDtypeStruct((batch_count, LANES), jnp.int32),
            jax.ShapeDtypeStruct((places, LANES), jnp.int32),
        ),
        in_specs=[ANY, ANY],
        out_specs=(VMEM, VMEM, VMEM),
        scratch_shapes=[
            pltpu.VMEM(owners.shape, owners.dtype),
            pltpu.VMEM(wanted.shape, wanted.dtype),
            pltpu.SemaphoreType.DMA((2,)),
        ],
        compiler_params=params(58),
        cost_estimate=cost(4 * total * places * LANES, 24 * total),
        name="requests",
    )(owners, wanted)


def lookup_body(stride, first, width, want_ref, store_in, out_ref, table, lines, store_ref, came):
    rows_all = store_ref.shape[0]
    halves = store_ref.shape[1] // LANES
    lane = lambda h: pl.ds(h * LANES, LANES)
    begin = pl.program_id(0) * stride + first

    @pl.when(pl.program_id(0) == 0)
    def _():
        pieces = came.shape[0]
        depth = rows_all // pieces
        copies = [
            pltpu.make_async_copy(
                store_in.at[pl.ds(n * depth, depth)], store_ref.at[pl.ds(n * depth, depth)], came.at[n]
            )
            for n in range(pieces)
        ]
        for copy in copies:
            copy.start()
        for n, copy in enumerate(copies):
            copy.wait()

            @pl.loop(n * depth // TILE, (n + 1) * depth // TILE)
            def _(j):
                part = pl.ds(pl.multiple_of(j * TILE, TILE), TILE)
                for h in range(halves):
                    spot = pl.ds(pl.multiple_of(j * TILE * halves, TILE) + h, TILE, stride=halves)
                    table[spot, :] = store_ref[part, lane(h)].astype(jnp.float32)

    @pl.loop(0, width // SLOTS, unroll=2)
    def _(j):
        at = [want_ref[begin + j * SLOTS + u] for u in range(SLOTS)]
        rows = [table[pl.ds(pl.multiple_of(a, halves), halves), :] for a in at]
        block = lines.at[pl.ds(pl.multiple_of(j * SLOTS * halves, SLOTS * halves), SLOTS * halves)]
        for u in range(SLOTS):
            block[pl.ds(u * halves, halves), :] = rows[u]

    for h in range(halves):
        out_ref[0, :, lane(h)] = lines[pl.ds(h, width, stride=halves), :].astype(jnp.bfloat16)


def lookup(store, places, groups, first, width, mib):
    rows_all, features = store.shape
    halves = features // LANES
    apart = lambda rows: pltpu.VMEM((rows * halves, LANES), jnp.float32)
    return pl.pallas_call(
        functools.partial(lookup_body, places.shape[0] // groups, first, width),
        out_shape=jax.ShapeDtypeStruct((groups, width, features), jnp.bfloat16),
        grid=(groups,),
        in_specs=[SMEM, HBM],
        out_specs=pl.BlockSpec((1, width, features), lambda g: (g, 0, 0)),
        scratch_shapes=[
            apart(rows_all),
            apart(width),
            pltpu.VMEM((rows_all, features), store.dtype),
            pltpu.SemaphoreType.DMA((4,)),
        ],
        compiler_params=params(mib),
        cost_estimate=cost(groups * width * features * 40, 2 * rows_all * features),
        name="lookup",
    )(places, store)


def adjacency_body(tiles, me_ref, near_ref, table_ref, out_ref):
    groups = near_ref.shape[0]
    node_high = lax.broadcasted_iota(jnp.int32, (LANES, TILE), 0)
    own_row = (
        lax.shift_right_logical(lax.broadcasted_iota(jnp.int32, (SLOTS, TILE), 1), SLOT_BITS)
        == lax.broadcasted_iota(jnp.int32, (SLOTS, TILE), 0)
    )
    low_id = lax.broadcasted_iota(jnp.int32, (TILE, TILE), 0).astype(jnp.float32)

    def one_group(g):
        near = near_ref[pl.ds(g, 1), :]
        pick = jnp.where((near >> LANE_BITS) == node_high, 1.0, 0.0).astype(jnp.bfloat16)
        found = jnp.dot(table_ref[...], pick, preferred_element_type=jnp.float32)
        here = (near & (LANES - 1)) == node_high
        high = jnp.sum(jnp.where(here, found[:LANES], 0.0), axis=0, keepdims=True)
        low = jnp.sum(jnp.where(here, found[LANES:], 0.0), axis=0, keepdims=True)
        high = jnp.where(near < 0, -1.0, high)
        rows = jnp.where(own_row, high, -1.0)
        left = jnp.concatenate(
            [jnp.where(rows == float(t), 1.0, 0.0) for t in range(tiles)], axis=0
        ).astype(jnp.bfloat16)
        right = jnp.where(low == low_id, 1.0, 0.0).astype(jnp.bfloat16)
        return contract_cols(left, right).reshape(tiles, SLOTS, TILE)

    @pl.loop(0, groups // 2, unroll=2)
    def _(j):
        pair = jnp.concatenate([one_group(2 * j), one_group(2 * j + 1)], axis=1)
        out_ref[:, pl.ds(pl.multiple_of(j * 2 * SLOTS, 2 * SLOTS), 2 * SLOTS), :] = pair.astype(
            out_ref.dtype
        )


def adjacency(me, near, table, tiles, parts, seeds):
    groups = near.shape[0]
    nodes = groups * SLOTS
    step = LANES // SLOTS
    own, rest, share = (n // parts // LANES for n in (seeds, nodes - seeds, nodes))

    def place(block, me_ref):
        after = block - own * parts
        is_own = after < 0
        part = jnp.where(is_own, lax.div(block, own), lax.div(after, rest))
        at = jnp.where(is_own, lax.rem(block, own), own + lax.rem(after, rest))
        return (0, lax.rem(part - me_ref[0] + parts, parts) * share + at, 0)

    return pl.pallas_call(
        functools.partial(adjacency_body, tiles),
        out_shape=jax.ShapeDtypeStruct((tiles, nodes, TILE), jnp.float8_e4m3fn),
        grid_spec=pltpu.PrefetchScalarGridSpec(
            num_scalar_prefetch=1,
            grid=(groups // step,),
            in_specs=[
                pl.BlockSpec((step, TILE), lambda r, me: (r, 0)),
                pl.BlockSpec(table.shape, lambda r, me: (0, 0)),
            ],
            out_specs=pl.BlockSpec((tiles, LANES, TILE), place),
        ),
        compiler_params=params(48),
        cost_estimate=cost(2 * nodes * TILE * TILE * tiles * 2, nodes * TILE * tiles),
        name="adjacency",
    )(me, near, table)


def collect(piece, counts_ref, starts_ref, answer_ref, landed, arrived, packed):
    batch_count = answer_ref.shape[0]

    def each_used(what):
        @pl.loop(0, batch_count)
        def _(o):
            @pl.loop(0, pl.cdiv(counts_ref[o], piece))
            def _(c):
                part = pl.ds(pl.multiple_of(c * piece, piece), piece)
                what(
                    o,
                    c,
                    part,
                    pltpu.make_async_copy(
                        answer_ref.at[o, part], landed.at[o, part], arrived.at[o, c]
                    ),
                )

    def lay(o, c, part, copy):
        copy.wait()
        packed[pl.ds(pl.multiple_of(starts_ref[o] + c * piece, SLOTS), piece), :] = landed[o, part]

    each_used(lambda o, c, part, copy: copy.start())
    each_used(lay)
    end = starts_ref[batch_count]
    packed[pl.ds(pl.multiple_of(end, SLOTS), WIDE * TILE), :] = jnp.zeros(
        (WIDE * TILE, packed.shape[1]), packed.dtype
    )


def gather_sum_body(
    piece,
    last,
    row0,
    spans_ref,
    counts_ref,
    starts_ref,
    own_here_ref,
    answer_ref,
    notes_in,
    adj_ref,
    *refs,
):
    if last:
        (total_in, found_in, wself_in, wneigh_in, own_ref, mean_ref) = refs[:6]
        share_refs = refs[6:-11]
        packed, tiles_ref, ready, landed, arrived, notes_ref, carried = refs[-11:-4]
        total_ref, found_ref, wself_ref, wneigh_ref = refs[-4:]
        mine = pl.ds(row0, total_ref.shape[0])
        pairs = ((notes_in.at[mine], notes_ref), (total_in.at[mine], total_ref))
        pairs += ((found_in.at[mine], found_ref),)
        pairs += ((wself_in, wself_ref), (wneigh_in, wneigh_ref))
    else:
        total_ref, found_ref, packed, tiles_ref, ready, landed, arrived, notes_ref, carried = refs
        pairs = ((notes_in, notes_ref),)
    carry = [pltpu.make_async_copy(*pair, carried.at[n]) for n, pair in enumerate(pairs)]
    nodes = total_ref.shape[0]
    rows = math.gcd(adj_ref.shape[1], 3 * TILE)
    begin, count = spans_ref[0], spans_ref[1]

    def fetch(step, slot):
        return pltpu.make_async_copy(
            adj_ref.at[pl.ds(begin + step * WIDE, WIDE), pl.ds(row0, nodes)],
            tiles_ref.at[slot],
            ready.at[slot],
        )

    @pl.when(count > 0)
    def _():
        fetch(0, 0).start()

    for copy in carry:
        copy.start()
    collect(piece, counts_ref, starts_ref, answer_ref, landed, arrived, packed)
    for copy in carry:
        copy.wait()
    if not last:
        total_ref[...] = jnp.zeros(total_ref.shape, jnp.float32)
        found_ref[...] = jnp.zeros(found_ref.shape, jnp.float32)

    @pl.loop(0, count)
    def _(step):
        slot = step & 1

        @pl.when(step + 1 < count)
        def _():
            fetch(step + 1, 1 - slot).start()

        fetch(step, slot).wait()
        depth = WIDE * TILE
        block = packed[pl.ds(pl.multiple_of(step * depth, depth), depth), :]
        lane = lax.broadcasted_iota(jnp.int32, (rows, depth), 1) + (begin * TILE + step * depth)
        lane = lane.astype(jnp.float32)

        @pl.loop(0, nodes // rows)
        def _(r):
            part = pl.ds(pl.multiple_of(r * rows, rows), rows)
            near = jnp.concatenate(
                [tiles_ref[slot, w, part, :].astype(jnp.bfloat16) for w in range(WIDE)], axis=1
            )
            flag = (lax.div(begin, WIDE) + step) * (adj_ref.shape[1] // rows) + row0 // rows + r

            @pl.when(own_here_ref[flag] == 0)
            def _():
                total_ref[part, :] += jnp.dot(near, block, preferred_element_type=jnp.float32)

            @pl.when(own_here_ref[flag] != 0)
            def _():
                own = jnp.where(notes_ref[part, 0:1] == lane, 1.0, 0.0).astype(jnp.bfloat16)
                both = jnp.dot(
                    jnp.concatenate([near, own], axis=0), block, preferred_element_type=jnp.float32
                )
                total_ref[part, :] += both[:rows]
                found_ref[part, :] += both[rows:]

    if last:
        share = share_refs[0].shape[0]
        step_rows = math.gcd(share, 3 * TILE)
        for p, share_ref in enumerate(share_refs):
            for r in range(share // step_rows):
                part = pl.ds(p * share + r * step_rows, step_rows)
                own = found_ref[part, :].astype(jnp.bfloat16)
                mean = (total_ref[part, :] / notes_ref[part, 1:2]).astype(jnp.bfloat16)
                own_ref[part, :] = own
                mean_ref[part, :] = mean
                share_ref[pl.ds(r * step_rows, step_rows), :] = (
                    jnp.dot(own, wself_ref[...], preferred_element_type=jnp.float32)
                    + jnp.dot(mean, wneigh_ref[...], preferred_element_type=jnp.float32)
                ).astype(share_ref.dtype)


def gather_sum(inputs, scalars, answer, notes, adj, rest=None, row0=0, shares=()):
    batch_count, width, features = answer.shape
    tiles, nodes, _ = adj.shape
    nodes = sum(shares) or nodes
    piece = math.gcd(width, LANES)
    last = rest is not None
    room = min(batch_count * width, inputs) + SLOTS * batch_count + 2 * WIDE * TILE
    in_specs = [SMEM, SMEM, SMEM, SMEM, ANY, HBM, HBM]
    rows = lambda dtype: jax.ShapeDtypeStruct((nodes, features), dtype)
    scratch = [
        pltpu.VMEM((room, features), jnp.bfloat16),
        pltpu.VMEM((2, WIDE, nodes, TILE), adj.dtype),
        pltpu.SemaphoreType.DMA((2,)),
        pltpu.VMEM(answer.shape, answer.dtype),
        pltpu.SemaphoreType.DMA((batch_count, width // piece)),
        pltpu.VMEM((nodes, notes.shape[1]), notes.dtype),
        pltpu.SemaphoreType.DMA((5,)),
    ]
    operands = [answer, notes, adj]
    if last:
        operands += list(rest)
        in_specs += [HBM] * len(rest)
        out_shape = (rows(jnp.bfloat16), rows(jnp.bfloat16))
        out_shape += tuple(
            jax.ShapeDtypeStruct((n, rest[3].shape[1]), jnp.bfloat16) for n in shares
        )
        scratch += [pltpu.VMEM((nodes, features), jnp.float32)] * 2
        scratch += [pltpu.VMEM(x.shape, x.dtype) for x in rest[2:]]
    else:
        out_shape = (rows(jnp.float32), rows(jnp.float32))
    return pl.pallas_call(
        functools.partial(gather_sum_body, piece, last, row0),
        out_shape=out_shape,
        in_specs=in_specs,
        out_specs=(VMEM,) * len(out_shape),
        scratch_shapes=scratch,
        compiler_params=params(50),
        cost_estimate=cost(2 * nodes * features * TILE * tiles // (4 if last else 1), nodes * TILE),
        name="gather_sum",
    )(*scalars, *operands)


def share_order(array, parts, seeds):
    others = array.shape[0] - seeds
    own, rest = seeds // parts, others // parts
    tail = array.shape[1:]
    blocks = jnp.concatenate(
        [array[:seeds].reshape(parts, own, *tail), array[seeds:].reshape(parts, rest, *tail)],
        axis=1,
    )
    return ahead(blocks).reshape(array.shape)


def spread(part, axis, count):
    return lax.all_to_all(
        jnp.broadcast_to(part[None], (count,) + part.shape), axis, 0, 0, tiled=True
    )


def passed(part, shift, axis="feat"):
    parts = lax.axis_size(axis)
    return lax.ppermute(part, axis, [((i + shift) % parts, i) for i in range(parts)])


def turned(array, by):
    twice = jnp.concatenate([array, array], axis=0)
    return lax.dynamic_slice_in_dim(twice, by, array.shape[0], 0)


def ahead(array, axis="feat"):
    return turned(array, lax.axis_index(axis))


def in_order(blocks):
    parts = lax.axis_size("feat")
    total = jnp.zeros((parts,) + blocks[0].shape, blocks[0].dtype)
    for j, block in enumerate(blocks):
        spot = (lax.axis_index("feat") + j) % parts
        total = lax.dynamic_update_index_in_dim(total, block, spot, 0)
    return total


def spread_parts(part, axis="feat"):
    return [part] + [passed(part, j, axis) for j in range(1, lax.axis_size(axis))]


def sum_parts(blocks, axis="feat"):
    parts = lax.axis_size(axis)
    came = [blocks[0]] + [passed(blocks[j], -j, axis) for j in range(1, parts)]
    return sum(x.astype(jnp.float32) for x in came)


def swapped(part):
    return lax.ppermute(part, "batch", [(i, i ^ 1) for i in range(lax.axis_size("batch"))])


def total_over_batch(terms):
    count = lax.axis_size("batch")
    rows, width = terms.shape
    if count > FEW:
        pieces = terms.astype(jnp.bfloat16).reshape(count, rows // count, width)
        pieces = lax.all_to_all(pieces, "batch", 0, 0, tiled=True)
        total = jnp.sum(pieces.astype(jnp.float32), axis=0).astype(jnp.bfloat16)
        return spread(total, "batch", count).reshape(rows, width)
    chips = count // 2
    index = lax.axis_index("batch")
    first, chip = index % 2 == 0, index // 2
    upper, lower = terms[: rows // 2], terms[rows // 2 :]
    came = swapped(jnp.where(first, lower, upper).astype(jnp.bfloat16))
    mine = jnp.where(first, upper, lower) + came.astype(jnp.float32)
    pieces = turned(mine.reshape(chips, rows // count, width), chip)
    total = pieces[0]
    for j in range(1, chips):
        total = total + passed(pieces[j].astype(jnp.bfloat16), -2 * j, "batch").astype(jnp.float32)
    total = total.astype(jnp.bfloat16)
    mine = jnp.stack([total] + [passed(total, 2 * j, "batch") for j in range(1, chips)])
    other = swapped(mine)
    both = jnp.stack([jnp.where(first, mine, other), jnp.where(first, other, mine)], axis=1)
    return turned(both, (chips - chip) % chips).transpose(1, 0, 2, 3).reshape(rows, width)


def local(
    store,
    input_owner,
    input_row,
    nbr_one,
    deg_one,
    nbr_two,
    deg_two,
    cotangent,
    w1_self,
    w1_neigh,
    bias_one,
    w2_self,
    w2_neigh,
    bias_two,
):
    batch_count = lax.axis_size("batch")
    parts = lax.axis_size("feat")
    feat_index = lax.axis_index("feat")
    input_count = input_owner.shape[1]
    capacity = 2 * input_count // batch_count
    nodes = nbr_one.shape[1]
    seed_rows = nbr_two.shape[1]
    seeds = seed_rows * parts
    share = nodes // parts
    hidden_width = w1_self.shape[1]

    owners = input_owner.reshape(input_count // LANES, LANES)
    wanted = input_row.reshape(input_count // LANES, LANES)
    slots, counts, requests = make_requests(
        batch_count, capacity, store.shape[1] // LANES, owners, wanted
    )
    owners = owners.reshape(1, input_count)
    received = lax.all_to_all(
        requests.reshape(batch_count, capacity), "batch", split_axis=0, concat_axis=0, tiled=True
    )
    first = capacity * 13 // (24 * SLOTS) * SLOTS
    places = received.reshape(batch_count * capacity)
    looked_a = lookup(store, places, batch_count, 0, first, 60)
    near_first, looked_a = lax.optimization_barrier((nbr_one[0], looked_a))
    answer_a = lax.all_to_all(looked_a, "batch", split_axis=0, concat_axis=0, tiled=True)
    looked = lookup(store, places, batch_count, first, capacity - first, 24)

    depth = WIDE * TILE
    steps = -(-(input_count + 2 * (SLOTS - 1) * batch_count + depth - 1) // depth)
    tally = counts[:, 0]
    tally_a = jnp.minimum(tally, first)
    tally_b = tally - tally_a
    padded = lambda n: (n + SLOTS - 1) // SLOTS * SLOTS
    ends = lambda n: jnp.concatenate([jnp.zeros((1,), jnp.int32), jnp.cumsum(padded(n))])
    starts_a, starts_b = ends(tally_a), ends(tally_b)
    steps_a = (starts_a[batch_count] + depth - 1) // depth
    steps_b = (starts_b[batch_count] + depth - 1) // depth
    spans_a = jnp.stack([jnp.zeros_like(steps_a), steps_a])
    spans_b = jnp.stack([steps_a * WIDE, steps_b])
    slot = slots.reshape(1, input_count)
    shifted = jnp.where(
        slot < first,
        slot + starts_a[:batch_count, None],
        slot - first + steps_a * depth + starts_b[:batch_count, None],
    )
    mine = owners == jnp.arange(batch_count)[:, None]
    column = jnp.sum(jnp.where(mine, shifted, 0), axis=0)
    grid = jnp.pad(column.reshape(-1, LANES), ((0, LANES - input_count // LANES), (0, 0))).T
    finder = jnp.concatenate([grid // TILE, grid % TILE], axis=0).astype(jnp.bfloat16)
    notes = jnp.stack([column[:nodes], deg_one[0]], axis=1).astype(jnp.float32)
    notes = share_order(notes, parts, seeds)
    block = math.gcd(nodes, 3 * TILE)
    met = notes[:, 0].reshape(1, nodes // block, block) // depth
    met = met.astype(jnp.int32) == jnp.arange(steps)[:, None, None]
    own_here = jnp.any(met, axis=2).astype(jnp.int32).reshape(-1)

    fanout = nbr_one.shape[2]
    used = jnp.arange(fanout)[None, :] < deg_one[0][:, None]
    near = jnp.pad(jnp.where(used, near_first, -1), ((0, 0), (0, SLOTS - fanout)), constant_values=-1)
    me = feat_index.astype(jnp.int32).reshape(1)
    near = near.reshape(nodes // SLOTS, TILE)
    adj = adjacency(me, near, finder, steps * WIDE, parts, seeds)
    looked, answer_a, adj = lax.optimization_barrier((looked, answer_a, adj))
    answer_b = lax.all_to_all(looked, "batch", split_axis=0, concat_axis=0, tiled=True)

    scalars = (spans_a, tally_a, starts_a, own_here)
    total, found = gather_sum(input_count, scalars, answer_a, notes, adj)
    second = (nbr_two[0], deg_two, cotangent[0])
    total, second = lax.optimization_barrier((total, second))

    fanout_two = nbr_two.shape[2]
    used_two = jnp.arange(fanout_two)[:, None] < second[1]
    lists = jnp.concatenate([jnp.where(used_two, second[0].T, -1), second[1]], axis=0)
    lists = in_order(spread_parts(lists))
    upstream = in_order(spread_parts(second[2])).reshape(seeds, hidden_width)
    total, lists, upstream = lax.optimization_barrier((total, lists, upstream))

    near_two = lists[:, :fanout_two].transpose(1, 0, 2).reshape(fanout_two, seeds)
    deg_all = lists[:, fanout_two].reshape(seeds)
    rest = share - seed_rows
    after = near_two - seeds
    place = jnp.where(
        near_two < seeds,
        near_two // seed_rows * share + near_two % seed_rows,
        after // rest * share + seed_rows + after % rest,
    )
    place = jnp.where(near_two < 0, -1, place - feat_index * share)
    adj_two = jnp.sum(
        place[:, :, None] == jnp.arange(share)[None, None, :], axis=0, dtype=jnp.float32
    ).astype(jnp.bfloat16)

    def finish(begin, end):
        return gather_sum(
            input_count,
            (spans_b, tally_b, starts_b, own_here),
            answer_b,
            notes,
            adj,
            (total, found, w1_self, w1_neigh),
            begin * share,
            (share,) * (end - begin),
        )

    half = parts // 2
    cuts = [(half, parts), (1, half), (0, 1)]
    own_rows, mean_rows, z_blocks = [], [], []
    for begin, end in cuts:
        own, mean, *blocks = finish(begin, end)
        total, blocks = lax.optimization_barrier((total, blocks))
        own_rows.append(own)
        mean_rows.append(mean)
        z_blocks = blocks + z_blocks
    z_share = sum_parts(z_blocks) + bias_one
    hidden = jax.nn.silu(z_share).astype(jnp.bfloat16)

    agg_part = jnp.dot(adj_two, hidden, preferred_element_type=jnp.float32).astype(jnp.bfloat16)
    blocks = spread_parts(jnp.concatenate([agg_part, hidden[:seed_rows]]))
    deg_second = deg_all.astype(jnp.float32)[:, None]
    agg_two = sum(x[:seeds].astype(jnp.float32) for x in blocks) / deg_second
    agg_two = agg_two.astype(jnp.bfloat16)
    self_two = in_order([x[seeds:] for x in blocks]).reshape(seeds, hidden_width)
    z_two = (
        jnp.dot(self_two, w2_self, preferred_element_type=jnp.float32)
        + jnp.dot(agg_two, w2_neigh, preferred_element_type=jnp.float32)
        + bias_two
    )
    dz_two = (upstream.astype(jnp.float32) * silu_grad(z_two)).astype(jnp.bfloat16)
    mine = lambda x: lax.dynamic_slice_in_dim(x, feat_index * seed_rows, seed_rows, 0)
    activations = jax.nn.silu(mine(z_two)).astype(jnp.bfloat16)[None]

    back = contract_cols(dz_two, w2_neigh) / deg_second
    back_high = back.astype(jnp.bfloat16)
    back_low = (back - back_high.astype(jnp.float32)).astype(jnp.bfloat16)
    dh_share = contract_rows(adj_two, back_high) + contract_rows(adj_two, back_low)
    dh_share = dh_share + jnp.pad(contract_cols(mine(dz_two), w2_self), ((0, rest), (0, 0)))
    dz_share = (dh_share * silu_grad(z_share)).astype(jnp.bfloat16)
    dz_blocks = spread_parts(dz_share)
    dz_rows = [jnp.concatenate(dz_blocks[begin:end]) for begin, end in cuts]
    grads = [contract_rows(self_two, dz_two), contract_rows(agg_two, dz_two)]
    for rows in (own_rows, mean_rows):
        grads.append(sum(contract_rows(x, y) for x, y in zip(rows, dz_rows)))
    total = total_over_batch(jnp.concatenate(grads)).astype(jnp.float32)
    return (activations, *total.reshape(len(grads), -1, hidden_width))


def solution(mesh):
    in_specs = (
        P("batch", "feat"),
        P("batch", None, None),
        P("batch", None),
        P("batch", None, None),
        P("batch", None),
        P("batch", "feat", None),
        P("batch", "feat"),
        P("batch", "feat", None),
        P("feat", None),
        P("feat", None),
        P(),
        P(),
        P(),
        P(),
    )
    out_specs = (P("batch", "feat", None), P(), P(), P("feat", None), P("feat", None))
    return jax.shard_map(local, mesh=mesh, in_specs=in_specs, out_specs=out_specs, check_vma=False)
```

```python
import functools
import math

import jax
import jax.numpy as jnp
from jax import lax
from jax.experimental import pallas as pl
from jax.experimental.pallas import tpu as pltpu
from jax.sharding import PartitionSpec as P

TILE = 256
LANES = 128
SLOTS = 16
WIDE = 2
FEW = 16
TILE_BITS, LANE_BITS, SLOT_BITS = 8, 7, 4
MIB = 1024 * 1024
VMEM = pl.BlockSpec(memory_space=pltpu.VMEM)
SMEM = pl.BlockSpec(memory_space=pltpu.SMEM)
ANY = pl.BlockSpec(memory_space=pl.ANY)
HBM = pl.BlockSpec(memory_space=pltpu.HBM)


def silu_grad(values):
    sig = jax.nn.sigmoid(values)
    return sig * (1.0 + values * (1.0 - sig))


def contract_rows(left_side, right_side):
    return lax.dot_general(
        left_side, right_side, (((0,), (0,)), ((), ())), preferred_element_type=jnp.float32
    )


def contract_cols(left_side, right_side):
    return lax.dot_general(
        left_side, right_side, (((1,), (1,)), ((), ())), preferred_element_type=jnp.float32
    )


def params(mib):
    return pltpu.CompilerParams(vmem_limit_bytes=mib * MIB)


def cost(flops, moved):
    return pl.CostEstimate(flops=int(flops), bytes_accessed=int(moved), transcendentals=0)


def requests_body(
    batch_count,
    capacity,
    scale,
    owner_in,
    row_in,
    slot_ref,
    count_ref,
    request_ref,
    owner_ref,
    row_ref,
    came,
):
    copies = [
        pltpu.make_async_copy(owner_in, owner_ref, came.at[0]),
        pltpu.make_async_copy(row_in, row_ref, came.at[1]),
    ]
    for copy in copies:
        copy.start()
    for copy in copies:
        copy.wait()
    blocks, width = owner_ref.shape[0] // 2, TILE
    places = request_ref.shape[0]
    line = lambda ref, b: jnp.concatenate([ref[2 * b : 2 * b + 1], ref[2 * b + 1 : 2 * b + 2]], axis=1)
    owner_id = lax.broadcasted_iota(jnp.int32, (batch_count, width), 0)
    earlier = lax.broadcasted_iota(jnp.int32, (width, width), 0)
    later = lax.broadcasted_iota(jnp.int32, (width, width), 1)
    upper = jnp.where(earlier <= later, 1.0, 0.0).astype(jnp.bfloat16)
    high_id = lax.broadcasted_iota(jnp.int32, (places, width), 0)
    low_id = lax.broadcasted_iota(jnp.int32, (LANES, width), 0)
    marks = [
        jnp.where(line(owner_ref, b) == owner_id, 1.0, 0.0) for b in range(blocks)
    ]
    stacked = jnp.concatenate(marks, axis=0).astype(jnp.bfloat16)
    prefix = jnp.dot(stacked, upper, preferred_element_type=jnp.float32)
    running = jnp.zeros((batch_count, 1), jnp.float32)
    total = jnp.zeros((2 * places, LANES), jnp.float32)
    for b in range(blocks):
        part = prefix[b * batch_count : (b + 1) * batch_count]
        slots = jnp.sum(marks[b] * (part + running - 1.0), axis=0, keepdims=True)
        slots = slots.astype(jnp.int32)
        slot_ref[2 * b : 2 * b + 1, :] = slots[:, :LANES]
        slot_ref[2 * b + 1 : 2 * b + 2, :] = slots[:, LANES:]
        running = running + part[:, width - 1 : width]
        bucket = line(owner_ref, b) * capacity + slots
        rows = line(row_ref, b)
        hit = (bucket >> LANE_BITS) == high_id
        left = jnp.concatenate(
            [
                jnp.where(hit, (rows >> TILE_BITS).astype(jnp.float32), 0.0),
                jnp.where(hit, (rows & (TILE - 1)).astype(jnp.float32), 0.0),
            ],
            axis=0,
        ).astype(jnp.bfloat16)
        right = jnp.where((bucket & (LANES - 1)) == low_id, 1.0, 0.0).astype(jnp.bfloat16)
        total = total + contract_cols(left, right)
    count_ref[...] = jnp.broadcast_to(running, count_ref.shape).astype(jnp.int32)
    request_ref[...] = (total[:places] * TILE + total[places:]).astype(jnp.int32) * scale


def make_requests(batch_count, capacity, scale, owners, wanted):
    total = owners.shape[0] * LANES
    places = batch_count * capacity // LANES
    return pl.pallas_call(
        functools.partial(requests_body, batch_count, capacity, scale),
        out_shape=(
            jax.ShapeDtypeStruct(owners.shape, jnp.int32),
            jax.ShapeDtypeStruct((batch_count, LANES), jnp.int32),
            jax.ShapeDtypeStruct((places, LANES), jnp.int32),
        ),
        in_specs=[ANY, ANY],
        out_specs=(VMEM, VMEM, VMEM),
        scratch_shapes=[
            pltpu.VMEM(owners.shape, owners.dtype),
            pltpu.VMEM(wanted.shape, wanted.dtype),
            pltpu.SemaphoreType.DMA((2,)),
        ],
        compiler_params=params(58),
        cost_estimate=cost(4 * total * places * LANES, 24 * total),
        name="requests",
    )(owners, wanted)


def lookup_body(stride, first, width, want_ref, store_in, out_ref, table, lines, store_ref, came):
    rows_all = store_ref.shape[0]
    halves = store_ref.shape[1] // LANES
    lane = lambda h: pl.ds(h * LANES, LANES)
    begin = pl.program_id(0) * stride + first

    @pl.when(pl.program_id(0) == 0)
    def _():
        pieces = came.shape[0]
        depth = rows_all // pieces
        copies = [
            pltpu.make_async_copy(
                store_in.at[pl.ds(n * depth, depth)], store_ref.at[pl.ds(n * depth, depth)], came.at[n]
            )
            for n in range(pieces)
        ]
        for copy in copies:
            copy.start()
        for n, copy in enumerate(copies):
            copy.wait()

            @pl.loop(n * depth // TILE, (n + 1) * depth // TILE)
            def _(j):
                part = pl.ds(pl.multiple_of(j * TILE, TILE), TILE)
                for h in range(halves):
                    spot = pl.ds(pl.multiple_of(j * TILE * halves, TILE) + h, TILE, stride=halves)
                    table[spot, :] = store_ref[part, lane(h)].astype(jnp.float32)

    @pl.loop(0, width // SLOTS, unroll=math.gcd(width // SLOTS, 4))
    def _(j):
        at = [want_ref[begin + j * SLOTS + u] for u in range(SLOTS)]
        rows = [table[pl.ds(pl.multiple_of(a, halves), halves), :] for a in at]
        block = lines.at[pl.ds(pl.multiple_of(j * SLOTS * halves, SLOTS * halves), SLOTS * halves)]
        for u in range(SLOTS):
            block[pl.ds(u * halves, halves), :] = rows[u]

    for h in range(halves):
        out_ref[0, :, lane(h)] = lines[pl.ds(h, width, stride=halves), :].astype(jnp.bfloat16)


def lookup(store, places, groups, first, width, mib):
    rows_all, features = store.shape
    halves = features // LANES
    apart = lambda rows: pltpu.VMEM((rows * halves, LANES), jnp.float32)
    return pl.pallas_call(
        functools.partial(lookup_body, places.shape[0] // groups, first, width),
        out_shape=jax.ShapeDtypeStruct((groups, width, features), jnp.bfloat16),
        grid=(groups,),
        in_specs=[SMEM, HBM],
        out_specs=pl.BlockSpec((1, width, features), lambda g: (g, 0, 0)),
        scratch_shapes=[
            apart(rows_all),
            apart(width),
            pltpu.VMEM((rows_all, features), store.dtype),
            pltpu.SemaphoreType.DMA((4,)),
        ],
        compiler_params=params(mib),
        cost_estimate=cost(groups * width * features * 40, 2 * rows_all * features),
        name="lookup",
    )(places, store)


def adjacency_body(tiles, me_ref, near_ref, table_ref, out_ref):
    groups = near_ref.shape[0]
    node_high = lax.broadcasted_iota(jnp.int32, (LANES, TILE), 0)
    own_row = (
        lax.shift_right_logical(lax.broadcasted_iota(jnp.int32, (SLOTS, TILE), 1), SLOT_BITS)
        == lax.broadcasted_iota(jnp.int32, (SLOTS, TILE), 0)
    )
    low_id = lax.broadcasted_iota(jnp.int32, (TILE, TILE), 0).astype(jnp.float32)

    def one_group(g):
        near = near_ref[pl.ds(g, 1), :]
        pick = jnp.where((near >> LANE_BITS) == node_high, 1.0, 0.0).astype(jnp.bfloat16)
        found = jnp.dot(table_ref[...], pick, preferred_element_type=jnp.float32)
        here = (near & (LANES - 1)) == node_high
        high = jnp.sum(jnp.where(here, found[:LANES], 0.0), axis=0, keepdims=True)
        low = jnp.sum(jnp.where(here, found[LANES:], 0.0), axis=0, keepdims=True)
        high = jnp.where(near < 0, -1.0, high)
        rows = jnp.where(own_row, high, -1.0)
        left = jnp.concatenate(
            [jnp.where(rows == float(t), 1.0, 0.0) for t in range(tiles)], axis=0
        ).astype(jnp.bfloat16)
        right = jnp.where(low == low_id, 1.0, 0.0).astype(jnp.bfloat16)
        return contract_cols(left, right).reshape(tiles, SLOTS, TILE)

    @pl.loop(0, groups // 2, unroll=2)
    def _(j):
        pair = jnp.concatenate([one_group(2 * j), one_group(2 * j + 1)], axis=1)
        out_ref[:, pl.ds(pl.multiple_of(j * 2 * SLOTS, 2 * SLOTS), 2 * SLOTS), :] = pair.astype(
            out_ref.dtype
        )


def adjacency(me, near, table, tiles, parts, seeds):
    groups = near.shape[0]
    nodes = groups * SLOTS
    step = LANES // SLOTS
    own, rest, share = (n // parts // LANES for n in (seeds, nodes - seeds, nodes))

    def place(block, me_ref):
        after = block - own * parts
        is_own = after < 0
        part = jnp.where(is_own, lax.div(block, own), lax.div(after, rest))
        at = jnp.where(is_own, lax.rem(block, own), own + lax.rem(after, rest))
        return (0, lax.rem(part - me_ref[0] + parts, parts) * share + at, 0)

    return pl.pallas_call(
        functools.partial(adjacency_body, tiles),
        out_shape=jax.ShapeDtypeStruct((tiles, nodes, TILE), jnp.float8_e4m3fn),
        grid_spec=pltpu.PrefetchScalarGridSpec(
            num_scalar_prefetch=1,
            grid=(groups // step,),
            in_specs=[
                pl.BlockSpec((step, TILE), lambda r, me: (r, 0)),
                pl.BlockSpec(table.shape, lambda r, me: (0, 0)),
            ],
            out_specs=pl.BlockSpec((tiles, LANES, TILE), place),
        ),
        compiler_params=params(48),
        cost_estimate=cost(2 * nodes * TILE * TILE * tiles * 2, nodes * TILE * tiles),
        name="adjacency",
    )(me, near, table)


def collect(piece, counts_ref, starts_ref, answer_ref, landed, arrived, packed):
    batch_count = answer_ref.shape[0]

    def each_used(what):
        @pl.loop(0, batch_count)
        def _(o):
            @pl.loop(0, pl.cdiv(counts_ref[o], piece))
            def _(c):
                part = pl.ds(pl.multiple_of(c * piece, piece), piece)
                what(
                    o,
                    c,
                    part,
                    pltpu.make_async_copy(
                        answer_ref.at[o, part], landed.at[o, part], arrived.at[o, c]
                    ),
                )

    def lay(o, c, part, copy):
        copy.wait()
        packed[pl.ds(pl.multiple_of(starts_ref[o] + c * piece, SLOTS), piece), :] = landed[o, part]

    each_used(lambda o, c, part, copy: copy.start())
    each_used(lay)
    end = starts_ref[batch_count]
    packed[pl.ds(pl.multiple_of(end, SLOTS), WIDE * TILE), :] = jnp.zeros(
        (WIDE * TILE, packed.shape[1]), packed.dtype
    )


def gather_sum_body(
    piece,
    last,
    row0,
    spans_ref,
    counts_ref,
    starts_ref,
    own_here_ref,
    answer_ref,
    notes_in,
    adj_ref,
    *refs,
):
    if last:
        (total_in, found_in, wself_in, wneigh_in, own_ref, mean_ref) = refs[:6]
        share_refs = refs[6:-11]
        packed, tiles_ref, ready, landed, arrived, notes_ref, carried = refs[-11:-4]
        total_ref, found_ref, wself_ref, wneigh_ref = refs[-4:]
        mine = pl.ds(row0, total_ref.shape[0])
        pairs = ((notes_in.at[mine], notes_ref), (total_in.at[mine], total_ref))
        pairs += ((found_in.at[mine], found_ref),)
        pairs += ((wself_in, wself_ref), (wneigh_in, wneigh_ref))
    else:
        total_ref, found_ref, packed, tiles_ref, ready, landed, arrived, notes_ref, carried = refs
        pairs = ((notes_in, notes_ref),)
    carry = [pltpu.make_async_copy(*pair, carried.at[n]) for n, pair in enumerate(pairs)]
    nodes = total_ref.shape[0]
    rows = math.gcd(adj_ref.shape[1], 3 * TILE)
    begin, count = spans_ref[0], spans_ref[1]

    def fetch(step, slot):
        return pltpu.make_async_copy(
            adj_ref.at[pl.ds(begin + step * WIDE, WIDE), pl.ds(row0, nodes)],
            tiles_ref.at[slot],
            ready.at[slot],
        )

    @pl.when(count > 0)
    def _():
        fetch(0, 0).start()

    for copy in carry:
        copy.start()
    collect(piece, counts_ref, starts_ref, answer_ref, landed, arrived, packed)
    for copy in carry:
        copy.wait()
    if not last:
        total_ref[...] = jnp.zeros(total_ref.shape, jnp.float32)
        found_ref[...] = jnp.zeros(found_ref.shape, jnp.float32)

    @pl.loop(0, count)
    def _(step):
        slot = step & 1

        @pl.when(step + 1 < count)
        def _():
            fetch(step + 1, 1 - slot).start()

        fetch(step, slot).wait()
        depth = WIDE * TILE
        block = packed[pl.ds(pl.multiple_of(step * depth, depth), depth), :]
        lane = lax.broadcasted_iota(jnp.int32, (rows, depth), 1) + (begin * TILE + step * depth)
        lane = lane.astype(jnp.float32)

        @pl.loop(0, nodes // rows)
        def _(r):
            part = pl.ds(pl.multiple_of(r * rows, rows), rows)
            near = jnp.concatenate(
                [tiles_ref[slot, w, part, :].astype(jnp.bfloat16) for w in range(WIDE)], axis=1
            )
            flag = (lax.div(begin, WIDE) + step) * (adj_ref.shape[1] // rows) + row0 // rows + r

            @pl.when(own_here_ref[flag] == 0)
            def _():
                total_ref[part, :] += jnp.dot(near, block, preferred_element_type=jnp.float32)

            @pl.when(own_here_ref[flag] != 0)
            def _():
                own = jnp.where(notes_ref[part, 0:1] == lane, 1.0, 0.0).astype(jnp.bfloat16)
                both = jnp.dot(
                    jnp.concatenate([near, own], axis=0), block, preferred_element_type=jnp.float32
                )
                total_ref[part, :] += both[:rows]
                found_ref[part, :] += both[rows:]

    if last:
        share = share_refs[0].shape[0]
        step_rows = math.gcd(share, 3 * TILE)
        for p, share_ref in enumerate(share_refs):
            for r in range(share // step_rows):
                part = pl.ds(p * share + r * step_rows, step_rows)
                own = found_ref[part, :].astype(jnp.bfloat16)
                mean = (total_ref[part, :] / notes_ref[part, 1:2]).astype(jnp.bfloat16)
                own_ref[part, :] = own
                mean_ref[part, :] = mean
                share_ref[pl.ds(r * step_rows, step_rows), :] = (
                    jnp.dot(own, wself_ref[...], preferred_element_type=jnp.float32)
                    + jnp.dot(mean, wneigh_ref[...], preferred_element_type=jnp.float32)
                ).astype(share_ref.dtype)


def gather_sum(inputs, scalars, answer, notes, adj, rest=None, row0=0, shares=()):
    batch_count, width, features = answer.shape
    tiles, nodes, _ = adj.shape
    nodes = sum(shares) or nodes
    piece = math.gcd(width, LANES)
    last = rest is not None
    room = min(batch_count * width, inputs) + SLOTS * batch_count + 2 * WIDE * TILE
    in_specs = [SMEM, SMEM, SMEM, SMEM, ANY, HBM, HBM]
    rows = lambda dtype: jax.ShapeDtypeStruct((nodes, features), dtype)
    scratch = [
        pltpu.VMEM((room, features), jnp.bfloat16),
        pltpu.VMEM((2, WIDE, nodes, TILE), adj.dtype),
        pltpu.SemaphoreType.DMA((2,)),
        pltpu.VMEM(answer.shape, answer.dtype),
        pltpu.SemaphoreType.DMA((batch_count, width // piece)),
        pltpu.VMEM((nodes, notes.shape[1]), notes.dtype),
        pltpu.SemaphoreType.DMA((5,)),
    ]
    operands = [answer, notes, adj]
    if last:
        operands += list(rest)
        in_specs += [HBM] * len(rest)
        out_shape = (rows(jnp.bfloat16), rows(jnp.bfloat16))
        out_shape += tuple(
            jax.ShapeDtypeStruct((n, rest[3].shape[1]), jnp.bfloat16) for n in shares
        )
        scratch += [pltpu.VMEM((nodes, features), jnp.float32)] * 2
        scratch += [pltpu.VMEM(x.shape, x.dtype) for x in rest[2:]]
    else:
        out_shape = (rows(jnp.float32), rows(jnp.float32))
    return pl.pallas_call(
        functools.partial(gather_sum_body, piece, last, row0),
        out_shape=out_shape,
        in_specs=in_specs,
        out_specs=(VMEM,) * len(out_shape),
        scratch_shapes=scratch,
        compiler_params=params(50),
        cost_estimate=cost(2 * nodes * features * TILE * tiles // (4 if last else 1), nodes * TILE),
        name="gather_sum",
    )(*scalars, *operands)


def share_order(array, parts, seeds):
    others = array.shape[0] - seeds
    own, rest = seeds // parts, others // parts
    tail = array.shape[1:]
    blocks = jnp.concatenate(
        [array[:seeds].reshape(parts, own, *tail), array[seeds:].reshape(parts, rest, *tail)],
        axis=1,
    )
    return ahead(blocks).reshape(array.shape)


def spread(part, axis, count):
    return lax.all_to_all(
        jnp.broadcast_to(part[None], (count,) + part.shape), axis, 0, 0, tiled=True
    )


def passed(part, shift, axis="feat"):
    parts = lax.axis_size(axis)
    return lax.ppermute(part, axis, [((i + shift) % parts, i) for i in range(parts)])


def turned(array, by):
    twice = jnp.concatenate([array, array], axis=0)
    return lax.dynamic_slice_in_dim(twice, by, array.shape[0], 0)


def ahead(array, axis="feat"):
    return turned(array, lax.axis_index(axis))


def in_order(blocks):
    parts = lax.axis_size("feat")
    total = jnp.zeros((parts,) + blocks[0].shape, blocks[0].dtype)
    for j, block in enumerate(blocks):
        spot = (lax.axis_index("feat") + j) % parts
        total = lax.dynamic_update_index_in_dim(total, block, spot, 0)
    return total


def spread_parts(part, axis="feat"):
    return [part] + [passed(part, j, axis) for j in range(1, lax.axis_size(axis))]


def sum_parts(blocks, axis="feat"):
    parts = lax.axis_size(axis)
    came = [blocks[0]] + [passed(blocks[j], -j, axis) for j in range(1, parts)]
    return sum(x.astype(jnp.float32) for x in came)


def swapped(part):
    return lax.ppermute(part, "batch", [(i, i ^ 1) for i in range(lax.axis_size("batch"))])


def total_over_batch(terms):
    count = lax.axis_size("batch")
    rows, width = terms.shape
    if count > FEW:
        pieces = terms.astype(jnp.bfloat16).reshape(count, rows // count, width)
        pieces = lax.all_to_all(pieces, "batch", 0, 0, tiled=True)
        total = jnp.sum(pieces.astype(jnp.float32), axis=0).astype(jnp.bfloat16)
        return spread(total, "batch", count).reshape(rows, width)
    chips = count // 2
    index = lax.axis_index("batch")
    first, chip = index % 2 == 0, index // 2
    upper, lower = terms[: rows // 2], terms[rows // 2 :]
    came = swapped(jnp.where(first, lower, upper).astype(jnp.bfloat16))
    mine = jnp.where(first, upper, lower) + came.astype(jnp.float32)
    pieces = turned(mine.reshape(chips, rows // count, width), chip)
    total = pieces[0]
    for j in range(1, chips):
        total = total + passed(pieces[j].astype(jnp.bfloat16), -2 * j, "batch").astype(jnp.float32)
    total = total.astype(jnp.bfloat16)
    mine = jnp.stack([total] + [passed(total, 2 * j, "batch") for j in range(1, chips)])
    other = swapped(mine)
    both = jnp.stack([jnp.where(first, mine, other), jnp.where(first, other, mine)], axis=1)
    return turned(both, (chips - chip) % chips).transpose(1, 0, 2, 3).reshape(rows, width)


def local(
    store,
    input_owner,
    input_row,
    nbr_one,
    deg_one,
    nbr_two,
    deg_two,
    cotangent,
    w1_self,
    w1_neigh,
    bias_one,
    w2_self,
    w2_neigh,
    bias_two,
):
    batch_count = lax.axis_size("batch")
    parts = lax.axis_size("feat")
    feat_index = lax.axis_index("feat")
    input_count = input_owner.shape[1]
    capacity = 2 * input_count // batch_count
    nodes = nbr_one.shape[1]
    seed_rows = nbr_two.shape[1]
    seeds = seed_rows * parts
    share = nodes // parts
    hidden_width = w1_self.shape[1]

    owners = input_owner.reshape(input_count // LANES, LANES)
    wanted = input_row.reshape(input_count // LANES, LANES)
    slots, counts, requests = make_requests(
        batch_count, capacity, store.shape[1] // LANES, owners, wanted
    )
    owners = owners.reshape(1, input_count)
    received = lax.all_to_all(
        requests.reshape(batch_count, capacity), "batch", split_axis=0, concat_axis=0, tiled=True
    )
    first = capacity * 13 // (24 * SLOTS) * SLOTS
    places = received.reshape(batch_count * capacity)
    looked_a = lookup(store, places, batch_count, 0, first, 60)
    near_first, looked_a = lax.optimization_barrier((nbr_one[0], looked_a))
    answer_a = lax.all_to_all(looked_a, "batch", split_axis=0, concat_axis=0, tiled=True)
    looked = lookup(store, places, batch_count, first, capacity - first, 24)

    depth = WIDE * TILE
    steps = -(-(input_count + 2 * (SLOTS - 1) * batch_count + depth - 1) // depth)
    tally = counts[:, 0]
    tally_a = jnp.minimum(tally, first)
    tally_b = tally - tally_a
    padded = lambda n: (n + SLOTS - 1) // SLOTS * SLOTS
    ends = lambda n: jnp.concatenate([jnp.zeros((1,), jnp.int32), jnp.cumsum(padded(n))])
    starts_a, starts_b = ends(tally_a), ends(tally_b)
    steps_a = (starts_a[batch_count] + depth - 1) // depth
    steps_b = (starts_b[batch_count] + depth - 1) // depth
    spans_a = jnp.stack([jnp.zeros_like(steps_a), steps_a])
    spans_b = jnp.stack([steps_a * WIDE, steps_b])
    slot = slots.reshape(1, input_count)
    shifted = jnp.where(
        slot < first,
        slot + starts_a[:batch_count, None],
        slot - first + steps_a * depth + starts_b[:batch_count, None],
    )
    mine = owners == jnp.arange(batch_count)[:, None]
    column = jnp.sum(jnp.where(mine, shifted, 0), axis=0)
    grid = jnp.pad(column.reshape(-1, LANES), ((0, LANES - input_count // LANES), (0, 0))).T
    finder = jnp.concatenate([grid // TILE, grid % TILE], axis=0).astype(jnp.bfloat16)
    notes = jnp.stack([column[:nodes], deg_one[0]], axis=1).astype(jnp.float32)
    notes = share_order(notes, parts, seeds)
    block = math.gcd(nodes, 3 * TILE)
    met = notes[:, 0].reshape(1, nodes // block, block) // depth
    met = met.astype(jnp.int32) == jnp.arange(steps)[:, None, None]
    own_here = jnp.any(met, axis=2).astype(jnp.int32).reshape(-1)

    fanout = nbr_one.shape[2]
    used = jnp.arange(fanout)[None, :] < deg_one[0][:, None]
    near = jnp.pad(jnp.where(used, near_first, -1), ((0, 0), (0, SLOTS - fanout)), constant_values=-1)
    me = feat_index.astype(jnp.int32).reshape(1)
    near = near.reshape(nodes // SLOTS, TILE)
    adj = adjacency(me, near, finder, steps * WIDE, parts, seeds)
    looked, answer_a, adj = lax.optimization_barrier((looked, answer_a, adj))
    answer_b = lax.all_to_all(looked, "batch", split_axis=0, concat_axis=0, tiled=True)

    scalars = (spans_a, tally_a, starts_a, own_here)
    total, found = gather_sum(input_count, scalars, answer_a, notes, adj)
    second = (nbr_two[0], deg_two, cotangent[0])
    total, second = lax.optimization_barrier((total, second))

    fanout_two = nbr_two.shape[2]
    used_two = jnp.arange(fanout_two)[:, None] < second[1]
    lists = jnp.concatenate([jnp.where(used_two, second[0].T, -1), second[1]], axis=0)
    lists = in_order(spread_parts(lists))
    upstream = in_order(spread_parts(second[2])).reshape(seeds, hidden_width)
    total, lists, upstream = lax.optimization_barrier((total, lists, upstream))

    near_two = lists[:, :fanout_two].transpose(1, 0, 2).reshape(fanout_two, seeds)
    deg_all = lists[:, fanout_two].reshape(seeds)
    rest = share - seed_rows
    after = near_two - seeds
    place = jnp.where(
        near_two < seeds,
        near_two // seed_rows * share + near_two % seed_rows,
        after // rest * share + seed_rows + after % rest,
    )
    place = jnp.where(near_two < 0, -1, place - feat_index * share)
    adj_two = jnp.sum(
        place[:, :, None] == jnp.arange(share)[None, None, :], axis=0, dtype=jnp.float32
    ).astype(jnp.bfloat16)

    def finish(begin, end):
        return gather_sum(
            input_count,
            (spans_b, tally_b, starts_b, own_here),
            answer_b,
            notes,
            adj,
            (total, found, w1_self, w1_neigh),
            begin * share,
            (share,) * (end - begin),
        )

    half = parts // 2
    cuts = [(half, parts), (1, half), (0, 1)]
    own_rows, mean_rows, z_blocks = [], [], []
    for begin, end in cuts:
        own, mean, *blocks = finish(begin, end)
        total, blocks = lax.optimization_barrier((total, blocks))
        own_rows.append(own)
        mean_rows.append(mean)
        z_blocks = blocks + z_blocks
    z_share = sum_parts(z_blocks) + bias_one
    hidden = jax.nn.silu(z_share).astype(jnp.bfloat16)

    agg_part = jnp.dot(adj_two, hidden, preferred_element_type=jnp.float32).astype(jnp.bfloat16)
    blocks = spread_parts(jnp.concatenate([agg_part, hidden[:seed_rows]]))
    deg_second = deg_all.astype(jnp.float32)[:, None]
    agg_two = sum(x[:seeds].astype(jnp.float32) for x in blocks) / deg_second
    agg_two = agg_two.astype(jnp.bfloat16)
    self_two = in_order([x[seeds:] for x in blocks]).reshape(seeds, hidden_width)
    z_two = (
        jnp.dot(self_two, w2_self, preferred_element_type=jnp.float32)
        + jnp.dot(agg_two, w2_neigh, preferred_element_type=jnp.float32)
        + bias_two
    )
    dz_two = (upstream.astype(jnp.float32) * silu_grad(z_two)).astype(jnp.bfloat16)
    mine = lambda x: lax.dynamic_slice_in_dim(x, feat_index * seed_rows, seed_rows, 0)
    activations = jax.nn.silu(mine(z_two)).astype(jnp.bfloat16)[None]

    back = contract_cols(dz_two, w2_neigh) / deg_second
    back_high = back.astype(jnp.bfloat16)
    back_low = (back - back_high.astype(jnp.float32)).astype(jnp.bfloat16)
    dh_share = contract_rows(adj_two, back_high) + contract_rows(adj_two, back_low)
    dh_share = dh_share + jnp.pad(contract_cols(mine(dz_two), w2_self), ((0, rest), (0, 0)))
    dz_share = (dh_share * silu_grad(z_share)).astype(jnp.bfloat16)
    dz_blocks = spread_parts(dz_share)
    dz_rows = [jnp.concatenate(dz_blocks[begin:end]) for begin, end in cuts]
    grads = [contract_rows(self_two, dz_two), contract_rows(agg_two, dz_two)]
    for rows in (own_rows, mean_rows):
        grads.append(sum(contract_rows(x, y) for x, y in zip(rows, dz_rows)))
    total = total_over_batch(jnp.concatenate(grads)).astype(jnp.float32)
    return (activations, *total.reshape(len(grads), -1, hidden_width))


def solution(mesh):
    in_specs = (
        P("batch", "feat"),
        P("batch", None, None),
        P("batch", None),
        P("batch", None, None),
        P("batch", None),
        P("batch", "feat", None),
        P("batch", "feat"),
        P("batch", "feat", None),
        P("feat", None),
        P("feat", None),
        P(),
        P(),
        P(),
        P(),
    )
    out_specs = (P("batch", "feat", None), P(), P(), P("feat", None), P("feat", None))
    return jax.shard_map(local, mesh=mesh, in_specs=in_specs, out_specs=out_specs, check_vma=False)
```

```python
import functools
import math

import jax
import jax.numpy as jnp
from jax import lax
from jax.experimental import pallas as pl
from jax.experimental.pallas import tpu as pltpu
from jax.sharding import PartitionSpec as P

TILE = 256
LANES = 128
SLOTS = 16
WIDE = 2
FEW = 16
TILE_BITS, LANE_BITS, SLOT_BITS = 8, 7, 4
MIB = 1024 * 1024
VMEM = pl.BlockSpec(memory_space=pltpu.VMEM)
SMEM = pl.BlockSpec(memory_space=pltpu.SMEM)
ANY = pl.BlockSpec(memory_space=pl.ANY)
HBM = pl.BlockSpec(memory_space=pltpu.HBM)


def silu_grad(values):
    sig = jax.nn.sigmoid(values)
    return sig * (1.0 + values * (1.0 - sig))


def contract_rows(left_side, right_side):
    return lax.dot_general(
        left_side, right_side, (((0,), (0,)), ((), ())), preferred_element_type=jnp.float32
    )


def contract_cols(left_side, right_side):
    return lax.dot_general(
        left_side, right_side, (((1,), (1,)), ((), ())), preferred_element_type=jnp.float32
    )


def params(mib):
    return pltpu.CompilerParams(vmem_limit_bytes=mib * MIB)


def cost(flops, moved):
    return pl.CostEstimate(flops=int(flops), bytes_accessed=int(moved), transcendentals=0)


def requests_body(
    batch_count,
    capacity,
    scale,
    owner_in,
    row_in,
    slot_ref,
    count_ref,
    request_ref,
    owner_ref,
    row_ref,
    came,
):
    copies = [
        pltpu.make_async_copy(owner_in, owner_ref, came.at[0]),
        pltpu.make_async_copy(row_in, row_ref, came.at[1]),
    ]
    for copy in copies:
        copy.start()
    for copy in copies:
        copy.wait()
    blocks, width = owner_ref.shape[0] // 2, TILE
    places = request_ref.shape[0]
    line = lambda ref, b: jnp.concatenate([ref[2 * b : 2 * b + 1], ref[2 * b + 1 : 2 * b + 2]], axis=1)
    owner_id = lax.broadcasted_iota(jnp.int32, (batch_count, width), 0)
    earlier = lax.broadcasted_iota(jnp.int32, (width, width), 0)
    later = lax.broadcasted_iota(jnp.int32, (width, width), 1)
    upper = jnp.where(earlier <= later, 1.0, 0.0).astype(jnp.bfloat16)
    high_id = lax.broadcasted_iota(jnp.int32, (places, width), 0)
    low_id = lax.broadcasted_iota(jnp.int32, (LANES, width), 0)
    marks = [
        jnp.where(line(owner_ref, b) == owner_id, 1.0, 0.0) for b in range(blocks)
    ]
    stacked = jnp.concatenate(marks, axis=0).astype(jnp.bfloat16)
    prefix = jnp.dot(stacked, upper, preferred_element_type=jnp.float32)
    running = jnp.zeros((batch_count, 1), jnp.float32)
    total = jnp.zeros((2 * places, LANES), jnp.float32)
    for b in range(blocks):
        part = prefix[b * batch_count : (b + 1) * batch_count]
        slots = jnp.sum(marks[b] * (part + running - 1.0), axis=0, keepdims=True)
        slots = slots.astype(jnp.int32)
        slot_ref[2 * b : 2 * b + 1, :] = slots[:, :LANES]
        slot_ref[2 * b + 1 : 2 * b + 2, :] = slots[:, LANES:]
        running = running + part[:, width - 1 : width]
        bucket = line(owner_ref, b) * capacity + slots
        rows = line(row_ref, b)
        hit = (bucket >> LANE_BITS) == high_id
        left = jnp.concatenate(
            [
                jnp.where(hit, (rows >> TILE_BITS).astype(jnp.float32), 0.0),
                jnp.where(hit, (rows & (TILE - 1)).astype(jnp.float32), 0.0),
            ],
            axis=0,
        ).astype(jnp.bfloat16)
        right = jnp.where((bucket & (LANES - 1)) == low_id, 1.0, 0.0).astype(jnp.bfloat16)
        total = total + contract_cols(left, right)
    count_ref[...] = jnp.broadcast_to(running, count_ref.shape).astype(jnp.int32)
    request_ref[...] = (total[:places] * TILE + total[places:]).astype(jnp.int32) * scale


def make_requests(batch_count, capacity, scale, owners, wanted):
    total = owners.shape[0] * LANES
    places = batch_count * capacity // LANES
    return pl.pallas_call(
        functools.partial(requests_body, batch_count, capacity, scale),
        out_shape=(
            jax.ShapeDtypeStruct(owners.shape, jnp.int32),
            jax.ShapeDtypeStruct((batch_count, LANES), jnp.int32),
            jax.ShapeDtypeStruct((places, LANES), jnp.int32),
        ),
        in_specs=[ANY, ANY],
        out_specs=(VMEM, VMEM, VMEM),
        scratch_shapes=[
            pltpu.VMEM(owners.shape, owners.dtype),
            pltpu.VMEM(wanted.shape, wanted.dtype),
            pltpu.SemaphoreType.DMA((2,)),
        ],
        compiler_params=params(58),
        cost_estimate=cost(4 * total * places * LANES, 24 * total),
        name="requests",
    )(owners, wanted)


def lookup_body(stride, first, width, want_ref, store_in, out_ref, table, lines, store_ref, came):
    rows_all = store_ref.shape[0]
    halves = store_ref.shape[1] // LANES
    lane = lambda h: pl.ds(h * LANES, LANES)
    begin = pl.program_id(0) * stride + first

    @pl.when(pl.program_id(0) == 0)
    def _():
        pieces = came.shape[0]
        depth = rows_all // pieces
        copies = [
            pltpu.make_async_copy(
                store_in.at[pl.ds(n * depth, depth)], store_ref.at[pl.ds(n * depth, depth)], came.at[n]
            )
            for n in range(pieces)
        ]
        for copy in copies:
            copy.start()
        for n, copy in enumerate(copies):
            copy.wait()

            @pl.loop(n * depth // TILE, (n + 1) * depth // TILE)
            def _(j):
                part = pl.ds(pl.multiple_of(j * TILE, TILE), TILE)
                for h in range(halves):
                    spot = pl.ds(pl.multiple_of(j * TILE * halves, TILE) + h, TILE, stride=halves)
                    table[spot, :] = store_ref[part, lane(h)].astype(jnp.float32)

    @pl.loop(0, width // SLOTS, unroll=math.gcd(width // SLOTS, 4))
    def _(j):
        at = [want_ref[begin + j * SLOTS + u] for u in range(SLOTS)]
        rows = [table[pl.ds(pl.multiple_of(a, halves), halves), :] for a in at]
        block = lines.at[pl.ds(pl.multiple_of(j * SLOTS * halves, SLOTS * halves), SLOTS * halves)]
        for u in range(SLOTS):
            block[pl.ds(u * halves, halves), :] = rows[u]

    for h in range(halves):
        out_ref[0, :, lane(h)] = lines[pl.ds(h, width, stride=halves), :].astype(jnp.bfloat16)


def lookup(store, places, groups, first, width, mib):
    rows_all, features = store.shape
    halves = features // LANES
    apart = lambda rows: pltpu.VMEM((rows * halves, LANES), jnp.float32)
    return pl.pallas_call(
        functools.partial(lookup_body, places.shape[0] // groups, first, width),
        out_shape=jax.ShapeDtypeStruct((groups, width, features), jnp.bfloat16),
        grid=(groups,),
        in_specs=[SMEM, HBM],
        out_specs=pl.BlockSpec((1, width, features), lambda g: (g, 0, 0)),
        scratch_shapes=[
            apart(rows_all),
            apart(width),
            pltpu.VMEM((rows_all, features), store.dtype),
            pltpu.SemaphoreType.DMA((4,)),
        ],
        compiler_params=params(mib),
        cost_estimate=cost(groups * width * features * 40, 2 * rows_all * features),
        name="lookup",
    )(places, store)


def adjacency_body(tiles, me_ref, near_ref, table_ref, out_ref):
    groups = near_ref.shape[0]
    node_high = lax.broadcasted_iota(jnp.int32, (LANES, TILE), 0)
    own_row = (
        lax.shift_right_logical(lax.broadcasted_iota(jnp.int32, (SLOTS, TILE), 1), SLOT_BITS)
        == lax.broadcasted_iota(jnp.int32, (SLOTS, TILE), 0)
    )
    low_id = lax.broadcasted_iota(jnp.int32, (TILE, TILE), 0).astype(jnp.float32)

    def one_group(g):
        near = near_ref[pl.ds(g, 1), :]
        pick = jnp.where((near >> LANE_BITS) == node_high, 1.0, 0.0).astype(jnp.bfloat16)
        found = jnp.dot(table_ref[...], pick, preferred_element_type=jnp.float32)
        here = (near & (LANES - 1)) == node_high
        high = jnp.sum(jnp.where(here, found[:LANES], 0.0), axis=0, keepdims=True)
        low = jnp.sum(jnp.where(here, found[LANES:], 0.0), axis=0, keepdims=True)
        high = jnp.where(near < 0, -1.0, high)
        rows = jnp.where(own_row, high, -1.0)
        left = jnp.concatenate(
            [jnp.where(rows == float(t), 1.0, 0.0) for t in range(tiles)], axis=0
        ).astype(jnp.bfloat16)
        right = jnp.where(low == low_id, 1.0, 0.0).astype(jnp.bfloat16)
        return contract_cols(left, right).reshape(tiles, SLOTS, TILE)

    @pl.loop(0, groups // 2, unroll=2)
    def _(j):
        pair = jnp.concatenate([one_group(2 * j), one_group(2 * j + 1)], axis=1)
        out_ref[:, pl.ds(pl.multiple_of(j * 2 * SLOTS, 2 * SLOTS), 2 * SLOTS), :] = pair.astype(
            out_ref.dtype
        )


def adjacency(me, near, table, tiles, parts, seeds):
    groups = near.shape[0]
    nodes = groups * SLOTS
    step = LANES // SLOTS
    own, rest, share = (n // parts // LANES for n in (seeds, nodes - seeds, nodes))

    def place(block, me_ref):
        after = block - own * parts
        is_own = after < 0
        part = jnp.where(is_own, lax.div(block, own), lax.div(after, rest))
        at = jnp.where(is_own, lax.rem(block, own), own + lax.rem(after, rest))
        return (0, lax.rem(part - me_ref[0] + parts, parts) * share + at, 0)

    return pl.pallas_call(
        functools.partial(adjacency_body, tiles),
        out_shape=jax.ShapeDtypeStruct((tiles, nodes, TILE), jnp.float8_e4m3fn),
        grid_spec=pltpu.PrefetchScalarGridSpec(
            num_scalar_prefetch=1,
            grid=(groups // step,),
            in_specs=[
                pl.BlockSpec((step, TILE), lambda r, me: (r, 0)),
                pl.BlockSpec(table.shape, lambda r, me: (0, 0)),
            ],
            out_specs=pl.BlockSpec((tiles, LANES, TILE), place),
        ),
        compiler_params=params(48),
        cost_estimate=cost(2 * nodes * TILE * TILE * tiles * 2, nodes * TILE * tiles),
        name="adjacency",
    )(me, near, table)


def collect(piece, counts_ref, starts_ref, answer_ref, landed, arrived, packed):
    batch_count = answer_ref.shape[0]

    def each_used(what):
        @pl.loop(0, batch_count)
        def _(o):
            @pl.loop(0, pl.cdiv(counts_ref[o], piece))
            def _(c):
                part = pl.ds(pl.multiple_of(c * piece, piece), piece)
                what(
                    o,
                    c,
                    part,
                    pltpu.make_async_copy(
                        answer_ref.at[o, part], landed.at[o, part], arrived.at[o, c]
                    ),
                )

    def lay(o, c, part, copy):
        copy.wait()
        packed[pl.ds(pl.multiple_of(starts_ref[o] + c * piece, SLOTS), piece), :] = landed[o, part]

    each_used(lambda o, c, part, copy: copy.start())
    each_used(lay)
    end = starts_ref[batch_count]
    packed[pl.ds(pl.multiple_of(end, SLOTS), WIDE * TILE), :] = jnp.zeros(
        (WIDE * TILE, packed.shape[1]), packed.dtype
    )


def gather_sum_body(
    piece,
    last,
    row0,
    spans_ref,
    counts_ref,
    starts_ref,
    own_here_ref,
    answer_ref,
    notes_in,
    adj_ref,
    *refs,
):
    if last:
        (total_in, found_in, wself_in, wneigh_in, own_ref, mean_ref) = refs[:6]
        share_refs = refs[6:-13]
        packed, tiles_ref, ready, landed, arrived, notes_ref, carried = refs[-13:-6]
        total_ref, found_ref, before_ref, had_ref, wself_ref, wneigh_ref = refs[-6:]
        mine = pl.ds(row0, total_ref.shape[0])
        pairs = ((notes_in.at[mine], notes_ref), (total_in.at[mine], before_ref))
        pairs += ((found_in.at[mine], had_ref),)
        pairs += ((wself_in, wself_ref), (wneigh_in, wneigh_ref))
    else:
        total_ref, found_ref, packed, tiles_ref, ready, landed, arrived, notes_ref, carried = refs
        pairs = ((notes_in, notes_ref),)
    carry = [pltpu.make_async_copy(*pair, carried.at[n]) for n, pair in enumerate(pairs)]
    nodes = total_ref.shape[0]
    rows = math.gcd(adj_ref.shape[1], 3 * TILE)
    begin, count = spans_ref[0], spans_ref[1]

    def fetch(step, slot):
        return pltpu.make_async_copy(
            adj_ref.at[pl.ds(begin + step * WIDE, WIDE), pl.ds(row0, nodes)],
            tiles_ref.at[slot],
            ready.at[slot],
        )

    @pl.when(count > 0)
    def _():
        fetch(0, 0).start()

    for copy in carry:
        copy.start()
    collect(piece, counts_ref, starts_ref, answer_ref, landed, arrived, packed)
    total_ref[...] = jnp.zeros(total_ref.shape, jnp.float32)
    found_ref[...] = jnp.zeros(found_ref.shape, jnp.float32)
    carry[0].wait()

    @pl.loop(0, count)
    def _(step):
        slot = step & 1

        @pl.when(step + 1 < count)
        def _():
            fetch(step + 1, 1 - slot).start()

        fetch(step, slot).wait()
        depth = WIDE * TILE
        block = packed[pl.ds(pl.multiple_of(step * depth, depth), depth), :]
        lane = lax.broadcasted_iota(jnp.int32, (rows, depth), 1) + (begin * TILE + step * depth)
        lane = lane.astype(jnp.float32)

        @pl.loop(0, nodes // rows)
        def _(r):
            part = pl.ds(pl.multiple_of(r * rows, rows), rows)
            near = jnp.concatenate(
                [tiles_ref[slot, w, part, :].astype(jnp.bfloat16) for w in range(WIDE)], axis=1
            )
            flag = (lax.div(begin, WIDE) + step) * (adj_ref.shape[1] // rows) + row0 // rows + r

            @pl.when(own_here_ref[flag] == 0)
            def _():
                total_ref[part, :] += jnp.dot(near, block, preferred_element_type=jnp.float32)

            @pl.when(own_here_ref[flag] != 0)
            def _():
                own = jnp.where(notes_ref[part, 0:1] == lane, 1.0, 0.0).astype(jnp.bfloat16)
                both = jnp.dot(
                    jnp.concatenate([near, own], axis=0), block, preferred_element_type=jnp.float32
                )
                total_ref[part, :] += both[:rows]
                found_ref[part, :] += both[rows:]

    for copy in carry[1:]:
        copy.wait()
    if last:
        share = share_refs[0].shape[0]
        step_rows = math.gcd(share, 3 * TILE)
        for p, share_ref in enumerate(share_refs):
            for r in range(share // step_rows):
                part = pl.ds(p * share + r * step_rows, step_rows)
                own = (found_ref[part, :] + had_ref[part, :]).astype(jnp.bfloat16)
                mean = ((total_ref[part, :] + before_ref[part, :]) / notes_ref[part, 1:2]).astype(jnp.bfloat16)
                own_ref[part, :] = own
                mean_ref[part, :] = mean
                share_ref[pl.ds(r * step_rows, step_rows), :] = (
                    jnp.dot(own, wself_ref[...], preferred_element_type=jnp.float32)
                    + jnp.dot(mean, wneigh_ref[...], preferred_element_type=jnp.float32)
                ).astype(share_ref.dtype)


def gather_sum(inputs, scalars, answer, notes, adj, rest=None, row0=0, shares=()):
    batch_count, width, features = answer.shape
    tiles, nodes, _ = adj.shape
    nodes = sum(shares) or nodes
    piece = math.gcd(width, LANES)
    last = rest is not None
    room = min(batch_count * width, inputs) + SLOTS * batch_count + 2 * WIDE * TILE
    in_specs = [SMEM, SMEM, SMEM, SMEM, ANY, HBM, HBM]
    rows = lambda dtype: jax.ShapeDtypeStruct((nodes, features), dtype)
    scratch = [
        pltpu.VMEM((room, features), jnp.bfloat16),
        pltpu.VMEM((2, WIDE, nodes, TILE), adj.dtype),
        pltpu.SemaphoreType.DMA((2,)),
        pltpu.VMEM(answer.shape, answer.dtype),
        pltpu.SemaphoreType.DMA((batch_count, width // piece)),
        pltpu.VMEM((nodes, notes.shape[1]), notes.dtype),
        pltpu.SemaphoreType.DMA((5,)),
    ]
    operands = [answer, notes, adj]
    if last:
        operands += list(rest)
        in_specs += [HBM] * len(rest)
        out_shape = (rows(jnp.bfloat16), rows(jnp.bfloat16))
        out_shape += tuple(
            jax.ShapeDtypeStruct((n, rest[3].shape[1]), jnp.bfloat16) for n in shares
        )
        scratch += [pltpu.VMEM((nodes, features), jnp.float32)] * 4
        scratch += [pltpu.VMEM(x.shape, x.dtype) for x in rest[2:]]
    else:
        out_shape = (rows(jnp.float32), rows(jnp.float32))
    return pl.pallas_call(
        functools.partial(gather_sum_body, piece, last, row0),
        out_shape=out_shape,
        in_specs=in_specs,
        out_specs=(VMEM,) * len(out_shape),
        scratch_shapes=scratch,
        compiler_params=params(50),
        cost_estimate=cost(2 * nodes * features * TILE * tiles // (4 if last else 1), nodes * TILE),
        name="gather_sum",
    )(*scalars, *operands)


def share_order(array, parts, seeds):
    others = array.shape[0] - seeds
    own, rest = seeds // parts, others // parts
    tail = array.shape[1:]
    blocks = jnp.concatenate(
        [array[:seeds].reshape(parts, own, *tail), array[seeds:].reshape(parts, rest, *tail)],
        axis=1,
    )
    return ahead(blocks).reshape(array.shape)


def spread(part, axis, count):
    return lax.all_to_all(
        jnp.broadcast_to(part[None], (count,) + part.shape), axis, 0, 0, tiled=True
    )


def passed(part, shift, axis="feat"):
    parts = lax.axis_size(axis)
    return lax.ppermute(part, axis, [((i + shift) % parts, i) for i in range(parts)])


def turned(array, by):
    twice = jnp.concatenate([array, array], axis=0)
    return lax.dynamic_slice_in_dim(twice, by, array.shape[0], 0)


def ahead(array, axis="feat"):
    return turned(array, lax.axis_index(axis))


def in_order(blocks):
    parts = lax.axis_size("feat")
    total = jnp.zeros((parts,) + blocks[0].shape, blocks[0].dtype)
    for j, block in enumerate(blocks):
        spot = (lax.axis_index("feat") + j) % parts
        total = lax.dynamic_update_index_in_dim(total, block, spot, 0)
    return total


def spread_parts(part, axis="feat"):
    return [part] + [passed(part, j, axis) for j in range(1, lax.axis_size(axis))]


def sum_parts(blocks, axis="feat"):
    parts = lax.axis_size(axis)
    came = [blocks[0]] + [passed(blocks[j], -j, axis) for j in range(1, parts)]
    return sum(x.astype(jnp.float32) for x in came)


def swapped(part):
    return lax.ppermute(part, "batch", [(i, i ^ 1) for i in range(lax.axis_size("batch"))])


def total_over_batch(terms):
    count = lax.axis_size("batch")
    rows, width = terms.shape
    if count > FEW:
        pieces = terms.astype(jnp.bfloat16).reshape(count, rows // count, width)
        pieces = lax.all_to_all(pieces, "batch", 0, 0, tiled=True)
        total = jnp.sum(pieces.astype(jnp.float32), axis=0).astype(jnp.bfloat16)
        return spread(total, "batch", count).reshape(rows, width)
    chips = count // 2
    index = lax.axis_index("batch")
    first, chip = index % 2 == 0, index // 2
    upper, lower = terms[: rows // 2], terms[rows // 2 :]
    came = swapped(jnp.where(first, lower, upper).astype(jnp.bfloat16))
    mine = jnp.where(first, upper, lower) + came.astype(jnp.float32)
    pieces = turned(mine.reshape(chips, rows // count, width), chip)
    total = pieces[0]
    for j in range(1, chips):
        total = total + passed(pieces[j].astype(jnp.bfloat16), -2 * j, "batch").astype(jnp.float32)
    total = total.astype(jnp.bfloat16)
    mine = jnp.stack([total] + [passed(total, 2 * j, "batch") for j in range(1, chips)])
    other = swapped(mine)
    both = jnp.stack([jnp.where(first, mine, other), jnp.where(first, other, mine)], axis=1)
    return turned(both, (chips - chip) % chips).transpose(1, 0, 2, 3).reshape(rows, width)


def local(
    store,
    input_owner,
    input_row,
    nbr_one,
    deg_one,
    nbr_two,
    deg_two,
    cotangent,
    w1_self,
    w1_neigh,
    bias_one,
    w2_self,
    w2_neigh,
    bias_two,
):
    batch_count = lax.axis_size("batch")
    parts = lax.axis_size("feat")
    feat_index = lax.axis_index("feat")
    input_count = input_owner.shape[1]
    capacity = 2 * input_count // batch_count
    nodes = nbr_one.shape[1]
    seed_rows = nbr_two.shape[1]
    seeds = seed_rows * parts
    share = nodes // parts
    hidden_width = w1_self.shape[1]

    owners = input_owner.reshape(input_count // LANES, LANES)
    wanted = input_row.reshape(input_count // LANES, LANES)
    slots, counts, requests = make_requests(
        batch_count, capacity, store.shape[1] // LANES, owners, wanted
    )
    owners = owners.reshape(1, input_count)
    received = lax.all_to_all(
        requests.reshape(batch_count, capacity), "batch", split_axis=0, concat_axis=0, tiled=True
    )
    first = capacity * 13 // (24 * SLOTS) * SLOTS
    places = received.reshape(batch_count * capacity)
    looked_a = lookup(store, places, batch_count, 0, first, 60)
    near_first, looked_a = lax.optimization_barrier((nbr_one[0], looked_a))
    answer_a = lax.all_to_all(looked_a, "batch", split_axis=0, concat_axis=0, tiled=True)
    looked = lookup(store, places, batch_count, first, capacity - first, 24)

    depth = WIDE * TILE
    steps = -(-(input_count + 2 * (SLOTS - 1) * batch_count + depth - 1) // depth)
    tally = counts[:, 0]
    tally_a = jnp.minimum(tally, first)
    tally_b = tally - tally_a
    padded = lambda n: (n + SLOTS - 1) // SLOTS * SLOTS
    ends = lambda n: jnp.concatenate([jnp.zeros((1,), jnp.int32), jnp.cumsum(padded(n))])
    starts_a, starts_b = ends(tally_a), ends(tally_b)
    steps_a = (starts_a[batch_count] + depth - 1) // depth
    steps_b = (starts_b[batch_count] + depth - 1) // depth
    spans_a = jnp.stack([jnp.zeros_like(steps_a), steps_a])
    spans_b = jnp.stack([steps_a * WIDE, steps_b])
    slot = slots.reshape(1, input_count)
    shifted = jnp.where(
        slot < first,
        slot + starts_a[:batch_count, None],
        slot - first + steps_a * depth + starts_b[:batch_count, None],
    )
    mine = owners == jnp.arange(batch_count)[:, None]
    column = jnp.sum(jnp.where(mine, shifted, 0), axis=0)
    grid = jnp.pad(column.reshape(-1, LANES), ((0, LANES - input_count // LANES), (0, 0))).T
    finder = jnp.concatenate([grid // TILE, grid % TILE], axis=0).astype(jnp.bfloat16)
    notes = jnp.stack([column[:nodes], deg_one[0]], axis=1).astype(jnp.float32)
    notes = share_order(notes, parts, seeds)
    block = math.gcd(nodes, 3 * TILE)
    met = notes[:, 0].reshape(1, nodes // block, block) // depth
    met = met.astype(jnp.int32) == jnp.arange(steps)[:, None, None]
    own_here = jnp.any(met, axis=2).astype(jnp.int32).reshape(-1)

    fanout = nbr_one.shape[2]
    used = jnp.arange(fanout)[None, :] < deg_one[0][:, None]
    near = jnp.pad(jnp.where(used, near_first, -1), ((0, 0), (0, SLOTS - fanout)), constant_values=-1)
    me = feat_index.astype(jnp.int32).reshape(1)
    near = near.reshape(nodes // SLOTS, TILE)
    adj = adjacency(me, near, finder, steps * WIDE, parts, seeds)
    looked, answer_a, adj = lax.optimization_barrier((looked, answer_a, adj))
    answer_b = lax.all_to_all(looked, "batch", split_axis=0, concat_axis=0, tiled=True)

    scalars = (spans_a, tally_a, starts_a, own_here)
    total, found = gather_sum(input_count, scalars, answer_a, notes, adj)
    second = (nbr_two[0], deg_two, cotangent[0])
    total, second = lax.optimization_barrier((total, second))

    fanout_two = nbr_two.shape[2]
    used_two = jnp.arange(fanout_two)[:, None] < second[1]
    lists = jnp.concatenate([jnp.where(used_two, second[0].T, -1), second[1]], axis=0)
    lists = in_order(spread_parts(lists))
    upstream = in_order(spread_parts(second[2])).reshape(seeds, hidden_width)
    total, lists, upstream = lax.optimization_barrier((total, lists, upstream))

    near_two = lists[:, :fanout_two].transpose(1, 0, 2).reshape(fanout_two, seeds)
    deg_all = lists[:, fanout_two].reshape(seeds)
    rest = share - seed_rows
    after = near_two - seeds
    place = jnp.where(
        near_two < seeds,
        near_two // seed_rows * share + near_two % seed_rows,
        after // rest * share + seed_rows + after % rest,
    )
    place = jnp.where(near_two < 0, -1, place - feat_index * share)
    adj_two = jnp.sum(
        place[:, :, None] == jnp.arange(share)[None, None, :], axis=0, dtype=jnp.float32
    ).astype(jnp.bfloat16)

    def finish(begin, end):
        return gather_sum(
            input_count,
            (spans_b, tally_b, starts_b, own_here),
            answer_b,
            notes,
            adj,
            (total, found, w1_self, w1_neigh),
            begin * share,
            (share,) * (end - begin),
        )

    half = parts // 2
    cuts = [(half, parts), (1, half), (0, 1)]
    own_rows, mean_rows, z_blocks = [], [], []
    for begin, end in cuts:
        own, mean, *blocks = finish(begin, end)
        total, blocks = lax.optimization_barrier((total, blocks))
        own_rows.append(own)
        mean_rows.append(mean)
        z_blocks = blocks + z_blocks
    z_share = sum_parts(z_blocks) + bias_one
    hidden = jax.nn.silu(z_share).astype(jnp.bfloat16)

    agg_part = jnp.dot(adj_two, hidden, preferred_element_type=jnp.float32).astype(jnp.bfloat16)
    blocks = spread_parts(jnp.concatenate([agg_part, hidden[:seed_rows]]))
    deg_second = deg_all.astype(jnp.float32)[:, None]
    agg_two = sum(x[:seeds].astype(jnp.float32) for x in blocks) / deg_second
    agg_two = agg_two.astype(jnp.bfloat16)
    self_two = in_order([x[seeds:] for x in blocks]).reshape(seeds, hidden_width)
    z_two = (
        jnp.dot(self_two, w2_self, preferred_element_type=jnp.float32)
        + jnp.dot(agg_two, w2_neigh, preferred_element_type=jnp.float32)
        + bias_two
    )
    dz_two = (upstream.astype(jnp.float32) * silu_grad(z_two)).astype(jnp.bfloat16)
    mine = lambda x: lax.dynamic_slice_in_dim(x, feat_index * seed_rows, seed_rows, 0)
    activations = jax.nn.silu(mine(z_two)).astype(jnp.bfloat16)[None]

    back = contract_cols(dz_two, w2_neigh) / deg_second
    back_high = back.astype(jnp.bfloat16)
    back_low = (back - back_high.astype(jnp.float32)).astype(jnp.bfloat16)
    dh_share = contract_rows(adj_two, back_high) + contract_rows(adj_two, back_low)
    dh_share = dh_share + jnp.pad(contract_cols(mine(dz_two), w2_self), ((0, rest), (0, 0)))
    dz_share = (dh_share * silu_grad(z_share)).astype(jnp.bfloat16)
    dz_blocks = spread_parts(dz_share)
    dz_rows = [jnp.concatenate(dz_blocks[begin:end]) for begin, end in cuts]
    grads = [contract_rows(self_two, dz_two), contract_rows(agg_two, dz_two)]
    for rows in (own_rows, mean_rows):
        grads.append(sum(contract_rows(x, y) for x, y in zip(rows, dz_rows)))
    total = total_over_batch(jnp.concatenate(grads)).astype(jnp.float32)
    return (activations, *total.reshape(len(grads), -1, hidden_width))


def solution(mesh):
    in_specs = (
        P("batch", "feat"),
        P("batch", None, None),
        P("batch", None),
        P("batch", None, None),
        P("batch", None),
        P("batch", "feat", None),
        P("batch", "feat"),
        P("batch", "feat", None),
        P("feat", None),
        P("feat", None),
        P(),
        P(),
        P(),
        P(),
    )
    out_specs = (P("batch", "feat", None), P(), P(), P("feat", None), P("feat", None))
    return jax.shard_map(local, mesh=mesh, in_specs=in_specs, out_specs=out_specs, check_vma=False)
```

```python
import functools
import math

import jax
import jax.numpy as jnp
from jax import lax
from jax.experimental import pallas as pl
from jax.experimental.pallas import tpu as pltpu
from jax.sharding import PartitionSpec as P

TILE = 256
LANES = 128
SLOTS = 16
WIDE = 2
FEW = 16
TILE_BITS, LANE_BITS, SLOT_BITS = 8, 7, 4
MIB = 1024 * 1024
VMEM = pl.BlockSpec(memory_space=pltpu.VMEM)
SMEM = pl.BlockSpec(memory_space=pltpu.SMEM)
ANY = pl.BlockSpec(memory_space=pl.ANY)
HBM = pl.BlockSpec(memory_space=pltpu.HBM)


def silu_grad(values):
    sig = jax.nn.sigmoid(values)
    return sig * (1.0 + values * (1.0 - sig))


def contract_rows(left_side, right_side):
    return lax.dot_general(
        left_side, right_side, (((0,), (0,)), ((), ())), preferred_element_type=jnp.float32
    )


def contract_cols(left_side, right_side):
    return lax.dot_general(
        left_side, right_side, (((1,), (1,)), ((), ())), preferred_element_type=jnp.float32
    )


def params(mib):
    return pltpu.CompilerParams(vmem_limit_bytes=mib * MIB)


def cost(flops, moved):
    return pl.CostEstimate(flops=int(flops), bytes_accessed=int(moved), transcendentals=0)


def requests_body(
    batch_count,
    capacity,
    scale,
    owner_in,
    row_in,
    slot_ref,
    count_ref,
    request_ref,
    owner_ref,
    row_ref,
    came,
):
    copies = [
        pltpu.make_async_copy(owner_in, owner_ref, came.at[0]),
        pltpu.make_async_copy(row_in, row_ref, came.at[1]),
    ]
    for copy in copies:
        copy.start()
    for copy in copies:
        copy.wait()
    blocks, width = owner_ref.shape[0] // 2, TILE
    places = request_ref.shape[0]
    line = lambda ref, b: jnp.concatenate([ref[2 * b : 2 * b + 1], ref[2 * b + 1 : 2 * b + 2]], axis=1)
    owner_id = lax.broadcasted_iota(jnp.int32, (batch_count, width), 0)
    earlier = lax.broadcasted_iota(jnp.int32, (width, width), 0)
    later = lax.broadcasted_iota(jnp.int32, (width, width), 1)
    upper = jnp.where(earlier <= later, 1.0, 0.0).astype(jnp.bfloat16)
    high_id = lax.broadcasted_iota(jnp.int32, (places, width), 0)
    low_id = lax.broadcasted_iota(jnp.int32, (LANES, width), 0)
    marks = [
        jnp.where(line(owner_ref, b) == owner_id, 1.0, 0.0) for b in range(blocks)
    ]
    stacked = jnp.concatenate(marks, axis=0).astype(jnp.bfloat16)
    prefix = jnp.dot(stacked, upper, preferred_element_type=jnp.float32)
    running = jnp.zeros((batch_count, 1), jnp.float32)
    total = jnp.zeros((2 * places, LANES), jnp.float32)
    for b in range(blocks):
        part = prefix[b * batch_count : (b + 1) * batch_count]
        slots = jnp.sum(marks[b] * (part + running - 1.0), axis=0, keepdims=True)
        slots = slots.astype(jnp.int32)
        slot_ref[2 * b : 2 * b + 1, :] = slots[:, :LANES]
        slot_ref[2 * b + 1 : 2 * b + 2, :] = slots[:, LANES:]
        running = running + part[:, width - 1 : width]
        bucket = line(owner_ref, b) * capacity + slots
        rows = line(row_ref, b)
        hit = (bucket >> LANE_BITS) == high_id
        left = jnp.concatenate(
            [
                jnp.where(hit, (rows >> TILE_BITS).astype(jnp.float32), 0.0),
                jnp.where(hit, (rows & (TILE - 1)).astype(jnp.float32), 0.0),
            ],
            axis=0,
        ).astype(jnp.bfloat16)
        right = jnp.where((bucket & (LANES - 1)) == low_id, 1.0, 0.0).astype(jnp.bfloat16)
        total = total + contract_cols(left, right)
    count_ref[...] = jnp.broadcast_to(running, count_ref.shape).astype(jnp.int32)
    request_ref[...] = (total[:places] * TILE + total[places:]).astype(jnp.int32) * scale


def make_requests(batch_count, capacity, scale, owners, wanted):
    total = owners.shape[0] * LANES
    places = batch_count * capacity // LANES
    return pl.pallas_call(
        functools.partial(requests_body, batch_count, capacity, scale),
        out_shape=(
            jax.ShapeDtypeStruct(owners.shape, jnp.int32),
            jax.ShapeDtypeStruct((batch_count, LANES), jnp.int32),
            jax.ShapeDtypeStruct((places, LANES), jnp.int32),
        ),
        in_specs=[ANY, ANY],
        out_specs=(VMEM, VMEM, VMEM),
        scratch_shapes=[
            pltpu.VMEM(owners.shape, owners.dtype),
            pltpu.VMEM(wanted.shape, wanted.dtype),
            pltpu.SemaphoreType.DMA((2,)),
        ],
        compiler_params=params(58),
        cost_estimate=cost(4 * total * places * LANES, 24 * total),
        name="requests",
    )(owners, wanted)


def lookup_body(stride, first, width, want_ref, store_in, out_ref, table, lines, store_ref, came):
    rows_all = store_ref.shape[0]
    halves = store_ref.shape[1] // LANES
    lane = lambda h: pl.ds(h * LANES, LANES)
    begin = pl.program_id(0) * stride + first

    @pl.when(pl.program_id(0) == 0)
    def _():
        pieces = came.shape[0]
        depth = rows_all // pieces
        copies = [
            pltpu.make_async_copy(
                store_in.at[pl.ds(n * depth, depth)], store_ref.at[pl.ds(n * depth, depth)], came.at[n]
            )
            for n in range(pieces)
        ]
        for copy in copies:
            copy.start()
        for n, copy in enumerate(copies):
            copy.wait()

            @pl.loop(n * depth // TILE, (n + 1) * depth // TILE)
            def _(j):
                part = pl.ds(pl.multiple_of(j * TILE, TILE), TILE)
                for h in range(halves):
                    spot = pl.ds(pl.multiple_of(j * TILE * halves, TILE) + h, TILE, stride=halves)
                    table[spot, :] = store_ref[part, lane(h)].astype(jnp.float32)

    @pl.loop(0, width // SLOTS, unroll=math.gcd(width // SLOTS, 4))
    def _(j):
        at = [want_ref[begin + j * SLOTS + u] for u in range(SLOTS)]
        rows = [table[pl.ds(pl.multiple_of(a, halves), halves), :] for a in at]
        block = lines.at[pl.ds(pl.multiple_of(j * SLOTS * halves, SLOTS * halves), SLOTS * halves)]
        for u in range(SLOTS):
            block[pl.ds(u * halves, halves), :] = rows[u]

    for h in range(halves):
        out_ref[0, :, lane(h)] = lines[pl.ds(h, width, stride=halves), :].astype(jnp.bfloat16)


def lookup(store, places, groups, first, width, mib):
    rows_all, features = store.shape
    halves = features // LANES
    apart = lambda rows: pltpu.VMEM((rows * halves, LANES), jnp.float32)
    return pl.pallas_call(
        functools.partial(lookup_body, places.shape[0] // groups, first, width),
        out_shape=jax.ShapeDtypeStruct((groups, width, features), jnp.bfloat16),
        grid=(groups,),
        in_specs=[SMEM, HBM],
        out_specs=pl.BlockSpec((1, width, features), lambda g: (g, 0, 0)),
        scratch_shapes=[
            apart(rows_all),
            apart(width),
            pltpu.VMEM((rows_all, features), store.dtype),
            pltpu.SemaphoreType.DMA((8,)),
        ],
        compiler_params=params(mib),
        cost_estimate=cost(groups * width * features * 40, 2 * rows_all * features),
        name="lookup",
    )(places, store)


def adjacency_body(tiles, me_ref, near_ref, table_ref, out_ref):
    groups = near_ref.shape[0]
    node_high = lax.broadcasted_iota(jnp.int32, (LANES, TILE), 0)
    own_row = (
        lax.shift_right_logical(lax.broadcasted_iota(jnp.int32, (SLOTS, TILE), 1), SLOT_BITS)
        == lax.broadcasted_iota(jnp.int32, (SLOTS, TILE), 0)
    )
    low_id = lax.broadcasted_iota(jnp.int32, (TILE, TILE), 0).astype(jnp.float32)

    def one_group(g):
        near = near_ref[pl.ds(g, 1), :]
        pick = jnp.where((near >> LANE_BITS) == node_high, 1.0, 0.0).astype(jnp.bfloat16)
        found = jnp.dot(table_ref[...], pick, preferred_element_type=jnp.float32)
        here = (near & (LANES - 1)) == node_high
        high = jnp.sum(jnp.where(here, found[:LANES], 0.0), axis=0, keepdims=True)
        low = jnp.sum(jnp.where(here, found[LANES:], 0.0), axis=0, keepdims=True)
        high = jnp.where(near < 0, -1.0, high)
        rows = jnp.where(own_row, high, -1.0)
        left = jnp.concatenate(
            [jnp.where(rows == float(t), 1.0, 0.0) for t in range(tiles)], axis=0
        ).astype(jnp.bfloat16)
        right = jnp.where(low == low_id, 1.0, 0.0).astype(jnp.bfloat16)
        return contract_cols(left, right).reshape(tiles, SLOTS, TILE)

    @pl.loop(0, groups // 2, unroll=2)
    def _(j):
        pair = jnp.concatenate([one_group(2 * j), one_group(2 * j + 1)], axis=1)
        out_ref[:, pl.ds(pl.multiple_of(j * 2 * SLOTS, 2 * SLOTS), 2 * SLOTS), :] = pair.astype(
            out_ref.dtype
        )


def adjacency(me, near, table, tiles, parts, seeds):
    groups = near.shape[0]
    nodes = groups * SLOTS
    step = LANES // SLOTS
    own, rest, share = (n // parts // LANES for n in (seeds, nodes - seeds, nodes))

    def place(block, me_ref):
        after = block - own * parts
        is_own = after < 0
        part = jnp.where(is_own, lax.div(block, own), lax.div(after, rest))
        at = jnp.where(is_own, lax.rem(block, own), own + lax.rem(after, rest))
        return (0, lax.rem(part - me_ref[0] + parts, parts) * share + at, 0)

    return pl.pallas_call(
        functools.partial(adjacency_body, tiles),
        out_shape=jax.ShapeDtypeStruct((tiles, nodes, TILE), jnp.float8_e4m3fn),
        grid_spec=pltpu.PrefetchScalarGridSpec(
            num_scalar_prefetch=1,
            grid=(groups // step,),
            in_specs=[
                pl.BlockSpec((step, TILE), lambda r, me: (r, 0)),
                pl.BlockSpec(table.shape, lambda r, me: (0, 0)),
            ],
            out_specs=pl.BlockSpec((tiles, LANES, TILE), place),
        ),
        compiler_params=params(48),
        cost_estimate=cost(2 * nodes * TILE * TILE * tiles * 2, nodes * TILE * tiles),
        name="adjacency",
    )(me, near, table)


def collect(piece, counts_ref, starts_ref, answer_ref, landed, arrived, packed):
    batch_count = answer_ref.shape[0]

    def each_used(what):
        @pl.loop(0, batch_count)
        def _(o):
            @pl.loop(0, pl.cdiv(counts_ref[o], piece))
            def _(c):
                part = pl.ds(pl.multiple_of(c * piece, piece), piece)
                what(
                    o,
                    c,
                    part,
                    pltpu.make_async_copy(
                        answer_ref.at[o, part], landed.at[o, part], arrived.at[o, c]
                    ),
                )

    def lay(o, c, part, copy):
        copy.wait()
        packed[pl.ds(pl.multiple_of(starts_ref[o] + c * piece, SLOTS), piece), :] = landed[o, part]

    each_used(lambda o, c, part, copy: copy.start())
    each_used(lay)
    end = starts_ref[batch_count]
    packed[pl.ds(pl.multiple_of(end, SLOTS), WIDE * TILE), :] = jnp.zeros(
        (WIDE * TILE, packed.shape[1]), packed.dtype
    )


def gather_sum_body(
    piece,
    last,
    row0,
    spans_ref,
    counts_ref,
    starts_ref,
    own_here_ref,
    answer_ref,
    notes_in,
    adj_ref,
    *refs,
):
    if last:
        (total_in, found_in, wself_in, wneigh_in, own_ref, mean_ref) = refs[:6]
        share_refs = refs[6:-13]
        packed, tiles_ref, ready, landed, arrived, notes_ref, carried = refs[-13:-6]
        total_ref, found_ref, before_ref, had_ref, wself_ref, wneigh_ref = refs[-6:]
        mine = pl.ds(row0, total_ref.shape[0])
        pairs = ((notes_in.at[mine], notes_ref), (total_in.at[mine], before_ref))
        pairs += ((found_in.at[mine], had_ref),)
        pairs += ((wself_in, wself_ref), (wneigh_in, wneigh_ref))
    else:
        total_ref, found_ref, packed, tiles_ref, ready, landed, arrived, notes_ref, carried = refs
        pairs = ((notes_in, notes_ref),)
    carry = [pltpu.make_async_copy(*pair, carried.at[n]) for n, pair in enumerate(pairs)]
    nodes = total_ref.shape[0]
    rows = math.gcd(adj_ref.shape[1], 3 * TILE)
    begin, count = spans_ref[0], spans_ref[1]

    def fetch(step, slot):
        return pltpu.make_async_copy(
            adj_ref.at[pl.ds(begin + step * WIDE, WIDE), pl.ds(row0, nodes)],
            tiles_ref.at[slot],
            ready.at[slot],
        )

    @pl.when(count > 0)
    def _():
        fetch(0, 0).start()

    for copy in carry:
        copy.start()
    collect(piece, counts_ref, starts_ref, answer_ref, landed, arrived, packed)
    total_ref[...] = jnp.zeros(total_ref.shape, jnp.float32)
    found_ref[...] = jnp.zeros(found_ref.shape, jnp.float32)
    carry[0].wait()

    @pl.loop(0, count)
    def _(step):
        slot = step & 1

        @pl.when(step + 1 < count)
        def _():
            fetch(step + 1, 1 - slot).start()

        fetch(step, slot).wait()
        depth = WIDE * TILE
        block = packed[pl.ds(pl.multiple_of(step * depth, depth), depth), :]
        lane = lax.broadcasted_iota(jnp.int32, (rows, depth), 1) + (begin * TILE + step * depth)
        lane = lane.astype(jnp.float32)

        @pl.loop(0, nodes // rows)
        def _(r):
            part = pl.ds(pl.multiple_of(r * rows, rows), rows)
            near = jnp.concatenate(
                [tiles_ref[slot, w, part, :].astype(jnp.bfloat16) for w in range(WIDE)], axis=1
            )
            flag = (lax.div(begin, WIDE) + step) * (adj_ref.shape[1] // rows) + row0 // rows + r

            @pl.when(own_here_ref[flag] == 0)
            def _():
                total_ref[part, :] += jnp.dot(near, block, preferred_element_type=jnp.float32)

            @pl.when(own_here_ref[flag] != 0)
            def _():
                own = jnp.where(notes_ref[part, 0:1] == lane, 1.0, 0.0).astype(jnp.bfloat16)
                both = jnp.dot(
                    jnp.concatenate([near, own], axis=0), block, preferred_element_type=jnp.float32
                )
                total_ref[part, :] += both[:rows]
                found_ref[part, :] += both[rows:]

    for copy in carry[1:]:
        copy.wait()
    if last:
        share = share_refs[0].shape[0]
        step_rows = math.gcd(share, 3 * TILE)
        for p, share_ref in enumerate(share_refs):
            for r in range(share // step_rows):
                part = pl.ds(p * share + r * step_rows, step_rows)
                own = (found_ref[part, :] + had_ref[part, :]).astype(jnp.bfloat16)
                mean = ((total_ref[part, :] + before_ref[part, :]) / notes_ref[part, 1:2]).astype(jnp.bfloat16)
                own_ref[part, :] = own
                mean_ref[part, :] = mean
                share_ref[pl.ds(r * step_rows, step_rows), :] = (
                    jnp.dot(own, wself_ref[...], preferred_element_type=jnp.float32)
                    + jnp.dot(mean, wneigh_ref[...], preferred_element_type=jnp.float32)
                ).astype(share_ref.dtype)


def gather_sum(inputs, scalars, answer, notes, adj, rest=None, row0=0, shares=()):
    batch_count, width, features = answer.shape
    tiles, nodes, _ = adj.shape
    nodes = sum(shares) or nodes
    piece = math.gcd(width, LANES)
    last = rest is not None
    room = min(batch_count * width, inputs) + SLOTS * batch_count + 2 * WIDE * TILE
    in_specs = [SMEM, SMEM, SMEM, SMEM, ANY, HBM, HBM]
    rows = lambda dtype: jax.ShapeDtypeStruct((nodes, features), dtype)
    scratch = [
        pltpu.VMEM((room, features), jnp.bfloat16),
        pltpu.VMEM((2, WIDE, nodes, TILE), adj.dtype),
        pltpu.SemaphoreType.DMA((2,)),
        pltpu.VMEM(answer.shape, answer.dtype),
        pltpu.SemaphoreType.DMA((batch_count, width // piece)),
        pltpu.VMEM((nodes, notes.shape[1]), notes.dtype),
        pltpu.SemaphoreType.DMA((5,)),
    ]
    operands = [answer, notes, adj]
    if last:
        operands += list(rest)
        in_specs += [HBM] * len(rest)
        out_shape = (rows(jnp.bfloat16), rows(jnp.bfloat16))
        out_shape += tuple(
            jax.ShapeDtypeStruct((n, rest[3].shape[1]), jnp.bfloat16) for n in shares
        )
        scratch += [pltpu.VMEM((nodes, features), jnp.float32)] * 4
        scratch += [pltpu.VMEM(x.shape, x.dtype) for x in rest[2:]]
    else:
        out_shape = (rows(jnp.float32), rows(jnp.float32))
    return pl.pallas_call(
        functools.partial(gather_sum_body, piece, last, row0),
        out_shape=out_shape,
        in_specs=in_specs,
        out_specs=(VMEM,) * len(out_shape),
        scratch_shapes=scratch,
        compiler_params=params(50),
        cost_estimate=cost(2 * nodes * features * TILE * tiles // (4 if last else 1), nodes * TILE),
        name="gather_sum",
    )(*scalars, *operands)


def share_order(array, parts, seeds):
    others = array.shape[0] - seeds
    own, rest = seeds // parts, others // parts
    tail = array.shape[1:]
    blocks = jnp.concatenate(
        [array[:seeds].reshape(parts, own, *tail), array[seeds:].reshape(parts, rest, *tail)],
        axis=1,
    )
    return ahead(blocks).reshape(array.shape)


def spread(part, axis, count):
    return lax.all_to_all(
        jnp.broadcast_to(part[None], (count,) + part.shape), axis, 0, 0, tiled=True
    )


def passed(part, shift, axis="feat"):
    parts = lax.axis_size(axis)
    return lax.ppermute(part, axis, [((i + shift) % parts, i) for i in range(parts)])


def turned(array, by):
    twice = jnp.concatenate([array, array], axis=0)
    return lax.dynamic_slice_in_dim(twice, by, array.shape[0], 0)


def ahead(array, axis="feat"):
    return turned(array, lax.axis_index(axis))


def in_order(blocks):
    parts = lax.axis_size("feat")
    total = jnp.zeros((parts,) + blocks[0].shape, blocks[0].dtype)
    for j, block in enumerate(blocks):
        spot = (lax.axis_index("feat") + j) % parts
        total = lax.dynamic_update_index_in_dim(total, block, spot, 0)
    return total


def spread_parts(part, axis="feat"):
    return [part] + [passed(part, j, axis) for j in range(1, lax.axis_size(axis))]


def sum_parts(blocks, axis="feat"):
    parts = lax.axis_size(axis)
    came = [blocks[0]] + [passed(blocks[j], -j, axis) for j in range(1, parts)]
    return sum(x.astype(jnp.float32) for x in came)


def swapped(part):
    return lax.ppermute(part, "batch", [(i, i ^ 1) for i in range(lax.axis_size("batch"))])


def total_over_batch(terms):
    count = lax.axis_size("batch")
    rows, width = terms.shape
    if count > FEW:
        pieces = terms.astype(jnp.bfloat16).reshape(count, rows // count, width)
        pieces = lax.all_to_all(pieces, "batch", 0, 0, tiled=True)
        total = jnp.sum(pieces.astype(jnp.float32), axis=0).astype(jnp.bfloat16)
        return spread(total, "batch", count).reshape(rows, width)
    chips = count // 2
    index = lax.axis_index("batch")
    first, chip = index % 2 == 0, index // 2
    upper, lower = terms[: rows // 2], terms[rows // 2 :]
    came = swapped(jnp.where(first, lower, upper).astype(jnp.bfloat16))
    mine = jnp.where(first, upper, lower) + came.astype(jnp.float32)
    pieces = turned(mine.reshape(chips, rows // count, width), chip)
    total = pieces[0]
    for j in range(1, chips):
        total = total + passed(pieces[j].astype(jnp.bfloat16), -2 * j, "batch").astype(jnp.float32)
    total = total.astype(jnp.bfloat16)
    mine = jnp.stack([total] + [passed(total, 2 * j, "batch") for j in range(1, chips)])
    other = swapped(mine)
    both = jnp.stack([jnp.where(first, mine, other), jnp.where(first, other, mine)], axis=1)
    return turned(both, (chips - chip) % chips).transpose(1, 0, 2, 3).reshape(rows, width)


def local(
    store,
    input_owner,
    input_row,
    nbr_one,
    deg_one,
    nbr_two,
    deg_two,
    cotangent,
    w1_self,
    w1_neigh,
    bias_one,
    w2_self,
    w2_neigh,
    bias_two,
):
    batch_count = lax.axis_size("batch")
    parts = lax.axis_size("feat")
    feat_index = lax.axis_index("feat")
    input_count = input_owner.shape[1]
    capacity = 2 * input_count // batch_count
    nodes = nbr_one.shape[1]
    seed_rows = nbr_two.shape[1]
    seeds = seed_rows * parts
    share = nodes // parts
    hidden_width = w1_self.shape[1]

    owners = input_owner.reshape(input_count // LANES, LANES)
    wanted = input_row.reshape(input_count // LANES, LANES)
    slots, counts, requests = make_requests(
        batch_count, capacity, store.shape[1] // LANES, owners, wanted
    )
    owners = owners.reshape(1, input_count)
    received = lax.all_to_all(
        requests.reshape(batch_count, capacity), "batch", split_axis=0, concat_axis=0, tiled=True
    )
    first = capacity * 13 // (24 * SLOTS) * SLOTS
    places = received.reshape(batch_count * capacity)
    looked_a = lookup(store, places, batch_count, 0, first, 60)
    near_first, looked_a = lax.optimization_barrier((nbr_one[0], looked_a))
    answer_a = lax.all_to_all(looked_a, "batch", split_axis=0, concat_axis=0, tiled=True)
    looked = lookup(store, places, batch_count, first, capacity - first, 24)

    depth = WIDE * TILE
    steps = -(-(input_count + 2 * (SLOTS - 1) * batch_count + depth - 1) // depth)
    tally = counts[:, 0]
    tally_a = jnp.minimum(tally, first)
    tally_b = tally - tally_a
    padded = lambda n: (n + SLOTS - 1) // SLOTS * SLOTS
    ends = lambda n: jnp.concatenate([jnp.zeros((1,), jnp.int32), jnp.cumsum(padded(n))])
    starts_a, starts_b = ends(tally_a), ends(tally_b)
    steps_a = (starts_a[batch_count] + depth - 1) // depth
    steps_b = (starts_b[batch_count] + depth - 1) // depth
    spans_a = jnp.stack([jnp.zeros_like(steps_a), steps_a])
    spans_b = jnp.stack([steps_a * WIDE, steps_b])
    slot = slots.reshape(1, input_count)
    shifted = jnp.where(
        slot < first,
        slot + starts_a[:batch_count, None],
        slot - first + steps_a * depth + starts_b[:batch_count, None],
    )
    mine = owners == jnp.arange(batch_count)[:, None]
    column = jnp.sum(jnp.where(mine, shifted, 0), axis=0)
    grid = jnp.pad(column.reshape(-1, LANES), ((0, LANES - input_count // LANES), (0, 0))).T
    finder = jnp.concatenate([grid // TILE, grid % TILE], axis=0).astype(jnp.bfloat16)
    notes = jnp.stack([column[:nodes], deg_one[0]], axis=1).astype(jnp.float32)
    notes = share_order(notes, parts, seeds)
    block = math.gcd(nodes, 3 * TILE)
    met = notes[:, 0].reshape(1, nodes // block, block) // depth
    met = met.astype(jnp.int32) == jnp.arange(steps)[:, None, None]
    own_here = jnp.any(met, axis=2).astype(jnp.int32).reshape(-1)

    fanout = nbr_one.shape[2]
    used = jnp.arange(fanout)[None, :] < deg_one[0][:, None]
    near = jnp.pad(jnp.where(used, near_first, -1), ((0, 0), (0, SLOTS - fanout)), constant_values=-1)
    me = feat_index.astype(jnp.int32).reshape(1)
    near = near.reshape(nodes // SLOTS, TILE)
    adj = adjacency(me, near, finder, steps * WIDE, parts, seeds)
    looked, answer_a, adj = lax.optimization_barrier((looked, answer_a, adj))
    answer_b = lax.all_to_all(looked, "batch", split_axis=0, concat_axis=0, tiled=True)

    scalars = (spans_a, tally_a, starts_a, own_here)
    total, found = gather_sum(input_count, scalars, answer_a, notes, adj)
    second = (nbr_two[0], deg_two, cotangent[0])
    total, second = lax.optimization_barrier((total, second))

    fanout_two = nbr_two.shape[2]
    used_two = jnp.arange(fanout_two)[:, None] < second[1]
    lists = jnp.concatenate([jnp.where(used_two, second[0].T, -1), second[1]], axis=0)
    lists = in_order(spread_parts(lists))
    upstream = in_order(spread_parts(second[2])).reshape(seeds, hidden_width)
    total, lists, upstream = lax.optimization_barrier((total, lists, upstream))

    near_two = lists[:, :fanout_two].transpose(1, 0, 2).reshape(fanout_two, seeds)
    deg_all = lists[:, fanout_two].reshape(seeds)
    rest = share - seed_rows
    after = near_two - seeds
    place = jnp.where(
        near_two < seeds,
        near_two // seed_rows * share + near_two % seed_rows,
        after // rest * share + seed_rows + after % rest,
    )
    place = jnp.where(near_two < 0, -1, place - feat_index * share)
    adj_two = jnp.sum(
        place[:, :, None] == jnp.arange(share)[None, None, :], axis=0, dtype=jnp.float32
    ).astype(jnp.bfloat16)

    def finish(begin, end):
        return gather_sum(
            input_count,
            (spans_b, tally_b, starts_b, own_here),
            answer_b,
            notes,
            adj,
            (total, found, w1_self, w1_neigh),
            begin * share,
            (share,) * (end - begin),
        )

    half = parts // 2
    cuts = [(half, parts), (1, half), (0, 1)]
    own_rows, mean_rows, z_blocks = [], [], []
    for begin, end in cuts:
        own, mean, *blocks = finish(begin, end)
        total, blocks = lax.optimization_barrier((total, blocks))
        own_rows.append(own)
        mean_rows.append(mean)
        z_blocks = blocks + z_blocks
    z_share = sum_parts(z_blocks) + bias_one
    hidden = jax.nn.silu(z_share).astype(jnp.bfloat16)

    agg_part = jnp.dot(adj_two, hidden, preferred_element_type=jnp.float32).astype(jnp.bfloat16)
    blocks = spread_parts(jnp.concatenate([agg_part, hidden[:seed_rows]]))
    deg_second = deg_all.astype(jnp.float32)[:, None]
    agg_two = sum(x[:seeds].astype(jnp.float32) for x in blocks) / deg_second
    agg_two = agg_two.astype(jnp.bfloat16)
    self_two = in_order([x[seeds:] for x in blocks]).reshape(seeds, hidden_width)
    z_two = (
        jnp.dot(self_two, w2_self, preferred_element_type=jnp.float32)
        + jnp.dot(agg_two, w2_neigh, preferred_element_type=jnp.float32)
        + bias_two
    )
    dz_two = (upstream.astype(jnp.float32) * silu_grad(z_two)).astype(jnp.bfloat16)
    mine = lambda x: lax.dynamic_slice_in_dim(x, feat_index * seed_rows, seed_rows, 0)
    activations = jax.nn.silu(mine(z_two)).astype(jnp.bfloat16)[None]

    back = contract_cols(dz_two, w2_neigh) / deg_second
    back_high = back.astype(jnp.bfloat16)
    back_low = (back - back_high.astype(jnp.float32)).astype(jnp.bfloat16)
    dh_share = contract_rows(adj_two, back_high) + contract_rows(adj_two, back_low)
    dh_share = dh_share + jnp.pad(contract_cols(mine(dz_two), w2_self), ((0, rest), (0, 0)))
    dz_share = (dh_share * silu_grad(z_share)).astype(jnp.bfloat16)
    dz_blocks = spread_parts(dz_share)
    dz_rows = [jnp.concatenate(dz_blocks[begin:end]) for begin, end in cuts]
    grads = [contract_rows(self_two, dz_two), contract_rows(agg_two, dz_two)]
    for rows in (own_rows, mean_rows):
        grads.append(sum(contract_rows(x, y) for x, y in zip(rows, dz_rows)))
    total = total_over_batch(jnp.concatenate(grads)).astype(jnp.float32)
    return (activations, *total.reshape(len(grads), -1, hidden_width))


def solution(mesh):
    in_specs = (
        P("batch", "feat"),
        P("batch", None, None),
        P("batch", None),
        P("batch", None, None),
        P("batch", None),
        P("batch", "feat", None),
        P("batch", "feat"),
        P("batch", "feat", None),
        P("feat", None),
        P("feat", None),
        P(),
        P(),
        P(),
        P(),
    )
    out_specs = (P("batch", "feat", None), P(), P(), P("feat", None), P("feat", None))
    return jax.shard_map(local, mesh=mesh, in_specs=in_specs, out_specs=out_specs, check_vma=False)
```
